32 devices in a mesh: dp: 8 (over z, y), group: 4 (over x, core).
Axes of the slice: x: 2, y: 2, z: 4, core: 2. Of those that a mesh axis runs over, the one named last changes fastest.
Arguments:
- context: bfloat16 [12288, 768], P(('dp', 'group')), may hold values from -6 to 6
- segment_ids: int32 [32, 384], P(('dp', 'group')), may hold values from 0 to 3, never falling along the last dimension, each value on 1 to 192 neighbouring positions
- target_index: int32 [32, 4, 4, 40], P(('dp', 'group')), may hold values from 0 to 195
- target_length: int32 [32, 4, 4], P(('dp', 'group')), may hold values from 1 to 40, as said below
- pos_table: float32 [196, 384], replicated, may hold values from -1 to 1
- params: float32 [2066304], replicated
- first_moment: float32 [2066304], P('dp')
- second_moment: float32 [2066304], P('dp')
- cotangent: bfloat16 [32, 1024, 384], P(('dp', 'group')), may hold values from -6 to 6
Outputs:
- block_out: bfloat16 [32, 1024, 384], P(('dp', 'group'))
- context_grad: bfloat16 [12288, 768], P(('dp', 'group'))
- new_params: float32 [2066304], replicated
- new_first: float32 [2066304], P('dp')
- new_second: float32 [2066304], P('dp')
The draws below stay inside these ranges and needn't reach their ends.
Inputs may be any that keep to these rules, and one draw needn't show every extreme that they name: `target_length`: each packed row has at least one target block of length 40.
All inputs are finite; a program needn't handle non-finite values.
Results may differ from the reference program's by a relative error of at most 0.015.
Values may be sent and summed in bfloat16 or wider, within the bound.
No kernel may reach another device: no remote copies, remote signals or barrier semaphores. Data moves between devices by JAX's collectives and lax.ppermute only.
A program may use at most 256 MiB of HBM per device.

```python
import math
import jax
import jax.numpy as jnp
import numpy as np
from jax import lax

D_IN = 768
D = 384
HEADS = 12
HD = 32
FF = 1536
GRID = 196
BLOCKS = 4
TMAX = 40
CTX_IMG = 96
STEP = 10
IMG = 4
CTX = 384
SEG_MOST = 192
L = 1024
ROWS = 32
NP = 2066304
N_DP = 8
N_GROUP = 4


def moment_scale():
    overall = (N_DP * N_GROUP * (CTX + IMG * BLOCKS * TMAX)) ** 0.5
    pieces = [jnp.full((D_IN * D + 4 * D * D + 2 * D * FF,), 0.5 * overall, jnp.float32), jnp.full((5 * D,), overall, jnp.float32)]
    return jnp.concatenate(pieces)


def draw_params(key, part):
    key = jax.random.fold_in(key, 11)
    noise_all = jax.random.normal(key, (NP,), jnp.float32)
    scales = jnp.concatenate([jnp.full((D_IN * D,), D_IN ** (-0.5), jnp.float32), jnp.full((3 * D * D,), D ** (-0.5), jnp.float32), jnp.full((D * D,), (CTX_IMG / 2.0) ** 0.5 * D ** (-0.5), jnp.float32), jnp.full((D * FF,), D ** (-0.5), jnp.float32), jnp.full((FF * D,), FF ** (-0.5), jnp.float32), jnp.full((D,), 0.25, jnp.float32), jnp.full((D,), 0.5, jnp.float32), jnp.full((D,), 0.25, jnp.float32), jnp.full((D,), 0.5, jnp.float32), jnp.full((D,), 1.0, jnp.float32)])
    offsets = jnp.concatenate([jnp.zeros((D_IN * D + 4 * D * D + 2 * D * FF,), jnp.float32), jnp.ones((D,), jnp.float32), jnp.zeros((D,), jnp.float32), jnp.ones((D,), jnp.float32), jnp.zeros((2 * D,), jnp.float32)])
    return offsets + scales * noise_all


def draw_first_moment(key, part):
    key = jax.random.fold_in(key, 23)
    key_sign, key_size = jax.random.split(key)
    sign_all = jnp.where(jax.random.bernoulli(key_sign, 0.5, (NP,)), 1.0, -1.0)
    magnitude = jax.random.uniform(key_size, (NP,), jnp.float32, 0.5, 1.5)
    return sign_all * magnitude * moment_scale()


def draw_second_moment(key, part):
    key = jax.random.fold_in(key, 37)
    factor = jnp.exp(jax.random.uniform(key, (NP,), jnp.float32, 0.0, 1.3862944))
    return factor * (0.4 / 0.6) * moment_scale() ** 2


def draw_target_length(key, part):
    key = jax.random.fold_in(key, 5)
    key_len, key_pick = jax.random.split(key)
    lengths = jax.random.randint(key_len, (N_DP * N_GROUP, IMG * BLOCKS), 1, TMAX + 1)
    pick_at = jax.random.randint(key_pick, (N_DP * N_GROUP, 1), 0, IMG * BLOCKS)
    lengths = jnp.where(jnp.arange(IMG * BLOCKS)[None, :] == pick_at, TMAX, lengths)
    return lengths.reshape(N_DP * N_GROUP, IMG, BLOCKS).astype(jnp.int32)


def place_ends(values, rng, low, high):
    index_at = [jax.random.randint(jax.random.fold_in(rng, axis), (), 0, length) for axis, length in enumerate(values.shape)]
    widest = values.shape.index(max(values.shape))
    beside = index_at[:widest] + [(index_at[widest] + 1) % values.shape[widest]] + index_at[widest + 1:]
    return values.at[tuple(index_at)].set(low).at[tuple(beside)].set(high)


def block_levels(key, dims, shards, least, high):
    def one(dim, parts):
        steps = jax.random.uniform(jax.random.fold_in(jax.random.fold_in(key, 6), dim), (parts,), jnp.float32, least / len(shards), high / len(shards))
        return jnp.repeat(jnp.exp(steps), dims[dim] // parts).reshape((-1,) + (1,) * (len(dims) - dim - 1))

    factor_of = one(*shards[0])
    for cut in shards[1:]:
        factor_of = factor_of * one(*cut)
    return factor_of


def split_up(count, total, most, lean):
    portions = [(1 << 20) // math.isqrt(standing ** lean) + 1 for standing in range(2, count + 1)]
    spare, counts = total - most - (count - 1), [1] * (count - 1)
    while spare > 0:
        free = [i for i in range(count - 1) if counts[i] < most]
        pool, remaining = sum([portions[i] for i in free]), spare
        for i in free:
            extra = min(most - counts[i], max(1, remaining * portions[i] // pool), spare)
            counts[i] = counts[i] + extra
            spare = spare - extra
    return np.array([most] + counts)


def ragged(own_key, number_of, total, limit, slope):
    if number_of == 2:
        one = jax.random.randint(own_key, (), max(1, total - limit), min(limit, total - 1) + 1)
        return jnp.stack([one, total - one])
    tallies = jnp.asarray(split_up(number_of, total, limit, slope), jnp.int32)
    twos = (number_of - 1) // 2
    source_of, sink = tallies[1:1 + 2 * twos:2], tallies[2:2 + 2 * twos:2]
    margin = jnp.minimum(source_of - 1, limit - sink)
    passed = jax.random.randint(jax.random.fold_in(own_key, 1), (twos,), 0, 1 << 20) % (margin + 1)
    tallies = tallies.at[1:1 + 2 * twos:2].set(source_of - passed).at[2:2 + 2 * twos:2].set(sink + passed)
    return tallies[jax.random.permutation(jax.random.fold_in(own_key, 2), number_of)]


def scatter_about(key, dims, deviation, reach, cuts=(), kind=jnp.bfloat16):
    entries = jax.random.normal(key, dims, jnp.float32) * deviation
    if len(cuts) > 0:
        entries = block_levels(key, dims, cuts, -0.22, 0.18) * entries
    return jnp.clip(entries, min=-reach, max=reach).astype(kind)


def setup_inputs(seed: int = 0) -> dict:
    seeds = jax.random.split(jax.random.key(seed), 10)
    context = scatter_about(seeds[0], (N_DP * N_GROUP * CTX, D_IN), 1.0, 6.0, ((0, 32),))
    segment_ids = jax.vmap(lambda own: jnp.searchsorted(jnp.cumsum(ragged(own, IMG, CTX, SEG_MOST, 1)), jnp.arange(CTX), side="right"))(jax.random.split(seeds[1], ROWS)).reshape((ROWS, CTX)).astype(jnp.int32)
    target_index = place_ends(jax.random.randint(seeds[2], (ROWS, IMG, BLOCKS, TMAX), 0, GRID), jax.random.fold_in(seeds[2], 1), 0, GRID - 1).astype(jnp.int32)
    target_length = draw_target_length(jax.random.fold_in(seeds[9], 71), 0)
    pos_table = jnp.clip(jax.random.uniform(seeds[4], (GRID, D), jnp.float32, -1.0, 1.0), -1.0, 1.0)
    params = draw_params(jax.random.fold_in(seeds[9], 71), 0)
    first_moment = draw_first_moment(jax.random.fold_in(seeds[9], 71), 0)
    second_moment = draw_second_moment(jax.random.fold_in(seeds[9], 71), 0)
    cotangent = scatter_about(seeds[8], (ROWS, L, D), 1.0, 6.0, ((0, 32),))
    return {"context": context, "segment_ids": segment_ids, "target_index": target_index, "target_length": target_length, "pos_table": pos_table, "params": params, "first_moment": first_moment, "second_moment": second_moment, "cotangent": cotangent}


@jax.custom_vjp
def low(v):
    return lax.optimization_barrier(v.astype(jnp.bfloat16)).astype(jnp.float32)

@jax.custom_vjp
def low_back(v):
    return v

def low_keep(v):
    return (low(v), None)

def low_pass(kept, grad):
    return (grad,)

def back_keep(v):
    return (v, None)

def back_low(kept, grad):
    return (low(grad),)
low.defvjp(low_keep, low_pass)
low_back.defvjp(back_keep, back_low)
norm_eps = 1e-06
mask_value = -1e+30

def matmul(left, right):
    return jnp.dot(left, right, precision=lax.Precision.HIGHEST)

def unpack(flat_weights):
    pieces = []
    offset = 0
    for height, breadth in ((D_IN, D), (D, 3 * D), (D, D), (D, FF), (FF, D), (5, D)):
        pieces.append(flat_weights[offset:offset + height * breadth].reshape(height, breadth))
        offset = offset + height * breadth
    return pieces

def layer_norm(activations, gain_row, bias_row):
    centred = activations - lax.optimization_barrier(jnp.mean(activations, axis=-1, keepdims=True))
    spread = lax.optimization_barrier(jnp.mean(centred * centred, axis=-1, keepdims=True))
    return centred * lax.rsqrt(spread + norm_eps) * gain_row + bias_row

def labels(seg_row, len_row):
    slot_ids = jnp.arange(IMG * BLOCKS * TMAX, dtype=jnp.int32)
    target_image = slot_ids // (BLOCKS * TMAX)
    target_block = slot_ids // TMAX % BLOCKS
    target_live = slot_ids % TMAX < jnp.repeat(len_row.reshape(IMG * BLOCKS), TMAX)
    image_of = jnp.concatenate([seg_row.astype(jnp.int32), target_image])
    block_of = jnp.concatenate([jnp.full((CTX,), BLOCKS, jnp.int32), target_block])
    live_of = jnp.concatenate([jnp.ones((CTX,), jnp.float32), target_live.astype(jnp.float32)])
    return (image_of, block_of, live_of)

def attend(packed, image_of, block_of, live_of):
    length = packed.shape[0]
    queries = packed[:, :D].reshape(length, HEADS, HD)
    keys_all = packed[:, D:2 * D].reshape(length, HEADS, HD)
    values_all = packed[:, 2 * D:].reshape(length, HEADS, HD)
    step_rows = min(512, length)
    key_ok = live_of > 0.5

    def one_block(offset):
        query_block = lax.dynamic_slice_in_dim(queries, offset, step_rows, 0)
        query_image = lax.dynamic_slice_in_dim(image_of, offset, step_rows, 0)
        query_kind = lax.dynamic_slice_in_dim(block_of, offset, step_rows, 0)
        scores = jnp.einsum('qhd,khd->hqk', query_block, keys_all, precision=lax.Precision.HIGHEST) * HD ** (-0.5)
        scores = low_back(scores)
        allowed = (query_image[:, None] == image_of[None, :]) & key_ok[None, :] & ((block_of[None, :] == BLOCKS) | (block_of[None, :] == query_kind[:, None]))
        scores = jnp.where(allowed[None], scores, mask_value)
        row_top = lax.optimization_barrier(jnp.max(scores, axis=-1, keepdims=True))
        weights = jnp.exp(scores - row_top)
        weights = low(weights / lax.optimization_barrier(jnp.sum(weights, axis=-1, keepdims=True)))
        mixed_rows = jnp.einsum('hqk,khd->qhd', weights, values_all, precision=lax.Precision.HIGHEST)
        return mixed_rows.reshape(step_rows, D)
    starts = jnp.arange(length // step_rows, dtype=jnp.int32) * step_rows
    blocks_out = lax.map(jax.checkpoint(one_block), starts)
    return low(low_back(blocks_out.reshape(length, D)))

def row_forward(flat_weights, context_row, seg_row, index_row, len_row, pos_table):
    w_in, w_qkv, w_out, w_up, w_down, small_rows = unpack(flat_weights)
    w_in = low(w_in)
    w_qkv = low(w_qkv)
    w_out = low(w_out)
    w_up = low(w_up)
    w_down = low(w_down)
    hidden_ctx = low_back(matmul(context_row, w_in))
    one_hot = (index_row.reshape(-1)[:, None] == jnp.arange(GRID, dtype=jnp.int32)[None, :]).astype(jnp.float32)
    hidden_tgt = small_rows[4][None, :] + matmul(one_hot, pos_table)
    stream = jnp.concatenate([hidden_ctx, hidden_tgt], axis=0)
    image_of, block_of, live_of = labels(seg_row, len_row)
    normed = low(layer_norm(stream, small_rows[0], small_rows[1]))
    packed = low(low_back(matmul(normed, w_qkv)))
    mixed_rows = attend(packed, image_of, block_of, live_of)
    branch = low_back(matmul(mixed_rows, w_out))
    middle = stream + branch
    second = low(layer_norm(middle, small_rows[2], small_rows[3]))
    lifted = low_back(matmul(second, w_up))
    active = low(jax.nn.gelu(lifted, approximate=False))
    output = middle + low_back(matmul(active, w_down))
    return output * live_of[:, None]

def regroup(context_flat):
    shaped = context_flat.reshape(N_DP, N_GROUP, N_GROUP, CTX // N_GROUP, D_IN)
    return shaped.transpose(0, 2, 1, 3, 4).reshape(N_DP * N_GROUP, CTX, D_IN)

def adam_update(weight, gradient, moment_one, moment_two):
    first_new = 0.5 * moment_one + 0.5 * gradient
    second_new = 0.6 * moment_two + 0.4 * gradient * gradient
    first_hat = first_new / (1.0 - 0.5 ** STEP)
    second_hat = second_new / (1.0 - 0.6 ** STEP)
    weight_new = weight - 0.05 * (first_hat / (jnp.sqrt(second_hat) + 1e-08) + 0.05 * weight)
    return (first_new, second_new, weight_new)

def reference(context, segment_ids, target_index, target_length, pos_table, params, first_moment, second_moment, cotangent):

    def forward(flat_weights, context_flat):
        rows_all = regroup(context_flat)

        def one_row(inputs):
            context_row, seg_row, index_row, len_row = inputs
            return row_forward(flat_weights, context_row, seg_row, index_row, len_row, pos_table)
        return lax.map(jax.checkpoint(one_row), (rows_all, segment_ids, target_index, target_length))
    output, pullback = jax.vjp(forward, params, context.astype(jnp.float32))
    grad_flat, grad_context = pullback(cotangent.astype(jnp.float32))
    new_first, new_second, new_params = adam_update(params, grad_flat, first_moment, second_moment)
    return (output.astype(jnp.bfloat16), grad_context.astype(jnp.bfloat16), new_params, new_first, new_second)
```

```python
import functools

import jax
import jax.numpy as jnp
from jax import lax
from jax.experimental import pallas as pl
from jax.experimental.pallas import tpu as pltpu
from jax.sharding import PartitionSpec as P

D_IN = 768
D = 384
HEADS = 12
HD = 32
FF = 1536
GRID = 196
BLOCKS = 4
TMAX = 40
STEP = 10
IMG = 4
CTX = 384
TGT = IMG * BLOCKS * TMAX
L = CTX + TGT
NP = D_IN * D + 4 * D * D + 2 * D * FF + 5 * D
LANES = 128
GROUPS = D // LANES
PER = LANES // HD
WIN = 200
KEYS = 256
TILE = 256

ROW_IN = 0
ROW_QKV = D_IN * D // LANES
ROW_OUT = ROW_QKV + 3 * D * D // LANES
ROW_UP = ROW_OUT + D * D // LANES
ROW_DOWN = ROW_UP + D * FF // LANES
ROW_SMALL = ROW_DOWN + FF * D // LANES
ROWS_ALL = NP // LANES
SMALL = 5 * D
SMALL_ROWS = SMALL // LANES

norm_eps = 1e-06
mask_value = -1e30
LOG2E = 1.4426950408889634
SCALE = HD**-0.5
F32 = jnp.float32
BF16 = jnp.bfloat16
VMEM_CAP = 60 * 1024 * 1024


def dot(a, b):
    return jnp.dot(a, b, preferred_element_type=F32)


def dot_nt(a, b):
    return lax.dot_general(a, b, (((1,), (1,)), ((), ())), preferred_element_type=F32)


def dot_tn(a, b):
    return lax.dot_general(a, b, (((0,), (0,)), ((), ())), preferred_element_type=F32)


def ceil_to(n, m):
    return -(-n // m) * m


class Plan:
    def __init__(self, n_dp, n_group):
        self.n_dp, self.n_group = n_dp, n_group
        self.share = NP // n_dp
        self.row0 = [d * self.share // LANES for d in range(n_dp)]
        self.lane0 = [d * self.share % LANES for d in range(n_dp)]
        most = max(ceil_to(o + self.share, LANES) // LANES for o in self.lane0)
        self.piece = ceil_to(-(-most // n_group), 16)
        self.shard_rows = self.piece * n_group
        self.half_dp = n_dp // 2
        first = ROW_UP * LANES
        early = [d for d in range(n_dp) if d * self.share >= first]
        self.hi_early = -(-early[0] // 2)
        self.early0 = 2 * self.hi_early
        self.flat_rows = ceil_to(max(r + self.shard_rows for r in self.row0), 16)
        self.mid_rows = ceil_to(self.row0[self.early0 - 1] + self.shard_rows - ROW_UP, 8)


def layer_norm_parts(x):
    mu = jnp.mean(x, axis=-1, keepdims=True)
    xc = x - mu
    rstd = lax.rsqrt(jnp.mean(xc * xc, axis=-1, keepdims=True) + norm_eps)
    return xc * rstd, rstd


def layer_norm_back(dy, gain, xhat, rstd):
    dx = dy * gain
    a = jnp.mean(dx, axis=-1, keepdims=True)
    b = jnp.mean(dx * xhat, axis=-1, keepdims=True)
    return rstd * (dx - a - xhat * b)


def gelu_both(x):
    z = jnp.abs(x) * (0.5**0.5)
    t = 1.0 / (1.0 + 0.3275911 * z)
    e = jnp.exp2(x * x * (-0.5 * LOG2E))
    poly = ((((1.061405429 * t - 1.453152027) * t + 1.421413741) * t - 0.284496736) * t + 0.254829592) * t
    tail = 0.5 * poly * e
    cdf = jnp.where(x >= 0, 1.0 - tail, tail)
    pdf = e * 0.3989422804014327
    return x * cdf, cdf + x * pdf


def head_masks():
    lane = lax.broadcasted_iota(jnp.int32, (1, LANES), 1)
    return [(lane // HD == h).astype(F32) for h in range(PER)]


def stack_heads(x, masks):
    return jnp.concatenate([x * m for m in masks], axis=0)


def fold_heads(x, masks, rows):
    total = x[0:rows] * masks[0]
    for h in range(1, PER):
        total = total + x[h * rows : (h + 1) * rows] * masks[h]
    return total


def lane_slice(g, part):
    return pl.ds(pl.multiple_of(part * D + g * LANES, LANES), LANES)


def forward_kernel(
    plan,
    win_s, len_s, seg_s, own_s,
    params_hbm, ctx_ref, seg_row, seg_col, idx_col, live_col, pos_ref, cot_ref,
    out_ref, keep_ref, send_ref, mid_ref, own_ref,
    w_in_b, w_qkv_b, w_out_b, vec_out,
    stream, qkv, probs_c, probs_t, mixed, d_mixed, d_branch, d_middle, small_out,
    pbuf, w_up_b, w_down_b, vec, normed, bias, second, active, d_lift, e_down, gflat, sems,
):
    spans = [
        (ROW_SMALL, SMALL_ROWS), (ROW_IN, ROW_QKV - ROW_IN), (ROW_QKV, ROW_OUT - ROW_QKV),
        (ROW_OUT, ROW_UP - ROW_OUT), (ROW_UP, ROW_DOWN - ROW_UP), (ROW_DOWN, ROW_SMALL - ROW_DOWN),
    ]
    copies = [
        pltpu.make_async_copy(params_hbm.at[pl.ds(r, n)], pbuf.at[pl.ds(r, n)], sems.at[i])
        for i, (r, n) in enumerate(spans)
    ]
    for c in copies:
        c.start()

    def take(base, rows, tiles, dst, step):
        def body(i, _):
            for c in range(tiles):
                src = pl.ds(base + i * (step * tiles) + c, step, stride=tiles)
                dst[pl.ds(pl.multiple_of(i * step, step), step), c * LANES : (c + 1) * LANES] = pbuf[src, :].astype(BF16)
            return 0
        lax.fori_loop(0, rows // step, body, 0)

    copies[0].wait()
    vec[...] = jnp.zeros_like(vec)
    for k in range(5):
        for c in range(D // LANES):
            vec[k : k + 1, c * LANES : (c + 1) * LANES] = pbuf[pl.ds(ROW_SMALL + k * 3 + c, 1), :]
    vec_out[...] = vec[...]
    gain1, bias1, gain2, bias2, mask_tok = [vec[k : k + 1, :] for k in range(5)]

    pos = pos_ref[...]
    pos_hi = pos.astype(BF16)
    pos_lo = (pos - pos_hi.astype(F32)).astype(BF16)
    for i in range(TGT // 128):
        rows = slice(i * 128, (i + 1) * 128)
        grid_id = lax.broadcasted_iota(jnp.int32, (128, GRID), 1)
        hot = (idx_col[rows, :] == grid_id).astype(F32).astype(BF16)
        stream[CTX + i * 128 : CTX + (i + 1) * 128, :] = mask_tok + (dot(hot, pos_hi) + dot(hot, pos_lo))

    bias[...] = jnp.where(seg_col[...] == seg_row[...], 0.0, mask_value)

    copies[1].wait()
    take(ROW_IN, D_IN, 3, w_in_b, 128)
    stream[0:CTX, :] = dot(ctx_ref[...], w_in_b[...])

    copies[2].wait()
    take(ROW_QKV, D, 9, w_qkv_b, 128)

    def qkv_body(i, _):
        rows = pl.ds(pl.multiple_of(i * TILE, TILE), TILE)
        xhat, _r = layer_norm_parts(stream[rows, :])
        n = (xhat * gain1 + bias1).astype(BF16)
        normed[rows, :] = n
        qkv[rows, :] = dot(n, w_qkv_b[...]).astype(BF16).astype(F32)
        return 0

    lax.fori_loop(0, L // TILE, qkv_body, 0)

    masks = head_masks()
    c2 = SCALE * LOG2E

    def ctx_body(i, _):
        g, chunk = i // 3, i % 3
        rows = pl.ds(pl.multiple_of(chunk * 128, 128), 128)
        q = qkv[rows, lane_slice(g, 0)]
        k = qkv[0:CTX, lane_slice(g, 1)].astype(BF16)
        v = qkv[0:CTX, lane_slice(g, 2)].astype(BF16)
        b = bias[rows, :]
        total = jnp.zeros((128, LANES), F32)
        for h in range(PER):
            t = dot_nt((q * masks[h]).astype(BF16), k) * c2 + b
            p = jnp.exp2(t - jnp.max(t, axis=-1, keepdims=True))
            p = (p * (1.0 / jnp.sum(p, axis=-1, keepdims=True))).astype(BF16)
            probs_c[g * PER + h, rows, :] = p
            total = total + dot(p, v) * masks[h]
        mixed[rows, pl.ds(pl.multiple_of(g * LANES, LANES), LANES)] = total.astype(BF16).astype(F32)
        return 0

    lax.fori_loop(0, GROUPS * 3, ctx_body, 0)

    key_id = lax.broadcasted_iota(jnp.int32, (1, KEYS), 1)
    fill = jnp.zeros((KEYS - WIN - TMAX, LANES), F32)

    def tgt_body(i, _):
        g, img = i // IMG, i % IMG
        first = pl.multiple_of(win_s[img], 8)
        kw = qkv[pl.ds(first, WIN), lane_slice(g, 1)]
        vw = qkv[pl.ds(first, WIN), lane_slice(g, 2)]
        lo, hi = seg_s[img] - first, seg_s[img + 1] - first
        in_win = (key_id >= lo) & (key_id < hi) & (key_id < WIN)
        for blk in range(BLOCKS):
            j = img * BLOCKS + blk
            rows = pl.ds(pl.multiple_of(CTX + j * TMAX, 8), TMAX)
            k = jnp.concatenate([kw, qkv[rows, lane_slice(g, 1)], fill], axis=0).astype(BF16)
            v = jnp.concatenate([vw, qkv[rows, lane_slice(g, 2)], fill], axis=0).astype(BF16)
            q = stack_heads(qkv[rows, lane_slice(g, 0)], masks).astype(BF16)
            ok = in_win | ((key_id >= WIN) & (key_id < WIN + len_s[j]))
            t = dot_nt(q, k) * c2 + jnp.where(ok, 0.0, mask_value)
            p = jnp.exp2(t - jnp.max(t, axis=-1, keepdims=True))
            p = (p * (1.0 / jnp.sum(p, axis=-1, keepdims=True))).astype(BF16)
            probs_t[i * BLOCKS + blk] = p
            mixed[rows, pl.ds(pl.multiple_of(g * LANES, LANES), LANES)] = (
                fold_heads(dot(p, v), masks, TMAX).astype(BF16).astype(F32)
            )
        return 0

    lax.fori_loop(0, GROUPS * IMG, tgt_body, 0)

    copies[3].wait()
    take(ROW_OUT, D, 3, w_out_b, 128)
    copies[4].wait()
    take(ROW_UP, D, 12, w_up_b, 128)
    copies[5].wait()
    take(ROW_DOWN, FF, 3, w_down_b, 128)
    own_ref[...] = pbuf[pl.ds(own_s[0], plan.piece), :]

    def block_body(i, carry):
        dg2, db2 = carry
        rows = pl.ds(pl.multiple_of(i * TILE, TILE), TILE)
        live = live_col[rows, :]
        middle = stream[rows, :] + dot(mixed[rows, :].astype(BF16), w_out_b[...])
        xhat, rstd = layer_norm_parts(middle)
        sec = (xhat * gain2 + bias2).astype(BF16)
        second[rows, :] = sec
        top = live * cot_ref[rows, :].astype(F32)
        e = top.astype(BF16)
        e_down[rows, :] = e
        out = middle
        d_second = jnp.zeros((TILE, D), F32)
        for j in range(4):
            cols = slice(j * D, (j + 1) * D)
            lifted = dot(sec, w_up_b[:, cols])
            act, slope = gelu_both(lifted)
            act = act.astype(BF16)
            active[rows, cols] = act
            dl = (dot_nt(e, w_down_b[cols, :]) * slope).astype(BF16)
            d_lift[rows, cols] = dl
            out = out + dot(act, w_down_b[cols, :])
            d_second = d_second + dot_nt(dl, w_up_b[:, cols])
        out_ref[rows, :] = (live * out).astype(BF16)
        dm = top + layer_norm_back(d_second, gain2, xhat, rstd)
        d_middle[rows, :] = dm
        db = dm.astype(BF16)
        d_branch[rows, :] = db
        d_mixed[rows, :] = dot_nt(db, w_out_b[...]).astype(BF16).astype(F32)
        dg2 = dg2 + jnp.sum(d_second * xhat, axis=0, keepdims=True)
        db2 = db2 + jnp.sum(d_second, axis=0, keepdims=True)
        return dg2, db2

    zero = jnp.zeros((1, D), F32)
    dg2, db2 = lax.fori_loop(0, L // TILE, block_body, (zero, zero))
    small_out[...] = jnp.concatenate([dg2, db2, jnp.zeros((6, D), F32)], axis=0)

    end = ROW_SMALL - ROW_UP
    gflat[end:, :] = jnp.zeros((gflat.shape[0] - end, LANES), F32)

    def up_body(j, _):
        cols = pl.ds(pl.multiple_of(j * D, D), D)
        g = dot_tn(second[...], d_lift[:, cols])
        for c in range(3):
            gflat[pl.ds(3 * j + c, D, stride=12), :] = g[:, c * LANES : (c + 1) * LANES]
        return 0

    lax.fori_loop(0, 4, up_body, 0)

    def down_body(j, _):
        cols = pl.ds(pl.multiple_of(j * D, D), D)
        g = dot_tn(active[:, cols], e_down[...])
        for c in range(3):
            gflat[pl.ds(ROW_DOWN - ROW_UP + j * (3 * D) + c, D, stride=3), :] = g[:, c * LANES : (c + 1) * LANES]
        return 0

    lax.fori_loop(0, 4, down_body, 0)

    mid_ref[...] = gflat[0 : plan.mid_rows, :]
    put_pieces(plan, gflat, ROW_UP, range(plan.early0, plan.n_dp), plan.hi_early, own_s[1], keep_ref, send_ref)


def put_pieces(plan, gflat, base, shards, hi0, core, keep_ref, send_ref):
    for d in shards:
        for q in range(plan.n_group):
            start = plan.row0[d] - base + q * plan.piece
            block = gflat[start : start + plan.piece, :].astype(BF16)

            @pl.when(core == q % 2)
            def _():
                keep_ref[q // 2, d % 2, d // 2 - hi0] = block

            @pl.when(core != q % 2)
            def _():
                send_ref[q // 2, d % 2, d // 2 - hi0] = block


def backward_kernel(
    plan,
    win_s, own_s,
    ctx_ref, w_in_b, w_qkv_b, vec, stream, qkv, probs_c, probs_t, mixed, d_mixed, d_branch, d_middle,
    small_in, mid_ref,
    keep_ref, send_ref, small_out, ctx_grad,
    normed, d_qkv, dpk, d_hidden, gflat,
):
    gain1, bias1 = vec[0:1, :], vec[1:2, :]
    masks = head_masks()

    g = dot_tn(mixed[...].astype(BF16), d_branch[...])
    for c in range(3):
        gflat[pl.ds(ROW_OUT + c, D, stride=3), :] = g[:, c * LANES : (c + 1) * LANES]
    gflat[ROW_UP : ROW_UP + plan.mid_rows, :] = mid_ref[...]

    d_qkv[0:CTX, :] = jnp.zeros((CTX, 3 * D), F32)

    def ctx_body(i, _):
        g, chunk = i // 3, i % 3
        rows = pl.ds(pl.multiple_of(chunk * 128, 128), 128)
        lanes = pl.ds(pl.multiple_of(g * LANES, LANES), LANES)
        q = qkv[rows, lane_slice(g, 0)]
        k = qkv[0:CTX, lane_slice(g, 1)].astype(BF16)
        v = qkv[0:CTX, lane_slice(g, 2)].astype(BF16)
        do = d_mixed[rows, lanes]
        both = do * mixed[rows, lanes]
        dq = jnp.zeros((128, LANES), F32)
        dk = jnp.zeros((CTX, LANES), F32)
        dv = jnp.zeros((CTX, LANES), F32)
        for h in range(PER):
            p = probs_c[g * PER + h, rows, :]
            doh = (do * masks[h]).astype(BF16)
            delta = jnp.sum(both * masks[h], axis=-1, keepdims=True)
            ds = (p.astype(F32) * (dot_nt(doh, v) - delta)).astype(BF16)
            dq = dq + dot(ds, k) * masks[h]
            dk = dk + dot_tn(ds, (q * masks[h]).astype(BF16))
            dv = dv + dot_tn(p, doh)
        d_qkv[rows, lane_slice(g, 0)] = dq
        d_qkv[0:CTX, lane_slice(g, 1)] += dk
        d_qkv[0:CTX, lane_slice(g, 2)] += dv
        return 0

    lax.fori_loop(0, GROUPS * 3, ctx_body, 0)

    fill = jnp.zeros((KEYS - WIN - TMAX, LANES), F32)

    def tgt_body(i, _):
        g, img = i // IMG, i % IMG
        first = pl.multiple_of(win_s[img], 8)
        win = pl.ds(first, WIN)
        lanes = pl.ds(pl.multiple_of(g * LANES, LANES), LANES)
        kw = qkv[win, lane_slice(g, 1)]
        vw = qkv[win, lane_slice(g, 2)]
        dkw = jnp.zeros((WIN, LANES), F32)
        dvw = jnp.zeros((WIN, LANES), F32)
        for blk in range(BLOCKS):
            rows = pl.ds(pl.multiple_of(CTX + (img * BLOCKS + blk) * TMAX, 8), TMAX)
            k = jnp.concatenate([kw, qkv[rows, lane_slice(g, 1)], fill], axis=0).astype(BF16)
            v = jnp.concatenate([vw, qkv[rows, lane_slice(g, 2)], fill], axis=0).astype(BF16)
            q = stack_heads(qkv[rows, lane_slice(g, 0)], masks).astype(BF16)
            do = d_mixed[rows, lanes]
            delta = jnp.sum(stack_heads(do * mixed[rows, lanes], masks), axis=-1, keepdims=True)
            doh = stack_heads(do, masks).astype(BF16)
            p = probs_t[i * BLOCKS + blk]
            ds = (p.astype(F32) * (dot_nt(doh, v) - delta)).astype(BF16)
            d_qkv[rows, lane_slice(g, 0)] = fold_heads(dot(ds, k), masks, TMAX)
            dk = dot_tn(ds, q)
            dv = dot_tn(p, doh)
            d_qkv[rows, lane_slice(g, 1)] = dk[WIN : WIN + TMAX]
            d_qkv[rows, lane_slice(g, 2)] = dv[WIN : WIN + TMAX]
            dkw = dkw + dk[:WIN]
            dvw = dvw + dv[:WIN]
        d_qkv[win, lane_slice(g, 1)] += dkw
        d_qkv[win, lane_slice(g, 2)] += dvw
        return 0

    lax.fori_loop(0, GROUPS * IMG, tgt_body, 0)

    def row_body(i, carry):
        dg1, db1, dmask = carry
        rows = pl.ds(pl.multiple_of(i * 128, 128), 128)
        xhat, rstd = layer_norm_parts(stream[rows, :])
        normed[rows, :] = (xhat * gain1 + bias1).astype(BF16)
        raw = d_qkv[rows, :]
        dp = jnp.concatenate([raw[:, : 2 * D] * SCALE, raw[:, 2 * D :]], axis=1).astype(BF16)
        dpk[rows, :] = dp
        d_normed = dot_nt(dp, w_qkv_b[...])
        d_stream = d_middle[rows, :] + layer_norm_back(d_normed, gain1, xhat, rstd)
        dg1 = dg1 + jnp.sum(d_normed * xhat, axis=0, keepdims=True)
        db1 = db1 + jnp.sum(d_normed, axis=0, keepdims=True)
        is_tgt = (i >= CTX // 128).astype(F32)
        dmask = dmask + is_tgt * jnp.sum(d_stream, axis=0, keepdims=True)

        @pl.when(i < CTX // 128)
        def _():
            d_hidden[rows, :] = d_stream.astype(BF16)

        return dg1, db1, dmask

    zero = jnp.zeros((1, D), F32)
    dg1, db1, dmask = lax.fori_loop(0, L // 128, row_body, (zero, zero, zero))
    small_out[...] = jnp.concatenate([dg1, db1, small_in[0:2, :], dmask, jnp.zeros((3, D), F32)], axis=0)

    ctx_grad[...] = dot_nt(d_hidden[...], w_in_b[...]).astype(BF16)
    for j in range(2):
        g = dot_tn(ctx_ref[:, j * D : (j + 1) * D], d_hidden[...])
        for c in range(3):
            gflat[pl.ds(ROW_IN + j * 3 * D + c, D, stride=3), :] = g[:, c * LANES : (c + 1) * LANES]
    for j in range(3):
        g = dot_tn(normed[...], dpk[:, j * D : (j + 1) * D])
        for c in range(3):
            gflat[pl.ds(ROW_QKV + 3 * j + c, D, stride=9), :] = g[:, c * LANES : (c + 1) * LANES]
    put_pieces(plan, gflat, 0, range(plan.early0), 0, own_s[1], keep_ref, send_ref)


def vmem(n):
    return [pl.BlockSpec(memory_space=pltpu.VMEM)] * n


def smem(n):
    return [pl.BlockSpec(memory_space=pltpu.SMEM)] * n


def shape(dims, dtype):
    return jax.ShapeDtypeStruct(dims, dtype)


def assemble_kernel(plan, own_s, late_refs, early_refs, small_ref, out_ref, late, early, sems):
    n_hi = plan.n_group // 2
    copies = []
    for refs, dst in ((late_refs, late), (early_refs, early)):
        for i, ref in enumerate(refs):
            c_rel, a_rel, b_rel = i // (2 * n_hi), i // 2 % n_hi, i % 2
            core = lax.rem(own_s[1] + c_rel, 2)
            hi = lax.rem(own_s[2] + a_rel, n_hi)
            lo = lax.rem(own_s[3] + b_rel, 2)
            copy = pltpu.make_async_copy(ref, dst.at[core, hi, lo], sems.at[len(copies)])
            copy.start()
            copies.append(copy)
    for copy in copies:
        copy.wait()
    for d in range(plan.n_dp):
        src, hi = (late, d // 2) if d < plan.early0 else (early, d // 2 - plan.hi_early)
        lane0 = plan.lane0[d]
        rows = ceil_to(lane0 + plan.share, LANES) // LANES
        for q in range(plan.n_group):
            start = q * plan.piece
            n = min(plan.piece, rows - start)
            if n <= 0:
                continue
            block = src[q % 2, q // 2, d % 2, hi].astype(F32)
            base = plan.row0[d] + start
            if q == 0 and lane0:
                lane = lax.broadcasted_iota(jnp.int32, (1, LANES), 1)
                out_ref[base : base + 1, :] = jnp.where(lane < lane0, out_ref[base : base + 1, :], block[0:1])
                out_ref[base + 1 : base + n, :] = block[1:n]
            else:
                out_ref[base : base + n, :] = block[:n]
    out_ref[ROW_SMALL:, :] = small_ref[0:SMALL_ROWS, :]


def adam(weight, grad, one, two):
    first = 0.5 * one + 0.5 * grad
    second = 0.6 * two + 0.4 * grad * grad
    step = (first / (1.0 - 0.5**STEP)) / (jnp.sqrt(second / (1.0 - 0.6**STEP)) + 1e-08)
    return first, second, weight - 0.05 * (step + 0.05 * weight)


def build(mesh):
    n_dp, n_group = mesh.shape["dp"], mesh.shape["group"]
    plan = Plan(n_dp, n_group)
    both = ("dp", "group")
    n_hi, half = n_group // 2, n_dp // 2
    piece = plan.piece
    n_late, n_early = plan.hi_early, half - plan.hi_early

    def pairs(move):
        out = []
        for d in range(n_dp):
            for g in range(n_group):
                hit = move(g // 2, g % 2, d // 2, d % 2)
                if hit is None:
                    continue
                ghi, glo, dhi, dlo = hit
                out.append((d * n_group + g, (dhi * 2 + dlo) * n_group + ghi * 2 + glo))
        return out

    core_pairs = pairs(lambda gh, gl, dh, dl: (gh, 1 - gl, dh, dl))

    def xy_pairs(a, b):
        return pairs(lambda gh, gl, dh, dl: ((gh + a) % n_hi, gl, dh, (dl + b) % 2))

    def z_pairs(r, sources, targets):
        def move(gh, gl, dh, dl):
            to = (dh + r) % half
            return (gh, gl, to, dl) if dh in sources and to in targets else None
        return pairs(move)

    rels = [(a, b) for a in range(n_hi) for b in range(2)]

    def pick(array, index):
        return lax.dynamic_index_in_dim(array, index, 0, keepdims=False)

    def add_round(a, b):
        return (a.astype(F32) + b.astype(F32)).astype(BF16)

    def reduce_pieces(keep, send, hi0, count, gh, dh, dl):
        got = lax.ppermute(send, both, core_pairs)

        def block(a, b):
            i, j = (gh + a) % n_hi, (dl + b) % 2
            return add_round(pick(pick(keep, i), j), pick(pick(got, i), j))

        arrived = [
            lax.ppermute(block(a, b), both, xy_pairs(a, b)) for a, b in rels[1:]
        ]
        total = block(0, 0).astype(F32)
        for part in arrived:
            total = total + part.astype(F32)
        total = total.astype(BF16)
        targets = range(hi0, hi0 + count)
        own = pick(total, jnp.clip(dh - hi0, 0, count - 1)).astype(F32)
        for r in range(1, half):
            slot = jnp.clip((dh + r) % half - hi0, 0, count - 1)
            part = lax.ppermute(pick(total, slot), both, z_pairs(r, range(half), targets))
            own = own + part.astype(F32)
        return own

    def gather_pieces(mine, hi0, count, dh):
        sources = range(hi0, hi0 + count)
        got = [mine] + [
            lax.ppermute(mine, both, z_pairs(r, sources, range(half))) for r in range(1, half)
        ]
        blocks = []
        for t in sources:
            rel = (dh - t) % half
            block = got[0]
            for r in range(1, half):
                block = jnp.where(rel == r, got[r], block)
            blocks.append(block)
        block = jnp.stack(blocks)
        near = [block] + [
            lax.ppermute(block, both, xy_pairs(-a, -b)) for a, b in rels[1:]
        ]
        far = [lax.ppermute(b, both, core_pairs) for b in near]
        return near + far

    def gather_group(own):
        low = own.astype(BF16)
        me = lax.axis_index("group")
        got = [low] + [
            lax.ppermute(low, "group", [((i + r) % n_group, i) for i in range(n_group)])
            for r in range(1, n_group)
        ]
        quarters = []
        for q in range(n_group):
            rel = (q - me) % n_group
            part = got[0]
            for r in range(1, n_group):
                part = jnp.where(rel == r, got[r], part)
            quarters.append(part)
        return jnp.concatenate(quarters, axis=0).astype(F32)

    def per_device(
        context, segment_ids, target_index, target_length, pos_table, params, first_moment, second_moment, cotangent
    ):
        stored = context.shape[0]
        dp, me = lax.axis_index("dp"), lax.axis_index("group")
        gh, gl, dh, dl = me // 2, me % 2, dp // 2, dp % 2
        share = plan.share

        arrived = lax.all_to_all(
            context.reshape(n_group, stored // n_group, D_IN), "group", split_axis=0, concat_axis=0, tiled=True
        ).reshape(stored, D_IN)

        seg = segment_ids[0]
        lens = target_length.reshape(-1)
        starts = jnp.sum(seg[None, :] < jnp.arange(IMG + 1, dtype=jnp.int32)[:, None], axis=1).astype(jnp.int32)
        windows = jnp.minimum(starts[:IMG] // 8 * 8, CTX - WIN)
        slot_live = (jnp.arange(TMAX, dtype=jnp.int32)[None, :] < lens[:, None]).astype(F32).reshape(-1)
        live = jnp.concatenate([jnp.ones((CTX,), F32), slot_live])[:, None]
        own_row = (dp * share) // LANES + me * piece
        own_s = jnp.stack([own_row, gl, gh, dl]).astype(jnp.int32)
        params2 = params.reshape(ROWS_ALL, LANES)

        last = dp == n_dp - 1
        tails = jnp.concatenate([first_moment[share - SMALL :], second_moment[share - SMALL :]])
        tails = lax.psum(jnp.where(last, tails, 0.0), "dp")

        fwd_out = [
            shape((L, D), BF16),
            shape((n_hi, 2, n_early, piece, LANES), BF16),
            shape((n_hi, 2, n_early, piece, LANES), BF16),
            shape((plan.mid_rows, LANES), F32),
            shape((piece, LANES), F32),
            shape((D_IN, D), BF16),
            shape((D, 3 * D), BF16),
            shape((D, D), BF16),
            shape((8, D), F32),
            shape((L, D), F32),
            shape((L, 3 * D), F32),
            shape((HEADS, CTX, CTX), BF16),
            shape((GROUPS * IMG * BLOCKS, PER * TMAX, KEYS), BF16),
            shape((L, D), F32),
            shape((L, D), F32),
            shape((L, D), BF16),
            shape((L, D), F32),
            shape((8, D), F32),
        ]
        fwd = pl.pallas_call(
            functools.partial(forward_kernel, plan),
            out_shape=fwd_out,
            in_specs=smem(4) + [pl.BlockSpec(memory_space=pl.ANY)] + vmem(7),
            out_specs=vmem(len(fwd_out)),
            scratch_shapes=[
                pltpu.VMEM((plan.flat_rows, LANES), F32),
                pltpu.VMEM((D, FF), BF16),
                pltpu.VMEM((FF, D), BF16),
                pltpu.VMEM((8, D), F32),
                pltpu.VMEM((L, D), BF16),
                pltpu.VMEM((CTX, CTX), F32),
                pltpu.VMEM((L, D), BF16),
                pltpu.VMEM((L, FF), BF16),
                pltpu.VMEM((L, FF), BF16),
                pltpu.VMEM((L, D), BF16),
                pltpu.VMEM((plan.flat_rows - ROW_UP, LANES), F32),
                pltpu.SemaphoreType.DMA((6,)),
            ],
            compiler_params=pltpu.CompilerParams(vmem_limit_bytes=VMEM_CAP),
        )(
            windows, lens, starts, own_s,
            params2, arrived, segment_ids, seg[:, None], target_index.reshape(-1, 1), live, pos_table, cotangent[0],
        )
        (out, keep_e, send_e, mid, own_w, w_in_b, w_qkv_b, _w_out_b, vec, stream, qkv, probs_c, probs_t, mixed,
         d_mixed, d_branch, d_middle, small_in) = fwd

        bwd_out = [
            shape((n_hi, 2, n_late, piece, LANES), BF16),
            shape((n_hi, 2, n_late, piece, LANES), BF16),
            shape((8, D), F32),
            shape((CTX, D_IN), BF16),
        ]
        keep_l, send_l, small_g, ctx_grad = pl.pallas_call(
            functools.partial(backward_kernel, plan),
            out_shape=bwd_out,
            in_specs=smem(2) + vmem(14),
            out_specs=vmem(len(bwd_out)),
            scratch_shapes=[
                pltpu.VMEM((L, D), BF16),
                pltpu.VMEM((L, 3 * D), F32),
                pltpu.VMEM((L, 3 * D), BF16),
                pltpu.VMEM((CTX, D), BF16),
                pltpu.VMEM((ROW_UP + plan.mid_rows, LANES), F32),
            ],
            compiler_params=pltpu.CompilerParams(vmem_limit_bytes=VMEM_CAP),
        )(
            windows, own_s, arrived, w_in_b, w_qkv_b, vec, stream, qkv, probs_c, probs_t, mixed, d_mixed, d_branch,
            d_middle, small_in, mid,
        )

        context_grad = lax.all_to_all(
            ctx_grad.reshape(n_group, stored // n_group, D_IN), "group", split_axis=0, concat_axis=0, tiled=True
        ).reshape(stored, D_IN)

        lane0 = (dp * share) % LANES
        total = plan.shard_rows * LANES

        def align(moment):
            flat = lax.dynamic_update_slice(jnp.zeros((total,), F32), moment, (lane0,))
            return flat.reshape(plan.shard_rows, LANES)

        one, two = align(first_moment), align(second_moment)
        own_one = lax.dynamic_slice_in_dim(one, me * piece, piece)
        own_two = lax.dynamic_slice_in_dim(two, me * piece, piece)

        own_e = reduce_pieces(keep_e, send_e, plan.hi_early, n_early, gh, dh, dl)
        new_e = adam(own_w, own_e, own_one, own_two)[2].astype(BF16)
        all_e = gather_pieces(new_e, plan.hi_early, n_early, dh)

        own_l = reduce_pieces(keep_l, send_l, 0, n_late, gh, dh, dl)
        new_l = adam(own_w, own_l, own_one, own_two)[2].astype(BF16)
        all_l = gather_pieces(new_l, 0, n_late, dh)

        small_sum = lax.psum(small_g[:5], both).reshape(-1)
        small_first, small_second, small_new = adam(params[NP - SMALL :], small_sum, tails[:SMALL], tails[SMALL:])
        small_new = jnp.pad(small_new.astype(BF16).astype(F32).reshape(SMALL_ROWS, LANES), ((0, 1), (0, 0)))

        own = jnp.where(dh >= plan.hi_early, own_e, own_l)
        grad = gather_group(own).reshape(-1)
        grad = lax.dynamic_slice(grad, (lane0,), (share,))
        first, second, _ = adam(0.0, grad, first_moment, second_moment)
        new_first = jnp.concatenate([first[: share - SMALL], jnp.where(last, small_first, first[share - SMALL :])])
        new_second = jnp.concatenate([second[: share - SMALL], jnp.where(last, small_second, second[share - SMALL :])])

        n_parts = len(all_l)

        def assemble(own_ref, *refs):
            late_refs, early_refs = refs[:n_parts], refs[n_parts : 2 * n_parts]
            assemble_kernel(plan, own_ref, late_refs, early_refs, *refs[2 * n_parts :])

        new_params = pl.pallas_call(
            assemble,
            out_shape=shape((ROWS_ALL, LANES), F32),
            in_specs=smem(1) + [pl.BlockSpec(memory_space=pl.ANY)] * (2 * n_parts) + vmem(1),
            out_specs=pl.BlockSpec(memory_space=pltpu.VMEM),
            scratch_shapes=[
                pltpu.VMEM((2, n_hi, 2, n_late, piece, LANES), BF16),
                pltpu.VMEM((2, n_hi, 2, n_early, piece, LANES), BF16),
                pltpu.SemaphoreType.DMA((2 * n_parts,)),
            ],
            compiler_params=pltpu.CompilerParams(vmem_limit_bytes=VMEM_CAP),
        )(own_s, *all_l, *all_e, small_new)

        return out[None], context_grad, new_params.reshape(-1), new_first, new_second

    return per_device


def solution(mesh):
    return jax.shard_map(
        build(mesh),
        mesh=mesh,
        in_specs=(
            P(("dp", "group"), None),
            P(("dp", "group"), None),
            P(("dp", "group"), None, None, None),
            P(("dp", "group"), None, None),
            P(),
            P(),
            P("dp"),
            P("dp"),
            P(("dp", "group"), None, None),
        ),
        out_specs=(P(("dp", "group"), None, None), P(("dp", "group"), None), P(), P("dp"), P("dp")),
        check_vma=False,
    )
```

```python
import functools

import jax
import jax.numpy as jnp
from jax import lax
from jax.experimental import pallas as pl
from jax.experimental.pallas import tpu as pltpu
from jax.sharding import PartitionSpec as P

D_IN = 768
D = 384
HEADS = 12
HD = 32
FF = 1536
GRID = 196
BLOCKS = 4
TMAX = 40
STEP = 10
IMG = 4
CTX = 384
TGT = IMG * BLOCKS * TMAX
L = CTX + TGT
NP = D_IN * D + 4 * D * D + 2 * D * FF + 5 * D
LANES = 128
GROUPS = D // LANES
PER = LANES // HD
WIN = 200
KEYS = WIN + TMAX
WIDE = 256
TILE = 256

ROW_IN = 0
ROW_QKV = D_IN * D // LANES
ROW_OUT = ROW_QKV + 3 * D * D // LANES
ROW_UP = ROW_OUT + D * D // LANES
ROW_DOWN = ROW_UP + D * FF // LANES
ROW_SMALL = ROW_DOWN + FF * D // LANES
ROWS_ALL = NP // LANES
SMALL = 5 * D
SMALL_ROWS = SMALL // LANES
SMALL_PAD = 16

norm_eps = 1e-06
mask_value = -1e30
LOG2E = 1.4426950408889634
SCALE = HD**-0.5
F32 = jnp.float32
BF16 = jnp.bfloat16
VMEM_CAP = 60 * 1024 * 1024


def dot(a, b):
    return jnp.dot(a, b, preferred_element_type=F32)


def dot_nt(a, b):
    return lax.dot_general(a, b, (((1,), (1,)), ((), ())), preferred_element_type=F32)


def dot_tn(a, b):
    return lax.dot_general(a, b, (((0,), (0,)), ((), ())), preferred_element_type=F32)


def ceil_to(n, m):
    return -(-n // m) * m


class Plan:
    def __init__(self, n_dp, n_group):
        self.n_dp, self.n_group = n_dp, n_group
        self.share = NP // n_dp
        self.row0 = [d * self.share // LANES for d in range(n_dp)]
        self.lane0 = [d * self.share % LANES for d in range(n_dp)]
        most = max(ceil_to(o + self.share, LANES) // LANES for o in self.lane0)
        self.piece = ceil_to(-(-most // n_group), 16)
        self.shard_rows = self.piece * n_group
        self.half_dp = n_dp // 2
        self.helper = 1
        first = ROW_UP * LANES
        early = [d for d in range(n_dp) if d * self.share >= first]
        self.hi_early = -(-early[0] // 2)
        self.early0 = 2 * self.hi_early
        self.flat_rows = ceil_to(max(r + self.shard_rows for r in self.row0), 16)
        self.mid_rows = ceil_to(self.row0[self.early0 - 1] + self.shard_rows - ROW_OUT, 8)


def layer_norm_parts(x):
    mu = jnp.mean(x, axis=-1, keepdims=True)
    xc = x - mu
    rstd = lax.rsqrt(jnp.mean(xc * xc, axis=-1, keepdims=True) + norm_eps)
    return xc * rstd, rstd


def layer_norm_back(dy, gain, xhat, rstd):
    dx = dy * gain
    a = jnp.mean(dx, axis=-1, keepdims=True)
    b = jnp.mean(dx * xhat, axis=-1, keepdims=True)
    return rstd * (dx - a - xhat * b)


def reciprocal(x):
    r = pl.reciprocal(x, approx=True)
    return r * (2.0 - x * r)


def gelu_both(x):
    z = jnp.abs(x) * (0.5**0.5)
    t = reciprocal(1.0 + 0.3275911 * z)
    e = jnp.exp2(x * x * (-0.5 * LOG2E))
    poly = ((((1.061405429 * t - 1.453152027) * t + 1.421413741) * t - 0.284496736) * t + 0.254829592) * t
    tail = 0.5 * poly * e
    cdf = jnp.where(x >= 0, 1.0 - tail, tail)
    pdf = e * 0.3989422804014327
    return x * cdf, cdf + x * pdf


def head_masks(first, count, width):
    lane = lax.broadcasted_iota(jnp.int32, (1, width), 1)
    return [(lane // HD == first + h).astype(F32) for h in range(count)]


def stack_heads(x, masks):
    return jnp.concatenate([x * m for m in masks], axis=0)


def diagonal(x, rows):
    return jnp.concatenate(
        [x[h * HD : (h + 1) * HD, h * rows : (h + 1) * rows] for h in range(PER)], axis=0
    )


def stack_six(x, masks):
    gap = jnp.zeros((WIDE // 2 - 3 * TMAX, WIDE), F32)
    parts = [x * m for m in masks]
    return jnp.concatenate(parts[:3] + [gap] + parts[3:] + [gap], axis=0).astype(BF16)


def fold_six(x, masks):
    total = None
    for h in range(6):
        at = (h // 3) * (WIDE // 2) + (h % 3) * TMAX
        part = x[at : at + TMAX] * masks[h]
        total = part if total is None else total + part
    return total


def half_masks(half):
    lane = lax.broadcasted_iota(jnp.int32, (1, WIDE), 1)
    head = (lane + half * LANES) // HD
    return [(head == 6 * half + h).astype(F32) for h in range(6)]


def half_slice(half, part):
    return pl.ds(pl.multiple_of(part * D + half * LANES, LANES), WIDE)


def lane_slice(g, part):
    return pl.ds(pl.multiple_of(part * D + g * LANES, LANES), LANES)


def forward_kernel(
    plan,
    win_s, len_s, seg_s, own_s,
    params_hbm, one_hbm, two_hbm, ctx_ref, seg_row, seg_col, idx_col, live_col, pos_ref, cot_ref,
    out_ref, keep_ref, send_ref, mid_ref, own_ref, own_one, own_two, vec_out, small_out,
    w_in_hbm, w_qkv_hbm, stream_hbm, qkv_hbm, probs_c_hbm, probs_t_hbm, d_mixed_hbm, d_middle_hbm,
    w_in_b, w_qkv_b, w_out_b, stream, qkv, probs_c, probs_t, mixed, mixed_b, d_mixed, d_branch, d_middle,
    pbuf, w_up_b, w_down_b, vec, normed, bias, v_t, second, active, d_lift, e_down, gflat, mom, sems, out_sems,
):
    spans = [
        (ROW_SMALL, SMALL_ROWS), (ROW_IN, ROW_QKV - ROW_IN), (ROW_QKV, ROW_OUT - ROW_QKV),
        (ROW_OUT, ROW_UP - ROW_OUT), (ROW_UP, ROW_DOWN - ROW_UP), (ROW_DOWN, ROW_SMALL - ROW_DOWN),
    ]
    copies = [
        pltpu.make_async_copy(params_hbm.at[pl.ds(r, n)], pbuf.at[pl.ds(r, n)], sems.at[i])
        for i, (r, n) in enumerate(spans)
    ]
    for c in copies:
        c.start()
    moments = [
        pltpu.make_async_copy(src.at[pl.ds(own_s[4], plan.piece + 8)], mom.at[i], sems.at[6 + i])
        for i, src in enumerate((one_hbm, two_hbm))
    ]
    for c in moments:
        c.start()
    outgoing = []

    def send_out(src, dst):
        copy = pltpu.make_async_copy(src, dst, out_sems.at[len(outgoing)])
        copy.start()
        outgoing.append(copy)

    def take(base, rows, tiles, dst, step):
        def body(i, _):
            for c in range(tiles):
                src = pl.ds(base + i * (step * tiles) + c, step, stride=tiles)
                dst[pl.ds(pl.multiple_of(i * step, step), step), c * LANES : (c + 1) * LANES] = pbuf[src, :].astype(BF16)
            return 0
        lax.fori_loop(0, rows // step, body, 0)

    copies[0].wait()
    vec[...] = jnp.zeros_like(vec)
    for k in range(5):
        for c in range(D // LANES):
            vec[k : k + 1, c * LANES : (c + 1) * LANES] = pbuf[pl.ds(ROW_SMALL + k * 3 + c, 1), :]
    vec_out[...] = vec[...]
    gain1, bias1, gain2, bias2, mask_tok = [vec[k : k + 1, :] for k in range(5)]

    pos = pos_ref[...]
    pos_hi = pos.astype(BF16)
    pos_lo = (pos - pos_hi.astype(F32)).astype(BF16)
    for i in range(TGT // 128):
        rows = slice(i * 128, (i + 1) * 128)
        grid_id = lax.broadcasted_iota(jnp.int32, (128, GRID), 1)
        hot = (idx_col[rows, :] == grid_id).astype(F32).astype(BF16)
        stream[CTX + i * 128 : CTX + (i + 1) * 128, :] = mask_tok + (dot(hot, pos_hi) + dot(hot, pos_lo))

    bias[...] = jnp.where(seg_col[...] == seg_row[...], 0.0, mask_value)

    copies[1].wait()
    take(ROW_IN, D_IN, 3, w_in_b, 128)
    stream[0:CTX, :] = dot(ctx_ref[...], w_in_b[...])
    send_out(w_in_b, w_in_hbm)
    send_out(stream, stream_hbm)

    copies[2].wait()
    take(ROW_QKV, D, 9, w_qkv_b, 128)
    send_out(w_qkv_b, w_qkv_hbm)

    def qkv_body(i, _):
        rows = pl.ds(pl.multiple_of(i * TILE, TILE), TILE)
        xhat, _r = layer_norm_parts(stream[rows, :])
        n = (xhat * gain1 + bias1).astype(BF16)
        normed[rows, :] = n
        qkv[rows, :] = dot(n, w_qkv_b[...]).astype(BF16).astype(F32)
        return 0

    lax.fori_loop(0, L // TILE, qkv_body, 0)

    send_out(qkv, qkv_hbm)
    masks = head_masks(0, PER, LANES)
    c2 = SCALE * LOG2E
    for g in range(GROUPS):
        v_t[g * LANES : (g + 1) * LANES, :] = qkv[0:CTX, 2 * D + g * LANES : 2 * D + (g + 1) * LANES].T.astype(BF16)

    def softmax_down(t):
        p = jnp.exp2(t - jnp.max(t, axis=0, keepdims=True))
        return (p * (1.0 / jnp.sum(p, axis=0, keepdims=True))).astype(BF16)

    def ctx_body(i, _):
        g, chunk = i // 3, i % 3
        rows = pl.ds(pl.multiple_of(chunk * LANES, LANES), LANES)
        lanes = pl.ds(pl.multiple_of(g * LANES, LANES), LANES)
        q = stack_heads(qkv[rows, lane_slice(g, 0)], masks).astype(BF16)
        st = dot_nt(qkv[0:CTX, lane_slice(g, 1)].astype(BF16), q)
        for h in range(PER):
            cols = slice(h * LANES, (h + 1) * LANES)
            probs_c[i, :, cols] = softmax_down(st[:, cols] * c2 + bias[:, rows])
        o = dot(v_t[lanes, :], probs_c[i])
        mixed[rows, lanes] = diagonal(o, LANES).T
        return 0

    lax.fori_loop(0, GROUPS * 3, ctx_body, 0)
    send_out(probs_c, probs_c_hbm)

    key_id = lax.broadcasted_iota(jnp.int32, (KEYS, 1), 0)
    mixed[CTX:, :] = jnp.zeros((TGT, D), F32)

    def tgt_body(i, _):
        half, img = i // IMG, i % IMG
        hmasks = half_masks(half)
        first = pl.multiple_of(win_s[img], 8)
        kw = qkv[pl.ds(first, WIN), half_slice(half, 1)]
        vw = qkv[pl.ds(first, WIN), half_slice(half, 2)]
        lo, hi = seg_s[img] - first, seg_s[img + 1] - first
        in_win = (key_id >= lo) & (key_id < hi) & (key_id < WIN)
        units = []
        for blk in range(BLOCKS):
            j = img * BLOCKS + blk
            rows = pl.ds(pl.multiple_of(CTX + j * TMAX, 8), TMAX)
            k = jnp.concatenate([kw, qkv[rows, half_slice(half, 1)]], axis=0).astype(BF16)
            v = jnp.concatenate([vw, qkv[rows, half_slice(half, 2)]], axis=0).astype(BF16)
            q = stack_six(qkv[rows, half_slice(half, 0)], hmasks)
            ok = in_win | ((key_id >= WIN) & (key_id < WIN + len_s[j]))
            units.append((rows, v, dot_nt(k, q), jnp.where(ok, 0.0, mask_value)))
        for blk, (rows, v, st, bias_col) in enumerate(units):
            for n in range(2):
                cols = slice(n * LANES, (n + 1) * LANES)
                probs_t[i * BLOCKS + blk, :, cols] = softmax_down(st[:, cols] * c2 + bias_col)
        for blk, (rows, v, st, bias_col) in enumerate(units):
            o = dot_tn(probs_t[i * BLOCKS + blk], v)
            mixed[rows, pl.ds(pl.multiple_of(half * LANES, LANES), WIDE)] += fold_six(o, hmasks)
        return 0

    lax.fori_loop(0, 2 * IMG, tgt_body, 0)
    send_out(probs_t, probs_t_hbm)

    copies[3].wait()
    take(ROW_OUT, D, 3, w_out_b, 128)
    copies[4].wait()
    take(ROW_UP, D, 12, w_up_b, 128)
    copies[5].wait()
    take(ROW_DOWN, FF, 3, w_down_b, 128)
    own_ref[...] = pbuf[pl.ds(own_s[0], plan.piece), :]
    lane = lax.broadcasted_iota(jnp.int32, (1, LANES), 1)
    for i, dst in enumerate((own_one, own_two)):
        moments[i].wait()
        turned = pltpu.roll(mom[i], own_s[5], 1)
        dst[...] = jnp.where(lane >= own_s[5], turned[8:], turned[7:-1])

    def mixed_of(rows):
        low = mixed[rows, :].astype(BF16)
        mixed_b[rows, :] = low
        return low

    def block_body(i, carry):
        dg2, db2 = carry
        rows = pl.ds(pl.multiple_of(i * TILE, TILE), TILE)
        live = live_col[rows, :]
        middle = stream[rows, :] + dot(mixed_of(rows), w_out_b[...])
        xhat, rstd = layer_norm_parts(middle)
        sec = (xhat * gain2 + bias2).astype(BF16)
        second[rows, :] = sec
        top = live * cot_ref[rows, :].astype(F32)
        e = top.astype(BF16)
        e_down[rows, :] = e
        out = middle
        d_second = jnp.zeros((TILE, D), F32)
        for j in range(4):
            cols = slice(j * D, (j + 1) * D)
            lifted = dot(sec, w_up_b[:, cols])
            act, slope = gelu_both(lifted)
            act = act.astype(BF16)
            active[rows, cols] = act
            dl = (dot_nt(e, w_down_b[cols, :]) * slope).astype(BF16)
            d_lift[rows, cols] = dl
            out = out + dot(act, w_down_b[cols, :])
            d_second = d_second + dot_nt(dl, w_up_b[:, cols])
        out_ref[rows, :] = (live * out).astype(BF16)
        dm = top + layer_norm_back(d_second, gain2, xhat, rstd)
        d_middle[rows, :] = dm
        db = dm.astype(BF16)
        d_branch[rows, :] = db
        d_mixed[rows, :] = dot_nt(db, w_out_b[...])
        dg2 = dg2 + jnp.sum(d_second * xhat, axis=0, keepdims=True)
        db2 = db2 + jnp.sum(d_second, axis=0, keepdims=True)
        return dg2, db2

    zero = jnp.zeros((1, D), F32)
    dg2, db2 = lax.fori_loop(0, L // TILE, block_body, (zero, zero))
    small_out[...] = jnp.concatenate([dg2, db2, jnp.zeros((6, D), F32)], axis=0)

    send_out(d_mixed, d_mixed_hbm)
    send_out(d_middle, d_middle_hbm)

    end = ROW_SMALL - ROW_OUT
    gflat[end:, :] = jnp.zeros((gflat.shape[0] - end, LANES), F32)

    g = dot_tn(mixed_b[...], d_branch[...])
    for c in range(3):
        gflat[pl.ds(c, D, stride=3), :] = g[:, c * LANES : (c + 1) * LANES]

    def up_body(j, _):
        cols = pl.ds(pl.multiple_of(j * D, D), D)
        g = dot_tn(second[...], d_lift[:, cols])
        for c in range(3):
            gflat[pl.ds(ROW_UP - ROW_OUT + 3 * j + c, D, stride=12), :] = g[:, c * LANES : (c + 1) * LANES]
        return 0

    lax.fori_loop(0, 4, up_body, 0)

    def down_body(j, _):
        cols = pl.ds(pl.multiple_of(j * D, D), D)
        g = dot_tn(active[:, cols], e_down[...])
        for c in range(3):
            gflat[pl.ds(ROW_DOWN - ROW_OUT + j * (3 * D) + c, D, stride=3), :] = g[:, c * LANES : (c + 1) * LANES]
        return 0

    lax.fori_loop(0, 4, down_body, 0)

    mid_ref[...] = gflat[0 : plan.mid_rows, :]
    put_pieces(plan, gflat, ROW_OUT, range(plan.early0, plan.n_dp), plan.hi_early, own_s[1], keep_ref, send_ref)
    for copy in outgoing:
        copy.wait()


def put_pieces(plan, gflat, base, shards, hi0, core, keep_ref, send_ref, extra=None):
    for d in shards:
        for q in range(plan.n_group):
            start = plan.row0[d] - base + q * plan.piece
            block = gflat[start : start + plan.piece, :].astype(BF16)

            def put(ref):
                ref[q // 2, d % 2, d // 2 - hi0, 0 : plan.piece, :] = block
                if extra is not None:
                    ref[q // 2, d % 2, d // 2 - hi0, plan.piece :, :] = extra

            @pl.when(core == q % 2)
            def _():
                put(keep_ref)

            @pl.when(core != q % 2)
            def _():
                put(send_ref)


def backward_kernel(
    plan,
    win_s, own_s,
    ctx_ref, vec, small_in, mid_ref,
    w_in_hbm, w_qkv_hbm, stream_hbm, qkv_hbm, probs_c_hbm, probs_t_hbm, d_mixed_hbm, d_middle_hbm,
    keep_ref, send_ref, ctx_grad,
    w_in_b, w_qkv_b, stream, qkv, probs_c, probs_t, d_mixed, d_middle,
    normed, d_qkv, dpk, d_hidden, k_t, small_flat, gflat, sems,
):
    incoming = {}
    for n, (name, src, dst) in enumerate((
        ("qkv", qkv_hbm, qkv), ("d_mixed", d_mixed_hbm, d_mixed), ("probs_c", probs_c_hbm, probs_c),
        ("probs_t", probs_t_hbm, probs_t), ("w_qkv", w_qkv_hbm, w_qkv_b), ("stream", stream_hbm, stream),
        ("d_middle", d_middle_hbm, d_middle), ("w_in", w_in_hbm, w_in_b),
    )):
        incoming[name] = pltpu.make_async_copy(src, dst, sems.at[n])
        incoming[name].start()

    gain1, bias1 = vec[0:1, :], vec[1:2, :]
    gflat[ROW_OUT : ROW_OUT + plan.mid_rows, :] = mid_ref[...]
    d_qkv[...] = jnp.zeros_like(d_qkv)
    masks = head_masks(0, PER, LANES)
    incoming["qkv"].wait()
    for g in range(GROUPS):
        k_t[g * LANES : (g + 1) * LANES, :] = qkv[0:CTX, D + g * LANES : D + (g + 1) * LANES].T.astype(BF16)
    incoming["d_mixed"].wait()
    incoming["probs_c"].wait()

    def back_down(p, dp):
        p = p.astype(F32)
        delta = jnp.sum(p * dp, axis=0, keepdims=True)
        return (p * (dp - delta)).astype(BF16)

    def ctx_body(i, _):
        g, chunk = i // 3, i % 3
        rows = pl.ds(pl.multiple_of(chunk * LANES, LANES), LANES)
        lanes = pl.ds(pl.multiple_of(g * LANES, LANES), LANES)
        do = stack_heads(d_mixed[rows, lanes], masks).astype(BF16)
        dpt = dot_nt(qkv[0:CTX, lane_slice(g, 2)].astype(BF16), do)
        ds = []
        for h in range(PER):
            cols = slice(h * LANES, (h + 1) * LANES)
            ds.append(back_down(probs_c[i, :, cols], dpt[:, cols]))
        ds = jnp.concatenate(ds, axis=1)
        q = stack_heads(qkv[rows, lane_slice(g, 0)], masks).astype(BF16)
        d_qkv[rows, lane_slice(g, 0)] = diagonal(dot(k_t[lanes, :], ds), LANES).T
        d_qkv[0:CTX, lane_slice(g, 1)] += dot(ds, q)
        d_qkv[0:CTX, lane_slice(g, 2)] += dot(probs_c[i], do)
        return 0

    lax.fori_loop(0, GROUPS * 3, ctx_body, 0)
    incoming["probs_t"].wait()

    def tgt_body(i, _):
        half, img = i // IMG, i % IMG
        hmasks = half_masks(half)
        first = pl.multiple_of(win_s[img], 8)
        win = pl.ds(first, WIN)
        kw = qkv[win, half_slice(half, 1)]
        vw = qkv[win, half_slice(half, 2)]
        units = []
        for blk in range(BLOCKS):
            rows = pl.ds(pl.multiple_of(CTX + (img * BLOCKS + blk) * TMAX, 8), TMAX)
            v = jnp.concatenate([vw, qkv[rows, half_slice(half, 2)]], axis=0).astype(BF16)
            do = stack_six(d_mixed[rows, pl.ds(pl.multiple_of(half * LANES, LANES), WIDE)], hmasks)
            units.append((rows, do, dot_nt(v, do)))
        dkw = jnp.zeros((WIN, WIDE), F32)
        dvw = jnp.zeros((WIN, WIDE), F32)
        for blk, (rows, do, dpt) in enumerate(units):
            p = probs_t[i * BLOCKS + blk]
            ds = jnp.concatenate(
                [back_down(p[:, n * LANES : (n + 1) * LANES], dpt[:, n * LANES : (n + 1) * LANES]) for n in range(2)],
                axis=1,
            )
            k = jnp.concatenate([kw, qkv[rows, half_slice(half, 1)]], axis=0).astype(BF16)
            q = stack_six(qkv[rows, half_slice(half, 0)], hmasks)
            d_qkv[rows, half_slice(half, 0)] += fold_six(dot_tn(ds, k), hmasks)
            dk = dot(ds, q)
            dv = dot(p, do)
            d_qkv[rows, half_slice(half, 1)] += dk[WIN:]
            d_qkv[rows, half_slice(half, 2)] += dv[WIN:]
            dkw = dkw + dk[:WIN]
            dvw = dvw + dv[:WIN]
        d_qkv[win, half_slice(half, 1)] += dkw
        d_qkv[win, half_slice(half, 2)] += dvw
        return 0

    lax.fori_loop(0, 2 * IMG, tgt_body, 0)
    for name in ("w_qkv", "stream", "d_middle"):
        incoming[name].wait()

    def row_body(i, carry):
        dg1, db1, dmask = carry
        rows = pl.ds(pl.multiple_of(i * 128, 128), 128)
        xhat, rstd = layer_norm_parts(stream[rows, :])
        normed[rows, :] = (xhat * gain1 + bias1).astype(BF16)
        raw = d_qkv[rows, :]
        dp = jnp.concatenate([raw[:, : 2 * D] * SCALE, raw[:, 2 * D :]], axis=1).astype(BF16)
        dpk[rows, :] = dp
        d_normed = dot_nt(dp, w_qkv_b[...])
        d_stream = d_middle[rows, :] + layer_norm_back(d_normed, gain1, xhat, rstd)
        dg1 = dg1 + jnp.sum(d_normed * xhat, axis=0, keepdims=True)
        db1 = db1 + jnp.sum(d_normed, axis=0, keepdims=True)
        is_tgt = (i >= CTX // 128).astype(F32)
        dmask = dmask + is_tgt * jnp.sum(d_stream, axis=0, keepdims=True)

        @pl.when(i < CTX // 128)
        def _():
            d_hidden[rows, :] = d_stream.astype(BF16)

        return dg1, db1, dmask

    zero = jnp.zeros((1, D), F32)
    dg1, db1, dmask = lax.fori_loop(0, L // 128, row_body, (zero, zero, zero))
    for k, row in enumerate((dg1, db1, small_in[0:1, :], small_in[1:2, :], dmask)):
        for c in range(3):
            small_flat[3 * k + c : 3 * k + c + 1, :] = row[:, c * LANES : (c + 1) * LANES]
    small_flat[SMALL_ROWS:, :] = jnp.zeros((SMALL_PAD - SMALL_ROWS, LANES), F32)

    incoming["w_in"].wait()
    ctx_grad[...] = dot_nt(d_hidden[...], w_in_b[...]).astype(BF16)
    for j in range(2):
        g = dot_tn(ctx_ref[:, j * D : (j + 1) * D], d_hidden[...])
        for c in range(3):
            gflat[pl.ds(ROW_IN + j * 3 * D + c, D, stride=3), :] = g[:, c * LANES : (c + 1) * LANES]
    for j in range(3):
        g = dot_tn(normed[...], dpk[:, j * D : (j + 1) * D])
        for c in range(3):
            gflat[pl.ds(ROW_QKV + 3 * j + c, D, stride=9), :] = g[:, c * LANES : (c + 1) * LANES]
    put_pieces(plan, gflat, 0, range(plan.early0), 0, own_s[1], keep_ref, send_ref, small_flat[...].astype(BF16))


def vmem(n):
    return [pl.BlockSpec(memory_space=pltpu.VMEM)] * n


def smem(n):
    return [pl.BlockSpec(memory_space=pltpu.SMEM)] * n


def shape(dims, dtype):
    return jax.ShapeDtypeStruct(dims, dtype)


def assemble_kernel(plan, own_s, late_refs, early_refs, out_ref, late, early, sems):
    n_hi = plan.n_group // 2
    copies = []
    for refs, dst in ((late_refs, late), (early_refs, early)):
        for i, ref in enumerate(refs):
            c_rel, a_rel, b_rel = i // (2 * n_hi), i // 2 % n_hi, i % 2
            core = lax.rem(own_s[1] + c_rel, 2)
            hi = lax.rem(own_s[2] + a_rel, n_hi)
            lo = lax.rem(own_s[3] + b_rel, 2)
            copy = pltpu.make_async_copy(ref, dst.at[core, hi, lo], sems.at[len(copies)])
            copy.start()
            copies.append(copy)
    for copy in copies:
        copy.wait()
    for d in range(plan.n_dp):
        src, hi = (late, d // 2) if d < plan.early0 else (early, d // 2 - plan.hi_early)
        lane0 = plan.lane0[d]
        rows = ceil_to(lane0 + plan.share, LANES) // LANES
        for q in range(plan.n_group):
            start = q * plan.piece
            n = min(plan.piece, rows - start)
            if n <= 0:
                continue
            block = src[q % 2, q // 2, d % 2, hi, 0 : plan.piece, :].astype(F32)
            base = plan.row0[d] + start
            if q == 0 and lane0:
                lane = lax.broadcasted_iota(jnp.int32, (1, LANES), 1)
                out_ref[base : base + 1, :] = jnp.where(lane < lane0, out_ref[base : base + 1, :], block[0:1])
                out_ref[base + 1 : base + n, :] = block[1:n]
            else:
                out_ref[base : base + n, :] = block[:n]
    small = late[0, 0, plan.helper % 2, plan.helper // 2, plan.piece :, :].astype(F32)
    out_ref[ROW_SMALL:, :] = small[:SMALL_ROWS]


def moment_kernel(plan, own_s, own_ref, got_refs, small_ref, one_ref, two_ref, first_ref, second_ref, grad):
    rows = plan.shard_rows
    parts = [own_ref[...]] + [ref[...].astype(F32) for ref in got_refs]
    for r, part in enumerate(parts):
        at = pl.multiple_of(lax.rem(own_s[6] + r, plan.n_group) * plan.piece, 16)
        grad[pl.ds(at, plan.piece), :] = part
    grad[rows:, :] = jnp.zeros((8, LANES), F32)

    @pl.when(own_s[7] == plan.n_dp - 1)
    def _():
        at = ROW_SMALL - plan.row0[-1]
        grad[at : at + SMALL_ROWS, :] = small_ref[0:SMALL_ROWS, :]

    lane = lax.broadcasted_iota(jnp.int32, (1, LANES), 1)
    back = LANES - own_s[5]
    for i in range(plan.n_group):
        at = slice(i * plan.piece, (i + 1) * plan.piece)
        turned = pltpu.roll(grad[i * plan.piece : (i + 1) * plan.piece + 8, :], back, 1)
        g = jnp.where(lane < back, turned[: plan.piece], turned[1 : plan.piece + 1])
        first_ref[at, :] = 0.5 * one_ref[8 + i * plan.piece : 8 + (i + 1) * plan.piece, :] + 0.5 * g
        second_ref[at, :] = 0.6 * two_ref[8 + i * plan.piece : 8 + (i + 1) * plan.piece, :] + 0.4 * g * g


def adam(weight, grad, one, two):
    first = 0.5 * one + 0.5 * grad
    second = 0.6 * two + 0.4 * grad * grad
    step = (first / (1.0 - 0.5**STEP)) / (jnp.sqrt(second / (1.0 - 0.6**STEP)) + 1e-08)
    return weight - 0.05 * (step + 0.05 * weight)


def build(mesh):
    n_dp, n_group = mesh.shape["dp"], mesh.shape["group"]
    plan = Plan(n_dp, n_group)
    both = ("dp", "group")
    n_hi, half = n_group // 2, n_dp // 2
    piece = plan.piece
    n_late, n_early = plan.hi_early, half - plan.hi_early

    def pairs(move):
        out = []
        for d in range(n_dp):
            for g in range(n_group):
                hit = move(g // 2, g % 2, d // 2, d % 2)
                if hit is None:
                    continue
                ghi, glo, dhi, dlo = hit
                out.append((d * n_group + g, (dhi * 2 + dlo) * n_group + ghi * 2 + glo))
        return out

    core_pairs = pairs(lambda gh, gl, dh, dl: (gh, 1 - gl, dh, dl))

    def xy_pairs(a, b):
        return pairs(lambda gh, gl, dh, dl: ((gh + a) % n_hi, gl, dh, (dl + b) % 2))

    def z_pairs(r, sources, targets):
        def move(gh, gl, dh, dl):
            to = (dh + r) % half
            return (gh, gl, to, dl) if dh in sources and to in targets else None
        return pairs(move)

    rels = [(a, b) for a in range(n_hi) for b in range(2)]

    def pick(array, index):
        return lax.dynamic_index_in_dim(array, index, 0, keepdims=False)

    def add_round(a, b):
        return (a.astype(F32) + b.astype(F32)).astype(BF16)

    def reduce_pieces(keep, send, hi0, count, dh, gh, dl):
        got = lax.ppermute(send, both, core_pairs)

        def block(a, b):
            i, j = (gh + a) % n_hi, (dl + b) % 2
            return add_round(pick(pick(keep, i), j), pick(pick(got, i), j))

        arrived = [
            lax.ppermute(block(a, b), both, xy_pairs(a, b)) for a, b in rels[1:]
        ]
        total = block(0, 0).astype(F32)
        for part in arrived:
            total = total + part.astype(F32)
        total = total.astype(BF16)
        targets = range(hi0, hi0 + count)
        own = pick(total, jnp.clip(dh - hi0, 0, count - 1)).astype(F32)
        for r in range(1, half):
            slot = jnp.clip((dh + r) % half - hi0, 0, count - 1)
            part = lax.ppermute(pick(total, slot), both, z_pairs(r, range(half), targets))
            own = own + part.astype(F32)
        return own

    def gather_pieces(mine, hi0, count, dh):
        sources = range(hi0, hi0 + count)
        got = [mine] + [
            lax.ppermute(mine, both, z_pairs(r, sources, range(half))) for r in range(1, half)
        ]
        blocks = []
        for t in sources:
            rel = (dh - t) % half
            block = got[0]
            for r in range(1, half):
                block = jnp.where(rel == r, got[r], block)
            blocks.append(block)
        block = jnp.stack(blocks)
        near = [block] + [
            lax.ppermute(block, both, xy_pairs(-a, -b)) for a, b in rels[1:]
        ]
        far = [lax.ppermute(b, both, core_pairs) for b in near]
        return near + far

    def gather_group(own):
        low = own.astype(BF16)
        return [
            lax.ppermute(low, "group", [((i + r) % n_group, i) for i in range(n_group)]) for r in range(1, n_group)
        ]

    to_helper = [((n_dp - 1) * n_group + g, plan.helper * n_group + g) for g in range(n_group)]
    from_helper = [(b, a) for a, b in to_helper]

    def per_device(
        context, segment_ids, target_index, target_length, pos_table, params, first_moment, second_moment, cotangent
    ):
        stored = context.shape[0]
        dp, me = lax.axis_index("dp"), lax.axis_index("group")
        gh, gl, dh, dl = me // 2, me % 2, dp // 2, dp % 2
        share = plan.share

        arrived = lax.all_to_all(
            context.reshape(n_group, stored // n_group, D_IN), "group", split_axis=0, concat_axis=0, tiled=True
        ).reshape(stored, D_IN)

        seg = segment_ids[0]
        lens = target_length.reshape(-1)
        starts = jnp.sum(seg[None, :] < jnp.arange(IMG + 1, dtype=jnp.int32)[:, None], axis=1).astype(jnp.int32)
        windows = jnp.minimum(starts[:IMG] // 8 * 8, CTX - WIN)
        slot_live = (jnp.arange(TMAX, dtype=jnp.int32)[None, :] < lens[:, None]).astype(F32).reshape(-1)
        live = jnp.concatenate([jnp.ones((CTX,), F32), slot_live])[:, None]
        own_row = (dp * share) // LANES + me * piece
        lane0 = (dp * share) % LANES
        own_s = jnp.stack([own_row, gl, gh, dl, me * piece, lane0, me, dp]).astype(jnp.int32)
        params2 = params.reshape(ROWS_ALL, LANES)
        spare = plan.shard_rows * LANES - share
        one2, two2 = [
            jnp.pad(m, (8 * LANES, spare)).reshape(8 + plan.shard_rows, LANES) for m in (first_moment, second_moment)
        ]
        tails = jnp.stack([
            jnp.pad(m[share - SMALL :].reshape(SMALL_ROWS, LANES), ((0, SMALL_PAD - SMALL_ROWS), (0, 0)))
            for m in (first_moment, second_moment)
        ])
        tails = lax.ppermute(tails, both, to_helper)

        out_specs = [
            shape((L, D), BF16),
            shape((n_hi, 2, n_early, piece, LANES), BF16),
            shape((n_hi, 2, n_early, piece, LANES), BF16),
            shape((plan.mid_rows, LANES), F32),
            shape((piece, LANES), F32),
            shape((piece, LANES), F32),
            shape((piece, LANES), F32),
            shape((8, D), F32),
            shape((8, D), F32),
        ]
        saved = [
            ((D_IN, D), BF16),
            ((D, 3 * D), BF16),
            ((L, D), F32),
            ((L, 3 * D), F32),
            ((GROUPS * 3, CTX, PER * LANES), BF16),
            ((2 * IMG * BLOCKS, KEYS, WIDE), BF16),
            ((L, D), F32),
            ((L, D), F32),
        ]
        any_spec = pl.BlockSpec(memory_space=pl.ANY)
        fwd = pl.pallas_call(
            functools.partial(forward_kernel, plan),
            out_shape=out_specs + [shape(*s) for s in saved],
            in_specs=smem(4) + [any_spec] * 3 + vmem(7),
            out_specs=vmem(len(out_specs)) + [any_spec] * len(saved),
            scratch_shapes=[
                pltpu.VMEM((D_IN, D), BF16),
                pltpu.VMEM((D, 3 * D), BF16),
                pltpu.VMEM((D, D), BF16),
                pltpu.VMEM((L, D), F32),
                pltpu.VMEM((L, 3 * D), F32),
                pltpu.VMEM((GROUPS * 3, CTX, PER * LANES), BF16),
                pltpu.VMEM((2 * IMG * BLOCKS, KEYS, WIDE), BF16),
                pltpu.VMEM((L, D), F32),
                pltpu.VMEM((L, D), BF16),
                pltpu.VMEM((L, D), F32),
                pltpu.VMEM((L, D), BF16),
                pltpu.VMEM((L, D), F32),
                pltpu.VMEM((plan.flat_rows, LANES), F32),
                pltpu.VMEM((D, FF), BF16),
                pltpu.VMEM((FF, D), BF16),
                pltpu.VMEM((8, D), F32),
                pltpu.VMEM((L, D), BF16),
                pltpu.VMEM((CTX, CTX), F32),
                pltpu.VMEM((D, CTX), BF16),
                pltpu.VMEM((L, D), BF16),
                pltpu.VMEM((L, FF), BF16),
                pltpu.VMEM((L, FF), BF16),
                pltpu.VMEM((L, D), BF16),
                pltpu.VMEM((plan.flat_rows - ROW_OUT, LANES), F32),
                pltpu.VMEM((2, piece + 8, LANES), F32),
                pltpu.SemaphoreType.DMA((8,)),
                pltpu.SemaphoreType.DMA((len(saved),)),
            ],
            compiler_params=pltpu.CompilerParams(vmem_limit_bytes=VMEM_CAP),
        )(
            windows, lens, starts, own_s,
            params2, one2, two2,
            arrived, segment_ids, seg[:, None], target_index.reshape(-1, 1), live, pos_table, cotangent[0],
        )
        out, keep_e, send_e, mid, own_w, own_one, own_two, vec, small_in = fwd[: len(out_specs)]

        late_rows = piece + SMALL_PAD
        bwd_out = [
            shape((n_hi, 2, n_late, late_rows, LANES), BF16),
            shape((n_hi, 2, n_late, late_rows, LANES), BF16),
            shape((CTX, D_IN), BF16),
        ]
        keep_l, send_l, ctx_grad = pl.pallas_call(
            functools.partial(backward_kernel, plan),
            out_shape=bwd_out,
            in_specs=smem(2) + vmem(4) + [any_spec] * len(saved),
            out_specs=vmem(len(bwd_out)),
            scratch_shapes=[pltpu.VMEM(*s) for s in saved] + [
                pltpu.VMEM((L, D), BF16),
                pltpu.VMEM((L, 3 * D), F32),
                pltpu.VMEM((L, 3 * D), BF16),
                pltpu.VMEM((CTX, D), BF16),
                pltpu.VMEM((D, CTX), BF16),
                pltpu.VMEM((SMALL_PAD, LANES), F32),
                pltpu.VMEM((ROW_OUT + plan.mid_rows, LANES), F32),
                pltpu.SemaphoreType.DMA((len(saved),)),
            ],
            compiler_params=pltpu.CompilerParams(vmem_limit_bytes=VMEM_CAP),
        )(windows, own_s, arrived, vec, small_in, mid, *fwd[len(out_specs) :])

        context_grad = lax.all_to_all(
            ctx_grad.reshape(n_group, stored // n_group, D_IN), "group", split_axis=0, concat_axis=0, tiled=True
        ).reshape(stored, D_IN)

        own_e = reduce_pieces(keep_e, send_e, plan.hi_early, n_early, dh, gh, dl)
        new_e = adam(own_w, own_e, own_one, own_two).astype(BF16)
        all_e = gather_pieces(new_e, plan.hi_early, n_early, dh)

        own_l = reduce_pieces(keep_l, send_l, 0, n_late, dh, gh, dl)
        small_sum = own_l[piece:]
        small_w = jnp.pad(params[NP - SMALL :].reshape(SMALL_ROWS, LANES), ((0, SMALL_PAD - SMALL_ROWS), (0, 0)))
        new_l = jnp.concatenate([
            adam(own_w, own_l[:piece], own_one, own_two), adam(small_w, small_sum, tails[0], tails[1])
        ]).astype(BF16)
        all_l = gather_pieces(new_l, 0, n_late, dh)

        own = jnp.where(dh >= plan.hi_early, own_e, own_l[:piece])
        small_got = lax.ppermute(small_sum, both, from_helper)
        parts = gather_group(own)

        def moment(own_ref, first_ref, *refs):
            moment_kernel(plan, own_ref, first_ref, refs[: n_group - 1], *refs[n_group - 1 :])

        new_first, new_second = pl.pallas_call(
            moment,
            out_shape=[shape((plan.shard_rows, LANES), F32)] * 2,
            in_specs=smem(1) + vmem(n_group + 3),
            out_specs=vmem(2),
            scratch_shapes=[pltpu.VMEM((plan.shard_rows + 8, LANES), F32)],
            compiler_params=pltpu.CompilerParams(vmem_limit_bytes=VMEM_CAP),
        )(own_s, own, *parts, small_got, one2, two2)
        new_first, new_second = [m.reshape(-1)[:share] for m in (new_first, new_second)]

        n_parts = len(all_l)

        def assemble(own_ref, *refs):
            late_refs, early_refs = refs[:n_parts], refs[n_parts : 2 * n_parts]
            assemble_kernel(plan, own_ref, late_refs, early_refs, *refs[2 * n_parts :])

        new_params = pl.pallas_call(
            assemble,
            out_shape=shape((ROWS_ALL, LANES), F32),
            in_specs=smem(1) + [any_spec] * (2 * n_parts),
            out_specs=pl.BlockSpec(memory_space=pltpu.VMEM),
            scratch_shapes=[
                pltpu.VMEM((2, n_hi, 2, n_late, late_rows, LANES), BF16),
                pltpu.VMEM((2, n_hi, 2, n_early, piece, LANES), BF16),
                pltpu.SemaphoreType.DMA((2 * n_parts,)),
            ],
            compiler_params=pltpu.CompilerParams(vmem_limit_bytes=VMEM_CAP),
        )(own_s, *all_l, *all_e)

        return out[None], context_grad, new_params.reshape(-1), new_first, new_second

    return per_device


def solution(mesh):
    return jax.shard_map(
        build(mesh),
        mesh=mesh,
        in_specs=(
            P(("dp", "group"), None),
            P(("dp", "group"), None),
            P(("dp", "group"), None, None, None),
            P(("dp", "group"), None, None),
            P(),
            P(),
            P("dp"),
            P("dp"),
            P(("dp", "group"), None, None),
        ),
        out_specs=(P(("dp", "group"), None, None), P(("dp", "group"), None), P(), P("dp"), P("dp")),
        check_vma=False,
    )
```

```python
import functools

import jax
import jax.numpy as jnp
from jax import lax
from jax.experimental import pallas as pl
from jax.experimental.pallas import tpu as pltpu
from jax.sharding import PartitionSpec as P

D_IN = 768
D = 384
HEADS = 12
HD = 32
FF = 1536
GRID = 196
BLOCKS = 4
TMAX = 40
STEP = 10
IMG = 4
CTX = 384
TGT = IMG * BLOCKS * TMAX
L = CTX + TGT
NP = D_IN * D + 4 * D * D + 2 * D * FF + 5 * D
LANES = 128
GROUPS = D // LANES
PER = LANES // HD
WIN = 200
KEYS = WIN + TMAX
WIDE = 256
TILE = 256
MLP_TILE = 512
CHUNK = 512

ROW_IN = 0
ROW_QKV = D_IN * D // LANES
ROW_OUT = ROW_QKV + 3 * D * D // LANES
ROW_UP = ROW_OUT + D * D // LANES
ROW_DOWN = ROW_UP + D * FF // LANES
ROW_SMALL = ROW_DOWN + FF * D // LANES
ROWS_ALL = NP // LANES
SMALL = 5 * D
SMALL_ROWS = SMALL // LANES
SMALL_PAD = 16

norm_eps = 1e-06
mask_value = -1e30
LOG2E = 1.4426950408889634
SCALE = HD**-0.5
F32 = jnp.float32
BF16 = jnp.bfloat16
VMEM_CAP = 60 * 1024 * 1024


def dot(a, b):
    return jnp.dot(a, b, preferred_element_type=F32)


def dot_nt(a, b):
    return lax.dot_general(a, b, (((1,), (1,)), ((), ())), preferred_element_type=F32)


def dot_tn(a, b):
    return lax.dot_general(a, b, (((0,), (0,)), ((), ())), preferred_element_type=F32)


def ceil_to(n, m):
    return -(-n // m) * m


class Plan:
    def __init__(self, n_dp, n_group):
        self.n_dp, self.n_group = n_dp, n_group
        self.share = NP // n_dp
        self.row0 = [d * self.share // LANES for d in range(n_dp)]
        self.lane0 = [d * self.share % LANES for d in range(n_dp)]
        most = max(ceil_to(o + self.share, LANES) // LANES for o in self.lane0)
        self.sub = ceil_to(-(-most // (2 * n_group)), 16)
        self.piece = 2 * self.sub
        self.shard_rows = self.piece * n_group
        self.n_hi, self.half = n_group // 2, n_dp // 2
        self.quarter = self.half // 2
        self.early0 = n_dp // 2
        assert self.early0 * self.share >= ROW_OUT * LANES
        self.helper = 1
        self.flat_rows = ceil_to(max(r + self.shard_rows for r in self.row0), 16)
        self.mid_rows = ceil_to(self.row0[self.early0 - 1] + self.shard_rows - ROW_OUT, 8)
        self.cut = ceil_to(self.early0 * self.share, 8 * LANES) // LANES


def layer_norm_parts(x):
    mu = jnp.mean(x, axis=-1, keepdims=True)
    xc = x - mu
    rstd = lax.rsqrt(jnp.mean(xc * xc, axis=-1, keepdims=True) + norm_eps)
    return xc * rstd, rstd


def layer_norm_back(dy, gain, xhat, rstd):
    dx = dy * gain
    a = jnp.mean(dx, axis=-1, keepdims=True)
    b = jnp.mean(dx * xhat, axis=-1, keepdims=True)
    return rstd * (dx - a - xhat * b)


def reciprocal(x):
    r = pl.reciprocal(x, approx=True)
    return r * (2.0 - x * r)


def gelu_both(x):
    z = jnp.abs(x) * (0.5**0.5)
    t = reciprocal(1.0 + 0.3275911 * z)
    e = jnp.exp2(x * x * (-0.5 * LOG2E))
    poly = ((((1.061405429 * t - 1.453152027) * t + 1.421413741) * t - 0.284496736) * t + 0.254829592) * t
    tail = 0.5 * poly * e
    cdf = jnp.where(x >= 0, 1.0 - tail, tail)
    pdf = e * 0.3989422804014327
    return x * cdf, cdf + x * pdf


def head_masks(first, count, width):
    lane = lax.broadcasted_iota(jnp.int32, (1, width), 1)
    return [(lane // HD == first + h).astype(F32) for h in range(count)]


def stack_heads(x, masks):
    return jnp.concatenate([x * m for m in masks], axis=0)


def diagonal(x, rows):
    return jnp.concatenate(
        [x[h * HD : (h + 1) * HD, h * rows : (h + 1) * rows] for h in range(PER)], axis=0
    )


def stack_six(x, masks):
    gap = jnp.zeros((WIDE // 2 - 3 * TMAX, WIDE), F32)
    parts = [x * m for m in masks]
    return jnp.concatenate(parts[:3] + [gap] + parts[3:] + [gap], axis=0).astype(BF16)


def fold_six(x, masks):
    total = None
    for h in range(6):
        at = (h // 3) * (WIDE // 2) + (h % 3) * TMAX
        part = x[at : at + TMAX] * masks[h]
        total = part if total is None else total + part
    return total


def half_masks(half):
    lane = lax.broadcasted_iota(jnp.int32, (1, WIDE), 1)
    head = (lane + half * LANES) // HD
    return [(head == 6 * half + h).astype(F32) for h in range(6)]


def half_slice(half, part):
    return pl.ds(pl.multiple_of(part * D + half * LANES, LANES), WIDE)


def lane_slice(g, part):
    return pl.ds(pl.multiple_of(part * D + g * LANES, LANES), LANES)


def prep_kernel(
    plan,
    own_s,
    params_hbm, one_hbm, two_hbm, idx_col, pos_ref,
    vec, own_ref, mine_ref, other_ref,
    w_in_hbm, w_qkv_hbm, w_out_hbm, w_up_hbm, w_down_hbm, stream_hbm,
    pbuf, w_in_b, w_qkv_b, w_out_b, w_up_b, w_down_b, stream, mom, sems, out_sems,
):
    spans = [
        (ROW_SMALL, SMALL_ROWS), (ROW_IN, ROW_QKV - ROW_IN), (ROW_QKV, ROW_OUT - ROW_QKV),
        (ROW_OUT, ROW_UP - ROW_OUT), (ROW_UP, ROW_DOWN - ROW_UP), (ROW_DOWN, ROW_SMALL - ROW_DOWN),
    ]
    copies = [
        pltpu.make_async_copy(params_hbm.at[pl.ds(r, n)], pbuf.at[pl.ds(r, n)], sems.at[i])
        for i, (r, n) in enumerate(spans)
    ]
    for c in copies:
        c.start()
    moments = [
        pltpu.make_async_copy(src.at[pl.ds(own_s[4], plan.piece + 8)], mom.at[i], sems.at[6 + i])
        for i, src in enumerate((one_hbm, two_hbm))
    ]
    for c in moments:
        c.start()
    outgoing = []

    def send_out(src, dst):
        copy = pltpu.make_async_copy(src, dst, out_sems.at[len(outgoing)])
        copy.start()
        outgoing.append(copy)

    def take(base, rows, tiles, dst, step):
        def body(i, _):
            for c in range(tiles):
                src = pl.ds(base + i * (step * tiles) + c, step, stride=tiles)
                dst[pl.ds(pl.multiple_of(i * step, step), step), c * LANES : (c + 1) * LANES] = pbuf[src, :].astype(BF16)
            return 0
        lax.fori_loop(0, rows // step, body, 0)

    copies[0].wait()
    vec[...] = jnp.zeros_like(vec)
    for k in range(5):
        for c in range(D // LANES):
            vec[k : k + 1, c * LANES : (c + 1) * LANES] = pbuf[pl.ds(ROW_SMALL + k * 3 + c, 1), :]
    mask_tok = vec[4:5, :]
    pos = pos_ref[...]
    pos_hi = pos.astype(BF16)
    pos_lo = (pos - pos_hi.astype(F32)).astype(BF16)
    for i in range(TGT // 128):
        rows = slice(i * 128, (i + 1) * 128)
        grid_id = lax.broadcasted_iota(jnp.int32, (128, GRID), 1)
        hot = (idx_col[rows, :] == grid_id).astype(F32).astype(BF16)
        stream[rows, :] = mask_tok + (dot(hot, pos_hi) + dot(hot, pos_lo))
    send_out(stream, stream_hbm)

    lane = lax.broadcasted_iota(jnp.int32, (1, LANES), 1)
    for i in range(2):
        moments[i].wait()
        turned = pltpu.roll(mom[i], own_s[5], 1)
        aligned = jnp.where(lane >= own_s[5], turned[8:], turned[7:-1])
        mine_ref[i] = aligned[: plan.sub]
        other_ref[i] = aligned[plan.sub :]

    for n, (base, rows, tiles, dst, out, step) in enumerate((
        (ROW_IN, D_IN, 3, w_in_b, w_in_hbm, 128), (ROW_QKV, D, 9, w_qkv_b, w_qkv_hbm, 128),
        (ROW_OUT, D, 3, w_out_b, w_out_hbm, 128), (ROW_UP, D, 12, w_up_b, w_up_hbm, 128),
        (ROW_DOWN, FF, 3, w_down_b, w_down_hbm, 128),
    )):
        copies[1 + n].wait()
        take(base, rows, tiles, dst, step)
        send_out(dst, out)
    for i in range(2):
        own_ref[i] = pbuf[pl.ds(own_s[8 + i], plan.sub), :]
    for copy in outgoing:
        copy.wait()


def place_pieces(own_s, dst, parts, rows):
    n = len(parts)
    for r, part in enumerate(parts):
        at = pl.multiple_of(lax.rem(own_s[6] + (n - r), n) * rows, 16)
        dst[pl.ds(at, rows), :] = part


def forward_kernel(
    plan,
    win_s, len_s, seg_s, own_s,
    vec, ctx_own, ctx_got, seg_row, seg_col, live_col, cot_ref,
    w_in_hbm, w_qkv_hbm, w_out_hbm, w_up_hbm, w_down_hbm, target_hbm,
    out_ref, keep_ref, send_ref, mid_ref, small_out,
    ctx_hbm, stream_hbm, qkv_hbm, probs_c_hbm, probs_t_hbm, d_mixed_hbm, d_middle_hbm,
    w_in_b, w_qkv_b, w_out_b, w_up_b, w_down_b, ctx, stream, qkv, probs_c, probs_t,
    mixed, mixed_b, d_mixed, d_branch, d_middle, normed, bias, v_t, second, active, d_lift, e_down, gflat,
    sems, out_sems,
):
    copies = [
        pltpu.make_async_copy(src, dst, sems.at[i])
        for i, (src, dst) in enumerate((
            (w_in_hbm, w_in_b), (w_qkv_hbm, w_qkv_b), (target_hbm, stream.at[pl.ds(CTX, TGT)]),
            (w_out_hbm, w_out_b), (w_up_hbm, w_up_b), (w_down_hbm, w_down_b),
        ))
    ]
    for c in copies:
        c.start()
    outgoing = []

    def send_out(src, dst):
        copy = pltpu.make_async_copy(src, dst, out_sems.at[len(outgoing)])
        copy.start()
        outgoing.append(copy)

    gain1, bias1, gain2, bias2 = [vec[k : k + 1, :] for k in range(4)]
    bias[...] = jnp.where(seg_col[...] == seg_row[...], 0.0, mask_value)

    stored = ctx_own.shape[0] // plan.n_group
    first = ctx_own[pl.ds(pl.multiple_of(own_s[6] * stored, 16), stored), :]
    place_pieces(own_s, ctx, [first] + [ref[...] for ref in ctx_got], stored)
    send_out(ctx, ctx_hbm)
    copies[0].wait()
    stream[0:CTX, :] = dot(ctx[...], w_in_b[...])
    copies[2].wait()
    send_out(stream, stream_hbm)
    copies[1].wait()

    def qkv_body(i, _):
        rows = pl.ds(pl.multiple_of(i * TILE, TILE), TILE)
        xhat, _r = layer_norm_parts(stream[rows, :])
        n = (xhat * gain1 + bias1).astype(BF16)
        normed[rows, :] = n
        qkv[rows, :] = dot(n, w_qkv_b[...]).astype(BF16).astype(F32)
        return 0

    lax.fori_loop(0, L // TILE, qkv_body, 0)

    send_out(qkv, qkv_hbm)
    masks = head_masks(0, PER, LANES)
    c2 = SCALE * LOG2E
    for g in range(GROUPS):
        v_t[g * LANES : (g + 1) * LANES, :] = qkv[0:CTX, 2 * D + g * LANES : 2 * D + (g + 1) * LANES].T.astype(BF16)

    def softmax_down(t):
        p = jnp.exp2(t - jnp.max(t, axis=0, keepdims=True))
        return (p * (1.0 / jnp.sum(p, axis=0, keepdims=True))).astype(BF16)

    def ctx_body(i, _):
        g, chunk = i // 3, i % 3
        rows = pl.ds(pl.multiple_of(chunk * LANES, LANES), LANES)
        lanes = pl.ds(pl.multiple_of(g * LANES, LANES), LANES)
        q = stack_heads(qkv[rows, lane_slice(g, 0)], masks).astype(BF16)
        st = dot_nt(qkv[0:CTX, lane_slice(g, 1)].astype(BF16), q)
        for h in range(PER):
            cols = slice(h * LANES, (h + 1) * LANES)
            probs_c[i, :, cols] = softmax_down(st[:, cols] * c2 + bias[:, rows])
        o = dot(v_t[lanes, :], probs_c[i])
        mixed[rows, lanes] = diagonal(o, LANES).T
        return 0

    lax.fori_loop(0, GROUPS * 3, ctx_body, 0)
    send_out(probs_c, probs_c_hbm)

    key_id = lax.broadcasted_iota(jnp.int32, (KEYS, 1), 0)
    mixed[CTX:, :] = jnp.zeros((TGT, D), F32)

    def tgt_body(i, _):
        half, img = i // IMG, i % IMG
        hmasks = half_masks(half)
        first = pl.multiple_of(win_s[img], 8)
        kw = qkv[pl.ds(first, WIN), half_slice(half, 1)]
        vw = qkv[pl.ds(first, WIN), half_slice(half, 2)]
        lo, hi = seg_s[img] - first, seg_s[img + 1] - first
        in_win = (key_id >= lo) & (key_id < hi) & (key_id < WIN)
        units = []
        for blk in range(BLOCKS):
            j = img * BLOCKS + blk
            rows = pl.ds(pl.multiple_of(CTX + j * TMAX, 8), TMAX)
            k = jnp.concatenate([kw, qkv[rows, half_slice(half, 1)]], axis=0).astype(BF16)
            v = jnp.concatenate([vw, qkv[rows, half_slice(half, 2)]], axis=0).astype(BF16)
            q = stack_six(qkv[rows, half_slice(half, 0)], hmasks)
            ok = in_win | ((key_id >= WIN) & (key_id < WIN + len_s[j]))
            units.append((rows, v, dot_nt(k, q), jnp.where(ok, 0.0, mask_value)))
        for blk, (rows, v, st, bias_col) in enumerate(units):
            for n in range(2):
                cols = slice(n * LANES, (n + 1) * LANES)
                probs_t[i * BLOCKS + blk, :, cols] = softmax_down(st[:, cols] * c2 + bias_col)
        for blk, (rows, v, st, bias_col) in enumerate(units):
            o = dot_tn(probs_t[i * BLOCKS + blk], v)
            mixed[rows, pl.ds(pl.multiple_of(half * LANES, LANES), WIDE)] += fold_six(o, hmasks)
        return 0

    lax.fori_loop(0, 2 * IMG, tgt_body, 0)
    send_out(probs_t, probs_t_hbm)

    for c in copies[3:]:
        c.wait()

    def mixed_of(rows):
        low = mixed[rows, :].astype(BF16)
        mixed_b[rows, :] = low
        return low

    def block_body(i, carry):
        dg2, db2 = carry
        rows = pl.ds(pl.multiple_of(i * MLP_TILE, MLP_TILE), MLP_TILE)
        live = live_col[rows, :]
        middle = stream[rows, :] + dot(mixed_of(rows), w_out_b[...])
        xhat, rstd = layer_norm_parts(middle)
        sec = (xhat * gain2 + bias2).astype(BF16)
        second[rows, :] = sec
        top = live * cot_ref[rows, :].astype(F32)
        e = top.astype(BF16)
        e_down[rows, :] = e
        out = middle
        d_second = jnp.zeros((MLP_TILE, D), F32)
        for j in range(FF // CHUNK):
            cols = slice(j * CHUNK, (j + 1) * CHUNK)
            lifted = dot(sec, w_up_b[:, cols])
            act, slope = gelu_both(lifted)
            act = act.astype(BF16)
            active[rows, cols] = act
            dl = (dot_nt(e, w_down_b[cols, :]) * slope).astype(BF16)
            d_lift[rows, cols] = dl
            out = out + dot(act, w_down_b[cols, :])
            d_second = d_second + dot_nt(dl, w_up_b[:, cols])
        out_ref[rows, :] = (live * out).astype(BF16)
        dm = top + layer_norm_back(d_second, gain2, xhat, rstd)
        d_middle[rows, :] = dm
        db = dm.astype(BF16)
        d_branch[rows, :] = db
        d_mixed[rows, :] = dot_nt(db, w_out_b[...])
        dg2 = dg2 + jnp.sum(d_second * xhat, axis=0, keepdims=True)
        db2 = db2 + jnp.sum(d_second, axis=0, keepdims=True)
        return dg2, db2

    zero = jnp.zeros((1, D), F32)
    dg2, db2 = lax.fori_loop(0, L // MLP_TILE, block_body, (zero, zero))
    small_out[...] = jnp.concatenate([dg2, db2, jnp.zeros((6, D), F32)], axis=0)

    send_out(d_mixed, d_mixed_hbm)
    send_out(d_middle, d_middle_hbm)

    end = ROW_SMALL - ROW_OUT
    gflat[end:, :] = jnp.zeros((gflat.shape[0] - end, LANES), F32)

    g = dot_tn(mixed_b[...], d_branch[...])
    for c in range(3):
        gflat[pl.ds(c, D, stride=3), :] = g[:, c * LANES : (c + 1) * LANES]

    def up_body(j, _):
        cols = pl.ds(pl.multiple_of(j * CHUNK, CHUNK), CHUNK)
        g = dot_tn(second[...], d_lift[:, cols])
        for c in range(CHUNK // LANES):
            gflat[pl.ds(ROW_UP - ROW_OUT + CHUNK // LANES * j + c, D, stride=12), :] = g[:, c * LANES : (c + 1) * LANES]
        return 0

    lax.fori_loop(0, FF // CHUNK, up_body, 0)

    def down_body(j, _):
        cols = pl.ds(pl.multiple_of(j * D, D), D)
        g = dot_tn(active[:, cols], e_down[...])
        for c in range(3):
            gflat[pl.ds(ROW_DOWN - ROW_OUT + j * (3 * D) + c, D, stride=3), :] = g[:, c * LANES : (c + 1) * LANES]
        return 0

    lax.fori_loop(0, 4, down_body, 0)

    mid_ref[...] = gflat[0 : plan.mid_rows, :]
    put_pieces(plan, gflat, ROW_OUT, range(plan.early0, plan.n_dp), plan.quarter, own_s[1], keep_ref, send_ref)
    for copy in outgoing:
        copy.wait()


def put_pieces(plan, gflat, base, shards, hi0, core, keep_ref, send_ref, extra=None):
    for d in shards:
        for q in range(plan.n_group):
            start = plan.row0[d] - base + q * plan.piece
            blocks = [gflat[start + n * plan.sub : start + (n + 1) * plan.sub, :].astype(BF16) for n in range(2)]

            def put(ref):
                for n in range(2):
                    ref[q // 2, d % 2, d // 2 - hi0, n, 0 : plan.sub, :] = blocks[n]
                    if extra is not None:
                        ref[q // 2, d % 2, d // 2 - hi0, n, plan.sub :, :] = extra

            @pl.when(core == q % 2)
            def _():
                put(keep_ref)

            @pl.when(core != q % 2)
            def _():
                put(send_ref)


def attention_back_kernel(
    plan,
    win_s, qkv_hbm, probs_c_hbm, probs_t_hbm, d_mixed_hbm,
    dpk, qkv, probs_c, probs_t, d_mixed, d_qkv, k_t, sems,
):
    incoming = {}
    for n, (name, src, dst) in enumerate((
        ("qkv", qkv_hbm, qkv), ("d_mixed", d_mixed_hbm, d_mixed), ("probs_c", probs_c_hbm, probs_c),
        ("probs_t", probs_t_hbm, probs_t),
    )):
        incoming[name] = pltpu.make_async_copy(src, dst, sems.at[n])
        incoming[name].start()

    d_qkv[...] = jnp.zeros_like(d_qkv)
    masks = head_masks(0, PER, LANES)
    incoming["qkv"].wait()
    for g in range(GROUPS):
        k_t[g * LANES : (g + 1) * LANES, :] = qkv[0:CTX, D + g * LANES : D + (g + 1) * LANES].T.astype(BF16)
    incoming["d_mixed"].wait()
    incoming["probs_c"].wait()

    def back_down(p, dp):
        p = p.astype(F32)
        delta = jnp.sum(p * dp, axis=0, keepdims=True)
        return (p * (dp - delta)).astype(BF16)

    def ctx_body(i, _):
        g, chunk = i // 3, i % 3
        rows = pl.ds(pl.multiple_of(chunk * LANES, LANES), LANES)
        lanes = pl.ds(pl.multiple_of(g * LANES, LANES), LANES)
        do = stack_heads(d_mixed[rows, lanes], masks).astype(BF16)
        dpt = dot_nt(qkv[0:CTX, lane_slice(g, 2)].astype(BF16), do)
        ds = []
        for h in range(PER):
            cols = slice(h * LANES, (h + 1) * LANES)
            ds.append(back_down(probs_c[i, :, cols], dpt[:, cols]))
        ds = jnp.concatenate(ds, axis=1)
        q = stack_heads(qkv[rows, lane_slice(g, 0)], masks).astype(BF16)
        d_qkv[rows, lane_slice(g, 0)] = diagonal(dot(k_t[lanes, :], ds), LANES).T
        d_qkv[0:CTX, lane_slice(g, 1)] += dot(ds, q)
        d_qkv[0:CTX, lane_slice(g, 2)] += dot(probs_c[i], do)
        return 0

    lax.fori_loop(0, GROUPS * 3, ctx_body, 0)
    incoming["probs_t"].wait()

    def tgt_body(i, _):
        half, img = i // IMG, i % IMG
        hmasks = half_masks(half)
        first = pl.multiple_of(win_s[img], 8)
        win = pl.ds(first, WIN)
        kw = qkv[win, half_slice(half, 1)]
        vw = qkv[win, half_slice(half, 2)]
        units = []
        for blk in range(BLOCKS):
            rows = pl.ds(pl.multiple_of(CTX + (img * BLOCKS + blk) * TMAX, 8), TMAX)
            v = jnp.concatenate([vw, qkv[rows, half_slice(half, 2)]], axis=0).astype(BF16)
            do = stack_six(d_mixed[rows, pl.ds(pl.multiple_of(half * LANES, LANES), WIDE)], hmasks)
            units.append((rows, do, dot_nt(v, do)))
        dkw = jnp.zeros((WIN, WIDE), F32)
        dvw = jnp.zeros((WIN, WIDE), F32)
        for blk, (rows, do, dpt) in enumerate(units):
            p = probs_t[i * BLOCKS + blk]
            ds = jnp.concatenate(
                [back_down(p[:, n * LANES : (n + 1) * LANES], dpt[:, n * LANES : (n + 1) * LANES]) for n in range(2)],
                axis=1,
            )
            k = jnp.concatenate([kw, qkv[rows, half_slice(half, 1)]], axis=0).astype(BF16)
            q = stack_six(qkv[rows, half_slice(half, 0)], hmasks)
            d_qkv[rows, half_slice(half, 0)] += fold_six(dot_tn(ds, k), hmasks)
            dk = dot(ds, q)
            dv = dot(p, do)
            d_qkv[rows, half_slice(half, 1)] += dk[WIN:]
            d_qkv[rows, half_slice(half, 2)] += dv[WIN:]
            dkw = dkw + dk[:WIN]
            dvw = dvw + dv[:WIN]
        d_qkv[win, half_slice(half, 1)] += dkw
        d_qkv[win, half_slice(half, 2)] += dvw
        return 0

    lax.fori_loop(0, 2 * IMG, tgt_body, 0)
    def round_body(i, _):
        rows = pl.ds(pl.multiple_of(i * 128, 128), 128)
        dpk[rows, 0 : 2 * D] = (d_qkv[rows, 0 : 2 * D] * SCALE).astype(BF16)
        dpk[rows, 2 * D :] = d_qkv[rows, 2 * D :].astype(BF16)
        return 0

    lax.fori_loop(0, L // 128, round_body, 0)


def backward_kernel(
    plan,
    own_s,
    vec, small_in, mid_ref, dpk,
    w_in_hbm, w_qkv_hbm, ctx_hbm, stream_hbm, d_middle_hbm,
    keep_ref, send_ref, same_ref, cross_ref,
    w_in_b, w_qkv_b, ctx_ref, stream, d_middle, normed, d_hidden, ctx_grad, small_flat, gflat, sems,
):
    incoming = {}
    for n, (name, src, dst) in enumerate((
        ("w_qkv", w_qkv_hbm, w_qkv_b), ("stream", stream_hbm, stream), ("d_middle", d_middle_hbm, d_middle),
        ("w_in", w_in_hbm, w_in_b), ("ctx", ctx_hbm, ctx_ref),
    )):
        incoming[name] = pltpu.make_async_copy(src, dst, sems.at[n])
        incoming[name].start()
    gain1, bias1 = vec[0:1, :], vec[1:2, :]
    gflat[ROW_OUT : ROW_OUT + plan.mid_rows, :] = mid_ref[...]
    for name in ("w_qkv", "stream", "d_middle"):
        incoming[name].wait()

    def row_body(i, carry):
        dg1, db1, dmask = carry
        rows = pl.ds(pl.multiple_of(i * 128, 128), 128)
        xhat, rstd = layer_norm_parts(stream[rows, :])
        normed[rows, :] = (xhat * gain1 + bias1).astype(BF16)
        d_normed = dot_nt(dpk[rows, :], w_qkv_b[...])
        d_stream = d_middle[rows, :] + layer_norm_back(d_normed, gain1, xhat, rstd)
        dg1 = dg1 + jnp.sum(d_normed * xhat, axis=0, keepdims=True)
        db1 = db1 + jnp.sum(d_normed, axis=0, keepdims=True)
        is_tgt = (i >= CTX // 128).astype(F32)
        dmask = dmask + is_tgt * jnp.sum(d_stream, axis=0, keepdims=True)

        @pl.when(i < CTX // 128)
        def _():
            d_hidden[rows, :] = d_stream.astype(BF16)

        return dg1, db1, dmask

    zero = jnp.zeros((1, D), F32)
    dg1, db1, dmask = lax.fori_loop(0, L // 128, row_body, (zero, zero, zero))
    for k, row in enumerate((dg1, db1, small_in[0:1, :], small_in[1:2, :], dmask)):
        for c in range(3):
            small_flat[3 * k + c : 3 * k + c + 1, :] = row[:, c * LANES : (c + 1) * LANES]
    small_flat[SMALL_ROWS:, :] = jnp.zeros((SMALL_PAD - SMALL_ROWS, LANES), F32)

    incoming["w_in"].wait()
    incoming["ctx"].wait()
    ctx_grad[...] = dot_nt(d_hidden[...], w_in_b[...]).astype(BF16)
    stored = CTX // plan.n_group
    for a in range(plan.n_hi):
        hi = lax.rem(own_s[2] + a, plan.n_hi) * 2
        for ref, core in ((same_ref, own_s[1]), (cross_ref, 1 - own_s[1])):
            ref[a] = ctx_grad[pl.ds(pl.multiple_of((hi + core) * stored, 16), stored), :]
    for j in range(2):
        g = dot_tn(ctx_ref[:, j * D : (j + 1) * D], d_hidden[...])
        for c in range(3):
            gflat[pl.ds(ROW_IN + j * 3 * D + c, D, stride=3), :] = g[:, c * LANES : (c + 1) * LANES]
    for j in range(3):
        g = dot_tn(normed[...], dpk[:, j * D : (j + 1) * D])
        for c in range(3):
            gflat[pl.ds(ROW_QKV + 3 * j + c, D, stride=9), :] = g[:, c * LANES : (c + 1) * LANES]
    put_pieces(plan, gflat, 0, range(plan.early0), 0, own_s[1], keep_ref, send_ref, small_flat[...].astype(BF16))


def vmem(n):
    return [pl.BlockSpec(memory_space=pltpu.VMEM)] * n


def smem(n):
    return [pl.BlockSpec(memory_space=pltpu.SMEM)] * n


def shape(dims, dtype):
    return jax.ShapeDtypeStruct(dims, dtype)


def fetch_blocks(plan, own_s, refs, rels, dst, sems):
    copies = []
    for i, (ref, (c_rel, a_rel, b_rel)) in enumerate(zip(refs, rels)):
        core = lax.rem(own_s[1] + c_rel, 2)
        hi = lax.rem(own_s[2] + a_rel, plan.n_hi)
        lo = lax.rem(own_s[3] + b_rel, 2)
        copies.append(pltpu.make_async_copy(ref, dst.at[core, hi, lo], sems.at[i]))
    for copy in copies:
        copy.start()
    for copy in copies:
        copy.wait()


def put_rows(plan, shards, hi0, src, out, base):
    for d in shards:
        lane0 = plan.lane0[d]
        rows = ceil_to(lane0 + plan.share, LANES) // LANES
        for q in range(plan.n_group):
            for n in range(2):
                start = q * plan.piece + n * plan.sub
                count = min(plan.sub, rows - start)
                if count <= 0:
                    continue
                block = src[q % 2, q // 2, d % 2, d // 2 - hi0, n, 0 : plan.sub, :].astype(F32)
                at = plan.row0[d] + start - base
                if start == 0 and lane0:
                    lane = lax.broadcasted_iota(jnp.int32, (1, LANES), 1)
                    out[at : at + 1, :] = jnp.where(lane < lane0, out[at : at + 1, :], block[0:1])
                    out[at + 1 : at + count, :] = block[1:count]
                else:
                    out[at : at + count, :] = block[:count]


def early_kernel(plan, own_s, near, far, out_hbm, edge_ref, blocks, buf, sems):
    rels = [(c, a, b) for c in range(2) for b in range(2) for a in range(plan.n_hi)]
    refs = [src.at[i] for src in (near, far) for i in range(2 * plan.n_hi)]
    fetch_blocks(plan, own_s, refs, rels, blocks, sems)
    base = plan.cut - 8
    buf[0:8, :] = jnp.zeros((8, LANES), F32)
    put_rows(plan, range(plan.early0, plan.n_dp), plan.quarter, blocks, buf, base)
    edge_ref[...] = buf[0:8, :]
    copy = pltpu.make_async_copy(
        buf.at[pl.ds(8, ROW_SMALL - plan.cut)], out_hbm.at[pl.ds(plan.cut, ROW_SMALL - plan.cut)], sems.at[0]
    )
    copy.start()
    copy.wait()


def late_kernel(plan, own_s, refs, edge_ref, done_hbm, out_hbm, blocks, buf, tail, sems):
    rels = [(c, a, b) for c in range(2) for a in range(plan.n_hi) for b in range(2)]
    fetch_blocks(plan, own_s, refs, rels, blocks, sems)
    small = blocks[0, 0, plan.helper % 2, plan.helper // 2, 0, plan.sub :, :].astype(F32)
    tail[...] = small[:SMALL_ROWS]
    copies = [pltpu.make_async_copy(tail, out_hbm.at[pl.ds(ROW_SMALL, SMALL_ROWS)], sems.at[0])]
    copies[0].start()
    done = 0
    for d in range(plan.early0):
        put_rows(plan, [d], 0, blocks, buf, 0)
        upto = (plan.row0[d + 1] // 8) * 8
        if d == plan.early0 - 1:
            upto = plan.cut
            at = plan.row0[d + 1]
            lane0 = plan.lane0[d + 1]
            if at < plan.cut:
                lane = lax.broadcasted_iota(jnp.int32, (1, LANES), 1)
                edge = edge_ref[at - plan.cut + 8 :, :]
                own = buf[at : plan.cut, :]
                row = lax.broadcasted_iota(jnp.int32, (plan.cut - at, 1), 0)
                buf[at : plan.cut, :] = jnp.where((row == 0) & (lane < lane0), own, edge)
        if (d + 1) % max(1, plan.early0 // 4) == 0:
            copies.append(pltpu.make_async_copy(
                buf.at[pl.ds(done, upto - done)], out_hbm.at[pl.ds(done, upto - done)], sems.at[len(copies)]
            ))
            copies[-1].start()
            done = upto
    for copy in copies:
        copy.wait()


def moment_kernel(plan, own_s, same, cross, small_ref, one_ref, two_ref, ctx_pairs, *rest):
    ctx_far, (first_ref, second_ref, ctx_ref, grad) = rest[: plan.n_hi - 1], rest[plan.n_hi - 1 :]
    rows, stored = plan.shard_rows, ctx_ref.shape[0] // plan.n_group
    for a in range(plan.n_hi):
        back = lax.rem(own_s[2] + plan.n_hi - a, plan.n_hi) * 2
        ahead = lax.rem(own_s[2] + a, plan.n_hi) * 2
        for n, core in enumerate((own_s[1], 1 - own_s[1])):
            at = pl.multiple_of((back + core) * stored, 16)
            ctx_ref[pl.ds(at, stored), :] = ctx_far[a - 1][n] if a else ctx_pairs[0, n]
            at = pl.multiple_of((ahead + core) * plan.piece, 16)
            grad[pl.ds(at, plan.piece), :] = (cross if n else same)[a].astype(F32)
    grad[rows:, :] = jnp.zeros((8, LANES), F32)

    @pl.when(own_s[7] == plan.n_dp - 1)
    def _():
        at = ROW_SMALL - plan.row0[-1]
        grad[at : at + SMALL_ROWS, :] = small_ref[0:SMALL_ROWS, :]

    lane = lax.broadcasted_iota(jnp.int32, (1, LANES), 1)
    back = LANES - own_s[5]
    for i in range(plan.n_group):
        at = slice(i * plan.piece, (i + 1) * plan.piece)
        turned = pltpu.roll(grad[i * plan.piece : (i + 1) * plan.piece + 8, :], back, 1)
        g = jnp.where(lane < back, turned[: plan.piece], turned[1 : plan.piece + 1])
        first_ref[at, :] = 0.5 * one_ref[8 + i * plan.piece : 8 + (i + 1) * plan.piece, :] + 0.5 * g
        second_ref[at, :] = 0.6 * two_ref[8 + i * plan.piece : 8 + (i + 1) * plan.piece, :] + 0.4 * g * g


def adam(weight, grad, one, two):
    first = 0.5 * one + 0.5 * grad
    second = 0.6 * two + 0.4 * grad * grad
    step = (first / (1.0 - 0.5**STEP)) / (jnp.sqrt(second / (1.0 - 0.6**STEP)) + 1e-08)
    return weight - 0.05 * (step + 0.05 * weight)


def after(value, *others):
    return lax.optimization_barrier((value, others))[0]


def build(mesh):
    n_dp, n_group = mesh.shape["dp"], mesh.shape["group"]
    plan = Plan(n_dp, n_group)
    both = ("dp", "group")
    n_hi, half, quarter = plan.n_hi, plan.half, plan.quarter
    piece, sub = plan.piece, plan.sub
    any_spec = pl.BlockSpec(memory_space=pl.ANY)
    brief = pl.CostEstimate(flops=0, bytes_accessed=0, transcendentals=0)
    params_of = pltpu.CompilerParams(vmem_limit_bytes=VMEM_CAP)

    def pairs(move):
        out = []
        for d in range(n_dp):
            for g in range(n_group):
                ghi, glo, dhi, dlo = move(g // 2, g % 2, d // 2, d % 2)
                out.append((d * n_group + g, (dhi * 2 + dlo) * n_group + ghi * 2 + glo))
        return out

    core_pairs = pairs(lambda gh, gl, dh, dl: (gh, 1 - gl, dh, dl))
    swap_pairs = pairs(lambda gh, gl, dh, dl: (gh, gl, (dh + quarter) % half, dl))

    def xy_pairs(a, b):
        return pairs(lambda gh, gl, dh, dl: ((gh + a) % n_hi, gl, dh, (dl + b) % 2))

    def z_pairs(r):
        return pairs(lambda gh, gl, dh, dl: (gh, gl, (dh + r) % half, dl))

    def group_pairs(r):
        return [(i, (i + r) % n_group) for i in range(n_group)]

    rels = [(a, b) for a in range(n_hi) for b in range(2)]
    to_helper = [((n_dp - 1) * n_group + g, plan.helper * n_group + g) for g in range(n_group)]
    from_helper = [(b, a) for a, b in to_helper]

    def pick(array, index):
        return lax.dynamic_index_in_dim(array, index, 0, keepdims=False)

    def slot_of(h, early):
        return (h % quarter) * 2 + (h // quarter + early) % 2

    def xy_blocks(keep, got, gh, dl):
        def block(a, b):
            i, j = (gh + a) % n_hi, (dl + b) % 2
            mine, theirs = pick(pick(keep, i), j), pick(pick(got, i), j)
            return (mine.astype(F32) + theirs.astype(F32)).astype(BF16)
        return [block(a, b) for a, b in rels]

    def xy_send(blocks):
        return [lax.ppermute(x, both, xy_pairs(a, b)) for x, (a, b) in zip(blocks[1:], rels[1:])]

    def z_blocks(block, arrived, dh, early):
        total = block.astype(F32)
        for part in arrived:
            total = total + part.astype(F32)
        total = total.astype(BF16)
        total = total.reshape((2 * quarter,) + total.shape[2:])
        return [pick(total, slot_of((dh + r) % half, early)) for r in range(half)]

    def z_send(blocks):
        return [lax.ppermute(x, both, z_pairs(r)) for r, x in enumerate(blocks) if r]

    def z_sum(block, arrived):
        total = block.astype(F32)
        for part in arrived:
            total = total + part.astype(F32)
        return total

    def z_gather(mine):
        return [lax.ppermute(mine, both, z_pairs(r)) for r in range(1, half)]

    def z_order(got, sender, early):
        blocks = []
        for t in range(quarter):
            for n in range(2):
                want = (t + early * quarter + n * quarter) % half
                block = got[0]
                for i in range(1, half):
                    block = jnp.where(sender(i) == want, got[i], block)
                blocks.append(block)
        return jnp.stack(blocks).reshape((quarter, 2) + blocks[0].shape)

    def xy_gather(block):
        return [lax.ppermute(block, both, xy_pairs(-a, -b)) for a, b in rels[1:]]

    def core_gather(blocks):
        return [lax.ppermute(b, both, core_pairs) for b in blocks]

    def per_device(
        context, segment_ids, target_index, target_length, pos_table, params, first_moment, second_moment, cotangent
    ):
        stored = context.shape[0] // n_group
        dp, me = lax.axis_index("dp"), lax.axis_index("group")
        gh, gl, dh, dl = me // 2, me % 2, dp // 2, dp % 2
        share = plan.share

        ctx_got = [
            lax.ppermute(
                lax.dynamic_slice_in_dim(context, (me + r) % n_group * stored, stored), "group", group_pairs(r)
            )
            for r in range(1, n_group)
        ]

        seg = segment_ids[0]
        lens = target_length.reshape(-1)
        starts = jnp.sum(seg[None, :] < jnp.arange(IMG + 1, dtype=jnp.int32)[:, None], axis=1).astype(jnp.int32)
        windows = jnp.minimum(starts[:IMG] // 8 * 8, CTX - WIN)
        slot_live = (jnp.arange(TMAX, dtype=jnp.int32)[None, :] < lens[:, None]).astype(F32).reshape(-1)
        live = jnp.concatenate([jnp.ones((CTX,), F32), slot_live])[:, None]
        lane0 = (dp * share) % LANES

        def own_row(early):
            t = dh % quarter + early * quarter
            n = (dh // quarter + early) % 2
            return ((t * 2 + dl) * share) // LANES + me * piece + n * sub

        own_s = jnp.stack(
            [0 * me, gl, gh, dl, me * piece, lane0, me, dp, own_row(0), own_row(1)]
        ).astype(jnp.int32)
        params2 = params.reshape(ROWS_ALL, LANES)
        spare = plan.shard_rows * LANES - share
        one2, two2 = [
            jnp.pad(m, (8 * LANES, spare)).reshape(8 + plan.shard_rows, LANES) for m in (first_moment, second_moment)
        ]

        weights = [((D_IN, D), BF16), ((D, 3 * D), BF16), ((D, D), BF16), ((D, FF), BF16), ((FF, D), BF16)]
        prep = pl.pallas_call(
            functools.partial(prep_kernel, plan),
            out_shape=[shape((8, D), F32)] + [shape((2, sub, LANES), F32)] * 3
            + [shape(*w) for w in weights] + [shape((TGT, D), F32)],
            in_specs=smem(1) + [any_spec] * 3 + vmem(2),
            out_specs=vmem(4) + [any_spec] * 6,
            scratch_shapes=[pltpu.VMEM((plan.flat_rows, LANES), F32)] + [pltpu.VMEM(*w) for w in weights] + [
                pltpu.VMEM((TGT, D), F32),
                pltpu.VMEM((2, piece + 8, LANES), F32),
                pltpu.SemaphoreType.DMA((8,)),
                pltpu.SemaphoreType.DMA((6,)),
            ],
            compiler_params=params_of,
        )(own_s, params2, one2, two2, target_index.reshape(-1, 1), pos_table)
        vec, own_w, own_mom, other_mom, w_in_b, w_qkv_b, w_out_b, w_up_b, w_down_b, target_rows = prep

        swapped = lax.ppermute(other_mom, both, swap_pairs)
        tails = jnp.stack([
            jnp.pad(m[share - SMALL :].reshape(SMALL_ROWS, LANES), ((0, SMALL_PAD - SMALL_ROWS), (0, 0)))
            for m in (first_moment, second_moment)
        ])
        tails = lax.ppermute(tails, both, to_helper)

        early_rows, late_rows = sub, sub + SMALL_PAD
        n_blocks = 2 * n_hi
        out_specs = [
            shape((L, D), BF16),
            shape((n_hi, 2, quarter, 2, early_rows, LANES), BF16),
            shape((n_hi, 2, quarter, 2, early_rows, LANES), BF16),
            shape((plan.mid_rows, LANES), F32),
            shape((8, D), F32),
        ]
        saved = [
            ((CTX, D_IN), BF16),
            ((L, D), F32),
            ((L, 3 * D), F32),
            ((GROUPS * 3, CTX, PER * LANES), BF16),
            ((2 * IMG * BLOCKS, KEYS, WIDE), BF16),
            ((L, D), F32),
            ((L, D), F32),
        ]

        def forward(*refs):
            n = 4 + 2
            forward_kernel(plan, *refs[:n], refs[n : n + n_group - 1], *refs[n + n_group - 1 :])

        fwd = pl.pallas_call(
            forward,
            out_shape=out_specs + [shape(*s) for s in saved],
            in_specs=smem(4) + vmem(2 + n_group - 1 + 4) + [any_spec] * 6,
            out_specs=vmem(len(out_specs)) + [any_spec] * len(saved),
            scratch_shapes=[pltpu.VMEM(*w) for w in weights] + [pltpu.VMEM(*s) for s in saved[:5]] + [
                pltpu.VMEM((L, D), F32),
                pltpu.VMEM((L, D), BF16),
                pltpu.VMEM((L, D), F32),
                pltpu.VMEM((L, D), BF16),
                pltpu.VMEM((L, D), F32),
                pltpu.VMEM((L, D), BF16),
                pltpu.VMEM((CTX, CTX), F32),
                pltpu.VMEM((D, CTX), BF16),
                pltpu.VMEM((L, D), BF16),
                pltpu.VMEM((L, FF), BF16),
                pltpu.VMEM((L, FF), BF16),
                pltpu.VMEM((L, D), BF16),
                pltpu.VMEM((plan.flat_rows - ROW_OUT, LANES), F32),
                pltpu.SemaphoreType.DMA((6,)),
                pltpu.SemaphoreType.DMA((len(saved),)),
            ],
            compiler_params=params_of,
        )(
            windows, lens, starts, own_s,
            vec, context, *ctx_got, segment_ids, seg[:, None], live, cotangent[0],
            w_in_b, w_qkv_b, w_out_b, w_up_b, w_down_b, target_rows,
        )
        out, keep_e, send_e, mid, small_in = fwd[: len(out_specs)]
        ctx_s, stream_s, qkv_s, probs_c_s, probs_t_s, d_mixed_s, d_middle_s = fwd[len(out_specs) :]

        swapped, tails = after(swapped, out), after(tails, out)
        got_e = lax.ppermute(after(send_e, swapped, tails), both, core_pairs)
        xy_e = xy_blocks(keep_e, got_e, gh, dl)
        xy_got_e = xy_send(xy_e)
        qkv_s = after(qkv_s, *xy_e)

        dpk = pl.pallas_call(
            functools.partial(attention_back_kernel, plan),
            out_shape=shape((L, 3 * D), BF16),
            in_specs=smem(1) + [any_spec] * 4,
            out_specs=pl.BlockSpec(memory_space=pltpu.VMEM),
            scratch_shapes=[pltpu.VMEM(*s) for s in saved[2:6]] + [
                pltpu.VMEM((L, 3 * D), F32),
                pltpu.VMEM((D, CTX), BF16),
                pltpu.SemaphoreType.DMA((4,)),
            ],
            compiler_params=params_of,
            cost_estimate=pl.CostEstimate(flops=10**10, bytes_accessed=20 * 10**6, transcendentals=0),
        )(windows, qkv_s, probs_c_s, probs_t_s, d_mixed_s)

        xy_got_e = [after(x, dpk) for x in xy_got_e]
        z_e = z_blocks(xy_e[0], xy_got_e, dh, 1)
        z_got_e = z_send(z_e)
        dpk = after(dpk, *z_e)

        bwd_out = [
            shape((n_hi, 2, quarter, 2, late_rows, LANES), BF16),
            shape((n_hi, 2, quarter, 2, late_rows, LANES), BF16),
            shape((n_hi, stored, D_IN), BF16),
            shape((n_hi, stored, D_IN), BF16),
        ]
        bwd = pl.pallas_call(
            functools.partial(backward_kernel, plan),
            out_shape=bwd_out,
            in_specs=smem(1) + vmem(4) + [any_spec] * 5,
            out_specs=vmem(len(bwd_out)),
            scratch_shapes=[
                pltpu.VMEM((D_IN, D), BF16),
                pltpu.VMEM((D, 3 * D), BF16),
                pltpu.VMEM((CTX, D_IN), BF16),
                pltpu.VMEM((L, D), F32),
                pltpu.VMEM((L, D), F32),
                pltpu.VMEM((L, D), BF16),
                pltpu.VMEM((CTX, D), BF16),
                pltpu.VMEM((CTX, D_IN), BF16),
                pltpu.VMEM((SMALL_PAD, LANES), F32),
                pltpu.VMEM((ROW_OUT + plan.mid_rows, LANES), F32),
                pltpu.SemaphoreType.DMA((5,)),
            ],
            compiler_params=params_of,
            cost_estimate=pl.CostEstimate(flops=5 * 10**9, bytes_accessed=15 * 10**6, transcendentals=0),
        )(own_s, vec, small_in, mid, dpk, w_in_b, w_qkv_b, ctx_s, stream_s, d_middle_s)
        keep_l, send_l, ctx_same, ctx_cross = bwd

        upper = dh // quarter
        own_is_late = upper == 0

        def moments_of(early):
            return jnp.where(upper == early, own_mom, swapped)

        def all_after(values, *others):
            return [after(x, *others) for x in values]

        def joint(*groups):
            return lax.optimization_barrier(groups)

        z_got_e = all_after(z_got_e, keep_l)
        got_l = lax.ppermute(after(send_l, *z_got_e), both, core_pairs)
        own_e = z_sum(z_e[0], z_got_e)
        mom = moments_of(1)
        new_e = adam(own_w[1], own_e, mom[0], mom[1]).astype(BF16)
        ctx_cross = lax.ppermute(after(ctx_cross, *z_got_e), both, core_pairs)
        got_l, ctx_cross, new_e = joint(got_l, ctx_cross, new_e)
        ctx_pairs = jnp.stack([ctx_same, ctx_cross], axis=1)

        xy_l = xy_blocks(keep_l, got_l, gh, dl)
        xy_got_l, z_new_e, own_e = joint(xy_send(xy_l), z_gather(after(new_e, *xy_l)), own_e)

        z_l = z_blocks(xy_l[0], xy_got_l, dh, 0)
        block_e = z_order([new_e] + list(z_new_e), lambda i: (dh - i) % half, 1)[None]
        z_got_l, near_e, ctx_far = joint(
            z_send(z_l), [lax.ppermute(block_e, both, xy_pairs(-a, 0)) for a in range(1, n_hi)],
            [lax.ppermute(after(ctx_pairs[a], *z_l), both, xy_pairs(a, 0)) for a in range(1, n_hi)],
        )
        own_l = z_sum(z_l[0], z_got_l)
        small_sum = own_l[sub:]
        small_w = jnp.pad(params[NP - SMALL :].reshape(SMALL_ROWS, LANES), ((0, SMALL_PAD - SMALL_ROWS), (0, 0)))
        mom = moments_of(0)
        new_l = jnp.concatenate([
            adam(own_w[0], own_l[:sub], mom[0], mom[1]), adam(small_w, small_sum, tails[0], tails[1])
        ]).astype(BF16)

        near_e = jnp.concatenate([block_e] + list(near_e))
        give = jnp.where(own_is_late, own_e, own_l[:sub]).astype(BF16)
        have = jnp.where(own_is_late, own_l[:sub], own_e).astype(BF16)
        z_new_l, y_near_e, taken = joint(
            z_gather(new_l), lax.ppermute(near_e, both, xy_pairs(0, 1)), lax.ppermute(give, both, swap_pairs)
        )

        block_l = z_order([new_l] + list(z_new_l), lambda i: (dh - i) % half, 0)
        near_e = jnp.concatenate([near_e, y_near_e])
        near_l = xy_gather(block_l)
        far_e = lax.ppermute(after(near_e, block_l), both, core_pairs)
        own = jnp.concatenate([have, taken])
        quarters = jnp.stack(
            [own] + [lax.ppermute(after(own, block_l), both, xy_pairs(-a, 0)) for a in range(1, n_hi)]
        )
        other_quarters = lax.ppermute(quarters, both, core_pairs)
        small_got = lax.ppermute(after(small_sum, far_e), both, from_helper)

        n_parts = 2 * n_blocks
        base = plan.cut - 8

        half_done, edge = pl.pallas_call(
            functools.partial(early_kernel, plan),
            out_shape=[shape((ROWS_ALL, LANES), F32), shape((8, LANES), F32)],
            in_specs=smem(1) + [any_spec] * 2,
            out_specs=[any_spec, pl.BlockSpec(memory_space=pltpu.VMEM)],
            scratch_shapes=[
                pltpu.VMEM((2, n_hi, 2, quarter, 2, early_rows, LANES), BF16),
                pltpu.VMEM((plan.flat_rows - base, LANES), F32),
                pltpu.SemaphoreType.DMA((n_parts,)),
            ],
            compiler_params=params_of,
            cost_estimate=brief,
        )(after(own_s, block_l), near_e, far_e)

        new_first, new_second, context_grad = pl.pallas_call(
            functools.partial(moment_kernel, plan),
            out_shape=[shape((plan.shard_rows, LANES), F32)] * 2 + [shape(context.shape, BF16)],
            in_specs=smem(1) + vmem(6 + n_hi - 1),
            out_specs=vmem(3),
            scratch_shapes=[pltpu.VMEM((plan.shard_rows + 8, LANES), F32)],
            compiler_params=params_of,
            cost_estimate=brief,
        )(after(own_s, edge), quarters, other_quarters, small_got, one2, two2, ctx_pairs, *ctx_far)
        new_first, new_second = [m.reshape(-1)[:share] for m in (new_first, new_second)]

        near_l, half_done, edge, new_first, new_second = joint(near_l, half_done, edge, new_first, new_second)
        near_l = [block_l] + list(near_l)
        all_l = near_l + core_gather(near_l)

        def late(own_ref, *refs):
            late_kernel(plan, own_ref, refs[:n_parts], *refs[n_parts:])

        new_params = pl.pallas_call(
            late,
            out_shape=shape((ROWS_ALL, LANES), F32),
            in_specs=smem(1) + [any_spec] * n_parts + vmem(1) + [any_spec],
            out_specs=any_spec,
            scratch_shapes=[
                pltpu.VMEM((2, n_hi, 2, quarter, 2, late_rows, LANES), BF16),
                pltpu.VMEM((plan.row0[plan.early0 - 1] + plan.shard_rows, LANES), F32),
                pltpu.VMEM((SMALL_ROWS, LANES), F32),
                pltpu.SemaphoreType.DMA((max(n_parts, 8),)),
            ],
            input_output_aliases={n_parts + 2: 0},
            compiler_params=params_of,
        )(own_s, *all_l, edge, half_done)

        return out[None], context_grad, new_params.reshape(-1), new_first, new_second

    return per_device


def solution(mesh):
    return jax.shard_map(
        build(mesh),
        mesh=mesh,
        in_specs=(
            P(("dp", "group"), None),
            P(("dp", "group"), None),
            P(("dp", "group"), None, None, None),
            P(("dp", "group"), None, None),
            P(),
            P(),
            P("dp"),
            P("dp"),
            P(("dp", "group"), None, None),
        ),
        out_specs=(P(("dp", "group"), None, None), P(("dp", "group"), None), P(), P("dp"), P("dp")),
        check_vma=False,
    )
```

```python
import functools

import jax
import jax.numpy as jnp
from jax import lax
from jax.experimental import pallas as pl
from jax.experimental.pallas import tpu as pltpu
from jax.sharding import PartitionSpec as P

D_IN = 768
D = 384
HEADS = 12
HD = 32
FF = 1536
GRID = 196
BLOCKS = 4
TMAX = 40
STEP = 10
IMG = 4
CTX = 384
TGT = IMG * BLOCKS * TMAX
L = CTX + TGT
NP = D_IN * D + 4 * D * D + 2 * D * FF + 5 * D
LANES = 128
GROUPS = D // LANES
PER = LANES // HD
WIN = 200
KEYS = WIN + TMAX
WIDE = 256
TILE = 256
MLP_TILE = 512
CHUNK = 512

ROW_IN = 0
ROW_QKV = D_IN * D // LANES
ROW_OUT = ROW_QKV + 3 * D * D // LANES
ROW_UP = ROW_OUT + D * D // LANES
ROW_DOWN = ROW_UP + D * FF // LANES
ROW_SMALL = ROW_DOWN + FF * D // LANES
ROWS_ALL = NP // LANES
SMALL = 5 * D
SMALL_ROWS = SMALL // LANES
SMALL_PAD = 16

norm_eps = 1e-06
mask_value = -1e30
LOG2E = 1.4426950408889634
SCALE = HD**-0.5
F32 = jnp.float32
BF16 = jnp.bfloat16
VMEM_CAP = 60 * 1024 * 1024


def dot(a, b):
    return jnp.dot(a, b, preferred_element_type=F32)


def dot_nt(a, b):
    return lax.dot_general(a, b, (((1,), (1,)), ((), ())), preferred_element_type=F32)


def dot_tn(a, b):
    return lax.dot_general(a, b, (((0,), (0,)), ((), ())), preferred_element_type=F32)


def ceil_to(n, m):
    return -(-n // m) * m


class Plan:
    def __init__(self, n_dp, n_group):
        self.n_dp, self.n_group = n_dp, n_group
        self.share = NP // n_dp
        self.row0 = [d * self.share // LANES for d in range(n_dp)]
        self.lane0 = [d * self.share % LANES for d in range(n_dp)]
        most = max(ceil_to(o + self.share, LANES) // LANES for o in self.lane0)
        self.sub = ceil_to(-(-most // (2 * n_group)), 16)
        self.piece = 2 * self.sub
        self.shard_rows = self.piece * n_group
        self.n_hi, self.half = n_group // 2, n_dp // 2
        self.quarter = self.half // 2
        self.early0 = n_dp // 2
        assert self.early0 * self.share >= ROW_OUT * LANES
        self.helper = 2 * (self.half - 1 - self.quarter) + 1
        self.tail = ROW_SMALL - self.row0[-1]
        self.flat_rows = ceil_to(max(r + self.shard_rows for r in self.row0), 16)
        self.mid_rows = ceil_to(self.row0[self.early0 - 1] + self.shard_rows - ROW_OUT, 8)
        self.cut = ceil_to(self.early0 * self.share, 8 * LANES) // LANES


def layer_norm_parts(x):
    mu = jnp.mean(x, axis=-1, keepdims=True)
    xc = x - mu
    rstd = lax.rsqrt(jnp.mean(xc * xc, axis=-1, keepdims=True) + norm_eps)
    return xc * rstd, rstd


def layer_norm_back(dy, gain, xhat, rstd):
    dx = dy * gain
    a = jnp.mean(dx, axis=-1, keepdims=True)
    b = jnp.mean(dx * xhat, axis=-1, keepdims=True)
    return rstd * (dx - a - xhat * b)


def reciprocal(x):
    r = pl.reciprocal(x, approx=True)
    return r * (2.0 - x * r)


def gelu_both(x):
    z = jnp.abs(x) * (0.5**0.5)
    t = reciprocal(1.0 + 0.3275911 * z)
    e = jnp.exp2(x * x * (-0.5 * LOG2E))
    poly = ((((1.061405429 * t - 1.453152027) * t + 1.421413741) * t - 0.284496736) * t + 0.254829592) * t
    tail = 0.5 * poly * e
    cdf = jnp.where(x >= 0, 1.0 - tail, tail)
    pdf = e * 0.3989422804014327
    return x * cdf, cdf + x * pdf


def head_masks(first, count, width):
    lane = lax.broadcasted_iota(jnp.int32, (1, width), 1)
    return [(lane // HD == first + h).astype(F32) for h in range(count)]


def stack_heads(x, masks):
    return jnp.concatenate([x * m for m in masks], axis=0)


def diagonal(x, rows):
    return jnp.concatenate(
        [x[h * HD : (h + 1) * HD, h * rows : (h + 1) * rows] for h in range(PER)], axis=0
    )


def stack_six(x, masks):
    gap = jnp.zeros((WIDE // 2 - 3 * TMAX, WIDE), F32)
    parts = [x * m for m in masks]
    return jnp.concatenate(parts[:3] + [gap] + parts[3:] + [gap], axis=0).astype(BF16)


def fold_six(x, masks):
    total = None
    for h in range(6):
        at = (h // 3) * (WIDE // 2) + (h % 3) * TMAX
        part = x[at : at + TMAX] * masks[h]
        total = part if total is None else total + part
    return total


def half_masks(half):
    lane = lax.broadcasted_iota(jnp.int32, (1, WIDE), 1)
    head = (lane + half * LANES) // HD
    return [(head == 6 * half + h).astype(F32) for h in range(6)]


def half_slice(half, part):
    return pl.ds(pl.multiple_of(part * D + half * LANES, LANES), WIDE)


def lane_slice(g, part):
    return pl.ds(pl.multiple_of(part * D + g * LANES, LANES), LANES)


def prep_kernel(
    plan,
    own_s,
    params_hbm, index_ref, pos_ref,
    vec, own_ref,
    w_in_hbm, w_qkv_hbm, w_out_hbm, w_up_hbm, w_down_hbm, stream_hbm,
    pbuf, w_in_b, w_qkv_b, w_out_b, w_up_b, w_down_b, stream, hot_ref, sems, out_sems,
):
    spans = [
        (ROW_SMALL, SMALL_ROWS), (ROW_IN, ROW_QKV - ROW_IN), (ROW_QKV, ROW_OUT - ROW_QKV),
        (ROW_OUT, ROW_UP - ROW_OUT), (ROW_UP, ROW_DOWN - ROW_UP), (ROW_DOWN, ROW_SMALL - ROW_DOWN),
    ]
    copies = [
        pltpu.make_async_copy(params_hbm.at[pl.ds(r, n)], pbuf.at[pl.ds(r, n)], sems.at[i])
        for i, (r, n) in enumerate(spans)
    ]
    for c in copies:
        c.start()
    outgoing = []

    def send_out(src, dst):
        copy = pltpu.make_async_copy(src, dst, out_sems.at[len(outgoing)])
        copy.start()
        outgoing.append(copy)

    def take(base, rows, tiles, dst, step):
        def body(i, _):
            for c in range(tiles):
                src = pl.ds(base + i * (step * tiles) + c, step, stride=tiles)
                dst[pl.ds(pl.multiple_of(i * step, step), step), c * LANES : (c + 1) * LANES] = pbuf[src, :].astype(BF16)
            return 0
        lax.fori_loop(0, rows // step, body, 0)

    eye = lax.broadcasted_iota(jnp.int32, (TMAX, TMAX), 0) == lax.broadcasted_iota(jnp.int32, (TMAX, TMAX), 1)
    grid_id = lax.broadcasted_iota(jnp.int32, (TMAX, GRID), 1)
    for j in range(IMG * BLOCKS):
        row = index_ref[0, j // BLOCKS, j % BLOCKS : j % BLOCKS + 1, :]
        col = jnp.sum(jnp.where(eye, row, 0), axis=1, keepdims=True)
        hot_ref[j * TMAX : (j + 1) * TMAX, :] = (col == grid_id).astype(F32)

    copies[0].wait()
    vec[...] = jnp.zeros_like(vec)
    for k in range(5):
        for c in range(D // LANES):
            vec[k : k + 1, c * LANES : (c + 1) * LANES] = pbuf[pl.ds(ROW_SMALL + k * 3 + c, 1), :]
    mask_tok = vec[4:5, :]
    pos = pos_ref[...]
    pos_hi = pos.astype(BF16)
    pos_lo = (pos - pos_hi.astype(F32)).astype(BF16)
    for i in range(TGT // 128):
        rows = slice(i * 128, (i + 1) * 128)
        hot = hot_ref[rows, :].astype(BF16)
        stream[rows, :] = mask_tok + (dot(hot, pos_hi) + dot(hot, pos_lo))
    send_out(stream, stream_hbm)

    for n, (base, rows, tiles, dst, out, step) in enumerate((
        (ROW_IN, D_IN, 3, w_in_b, w_in_hbm, 128), (ROW_QKV, D, 9, w_qkv_b, w_qkv_hbm, 128),
        (ROW_OUT, D, 3, w_out_b, w_out_hbm, 128), (ROW_UP, D, 12, w_up_b, w_up_hbm, 128),
        (ROW_DOWN, FF, 3, w_down_b, w_down_hbm, 128),
    )):
        copies[1 + n].wait()
        take(base, rows, tiles, dst, step)
        send_out(dst, out)
    for i in range(2):
        own_ref[i] = pbuf[pl.ds(own_s[8 + i], plan.sub), :]
    for copy in outgoing:
        copy.wait()


def place_pieces(own_s, dst, parts, rows):
    n = len(parts)
    for r, part in enumerate(parts):
        at = pl.multiple_of(lax.rem(own_s[6] + (n - r), n) * rows, 16)
        dst[pl.ds(at, rows), :] = part


def window(seg_s, img):
    return pl.multiple_of(jnp.minimum(seg_s[img] // 8 * 8, CTX - WIN), 8)


def forward_kernel(
    plan,
    len_s, own_s,
    vec, ctx_own, ctx_got, seg_row, cot_ref,
    w_in_hbm, w_qkv_hbm, w_out_hbm, w_up_hbm, w_down_hbm, target_hbm,
    out_ref, keep_ref, send_ref, mid_ref, small_out, seg_s,
    ctx_hbm, stream_hbm, qkv_hbm, probs_c_hbm, probs_t_hbm, d_mixed_hbm, d_middle_hbm,
    w_in_b, w_qkv_b, w_out_b, w_up_b, w_down_b, ctx, stream, qkv, probs_c, probs_t,
    mixed, mixed_b, d_mixed, d_branch, d_middle, normed, bias, v_t, second, active, d_lift, e_down, gflat, live_col,
    sems, out_sems,
):
    copies = [
        pltpu.make_async_copy(src, dst, sems.at[i])
        for i, (src, dst) in enumerate((
            (w_in_hbm, w_in_b), (w_qkv_hbm, w_qkv_b), (target_hbm, stream.at[pl.ds(CTX, TGT)]),
            (w_out_hbm, w_out_b), (w_up_hbm, w_up_b), (w_down_hbm, w_down_b),
        ))
    ]
    for c in copies:
        c.start()
    outgoing = []

    def send_out(src, dst):
        copy = pltpu.make_async_copy(src, dst, out_sems.at[len(outgoing)])
        copy.start()
        outgoing.append(copy)

    gain1, bias1, gain2, bias2 = [vec[k : k + 1, :] for k in range(4)]
    seg = seg_row[...]
    for i in range(IMG + 1):
        seg_s[i] = jnp.sum((seg < i).astype(jnp.int32))
    row_id = lax.broadcasted_iota(jnp.int32, (CTX, CTX), 0)
    row_image = sum((row_id >= seg_s[i]).astype(jnp.int32) for i in range(1, IMG))
    bias[...] = jnp.where(row_image == seg, 0.0, mask_value)
    live_col[0:CTX, :] = jnp.ones((CTX, LANES), F32)
    slot_id = lax.broadcasted_iota(jnp.int32, (TMAX, LANES), 0)
    for j in range(IMG * BLOCKS):
        live_col[CTX + j * TMAX : CTX + (j + 1) * TMAX, :] = (slot_id < len_s[0, j // BLOCKS, j % BLOCKS]).astype(F32)

    stored = ctx_own.shape[0] // plan.n_group
    first = ctx_own[pl.ds(pl.multiple_of(own_s[6] * stored, 16), stored), :]
    place_pieces(own_s, ctx, [first] + [ref[...] for ref in ctx_got], stored)
    send_out(ctx, ctx_hbm)
    copies[0].wait()
    stream[0:CTX, :] = dot(ctx[...], w_in_b[...])
    copies[2].wait()
    send_out(stream, stream_hbm)
    copies[1].wait()

    def qkv_body(i, _):
        rows = pl.ds(pl.multiple_of(i * TILE, TILE), TILE)
        xhat, _r = layer_norm_parts(stream[rows, :])
        n = (xhat * gain1 + bias1).astype(BF16)
        normed[rows, :] = n
        qkv[rows, :] = dot(n, w_qkv_b[...]).astype(BF16).astype(F32)
        return 0

    lax.fori_loop(0, L // TILE, qkv_body, 0)

    send_out(qkv, qkv_hbm)
    masks = head_masks(0, PER, LANES)
    c2 = SCALE * LOG2E
    for g in range(GROUPS):
        v_t[g * LANES : (g + 1) * LANES, :] = qkv[0:CTX, 2 * D + g * LANES : 2 * D + (g + 1) * LANES].T.astype(BF16)

    def softmax_down(t):
        p = jnp.exp2(t - jnp.max(t, axis=0, keepdims=True))
        return (p * (1.0 / jnp.sum(p, axis=0, keepdims=True))).astype(BF16)

    def ctx_body(i, _):
        g, chunk = i // 3, i % 3
        rows = pl.ds(pl.multiple_of(chunk * LANES, LANES), LANES)
        lanes = pl.ds(pl.multiple_of(g * LANES, LANES), LANES)
        q = stack_heads(qkv[rows, lane_slice(g, 0)], masks).astype(BF16)
        st = dot_nt(qkv[0:CTX, lane_slice(g, 1)].astype(BF16), q)
        for h in range(PER):
            cols = slice(h * LANES, (h + 1) * LANES)
            probs_c[i, :, cols] = softmax_down(st[:, cols] * c2 + bias[:, rows])
        o = dot(v_t[lanes, :], probs_c[i])
        mixed[rows, lanes] = diagonal(o, LANES).T
        return 0

    lax.fori_loop(0, GROUPS * 3, ctx_body, 0)
    send_out(probs_c, probs_c_hbm)

    key_id = lax.broadcasted_iota(jnp.int32, (KEYS, 1), 0)
    mixed[CTX:, :] = jnp.zeros((TGT, D), F32)

    def tgt_body(i, _):
        half, img = i // IMG, i % IMG
        hmasks = half_masks(half)
        first = window(seg_s, img)
        kw = qkv[pl.ds(first, WIN), half_slice(half, 1)]
        vw = qkv[pl.ds(first, WIN), half_slice(half, 2)]
        lo, hi = seg_s[img] - first, seg_s[img + 1] - first
        in_win = (key_id >= lo) & (key_id < hi) & (key_id < WIN)
        units = []
        for blk in range(BLOCKS):
            j = img * BLOCKS + blk
            rows = pl.ds(pl.multiple_of(CTX + j * TMAX, 8), TMAX)
            k = jnp.concatenate([kw, qkv[rows, half_slice(half, 1)]], axis=0).astype(BF16)
            v = jnp.concatenate([vw, qkv[rows, half_slice(half, 2)]], axis=0).astype(BF16)
            q = stack_six(qkv[rows, half_slice(half, 0)], hmasks)
            ok = in_win | ((key_id >= WIN) & (key_id < WIN + len_s[0, img, blk]))
            units.append((rows, v, dot_nt(k, q), jnp.where(ok, 0.0, mask_value)))
        for blk, (rows, v, st, bias_col) in enumerate(units):
            for n in range(2):
                cols = slice(n * LANES, (n + 1) * LANES)
                probs_t[i * BLOCKS + blk, :, cols] = softmax_down(st[:, cols] * c2 + bias_col)
        for blk, (rows, v, st, bias_col) in enumerate(units):
            o = dot_tn(probs_t[i * BLOCKS + blk], v)
            mixed[rows, pl.ds(pl.multiple_of(half * LANES, LANES), WIDE)] += fold_six(o, hmasks)
        return 0

    lax.fori_loop(0, 2 * IMG, tgt_body, 0)
    send_out(probs_t, probs_t_hbm)

    for c in copies[3:]:
        c.wait()

    def mixed_of(rows):
        low = mixed[rows, :].astype(BF16)
        mixed_b[rows, :] = low
        return low

    def block_body(i, carry):
        dg2, db2 = carry
        rows = pl.ds(pl.multiple_of(i * MLP_TILE, MLP_TILE), MLP_TILE)
        live = live_col[rows, 0:1]
        middle = stream[rows, :] + dot(mixed_of(rows), w_out_b[...])
        xhat, rstd = layer_norm_parts(middle)
        sec = (xhat * gain2 + bias2).astype(BF16)
        second[rows, :] = sec
        top = live * cot_ref[rows, :].astype(F32)
        e = top.astype(BF16)
        e_down[rows, :] = e
        out = middle
        d_second = jnp.zeros((MLP_TILE, D), F32)
        for j in range(FF // CHUNK):
            cols = slice(j * CHUNK, (j + 1) * CHUNK)
            lifted = dot(sec, w_up_b[:, cols])
            act, slope = gelu_both(lifted)
            act = act.astype(BF16)
            active[rows, cols] = act
            dl = (dot_nt(e, w_down_b[cols, :]) * slope).astype(BF16)
            d_lift[rows, cols] = dl
            out = out + dot(act, w_down_b[cols, :])
            d_second = d_second + dot_nt(dl, w_up_b[:, cols])
        out_ref[rows, :] = (live * out).astype(BF16)
        dm = top + layer_norm_back(d_second, gain2, xhat, rstd)
        d_middle[rows, :] = dm
        db = dm.astype(BF16)
        d_branch[rows, :] = db
        d_mixed[rows, :] = dot_nt(db, w_out_b[...])
        dg2 = dg2 + jnp.sum(d_second * xhat, axis=0, keepdims=True)
        db2 = db2 + jnp.sum(d_second, axis=0, keepdims=True)
        return dg2, db2

    zero = jnp.zeros((1, D), F32)
    dg2, db2 = lax.fori_loop(0, L // MLP_TILE, block_body, (zero, zero))
    small_out[...] = jnp.concatenate([dg2, db2, jnp.zeros((6, D), F32)], axis=0)

    send_out(d_mixed, d_mixed_hbm)
    send_out(d_middle, d_middle_hbm)

    end = ROW_SMALL - ROW_OUT
    gflat[end:, :] = jnp.zeros((gflat.shape[0] - end, LANES), F32)

    g = dot_tn(mixed_b[...], d_branch[...])
    for c in range(3):
        gflat[pl.ds(c, D, stride=3), :] = g[:, c * LANES : (c + 1) * LANES]

    def up_body(j, _):
        cols = pl.ds(pl.multiple_of(j * CHUNK, CHUNK), CHUNK)
        g = dot_tn(second[...], d_lift[:, cols])
        for c in range(CHUNK // LANES):
            gflat[pl.ds(ROW_UP - ROW_OUT + CHUNK // LANES * j + c, D, stride=12), :] = g[:, c * LANES : (c + 1) * LANES]
        return 0

    lax.fori_loop(0, FF // CHUNK, up_body, 0)

    def down_body(j, _):
        cols = pl.ds(pl.multiple_of(j * D, D), D)
        g = dot_tn(active[:, cols], e_down[...])
        for c in range(3):
            gflat[pl.ds(ROW_DOWN - ROW_OUT + j * (3 * D) + c, D, stride=3), :] = g[:, c * LANES : (c + 1) * LANES]
        return 0

    lax.fori_loop(0, 4, down_body, 0)

    mid_ref[...] = gflat[0 : plan.mid_rows, :]
    put_pieces(plan, gflat, ROW_OUT, range(plan.early0, plan.n_dp), plan.quarter, own_s[1], keep_ref, send_ref)
    for copy in outgoing:
        copy.wait()


def put_pieces(plan, gflat, base, shards, hi0, core, keep_ref, send_ref, extra=None):
    for d in shards:
        for q in range(plan.n_group):
            start = plan.row0[d] - base + q * plan.piece
            blocks = [gflat[start + n * plan.sub : start + (n + 1) * plan.sub, :].astype(BF16) for n in range(2)]

            def put(ref):
                for n in range(2):
                    ref[q // 2, d % 2, d // 2 - hi0, n, 0 : plan.sub, :] = blocks[n]
                    if extra is not None:
                        ref[q // 2, d % 2, d // 2 - hi0, n, plan.sub :, :] = extra

            @pl.when(core == q % 2)
            def _():
                put(keep_ref)

            @pl.when(core != q % 2)
            def _():
                put(send_ref)


def attention_back_kernel(
    plan,
    seg_s, own_s, qkv_hbm, probs_c_hbm, probs_t_hbm, d_mixed_hbm, one_hbm, two_hbm,
    dpk, mine_ref, other_ref, qkv, probs_c, probs_t, d_mixed, d_qkv, k_t, mom, tail, sems,
):
    incoming = {}
    for n, (name, src, dst) in enumerate((
        ("qkv", qkv_hbm, qkv), ("d_mixed", d_mixed_hbm, d_mixed), ("probs_c", probs_c_hbm, probs_c),
        ("probs_t", probs_t_hbm, probs_t),
    )):
        incoming[name] = pltpu.make_async_copy(src, dst, sems.at[n])
        incoming[name].start()

    tail0 = plan.tail // 8 * 8
    moments = []
    for i, src in enumerate((one_hbm, two_hbm)):
        moments.append(pltpu.make_async_copy(src.at[pl.ds(own_s[4], plan.piece + 8)], mom.at[i], sems.at[4 + 2 * i]))
        moments.append(pltpu.make_async_copy(src.at[pl.ds(tail0, 32)], tail.at[i], sems.at[5 + 2 * i]))
    for copy in moments:
        copy.start()

    d_qkv[...] = jnp.zeros_like(d_qkv)
    masks = head_masks(0, PER, LANES)
    incoming["qkv"].wait()
    for g in range(GROUPS):
        k_t[g * LANES : (g + 1) * LANES, :] = qkv[0:CTX, D + g * LANES : D + (g + 1) * LANES].T.astype(BF16)
    incoming["d_mixed"].wait()
    incoming["probs_c"].wait()

    def back_down(p, dp):
        p = p.astype(F32)
        delta = jnp.sum(p * dp, axis=0, keepdims=True)
        return (p * (dp - delta)).astype(BF16)

    def ctx_body(i, _):
        g, chunk = i // 3, i % 3
        rows = pl.ds(pl.multiple_of(chunk * LANES, LANES), LANES)
        lanes = pl.ds(pl.multiple_of(g * LANES, LANES), LANES)
        do = stack_heads(d_mixed[rows, lanes], masks).astype(BF16)
        dpt = dot_nt(qkv[0:CTX, lane_slice(g, 2)].astype(BF16), do)
        ds = []
        for h in range(PER):
            cols = slice(h * LANES, (h + 1) * LANES)
            ds.append(back_down(probs_c[i, :, cols], dpt[:, cols]))
        ds = jnp.concatenate(ds, axis=1)
        q = stack_heads(qkv[rows, lane_slice(g, 0)], masks).astype(BF16)
        d_qkv[rows, lane_slice(g, 0)] = diagonal(dot(k_t[lanes, :], ds), LANES).T
        d_qkv[0:CTX, lane_slice(g, 1)] += dot(ds, q)
        d_qkv[0:CTX, lane_slice(g, 2)] += dot(probs_c[i], do)
        return 0

    lax.fori_loop(0, GROUPS * 3, ctx_body, 0)
    incoming["probs_t"].wait()

    def tgt_body(i, _):
        half, img = i // IMG, i % IMG
        hmasks = half_masks(half)
        first = window(seg_s, img)
        win = pl.ds(first, WIN)
        kw = qkv[win, half_slice(half, 1)]
        vw = qkv[win, half_slice(half, 2)]
        units = []
        for blk in range(BLOCKS):
            rows = pl.ds(pl.multiple_of(CTX + (img * BLOCKS + blk) * TMAX, 8), TMAX)
            v = jnp.concatenate([vw, qkv[rows, half_slice(half, 2)]], axis=0).astype(BF16)
            do = stack_six(d_mixed[rows, pl.ds(pl.multiple_of(half * LANES, LANES), WIDE)], hmasks)
            units.append((rows, do, dot_nt(v, do)))
        dkw = jnp.zeros((WIN, WIDE), F32)
        dvw = jnp.zeros((WIN, WIDE), F32)
        for blk, (rows, do, dpt) in enumerate(units):
            p = probs_t[i * BLOCKS + blk]
            ds = jnp.concatenate(
                [back_down(p[:, n * LANES : (n + 1) * LANES], dpt[:, n * LANES : (n + 1) * LANES]) for n in range(2)],
                axis=1,
            )
            k = jnp.concatenate([kw, qkv[rows, half_slice(half, 1)]], axis=0).astype(BF16)
            q = stack_six(qkv[rows, half_slice(half, 0)], hmasks)
            d_qkv[rows, half_slice(half, 0)] += fold_six(dot_tn(ds, k), hmasks)
            dk = dot(ds, q)
            dv = dot(p, do)
            d_qkv[rows, half_slice(half, 1)] += dk[WIN:]
            d_qkv[rows, half_slice(half, 2)] += dv[WIN:]
            dkw = dkw + dk[:WIN]
            dvw = dvw + dv[:WIN]
        d_qkv[win, half_slice(half, 1)] += dkw
        d_qkv[win, half_slice(half, 2)] += dvw
        return 0

    lax.fori_loop(0, 2 * IMG, tgt_body, 0)
    for copy in moments:
        copy.wait()
    lane = lax.broadcasted_iota(jnp.int32, (1, LANES), 1)
    for i in range(2):
        turned = pltpu.roll(mom[i], own_s[5], 1)
        aligned = jnp.where(lane >= own_s[5], turned[8:], turned[7:-1])
        mine_ref[i] = aligned[: plan.sub]
        other_ref[i, 0 : plan.sub, :] = aligned[plan.sub :]
        turned = pltpu.roll(tail[i], own_s[5], 1)
        aligned = jnp.where(lane >= own_s[5], turned[1:], turned[:-1])
        at = plan.tail - tail0 + 7
        other_ref[i, plan.sub : plan.sub + SMALL_PAD, :] = aligned[at : at + SMALL_PAD]

    def round_body(i, _):
        rows = pl.ds(pl.multiple_of(i * 128, 128), 128)
        dpk[rows, 0 : 2 * D] = (d_qkv[rows, 0 : 2 * D] * SCALE).astype(BF16)
        dpk[rows, 2 * D :] = d_qkv[rows, 2 * D :].astype(BF16)
        return 0

    lax.fori_loop(0, L // 128, round_body, 0)


def backward_kernel(
    plan,
    own_s,
    vec, small_in, mid_ref, dpk,
    w_in_hbm, w_qkv_hbm, ctx_hbm, stream_hbm, d_middle_hbm,
    keep_ref, send_ref, same_ref, cross_ref,
    w_in_b, w_qkv_b, ctx_ref, stream, d_middle, normed, d_hidden, ctx_grad, small_flat, gflat, sems,
):
    incoming = {}
    for n, (name, src, dst) in enumerate((
        ("w_qkv", w_qkv_hbm, w_qkv_b), ("stream", stream_hbm, stream), ("d_middle", d_middle_hbm, d_middle),
        ("w_in", w_in_hbm, w_in_b), ("ctx", ctx_hbm, ctx_ref),
    )):
        incoming[name] = pltpu.make_async_copy(src, dst, sems.at[n])
        incoming[name].start()
    gain1, bias1 = vec[0:1, :], vec[1:2, :]
    gflat[ROW_OUT : ROW_OUT + plan.mid_rows, :] = mid_ref[...]
    for name in ("w_qkv", "stream", "d_middle"):
        incoming[name].wait()

    def row_body(i, carry):
        dg1, db1, dmask = carry
        rows = pl.ds(pl.multiple_of(i * 128, 128), 128)
        xhat, rstd = layer_norm_parts(stream[rows, :])
        normed[rows, :] = (xhat * gain1 + bias1).astype(BF16)
        d_normed = dot_nt(dpk[rows, :], w_qkv_b[...])
        d_stream = d_middle[rows, :] + layer_norm_back(d_normed, gain1, xhat, rstd)
        dg1 = dg1 + jnp.sum(d_normed * xhat, axis=0, keepdims=True)
        db1 = db1 + jnp.sum(d_normed, axis=0, keepdims=True)
        is_tgt = (i >= CTX // 128).astype(F32)
        dmask = dmask + is_tgt * jnp.sum(d_stream, axis=0, keepdims=True)

        @pl.when(i < CTX // 128)
        def _():
            d_hidden[rows, :] = d_stream.astype(BF16)

        return dg1, db1, dmask

    zero = jnp.zeros((1, D), F32)
    dg1, db1, dmask = lax.fori_loop(0, L // 128, row_body, (zero, zero, zero))
    for k, row in enumerate((dg1, db1, small_in[0:1, :], small_in[1:2, :], dmask)):
        for c in range(3):
            small_flat[3 * k + c : 3 * k + c + 1, :] = row[:, c * LANES : (c + 1) * LANES]
    small_flat[SMALL_ROWS:, :] = jnp.zeros((SMALL_PAD - SMALL_ROWS, LANES), F32)

    incoming["w_in"].wait()
    incoming["ctx"].wait()
    ctx_grad[...] = dot_nt(d_hidden[...], w_in_b[...]).astype(BF16)
    stored = CTX // plan.n_group
    for a in range(plan.n_hi):
        hi = lax.rem(own_s[2] + a, plan.n_hi) * 2
        for ref, core in ((same_ref, own_s[1]), (cross_ref, 1 - own_s[1])):
            ref[a] = ctx_grad[pl.ds(pl.multiple_of((hi + core) * stored, 16), stored), :]
    for j in range(2):
        g = dot_tn(ctx_ref[:, j * D : (j + 1) * D], d_hidden[...])
        for c in range(3):
            gflat[pl.ds(ROW_IN + j * 3 * D + c, D, stride=3), :] = g[:, c * LANES : (c + 1) * LANES]
    for j in range(3):
        g = dot_tn(normed[...], dpk[:, j * D : (j + 1) * D])
        for c in range(3):
            gflat[pl.ds(ROW_QKV + 3 * j + c, D, stride=9), :] = g[:, c * LANES : (c + 1) * LANES]
    put_pieces(plan, gflat, 0, range(plan.early0), 0, own_s[1], keep_ref, send_ref, small_flat[...].astype(BF16))


def vmem(n):
    return [pl.BlockSpec(memory_space=pltpu.VMEM)] * n


def smem(n):
    return [pl.BlockSpec(memory_space=pltpu.SMEM)] * n


def shape(dims, dtype):
    return jax.ShapeDtypeStruct(dims, dtype)


def fetch_blocks(plan, own_s, refs, rels, dst, sems):
    copies = []
    for i, (ref, (c_rel, a_rel, b_rel)) in enumerate(zip(refs, rels)):
        core = lax.rem(own_s[1] + c_rel, 2)
        hi = lax.rem(own_s[2] + a_rel, plan.n_hi)
        lo = lax.rem(own_s[3] + b_rel, 2)
        copies.append(pltpu.make_async_copy(ref, dst.at[core, hi, lo], sems.at[i]))
    for copy in copies:
        copy.start()
    for copy in copies:
        copy.wait()


def put_rows(plan, shards, hi0, src, out, base):
    for d in shards:
        lane0 = plan.lane0[d]
        rows = ceil_to(lane0 + plan.share, LANES) // LANES
        for q in range(plan.n_group):
            for n in range(2):
                start = q * plan.piece + n * plan.sub
                count = min(plan.sub, rows - start)
                if count <= 0:
                    continue
                block = src[q % 2, q // 2, d % 2, d // 2 - hi0, n, 0 : plan.sub, :].astype(F32)
                at = plan.row0[d] + start - base
                if start == 0 and lane0:
                    lane = lax.broadcasted_iota(jnp.int32, (1, LANES), 1)
                    out[at : at + 1, :] = jnp.where(lane < lane0, out[at : at + 1, :], block[0:1])
                    out[at + 1 : at + count, :] = block[1:count]
                else:
                    out[at : at + count, :] = block[:count]


def early_kernel(plan, own_s, near, far, out_hbm, edge_ref, blocks, buf, sems):
    rels = [(c, a, b) for c in range(2) for b in range(2) for a in range(plan.n_hi)]
    refs = [src.at[i] for src in (near, far) for i in range(2 * plan.n_hi)]
    fetch_blocks(plan, own_s, refs, rels, blocks, sems)
    base = plan.cut - 8
    buf[0:8, :] = jnp.zeros((8, LANES), F32)
    put_rows(plan, range(plan.early0, plan.n_dp), plan.quarter, blocks, buf, base)
    edge_ref[...] = buf[0:8, :]
    copy = pltpu.make_async_copy(
        buf.at[pl.ds(8, ROW_SMALL - plan.cut)], out_hbm.at[pl.ds(plan.cut, ROW_SMALL - plan.cut)], sems.at[0]
    )
    copy.start()
    copy.wait()


def late_kernel(plan, own_s, refs, edge_ref, done_hbm, out_hbm, blocks, buf, tail, sems):
    rels = [(c, a, b) for c in range(2) for a in range(plan.n_hi) for b in range(2)]
    fetch_blocks(plan, own_s, refs, rels, blocks, sems)
    small = blocks[0, 0, plan.helper % 2, plan.helper // 2, 0, plan.sub :, :].astype(F32)
    tail[...] = small[:SMALL_ROWS]
    copies = [pltpu.make_async_copy(tail, out_hbm.at[pl.ds(ROW_SMALL, SMALL_ROWS)], sems.at[0])]
    copies[0].start()
    done = 0
    for d in range(plan.early0):
        put_rows(plan, [d], 0, blocks, buf, 0)
        upto = (plan.row0[d + 1] // 8) * 8
        if d == plan.early0 - 1:
            upto = plan.cut
            at = plan.row0[d + 1]
            lane0 = plan.lane0[d + 1]
            if at < plan.cut:
                lane = lax.broadcasted_iota(jnp.int32, (1, LANES), 1)
                edge = edge_ref[at - plan.cut + 8 :, :]
                own = buf[at : plan.cut, :]
                row = lax.broadcasted_iota(jnp.int32, (plan.cut - at, 1), 0)
                buf[at : plan.cut, :] = jnp.where((row == 0) & (lane < lane0), own, edge)
        if (d + 1) % max(1, plan.early0 // 4) == 0:
            copies.append(pltpu.make_async_copy(
                buf.at[pl.ds(done, upto - done)], out_hbm.at[pl.ds(done, upto - done)], sems.at[len(copies)]
            ))
            copies[-1].start()
            done = upto
    for copy in copies:
        copy.wait()


def moment_kernel(plan, own_s, same, cross, given, one_ref, two_ref, ctx_pairs, *rest):
    ctx_far, (first_ref, second_ref, ctx_ref, grad) = rest[: plan.n_hi - 1], rest[plan.n_hi - 1 :]
    rows, stored = plan.shard_rows, ctx_ref.shape[0] // plan.n_group
    for a in range(plan.n_hi):
        back = lax.rem(own_s[2] + plan.n_hi - a, plan.n_hi) * 2
        ahead = lax.rem(own_s[2] + a, plan.n_hi) * 2
        for n, core in enumerate((own_s[1], 1 - own_s[1])):
            at = pl.multiple_of((back + core) * stored, 16)
            ctx_ref[pl.ds(at, stored), :] = ctx_far[a - 1][n] if a else ctx_pairs[0, n]
            at = pl.multiple_of((ahead + core) * plan.piece, 16)
            grad[pl.ds(at, plan.piece), :] = (cross if n else same)[a].astype(F32)
    grad[rows:, :] = jnp.zeros((8, LANES), F32)

    @pl.when(own_s[7] == plan.n_dp - 1)
    def _():
        at = ROW_SMALL - plan.row0[-1]
        grad[at : at + SMALL_ROWS, :] = given[plan.sub :, :].astype(F32)[:SMALL_ROWS]

    lane = lax.broadcasted_iota(jnp.int32, (1, LANES), 1)
    back = LANES - own_s[5]
    for i in range(plan.n_group):
        at = slice(i * plan.piece, (i + 1) * plan.piece)
        turned = pltpu.roll(grad[i * plan.piece : (i + 1) * plan.piece + 8, :], back, 1)
        g = jnp.where(lane < back, turned[: plan.piece], turned[1 : plan.piece + 1])
        first_ref[at, :] = 0.5 * one_ref[8 + i * plan.piece : 8 + (i + 1) * plan.piece, :] + 0.5 * g
        second_ref[at, :] = 0.6 * two_ref[8 + i * plan.piece : 8 + (i + 1) * plan.piece, :] + 0.4 * g * g


def adam(weight, grad, one, two):
    first = 0.5 * one + 0.5 * grad
    second = 0.6 * two + 0.4 * grad * grad
    step = (first / (1.0 - 0.5**STEP)) / (jnp.sqrt(second / (1.0 - 0.6**STEP)) + 1e-08)
    return weight - 0.05 * (step + 0.05 * weight)


def after(value, *others):
    return lax.optimization_barrier((value, others))[0]


def build(mesh):
    n_dp, n_group = mesh.shape["dp"], mesh.shape["group"]
    plan = Plan(n_dp, n_group)
    both = ("dp", "group")
    n_hi, half, quarter = plan.n_hi, plan.half, plan.quarter
    piece, sub = plan.piece, plan.sub
    any_spec = pl.BlockSpec(memory_space=pl.ANY)
    brief = pl.CostEstimate(flops=0, bytes_accessed=0, transcendentals=0)
    params_of = pltpu.CompilerParams(vmem_limit_bytes=VMEM_CAP)

    def pairs(move):
        out = []
        for d in range(n_dp):
            for g in range(n_group):
                ghi, glo, dhi, dlo = move(g // 2, g % 2, d // 2, d % 2)
                out.append((d * n_group + g, (dhi * 2 + dlo) * n_group + ghi * 2 + glo))
        return out

    core_pairs = pairs(lambda gh, gl, dh, dl: (gh, 1 - gl, dh, dl))
    swap_pairs = pairs(lambda gh, gl, dh, dl: (gh, gl, (dh + quarter) % half, dl))

    def xy_pairs(a, b):
        return pairs(lambda gh, gl, dh, dl: ((gh + a) % n_hi, gl, dh, (dl + b) % 2))

    def z_pairs(r):
        return pairs(lambda gh, gl, dh, dl: (gh, gl, (dh + r) % half, dl))

    def group_pairs(r):
        return [(i, (i + r) % n_group) for i in range(n_group)]

    rels = [(a, b) for a in range(n_hi) for b in range(2)]
    def pick(array, index):
        return lax.dynamic_index_in_dim(array, index, 0, keepdims=False)

    def slot_of(h, early):
        return (h % quarter) * 2 + (h // quarter + early) % 2

    def xy_blocks(keep, got, gh, dl):
        def block(a, b):
            i, j = (gh + a) % n_hi, (dl + b) % 2
            mine, theirs = pick(pick(keep, i), j), pick(pick(got, i), j)
            return (mine.astype(F32) + theirs.astype(F32)).astype(BF16)
        return [block(a, b) for a, b in rels]

    def xy_send(blocks):
        return [lax.ppermute(x, both, xy_pairs(a, b)) for x, (a, b) in zip(blocks[1:], rels[1:])]

    def z_blocks(block, arrived, dh, early):
        total = block.astype(F32)
        for part in arrived:
            total = total + part.astype(F32)
        total = total.astype(BF16)
        total = total.reshape((2 * quarter,) + total.shape[2:])
        return [pick(total, slot_of((dh + r) % half, early)) for r in range(half)]

    def z_send(blocks):
        return [lax.ppermute(x, both, z_pairs(r)) for r, x in enumerate(blocks) if r]

    def z_sum(block, arrived):
        total = block.astype(F32)
        for part in arrived:
            total = total + part.astype(F32)
        return total

    def z_gather(mine):
        return [lax.ppermute(mine, both, z_pairs(r)) for r in range(1, half)]

    def z_order(got, sender, early):
        blocks = []
        for t in range(quarter):
            for n in range(2):
                want = (t + early * quarter + n * quarter) % half
                block = got[0]
                for i in range(1, half):
                    block = jnp.where(sender(i) == want, got[i], block)
                blocks.append(block)
        return jnp.stack(blocks).reshape((quarter, 2) + blocks[0].shape)

    def xy_gather(block):
        return [lax.ppermute(block, both, xy_pairs(-a, -b)) for a, b in rels[1:]]

    def core_gather(blocks):
        return [lax.ppermute(b, both, core_pairs) for b in blocks]

    def per_device(
        context, segment_ids, target_index, target_length, pos_table, params, first_moment, second_moment, cotangent
    ):
        stored = context.shape[0] // n_group
        dp, me = lax.axis_index("dp"), lax.axis_index("group")
        gh, gl, dh, dl = me // 2, me % 2, dp // 2, dp % 2
        share = plan.share

        ctx_got = [
            lax.ppermute(
                lax.dynamic_slice_in_dim(context, (me + r) % n_group * stored, stored), "group", group_pairs(r)
            )
            for r in range(1, n_group)
        ]

        lane0 = (dp * share) % LANES

        def own_row(early):
            t = dh % quarter + early * quarter
            n = (dh // quarter + early) % 2
            return ((t * 2 + dl) * share) // LANES + me * piece + n * sub

        own_s = jnp.stack(
            [0 * me, gl, gh, dl, me * piece, lane0, me, dp, own_row(0), own_row(1)]
        ).astype(jnp.int32)
        params2 = params.reshape(ROWS_ALL, LANES)

        weights = [((D_IN, D), BF16), ((D, 3 * D), BF16), ((D, D), BF16), ((D, FF), BF16), ((FF, D), BF16)]
        prep = pl.pallas_call(
            functools.partial(prep_kernel, plan),
            out_shape=[shape((8, D), F32), shape((2, sub, LANES), F32)]
            + [shape(*w) for w in weights] + [shape((TGT, D), F32)],
            in_specs=smem(1) + [any_spec] + vmem(2),
            out_specs=vmem(2) + [any_spec] * 6,
            scratch_shapes=[pltpu.VMEM((plan.flat_rows, LANES), F32)] + [pltpu.VMEM(*w) for w in weights] + [
                pltpu.VMEM((TGT, D), F32),
                pltpu.VMEM((TGT, GRID), F32),
                pltpu.SemaphoreType.DMA((6,)),
                pltpu.SemaphoreType.DMA((6,)),
            ],
            compiler_params=params_of,
        )(own_s, params2, target_index, pos_table)
        vec, own_w, w_in_b, w_qkv_b, w_out_b, w_up_b, w_down_b, target_rows = prep

        early_rows, late_rows = sub, sub + SMALL_PAD
        n_blocks = 2 * n_hi
        out_specs = [
            shape((L, D), BF16),
            shape((n_hi, 2, quarter, 2, early_rows, LANES), BF16),
            shape((n_hi, 2, quarter, 2, early_rows, LANES), BF16),
            shape((plan.mid_rows, LANES), F32),
            shape((8, D), F32),
            shape((8,), jnp.int32),
        ]
        saved = [
            ((CTX, D_IN), BF16),
            ((L, D), F32),
            ((L, 3 * D), F32),
            ((GROUPS * 3, CTX, PER * LANES), BF16),
            ((2 * IMG * BLOCKS, KEYS, WIDE), BF16),
            ((L, D), F32),
            ((L, D), F32),
        ]

        def forward(*refs):
            n = 2 + 2
            forward_kernel(plan, *refs[:n], refs[n : n + n_group - 1], *refs[n + n_group - 1 :])

        fwd = pl.pallas_call(
            forward,
            out_shape=out_specs + [shape(*s) for s in saved],
            in_specs=smem(2) + vmem(2 + n_group - 1 + 2) + [any_spec] * 6,
            out_specs=vmem(len(out_specs) - 1) + smem(1) + [any_spec] * len(saved),
            scratch_shapes=[pltpu.VMEM(*w) for w in weights] + [pltpu.VMEM(*s) for s in saved[:5]] + [
                pltpu.VMEM((L, D), F32),
                pltpu.VMEM((L, D), BF16),
                pltpu.VMEM((L, D), F32),
                pltpu.VMEM((L, D), BF16),
                pltpu.VMEM((L, D), F32),
                pltpu.VMEM((L, D), BF16),
                pltpu.VMEM((CTX, CTX), F32),
                pltpu.VMEM((D, CTX), BF16),
                pltpu.VMEM((L, D), BF16),
                pltpu.VMEM((L, FF), BF16),
                pltpu.VMEM((L, FF), BF16),
                pltpu.VMEM((L, D), BF16),
                pltpu.VMEM((plan.flat_rows - ROW_OUT, LANES), F32),
                pltpu.VMEM((L, LANES), F32),
                pltpu.SemaphoreType.DMA((6,)),
                pltpu.SemaphoreType.DMA((len(saved),)),
            ],
            compiler_params=params_of,
        )(
            target_length, own_s,
            vec, context, *ctx_got, segment_ids, cotangent[0],
            w_in_b, w_qkv_b, w_out_b, w_up_b, w_down_b, target_rows,
        )
        out, keep_e, send_e, mid, small_in, seg_s = fwd[: len(out_specs)]
        ctx_s, stream_s, qkv_s, probs_c_s, probs_t_s, d_mixed_s, d_middle_s = fwd[len(out_specs) :]

        got_e = lax.ppermute(send_e, both, core_pairs)
        spare = plan.shard_rows * LANES - share
        one2, two2 = [
            jnp.pad(m, (8 * LANES, spare)).reshape(8 + plan.shard_rows, LANES) for m in after((first_moment, second_moment), seg_s)
        ]

        xy_e = xy_blocks(keep_e, got_e, gh, dl)
        xy_got_e = xy_send(xy_e)
        qkv_s = after(qkv_s, *xy_e)

        dpk, own_mom, other_mom = pl.pallas_call(
            functools.partial(attention_back_kernel, plan),
            out_shape=[
                shape((L, 3 * D), BF16), shape((2, sub, LANES), F32), shape((2, sub + SMALL_PAD, LANES), F32),
            ],
            in_specs=smem(2) + [any_spec] * 6,
            out_specs=vmem(3),
            scratch_shapes=[pltpu.VMEM(*s) for s in saved[2:6]] + [
                pltpu.VMEM((L, 3 * D), F32),
                pltpu.VMEM((D, CTX), BF16),
                pltpu.VMEM((2, piece + 8, LANES), F32),
                pltpu.VMEM((2, 32, LANES), F32),
                pltpu.SemaphoreType.DMA((8,)),
            ],
            compiler_params=params_of,
            cost_estimate=pl.CostEstimate(flops=10**10, bytes_accessed=20 * 10**6, transcendentals=0),
        )(seg_s, own_s, qkv_s, probs_c_s, probs_t_s, d_mixed_s, one2, two2)

        xy_got_e = [after(x, dpk) for x in xy_got_e]
        z_e = z_blocks(xy_e[0], xy_got_e, dh, 1)
        z_got_e = z_send(z_e)
        swapped = lax.ppermute(other_mom, both, swap_pairs)
        dpk = after(dpk, *z_e)

        bwd_out = [
            shape((n_hi, 2, quarter, 2, late_rows, LANES), BF16),
            shape((n_hi, 2, quarter, 2, late_rows, LANES), BF16),
            shape((n_hi, stored, D_IN), BF16),
            shape((n_hi, stored, D_IN), BF16),
        ]
        bwd = pl.pallas_call(
            functools.partial(backward_kernel, plan),
            out_shape=bwd_out,
            in_specs=smem(1) + vmem(4) + [any_spec] * 5,
            out_specs=vmem(len(bwd_out)),
            scratch_shapes=[
                pltpu.VMEM((D_IN, D), BF16),
                pltpu.VMEM((D, 3 * D), BF16),
                pltpu.VMEM((CTX, D_IN), BF16),
                pltpu.VMEM((L, D), F32),
                pltpu.VMEM((L, D), F32),
                pltpu.VMEM((L, D), BF16),
                pltpu.VMEM((CTX, D), BF16),
                pltpu.VMEM((CTX, D_IN), BF16),
                pltpu.VMEM((SMALL_PAD, LANES), F32),
                pltpu.VMEM((ROW_OUT + plan.mid_rows, LANES), F32),
                pltpu.SemaphoreType.DMA((5,)),
            ],
            compiler_params=params_of,
            cost_estimate=pl.CostEstimate(flops=5 * 10**9, bytes_accessed=15 * 10**6, transcendentals=0),
        )(own_s, vec, small_in, mid, dpk, w_in_b, w_qkv_b, ctx_s, stream_s, d_middle_s)
        keep_l, send_l, ctx_same, ctx_cross = bwd

        upper = dh // quarter
        own_is_late = upper == 0

        def moments_of(early):
            return jnp.where(upper == early, own_mom, swapped[:, :sub])

        def all_after(values, *others):
            return [after(x, *others) for x in values]

        def joint(*groups):
            return lax.optimization_barrier(groups)

        z_got_e, swapped = joint(all_after(z_got_e, keep_l), after(swapped, keep_l))
        tails = swapped[:, sub:]
        got_l = lax.ppermute(after(send_l, *z_got_e), both, core_pairs)
        own_e = z_sum(z_e[0], z_got_e)
        mom = moments_of(1)
        new_e = adam(own_w[1], own_e, mom[0], mom[1]).astype(BF16)
        ctx_cross = lax.ppermute(after(ctx_cross, *z_got_e), both, core_pairs)
        got_l, ctx_cross, new_e = joint(got_l, ctx_cross, new_e)
        ctx_pairs = jnp.stack([ctx_same, ctx_cross], axis=1)

        xy_l = xy_blocks(keep_l, got_l, gh, dl)
        xy_got_l, z_new_e, own_e = joint(xy_send(xy_l), z_gather(after(new_e, *xy_l)), own_e)

        z_l = z_blocks(xy_l[0], xy_got_l, dh, 0)
        block_e = z_order([new_e] + list(z_new_e), lambda i: (dh - i) % half, 1)[None]
        z_got_l, near_e, ctx_far = joint(
            z_send(z_l), [lax.ppermute(block_e, both, xy_pairs(-a, 0)) for a in range(1, n_hi)],
            [lax.ppermute(after(ctx_pairs[a], *z_l), both, xy_pairs(a, 0)) for a in range(1, n_hi)],
        )
        own_l = z_sum(z_l[0], z_got_l)
        small_sum = own_l[sub:]
        small_w = jnp.pad(params[NP - SMALL :].reshape(SMALL_ROWS, LANES), ((0, SMALL_PAD - SMALL_ROWS), (0, 0)))
        mom = moments_of(0)
        new_l = jnp.concatenate([
            adam(own_w[0], own_l[:sub], mom[0], mom[1]), adam(small_w, small_sum, tails[0], tails[1])
        ]).astype(BF16)

        near_e = jnp.concatenate([block_e] + list(near_e))
        give = jnp.where(own_is_late, own_e, own_l[:sub])
        give = jnp.concatenate([give, small_sum]).astype(BF16)
        have = jnp.where(own_is_late, own_l[:sub], own_e).astype(BF16)
        z_new_l, y_near_e, taken = joint(
            z_gather(new_l), lax.ppermute(near_e, both, xy_pairs(0, 1)), lax.ppermute(give, both, swap_pairs)
        )

        block_l = z_order([new_l] + list(z_new_l), lambda i: (dh - i) % half, 0)
        near_e = jnp.concatenate([near_e, y_near_e])
        near_l = xy_gather(block_l)
        far_e = lax.ppermute(after(near_e, block_l), both, core_pairs)
        own = jnp.concatenate([have, taken[:sub]])
        quarters = jnp.stack(
            [own] + [lax.ppermute(after(own, block_l), both, xy_pairs(-a, 0)) for a in range(1, n_hi)]
        )
        other_quarters = lax.ppermute(quarters, both, core_pairs)

        n_parts = 2 * n_blocks
        base = plan.cut - 8

        half_done, edge = pl.pallas_call(
            functools.partial(early_kernel, plan),
            out_shape=[shape((ROWS_ALL, LANES), F32), shape((8, LANES), F32)],
            in_specs=smem(1) + [any_spec] * 2,
            out_specs=[any_spec, pl.BlockSpec(memory_space=pltpu.VMEM)],
            scratch_shapes=[
                pltpu.VMEM((2, n_hi, 2, quarter, 2, early_rows, LANES), BF16),
                pltpu.VMEM((plan.flat_rows - base, LANES), F32),
                pltpu.SemaphoreType.DMA((n_parts,)),
            ],
            compiler_params=params_of,
            cost_estimate=brief,
        )(after(own_s, block_l), near_e, far_e)

        new_first, new_second, context_grad = pl.pallas_call(
            functools.partial(moment_kernel, plan),
            out_shape=[shape((plan.shard_rows, LANES), F32)] * 2 + [shape(context.shape, BF16)],
            in_specs=smem(1) + vmem(6 + n_hi - 1),
            out_specs=vmem(3),
            scratch_shapes=[pltpu.VMEM((plan.shard_rows + 8, LANES), F32)],
            compiler_params=params_of,
            cost_estimate=brief,
        )(after(own_s, edge), quarters, other_quarters, taken, one2, two2, ctx_pairs, *ctx_far)
        new_first, new_second = [m.reshape(-1)[:share] for m in (new_first, new_second)]

        near_l, half_done, edge, new_first, new_second = joint(near_l, half_done, edge, new_first, new_second)
        near_l = [block_l] + list(near_l)
        all_l = near_l + core_gather(near_l)

        def late(own_ref, *refs):
            late_kernel(plan, own_ref, refs[:n_parts], *refs[n_parts:])

        new_params = pl.pallas_call(
            late,
            out_shape=shape((ROWS_ALL, LANES), F32),
            in_specs=smem(1) + [any_spec] * n_parts + vmem(1) + [any_spec],
            out_specs=any_spec,
            scratch_shapes=[
                pltpu.VMEM((2, n_hi, 2, quarter, 2, late_rows, LANES), BF16),
                pltpu.VMEM((plan.row0[plan.early0 - 1] + plan.shard_rows, LANES), F32),
                pltpu.VMEM((SMALL_ROWS, LANES), F32),
                pltpu.SemaphoreType.DMA((max(n_parts, 8),)),
            ],
            input_output_aliases={n_parts + 2: 0},
            compiler_params=params_of,
        )(own_s, *all_l, edge, half_done)

        return out[None], context_grad, new_params.reshape(-1), new_first, new_second

    return per_device


def solution(mesh):
    return jax.shard_map(
        build(mesh),
        mesh=mesh,
        in_specs=(
            P(("dp", "group"), None),
            P(("dp", "group"), None),
            P(("dp", "group"), None, None, None),
            P(("dp", "group"), None, None),
            P(),
            P(),
            P("dp"),
            P("dp"),
            P(("dp", "group"), None, None),
        ),
        out_specs=(P(("dp", "group"), None, None), P(("dp", "group"), None), P(), P("dp"), P("dp")),
        check_vma=False,
    )
```

```python
import functools

import jax
import jax.numpy as jnp
from jax import lax
from jax.experimental import pallas as pl
from jax.experimental.pallas import tpu as pltpu
from jax.sharding import PartitionSpec as P

D_IN = 768
D = 384
HEADS = 12
HD = 32
FF = 1536
GRID = 196
BLOCKS = 4
TMAX = 40
STEP = 10
IMG = 4
CTX = 384
TGT = IMG * BLOCKS * TMAX
L = CTX + TGT
NP = D_IN * D + 4 * D * D + 2 * D * FF + 5 * D
LANES = 128
GROUPS = D // LANES
PER = LANES // HD
WIN = 200
KEYS = WIN + TMAX
WIDE = 256
TILE = 256
MLP_TILE = 512
CHUNK = 512

ROW_IN = 0
ROW_QKV = D_IN * D // LANES
ROW_OUT = ROW_QKV + 3 * D * D // LANES
ROW_UP = ROW_OUT + D * D // LANES
ROW_DOWN = ROW_UP + D * FF // LANES
ROW_SMALL = ROW_DOWN + FF * D // LANES
ROWS_ALL = NP // LANES
SMALL = 5 * D
SMALL_ROWS = SMALL // LANES
SMALL_PAD = 16

norm_eps = 1e-06
mask_value = -1e30
LOG2E = 1.4426950408889634
SCALE = HD**-0.5
F32 = jnp.float32
BF16 = jnp.bfloat16
VMEM_CAP = 60 * 1024 * 1024


def dot(a, b):
    return jnp.dot(a, b, preferred_element_type=F32)


def dot_nt(a, b):
    return lax.dot_general(a, b, (((1,), (1,)), ((), ())), preferred_element_type=F32)


def dot_tn(a, b):
    return lax.dot_general(a, b, (((0,), (0,)), ((), ())), preferred_element_type=F32)


def ceil_to(n, m):
    return -(-n // m) * m


class Plan:
    def __init__(self, n_dp, n_group):
        self.n_dp, self.n_group = n_dp, n_group
        self.share = NP // n_dp
        self.row0 = [d * self.share // LANES for d in range(n_dp)]
        self.lane0 = [d * self.share % LANES for d in range(n_dp)]
        most = max(ceil_to(o + self.share, LANES) // LANES for o in self.lane0)
        self.sub = ceil_to(-(-most // (2 * n_group)), 16)
        self.piece = 2 * self.sub
        self.shard_rows = self.piece * n_group
        self.n_hi, self.half = n_group // 2, n_dp // 2
        self.quarter = self.half // 2
        self.early0 = n_dp // 2
        assert self.early0 * self.share >= ROW_OUT * LANES
        self.helper = 2 * (self.half - 1 - self.quarter) + 1
        self.tail = ROW_SMALL - self.row0[-1]
        self.flat_rows = ceil_to(max(r + self.shard_rows for r in self.row0), 16)
        self.mid_rows = ceil_to(self.row0[self.early0 - 1] + self.shard_rows - ROW_OUT, 8)
        self.cut = ceil_to(self.early0 * self.share, 8 * LANES) // LANES


def layer_norm_parts(x):
    mu = jnp.mean(x, axis=-1, keepdims=True)
    xc = x - mu
    rstd = lax.rsqrt(jnp.mean(xc * xc, axis=-1, keepdims=True) + norm_eps)
    return xc * rstd, rstd


def layer_norm_back(dy, gain, xhat, rstd):
    dx = dy * gain
    a = jnp.mean(dx, axis=-1, keepdims=True)
    b = jnp.mean(dx * xhat, axis=-1, keepdims=True)
    return rstd * (dx - a - xhat * b)


def reciprocal(x):
    r = pl.reciprocal(x, approx=True)
    return r * (2.0 - x * r)


def gelu_both(x):
    z = jnp.abs(x) * (0.5**0.5)
    t = reciprocal(1.0 + 0.3275911 * z)
    e = jnp.exp2(x * x * (-0.5 * LOG2E))
    poly = ((((1.061405429 * t - 1.453152027) * t + 1.421413741) * t - 0.284496736) * t + 0.254829592) * t
    tail = 0.5 * poly * e
    cdf = jnp.where(x >= 0, 1.0 - tail, tail)
    pdf = e * 0.3989422804014327
    return x * cdf, cdf + x * pdf


def head_masks(first, count, width):
    lane = lax.broadcasted_iota(jnp.int32, (1, width), 1)
    return [(lane // HD == first + h).astype(F32) for h in range(count)]


def stack_heads(x, masks):
    return jnp.concatenate([x * m for m in masks], axis=0)


def diagonal(x, rows):
    return jnp.concatenate(
        [x[h * HD : (h + 1) * HD, h * rows : (h + 1) * rows] for h in range(PER)], axis=0
    )


def stack_six(x, masks):
    gap = jnp.zeros((WIDE // 2 - 3 * TMAX, WIDE), F32)
    parts = [x * m for m in masks]
    return jnp.concatenate(parts[:3] + [gap] + parts[3:] + [gap], axis=0).astype(BF16)


def fold_six(x, masks):
    total = None
    for h in range(6):
        at = (h // 3) * (WIDE // 2) + (h % 3) * TMAX
        part = x[at : at + TMAX] * masks[h]
        total = part if total is None else total + part
    return total


def half_masks(half):
    lane = lax.broadcasted_iota(jnp.int32, (1, WIDE), 1)
    head = (lane + half * LANES) // HD
    return [(head == 6 * half + h).astype(F32) for h in range(6)]


def half_slice(half, part):
    return pl.ds(pl.multiple_of(part * D + half * LANES, LANES), WIDE)


def lane_slice(g, part):
    return pl.ds(pl.multiple_of(part * D + g * LANES, LANES), LANES)


def prep_kernel(
    plan,
    own_s,
    params_hbm, index_ref, pos_ref,
    vec, own_ref,
    w_in_hbm, w_qkv_hbm, w_out_hbm, w_up_hbm, w_down_hbm, stream_hbm,
    pbuf, w_in_b, w_qkv_b, w_out_b, w_up_b, w_down_b, stream, hot_ref, sems, out_sems,
):
    spans = [
        (ROW_SMALL, SMALL_ROWS), (ROW_IN, ROW_QKV - ROW_IN), (ROW_QKV, ROW_OUT - ROW_QKV),
        (ROW_OUT, ROW_UP - ROW_OUT), (ROW_UP, ROW_DOWN - ROW_UP), (ROW_DOWN, ROW_SMALL - ROW_DOWN),
    ]
    copies = [
        pltpu.make_async_copy(params_hbm.at[pl.ds(r, n)], pbuf.at[pl.ds(r, n)], sems.at[i])
        for i, (r, n) in enumerate(spans)
    ]
    for c in copies:
        c.start()
    outgoing = []

    def send_out(src, dst):
        copy = pltpu.make_async_copy(src, dst, out_sems.at[len(outgoing)])
        copy.start()
        outgoing.append(copy)

    def take(base, rows, tiles, dst, step):
        def body(i, _):
            for c in range(tiles):
                src = pl.ds(base + i * (step * tiles) + c, step, stride=tiles)
                dst[pl.ds(pl.multiple_of(i * step, step), step), c * LANES : (c + 1) * LANES] = pbuf[src, :].astype(BF16)
            return 0
        lax.fori_loop(0, rows // step, body, 0, unroll=True)

    eye = lax.broadcasted_iota(jnp.int32, (TMAX, TMAX), 0) == lax.broadcasted_iota(jnp.int32, (TMAX, TMAX), 1)
    grid_id = lax.broadcasted_iota(jnp.int32, (TMAX, GRID), 1)
    for j in range(IMG * BLOCKS):
        row = index_ref[0, j // BLOCKS, j % BLOCKS : j % BLOCKS + 1, :]
        col = jnp.sum(jnp.where(eye, row, 0), axis=1, keepdims=True)
        hot_ref[j * TMAX : (j + 1) * TMAX, :] = (col == grid_id).astype(F32)

    copies[0].wait()
    vec[...] = jnp.zeros_like(vec)
    for k in range(5):
        for c in range(D // LANES):
            vec[k : k + 1, c * LANES : (c + 1) * LANES] = pbuf[pl.ds(ROW_SMALL + k * 3 + c, 1), :]
    mask_tok = vec[4:5, :]
    pos = pos_ref[...]
    pos_hi = pos.astype(BF16)
    pos_lo = (pos - pos_hi.astype(F32)).astype(BF16)
    for i in range(TGT // 128):
        rows = slice(i * 128, (i + 1) * 128)
        hot = hot_ref[rows, :].astype(BF16)
        stream[rows, :] = mask_tok + (dot(hot, pos_hi) + dot(hot, pos_lo))
    send_out(stream, stream_hbm)

    for n, (base, rows, tiles, dst, out, step) in enumerate((
        (ROW_IN, D_IN, 3, w_in_b, w_in_hbm, 128), (ROW_QKV, D, 9, w_qkv_b, w_qkv_hbm, 128),
        (ROW_OUT, D, 3, w_out_b, w_out_hbm, 128), (ROW_UP, D, 12, w_up_b, w_up_hbm, 128),
        (ROW_DOWN, FF, 3, w_down_b, w_down_hbm, 128),
    )):
        copies[1 + n].wait()
        take(base, rows, tiles, dst, step)
        send_out(dst, out)
    for i in range(2):
        own_ref[i] = pbuf[pl.ds(own_s[8 + i], plan.sub), :]
    for copy in outgoing:
        copy.wait()


def place_pieces(own_s, dst, parts, rows):
    n = len(parts)
    for r, part in enumerate(parts):
        at = pl.multiple_of(lax.rem(own_s[6] + (n - r), n) * rows, 16)
        dst[pl.ds(at, rows), :] = part


def window(seg_s, img):
    return pl.multiple_of(jnp.minimum(seg_s[img] // 8 * 8, CTX - WIN), 8)


def forward_kernel(
    plan,
    len_s, own_s,
    vec, ctx_own, ctx_got, seg_row, cot_ref,
    w_in_hbm, w_qkv_hbm, w_out_hbm, w_up_hbm, w_down_hbm, target_hbm,
    out_ref, keep_ref, send_ref, mid_ref, small_out, seg_s,
    ctx_hbm, stream_hbm, qkv_hbm, probs_c_hbm, probs_t_hbm, d_mixed_hbm, d_middle_hbm,
    w_in_b, w_qkv_b, w_out_b, w_up_b, w_down_b, ctx, stream, qkv, probs_c, probs_t,
    mixed, mixed_b, d_mixed, d_branch, d_middle, normed, bias, v_t, second, active, d_lift, e_down, gflat, live_col,
    sems, out_sems,
):
    copies = [
        pltpu.make_async_copy(src, dst, sems.at[i])
        for i, (src, dst) in enumerate((
            (w_in_hbm, w_in_b), (w_qkv_hbm, w_qkv_b), (target_hbm, stream.at[pl.ds(CTX, TGT)]),
            (w_out_hbm, w_out_b), (w_up_hbm, w_up_b), (w_down_hbm, w_down_b),
        ))
    ]
    for c in copies:
        c.start()
    outgoing = []

    def send_out(src, dst):
        copy = pltpu.make_async_copy(src, dst, out_sems.at[len(outgoing)])
        copy.start()
        outgoing.append(copy)

    gain1, bias1, gain2, bias2 = [vec[k : k + 1, :] for k in range(4)]
    seg = seg_row[...]
    for i in range(IMG + 1):
        seg_s[i] = jnp.sum((seg < i).astype(jnp.int32))
    row_id = lax.broadcasted_iota(jnp.int32, (CTX, CTX), 0)
    row_image = sum((row_id >= seg_s[i]).astype(jnp.int32) for i in range(1, IMG))
    bias[...] = jnp.where(row_image == seg, 0.0, mask_value)
    live_col[0:CTX, :] = jnp.ones((CTX, LANES), F32)
    slot_id = lax.broadcasted_iota(jnp.int32, (TMAX, LANES), 0)
    for j in range(IMG * BLOCKS):
        live_col[CTX + j * TMAX : CTX + (j + 1) * TMAX, :] = (slot_id < len_s[0, j // BLOCKS, j % BLOCKS]).astype(F32)

    stored = ctx_own.shape[0] // plan.n_group
    first = ctx_own[pl.ds(pl.multiple_of(own_s[6] * stored, 16), stored), :]
    place_pieces(own_s, ctx, [first] + [ref[...] for ref in ctx_got], stored)
    send_out(ctx, ctx_hbm)
    copies[0].wait()
    stream[0:CTX, :] = dot(ctx[...], w_in_b[...])
    copies[2].wait()
    send_out(stream, stream_hbm)
    copies[1].wait()

    def qkv_body(i, _):
        rows = pl.ds(pl.multiple_of(i * TILE, TILE), TILE)
        xhat, _r = layer_norm_parts(stream[rows, :])
        n = (xhat * gain1 + bias1).astype(BF16)
        normed[rows, :] = n
        qkv[rows, :] = dot(n, w_qkv_b[...]).astype(BF16).astype(F32)
        return 0

    lax.fori_loop(0, L // TILE, qkv_body, 0, unroll=4)

    send_out(qkv, qkv_hbm)
    masks = head_masks(0, PER, LANES)
    c2 = SCALE * LOG2E
    for g in range(GROUPS):
        v_t[g * LANES : (g + 1) * LANES, :] = qkv[0:CTX, 2 * D + g * LANES : 2 * D + (g + 1) * LANES].T.astype(BF16)

    def softmax_down(t):
        p = jnp.exp2(t - jnp.max(t, axis=0, keepdims=True))
        return (p * (1.0 / jnp.sum(p, axis=0, keepdims=True))).astype(BF16)

    def ctx_body(i, _):
        g, chunk = i // 3, i % 3
        rows = pl.ds(pl.multiple_of(chunk * LANES, LANES), LANES)
        lanes = pl.ds(pl.multiple_of(g * LANES, LANES), LANES)
        q = stack_heads(qkv[rows, lane_slice(g, 0)], masks).astype(BF16)
        st = dot_nt(qkv[0:CTX, lane_slice(g, 1)].astype(BF16), q)
        for h in range(PER):
            cols = slice(h * LANES, (h + 1) * LANES)
            probs_c[i, :, cols] = softmax_down(st[:, cols] * c2 + bias[:, rows])
        o = dot(v_t[lanes, :], probs_c[i])
        mixed[rows, lanes] = diagonal(o, LANES).T
        return 0

    lax.fori_loop(0, GROUPS * 3, ctx_body, 0, unroll=9)
    send_out(probs_c, probs_c_hbm)

    key_id = lax.broadcasted_iota(jnp.int32, (KEYS, 1), 0)
    mixed[CTX:, :] = jnp.zeros((TGT, D), F32)

    def tgt_body(i, _):
        half, img = i // IMG, i % IMG
        hmasks = half_masks(half)
        first = window(seg_s, img)
        kw = qkv[pl.ds(first, WIN), half_slice(half, 1)]
        vw = qkv[pl.ds(first, WIN), half_slice(half, 2)]
        lo, hi = seg_s[img] - first, seg_s[img + 1] - first
        in_win = (key_id >= lo) & (key_id < hi) & (key_id < WIN)
        units = []
        for blk in range(BLOCKS):
            j = img * BLOCKS + blk
            rows = pl.ds(pl.multiple_of(CTX + j * TMAX, 8), TMAX)
            k = jnp.concatenate([kw, qkv[rows, half_slice(half, 1)]], axis=0).astype(BF16)
            v = jnp.concatenate([vw, qkv[rows, half_slice(half, 2)]], axis=0).astype(BF16)
            q = stack_six(qkv[rows, half_slice(half, 0)], hmasks)
            ok = in_win | ((key_id >= WIN) & (key_id < WIN + len_s[0, img, blk]))
            units.append((rows, v, dot_nt(k, q), jnp.where(ok, 0.0, mask_value)))
        for blk, (rows, v, st, bias_col) in enumerate(units):
            for n in range(2):
                cols = slice(n * LANES, (n + 1) * LANES)
                probs_t[i * BLOCKS + blk, :, cols] = softmax_down(st[:, cols] * c2 + bias_col)
        for blk, (rows, v, st, bias_col) in enumerate(units):
            o = dot_tn(probs_t[i * BLOCKS + blk], v)
            mixed[rows, pl.ds(pl.multiple_of(half * LANES, LANES), WIDE)] += fold_six(o, hmasks)
        return 0

    lax.fori_loop(0, 2 * IMG, tgt_body, 0, unroll=4)
    send_out(probs_t, probs_t_hbm)

    for c in copies[3:]:
        c.wait()

    def mixed_of(rows):
        low = mixed[rows, :].astype(BF16)
        mixed_b[rows, :] = low
        return low

    def block_body(i, carry):
        dg2, db2 = carry
        rows = pl.ds(pl.multiple_of(i * MLP_TILE, MLP_TILE), MLP_TILE)
        live = live_col[rows, 0:1]
        middle = stream[rows, :] + dot(mixed_of(rows), w_out_b[...])
        xhat, rstd = layer_norm_parts(middle)
        sec = (xhat * gain2 + bias2).astype(BF16)
        second[rows, :] = sec
        top = live * cot_ref[rows, :].astype(F32)
        e = top.astype(BF16)
        e_down[rows, :] = e
        out = middle
        d_second = jnp.zeros((MLP_TILE, D), F32)
        for j in range(FF // CHUNK):
            cols = slice(j * CHUNK, (j + 1) * CHUNK)
            lifted = dot(sec, w_up_b[:, cols])
            act, slope = gelu_both(lifted)
            act = act.astype(BF16)
            active[rows, cols] = act
            dl = (dot_nt(e, w_down_b[cols, :]) * slope).astype(BF16)
            d_lift[rows, cols] = dl
            out = out + dot(act, w_down_b[cols, :])
            d_second = d_second + dot_nt(dl, w_up_b[:, cols])
        out_ref[rows, :] = (live * out).astype(BF16)
        dm = top + layer_norm_back(d_second, gain2, xhat, rstd)
        d_middle[rows, :] = dm
        db = dm.astype(BF16)
        d_branch[rows, :] = db
        d_mixed[rows, :] = dot_nt(db, w_out_b[...])
        dg2 = dg2 + jnp.sum(d_second * xhat, axis=0, keepdims=True)
        db2 = db2 + jnp.sum(d_second, axis=0, keepdims=True)
        return dg2, db2

    zero = jnp.zeros((1, D), F32)
    dg2, db2 = lax.fori_loop(0, L // MLP_TILE, block_body, (zero, zero))
    small_out[...] = jnp.concatenate([dg2, db2, jnp.zeros((6, D), F32)], axis=0)

    send_out(d_mixed, d_mixed_hbm)
    send_out(d_middle, d_middle_hbm)

    end = ROW_SMALL - ROW_OUT
    gflat[end:, :] = jnp.zeros((gflat.shape[0] - end, LANES), F32)

    g = dot_tn(mixed_b[...], d_branch[...])
    for c in range(3):
        gflat[pl.ds(c, D, stride=3), :] = g[:, c * LANES : (c + 1) * LANES]

    def up_body(j, _):
        cols = pl.ds(pl.multiple_of(j * CHUNK, CHUNK), CHUNK)
        g = dot_tn(second[...], d_lift[:, cols])
        for c in range(CHUNK // LANES):
            gflat[pl.ds(ROW_UP - ROW_OUT + CHUNK // LANES * j + c, D, stride=12), :] = g[:, c * LANES : (c + 1) * LANES]
        return 0

    lax.fori_loop(0, FF // CHUNK, up_body, 0, unroll=3)

    def down_body(j, _):
        cols = pl.ds(pl.multiple_of(j * D, D), D)
        g = dot_tn(active[:, cols], e_down[...])
        for c in range(3):
            gflat[pl.ds(ROW_DOWN - ROW_OUT + j * (3 * D) + c, D, stride=3), :] = g[:, c * LANES : (c + 1) * LANES]
        return 0

    lax.fori_loop(0, 4, down_body, 0, unroll=4)

    mid_ref[...] = gflat[0 : plan.mid_rows, :]
    put_pieces(plan, gflat, ROW_OUT, range(plan.early0, plan.n_dp), plan.quarter, own_s[1], keep_ref, send_ref)
    for copy in outgoing:
        copy.wait()


def put_pieces(plan, gflat, base, shards, hi0, core, keep_ref, send_ref, extra=None):
    for d in shards:
        for q in range(plan.n_group):
            start = plan.row0[d] - base + q * plan.piece
            blocks = [gflat[start + n * plan.sub : start + (n + 1) * plan.sub, :].astype(BF16) for n in range(2)]

            def put(ref):
                for n in range(2):
                    ref[q // 2, d % 2, d // 2 - hi0, n, 0 : plan.sub, :] = blocks[n]
                    if extra is not None:
                        ref[q // 2, d % 2, d // 2 - hi0, n, plan.sub :, :] = extra

            @pl.when(core == q % 2)
            def _():
                put(keep_ref)

            @pl.when(core != q % 2)
            def _():
                put(send_ref)


def attention_back_kernel(
    plan,
    seg_s, own_s, qkv_hbm, probs_c_hbm, probs_t_hbm, d_mixed_hbm, one_hbm, two_hbm,
    dpk, mine_ref, other_ref, qkv, probs_c, probs_t, d_mixed, d_qkv, k_t, mom, tail, sems,
):
    incoming = {}
    for n, (name, src, dst) in enumerate((
        ("qkv", qkv_hbm, qkv), ("d_mixed", d_mixed_hbm, d_mixed), ("probs_c", probs_c_hbm, probs_c),
        ("probs_t", probs_t_hbm, probs_t),
    )):
        incoming[name] = pltpu.make_async_copy(src, dst, sems.at[n])
        incoming[name].start()

    tail0 = plan.tail // 8 * 8
    moments = []
    for i, src in enumerate((one_hbm, two_hbm)):
        moments.append(pltpu.make_async_copy(src.at[pl.ds(own_s[4], plan.piece + 8)], mom.at[i], sems.at[4 + 2 * i]))
        moments.append(pltpu.make_async_copy(src.at[pl.ds(tail0, 32)], tail.at[i], sems.at[5 + 2 * i]))
    for copy in moments:
        copy.start()

    d_qkv[...] = jnp.zeros_like(d_qkv)
    masks = head_masks(0, PER, LANES)
    incoming["qkv"].wait()
    for g in range(GROUPS):
        k_t[g * LANES : (g + 1) * LANES, :] = qkv[0:CTX, D + g * LANES : D + (g + 1) * LANES].T.astype(BF16)
    incoming["d_mixed"].wait()
    incoming["probs_c"].wait()

    def back_down(p, dp):
        p = p.astype(F32)
        delta = jnp.sum(p * dp, axis=0, keepdims=True)
        return (p * (dp - delta)).astype(BF16)

    def ctx_body(i, _):
        g, chunk = i // 3, i % 3
        rows = pl.ds(pl.multiple_of(chunk * LANES, LANES), LANES)
        lanes = pl.ds(pl.multiple_of(g * LANES, LANES), LANES)
        do = stack_heads(d_mixed[rows, lanes], masks).astype(BF16)
        dpt = dot_nt(qkv[0:CTX, lane_slice(g, 2)].astype(BF16), do)
        ds = []
        for h in range(PER):
            cols = slice(h * LANES, (h + 1) * LANES)
            ds.append(back_down(probs_c[i, :, cols], dpt[:, cols]))
        ds = jnp.concatenate(ds, axis=1)
        q = stack_heads(qkv[rows, lane_slice(g, 0)], masks).astype(BF16)
        d_qkv[rows, lane_slice(g, 0)] = diagonal(dot(k_t[lanes, :], ds), LANES).T
        d_qkv[0:CTX, lane_slice(g, 1)] += dot(ds, q)
        d_qkv[0:CTX, lane_slice(g, 2)] += dot(probs_c[i], do)
        return 0

    lax.fori_loop(0, GROUPS * 3, ctx_body, 0, unroll=9)
    incoming["probs_t"].wait()

    def tgt_body(i, _):
        half, img = i // IMG, i % IMG
        hmasks = half_masks(half)
        first = window(seg_s, img)
        win = pl.ds(first, WIN)
        kw = qkv[win, half_slice(half, 1)]
        vw = qkv[win, half_slice(half, 2)]
        units = []
        for blk in range(BLOCKS):
            rows = pl.ds(pl.multiple_of(CTX + (img * BLOCKS + blk) * TMAX, 8), TMAX)
            v = jnp.concatenate([vw, qkv[rows, half_slice(half, 2)]], axis=0).astype(BF16)
            do = stack_six(d_mixed[rows, pl.ds(pl.multiple_of(half * LANES, LANES), WIDE)], hmasks)
            units.append((rows, do, dot_nt(v, do)))
        dkw = jnp.zeros((WIN, WIDE), F32)
        dvw = jnp.zeros((WIN, WIDE), F32)
        for blk, (rows, do, dpt) in enumerate(units):
            p = probs_t[i * BLOCKS + blk]
            ds = jnp.concatenate(
                [back_down(p[:, n * LANES : (n + 1) * LANES], dpt[:, n * LANES : (n + 1) * LANES]) for n in range(2)],
                axis=1,
            )
            k = jnp.concatenate([kw, qkv[rows, half_slice(half, 1)]], axis=0).astype(BF16)
            q = stack_six(qkv[rows, half_slice(half, 0)], hmasks)
            d_qkv[rows, half_slice(half, 0)] += fold_six(dot_tn(ds, k), hmasks)
            dk = dot(ds, q)
            dv = dot(p, do)
            d_qkv[rows, half_slice(half, 1)] += dk[WIN:]
            d_qkv[rows, half_slice(half, 2)] += dv[WIN:]
            dkw = dkw + dk[:WIN]
            dvw = dvw + dv[:WIN]
        d_qkv[win, half_slice(half, 1)] += dkw
        d_qkv[win, half_slice(half, 2)] += dvw
        return 0

    lax.fori_loop(0, 2 * IMG, tgt_body, 0, unroll=4)
    for copy in moments:
        copy.wait()
    lane = lax.broadcasted_iota(jnp.int32, (1, LANES), 1)
    for i in range(2):
        turned = pltpu.roll(mom[i], own_s[5], 1)
        aligned = jnp.where(lane >= own_s[5], turned[8:], turned[7:-1])
        mine_ref[i] = aligned[: plan.sub]
        other_ref[i, 0 : plan.sub, :] = aligned[plan.sub :]
        turned = pltpu.roll(tail[i], own_s[5], 1)
        aligned = jnp.where(lane >= own_s[5], turned[1:], turned[:-1])
        at = plan.tail - tail0 + 7
        other_ref[i, plan.sub : plan.sub + SMALL_PAD, :] = aligned[at : at + SMALL_PAD]

    def round_body(i, _):
        rows = pl.ds(pl.multiple_of(i * 128, 128), 128)
        dpk[rows, 0 : 2 * D] = (d_qkv[rows, 0 : 2 * D] * SCALE).astype(BF16)
        dpk[rows, 2 * D :] = d_qkv[rows, 2 * D :].astype(BF16)
        return 0

    lax.fori_loop(0, L // 128, round_body, 0, unroll=8)


def backward_kernel(
    plan,
    own_s,
    vec, small_in, mid_ref, dpk,
    w_in_hbm, w_qkv_hbm, ctx_hbm, stream_hbm, d_middle_hbm,
    keep_ref, send_ref, same_ref, cross_ref,
    w_in_b, w_qkv_b, ctx_ref, stream, d_middle, normed, d_hidden, ctx_grad, small_flat, gflat, sems,
):
    incoming = {}
    for n, (name, src, dst) in enumerate((
        ("w_qkv", w_qkv_hbm, w_qkv_b), ("stream", stream_hbm, stream), ("d_middle", d_middle_hbm, d_middle),
        ("w_in", w_in_hbm, w_in_b), ("ctx", ctx_hbm, ctx_ref),
    )):
        incoming[name] = pltpu.make_async_copy(src, dst, sems.at[n])
        incoming[name].start()
    gain1, bias1 = vec[0:1, :], vec[1:2, :]
    gflat[ROW_OUT : ROW_OUT + plan.mid_rows, :] = mid_ref[...]
    for name in ("w_qkv", "stream", "d_middle"):
        incoming[name].wait()

    def row_body(i, carry):
        dg1, db1, dmask = carry
        rows = pl.ds(pl.multiple_of(i * 128, 128), 128)
        xhat, rstd = layer_norm_parts(stream[rows, :])
        normed[rows, :] = (xhat * gain1 + bias1).astype(BF16)
        d_normed = dot_nt(dpk[rows, :], w_qkv_b[...])
        d_stream = d_middle[rows, :] + layer_norm_back(d_normed, gain1, xhat, rstd)
        dg1 = dg1 + jnp.sum(d_normed * xhat, axis=0, keepdims=True)
        db1 = db1 + jnp.sum(d_normed, axis=0, keepdims=True)
        is_tgt = (i >= CTX // 128).astype(F32)
        dmask = dmask + is_tgt * jnp.sum(d_stream, axis=0, keepdims=True)

        @pl.when(i < CTX // 128)
        def _():
            d_hidden[rows, :] = d_stream.astype(BF16)

        return dg1, db1, dmask

    zero = jnp.zeros((1, D), F32)
    dg1, db1, dmask = lax.fori_loop(0, L // 128, row_body, (zero, zero, zero), unroll=8)
    for k, row in enumerate((dg1, db1, small_in[0:1, :], small_in[1:2, :], dmask)):
        for c in range(3):
            small_flat[3 * k + c : 3 * k + c + 1, :] = row[:, c * LANES : (c + 1) * LANES]
    small_flat[SMALL_ROWS:, :] = jnp.zeros((SMALL_PAD - SMALL_ROWS, LANES), F32)

    incoming["w_in"].wait()
    incoming["ctx"].wait()
    ctx_grad[...] = dot_nt(d_hidden[...], w_in_b[...]).astype(BF16)
    stored = CTX // plan.n_group
    for a in range(plan.n_hi):
        hi = lax.rem(own_s[2] + a, plan.n_hi) * 2
        for ref, core in ((same_ref, own_s[1]), (cross_ref, 1 - own_s[1])):
            ref[a] = ctx_grad[pl.ds(pl.multiple_of((hi + core) * stored, 16), stored), :]
    for j in range(2):
        g = dot_tn(ctx_ref[:, j * D : (j + 1) * D], d_hidden[...])
        for c in range(3):
            gflat[pl.ds(ROW_IN + j * 3 * D + c, D, stride=3), :] = g[:, c * LANES : (c + 1) * LANES]
    for j in range(3):
        g = dot_tn(normed[...], dpk[:, j * D : (j + 1) * D])
        for c in range(3):
            gflat[pl.ds(ROW_QKV + 3 * j + c, D, stride=9), :] = g[:, c * LANES : (c + 1) * LANES]
    put_pieces(plan, gflat, 0, range(plan.early0), 0, own_s[1], keep_ref, send_ref, small_flat[...].astype(BF16))


def vmem(n):
    return [pl.BlockSpec(memory_space=pltpu.VMEM)] * n


def smem(n):
    return [pl.BlockSpec(memory_space=pltpu.SMEM)] * n


def shape(dims, dtype):
    return jax.ShapeDtypeStruct(dims, dtype)


def fetch_blocks(plan, own_s, refs, rels, dst, sems):
    copies = []
    for i, (ref, (c_rel, a_rel, b_rel)) in enumerate(zip(refs, rels)):
        core = lax.rem(own_s[1] + c_rel, 2)
        hi = lax.rem(own_s[2] + a_rel, plan.n_hi)
        lo = lax.rem(own_s[3] + b_rel, 2)
        copies.append(pltpu.make_async_copy(ref, dst.at[core, hi, lo], sems.at[i]))
    for copy in copies:
        copy.start()
    for copy in copies:
        copy.wait()


def put_rows(plan, shards, hi0, src, out, base):
    for d in shards:
        lane0 = plan.lane0[d]
        rows = ceil_to(lane0 + plan.share, LANES) // LANES
        for q in range(plan.n_group):
            for n in range(2):
                start = q * plan.piece + n * plan.sub
                count = min(plan.sub, rows - start)
                if count <= 0:
                    continue
                block = src[q % 2, q // 2, d % 2, d // 2 - hi0, n, 0 : plan.sub, :].astype(F32)
                at = plan.row0[d] + start - base
                if start == 0 and lane0:
                    lane = lax.broadcasted_iota(jnp.int32, (1, LANES), 1)
                    out[at : at + 1, :] = jnp.where(lane < lane0, out[at : at + 1, :], block[0:1])
                    out[at + 1 : at + count, :] = block[1:count]
                else:
                    out[at : at + count, :] = block[:count]


def early_kernel(plan, own_s, near, far, out_hbm, edge_ref, blocks, buf, sems):
    rels = [(c, a, b) for c in range(2) for b in range(2) for a in range(plan.n_hi)]
    refs = [src.at[i] for src in (near, far) for i in range(2 * plan.n_hi)]
    fetch_blocks(plan, own_s, refs, rels, blocks, sems)
    base = plan.cut - 8
    buf[0:8, :] = jnp.zeros((8, LANES), F32)
    put_rows(plan, range(plan.early0, plan.n_dp), plan.quarter, blocks, buf, base)
    edge_ref[...] = buf[0:8, :]
    copy = pltpu.make_async_copy(
        buf.at[pl.ds(8, ROW_SMALL - plan.cut)], out_hbm.at[pl.ds(plan.cut, ROW_SMALL - plan.cut)], sems.at[0]
    )
    copy.start()
    copy.wait()


def late_kernel(plan, own_s, refs, edge_ref, done_hbm, out_hbm, blocks, buf, tail, sems):
    rels = [(c, a, b) for c in range(2) for a in range(plan.n_hi) for b in range(2)]
    fetch_blocks(plan, own_s, refs, rels, blocks, sems)
    small = blocks[0, 0, plan.helper % 2, plan.helper // 2, 0, plan.sub :, :].astype(F32)
    tail[...] = small[:SMALL_ROWS]
    copies = [pltpu.make_async_copy(tail, out_hbm.at[pl.ds(ROW_SMALL, SMALL_ROWS)], sems.at[0])]
    copies[0].start()
    done = 0
    for d in range(plan.early0):
        put_rows(plan, [d], 0, blocks, buf, 0)
        upto = (plan.row0[d + 1] // 8) * 8
        if d == plan.early0 - 1:
            upto = plan.cut
            at = plan.row0[d + 1]
            lane0 = plan.lane0[d + 1]
            if at < plan.cut:
                lane = lax.broadcasted_iota(jnp.int32, (1, LANES), 1)
                edge = edge_ref[at - plan.cut + 8 :, :]
                own = buf[at : plan.cut, :]
                row = lax.broadcasted_iota(jnp.int32, (plan.cut - at, 1), 0)
                buf[at : plan.cut, :] = jnp.where((row == 0) & (lane < lane0), own, edge)
        if (d + 1) % max(1, plan.early0 // 4) == 0:
            copies.append(pltpu.make_async_copy(
                buf.at[pl.ds(done, upto - done)], out_hbm.at[pl.ds(done, upto - done)], sems.at[len(copies)]
            ))
            copies[-1].start()
            done = upto
    for copy in copies:
        copy.wait()


def moment_kernel(plan, own_s, same, cross, given, one_ref, two_ref, ctx_pairs, *rest):
    ctx_far, (first_ref, second_ref, ctx_ref, grad) = rest[: plan.n_hi - 1], rest[plan.n_hi - 1 :]
    rows, stored = plan.shard_rows, ctx_ref.shape[0] // plan.n_group
    for a in range(plan.n_hi):
        back = lax.rem(own_s[2] + plan.n_hi - a, plan.n_hi) * 2
        ahead = lax.rem(own_s[2] + a, plan.n_hi) * 2
        for n, core in enumerate((own_s[1], 1 - own_s[1])):
            at = pl.multiple_of((back + core) * stored, 16)
            ctx_ref[pl.ds(at, stored), :] = ctx_far[a - 1][n] if a else ctx_pairs[0, n]
            at = pl.multiple_of((ahead + core) * plan.piece, 16)
            grad[pl.ds(at, plan.piece), :] = (cross if n else same)[a].astype(F32)
    grad[rows:, :] = jnp.zeros((8, LANES), F32)

    @pl.when(own_s[7] == plan.n_dp - 1)
    def _():
        at = ROW_SMALL - plan.row0[-1]
        grad[at : at + SMALL_ROWS, :] = given[plan.sub :, :].astype(F32)[:SMALL_ROWS]

    lane = lax.broadcasted_iota(jnp.int32, (1, LANES), 1)
    back = LANES - own_s[5]
    for i in range(plan.n_group):
        at = slice(i * plan.piece, (i + 1) * plan.piece)
        turned = pltpu.roll(grad[i * plan.piece : (i + 1) * plan.piece + 8, :], back, 1)
        g = jnp.where(lane < back, turned[: plan.piece], turned[1 : plan.piece + 1])
        first_ref[at, :] = 0.5 * one_ref[8 + i * plan.piece : 8 + (i + 1) * plan.piece, :] + 0.5 * g
        second_ref[at, :] = 0.6 * two_ref[8 + i * plan.piece : 8 + (i + 1) * plan.piece, :] + 0.4 * g * g


def adam(weight, grad, one, two):
    first = 0.5 * one + 0.5 * grad
    second = 0.6 * two + 0.4 * grad * grad
    step = (first / (1.0 - 0.5**STEP)) / (jnp.sqrt(second / (1.0 - 0.6**STEP)) + 1e-08)
    return weight - 0.05 * (step + 0.05 * weight)


def after(value, *others):
    return lax.optimization_barrier((value, others))[0]


def build(mesh):
    n_dp, n_group = mesh.shape["dp"], mesh.shape["group"]
    plan = Plan(n_dp, n_group)
    both = ("dp", "group")
    n_hi, half, quarter = plan.n_hi, plan.half, plan.quarter
    piece, sub = plan.piece, plan.sub
    any_spec = pl.BlockSpec(memory_space=pl.ANY)
    brief = pl.CostEstimate(flops=0, bytes_accessed=0, transcendentals=0)
    params_of = pltpu.CompilerParams(vmem_limit_bytes=VMEM_CAP)

    def pairs(move):
        out = []
        for d in range(n_dp):
            for g in range(n_group):
                ghi, glo, dhi, dlo = move(g // 2, g % 2, d // 2, d % 2)
                out.append((d * n_group + g, (dhi * 2 + dlo) * n_group + ghi * 2 + glo))
        return out

    core_pairs = pairs(lambda gh, gl, dh, dl: (gh, 1 - gl, dh, dl))
    swap_pairs = pairs(lambda gh, gl, dh, dl: (gh, gl, (dh + quarter) % half, dl))

    def xy_pairs(a, b):
        return pairs(lambda gh, gl, dh, dl: ((gh + a) % n_hi, gl, dh, (dl + b) % 2))

    def z_pairs(r):
        return pairs(lambda gh, gl, dh, dl: (gh, gl, (dh + r) % half, dl))

    def group_pairs(r):
        return [(i, (i + r) % n_group) for i in range(n_group)]

    rels = [(a, b) for a in range(n_hi) for b in range(2)]
    def pick(array, index):
        return lax.dynamic_index_in_dim(array, index, 0, keepdims=False)

    def slot_of(h, early):
        return (h % quarter) * 2 + (h // quarter + early) % 2

    def xy_blocks(keep, got, gh, dl):
        def block(a, b):
            i, j = (gh + a) % n_hi, (dl + b) % 2
            mine, theirs = pick(pick(keep, i), j), pick(pick(got, i), j)
            return (mine.astype(F32) + theirs.astype(F32)).astype(BF16)
        return [block(a, b) for a, b in rels]

    def xy_send(blocks):
        return [lax.ppermute(x, both, xy_pairs(a, b)) for x, (a, b) in zip(blocks[1:], rels[1:])]

    def z_blocks(block, arrived, dh, early):
        total = block.astype(F32)
        for part in arrived:
            total = total + part.astype(F32)
        total = total.astype(BF16)
        total = total.reshape((2 * quarter,) + total.shape[2:])
        return [pick(total, slot_of((dh + r) % half, early)) for r in range(half)]

    def z_send(blocks):
        return [lax.ppermute(x, both, z_pairs(r)) for r, x in enumerate(blocks) if r]

    def z_sum(block, arrived):
        total = block.astype(F32)
        for part in arrived:
            total = total + part.astype(F32)
        return total

    def z_gather(mine):
        return [lax.ppermute(mine, both, z_pairs(r)) for r in range(1, half)]

    def z_order(got, sender, early):
        blocks = []
        for t in range(quarter):
            for n in range(2):
                want = (t + early * quarter + n * quarter) % half
                block = got[0]
                for i in range(1, half):
                    block = jnp.where(sender(i) == want, got[i], block)
                blocks.append(block)
        return jnp.stack(blocks).reshape((quarter, 2) + blocks[0].shape)

    def xy_gather(block):
        return [lax.ppermute(block, both, xy_pairs(-a, -b)) for a, b in rels[1:]]

    def core_gather(blocks):
        return [lax.ppermute(b, both, core_pairs) for b in blocks]

    def per_device(
        context, segment_ids, target_index, target_length, pos_table, params, first_moment, second_moment, cotangent
    ):
        stored = context.shape[0] // n_group
        dp, me = lax.axis_index("dp"), lax.axis_index("group")
        gh, gl, dh, dl = me // 2, me % 2, dp // 2, dp % 2
        share = plan.share

        ctx_got = [
            lax.ppermute(
                lax.dynamic_slice_in_dim(context, (me + r) % n_group * stored, stored), "group", group_pairs(r)
            )
            for r in range(1, n_group)
        ]

        lane0 = (dp * share) % LANES

        def own_row(early):
            t = dh % quarter + early * quarter
            n = (dh // quarter + early) % 2
            return ((t * 2 + dl) * share) // LANES + me * piece + n * sub

        own_s = jnp.stack(
            [0 * me, gl, gh, dl, me * piece, lane0, me, dp, own_row(0), own_row(1)]
        ).astype(jnp.int32)
        params2 = params.reshape(ROWS_ALL, LANES)

        weights = [((D_IN, D), BF16), ((D, 3 * D), BF16), ((D, D), BF16), ((D, FF), BF16), ((FF, D), BF16)]
        prep = pl.pallas_call(
            functools.partial(prep_kernel, plan),
            out_shape=[shape((8, D), F32), shape((2, sub, LANES), F32)]
            + [shape(*w) for w in weights] + [shape((TGT, D), F32)],
            in_specs=smem(1) + [any_spec] + vmem(2),
            out_specs=vmem(2) + [any_spec] * 6,
            scratch_shapes=[pltpu.VMEM((plan.flat_rows, LANES), F32)] + [pltpu.VMEM(*w) for w in weights] + [
                pltpu.VMEM((TGT, D), F32),
                pltpu.VMEM((TGT, GRID), F32),
                pltpu.SemaphoreType.DMA((6,)),
                pltpu.SemaphoreType.DMA((6,)),
            ],
            compiler_params=params_of,
        )(own_s, params2, target_index, pos_table)
        vec, own_w, w_in_b, w_qkv_b, w_out_b, w_up_b, w_down_b, target_rows = prep

        early_rows, late_rows = sub, sub + SMALL_PAD
        n_blocks = 2 * n_hi
        out_specs = [
            shape((L, D), BF16),
            shape((n_hi, 2, quarter, 2, early_rows, LANES), BF16),
            shape((n_hi, 2, quarter, 2, early_rows, LANES), BF16),
            shape((plan.mid_rows, LANES), F32),
            shape((8, D), F32),
            shape((8,), jnp.int32),
        ]
        saved = [
            ((CTX, D_IN), BF16),
            ((L, D), F32),
            ((L, 3 * D), F32),
            ((GROUPS * 3, CTX, PER * LANES), BF16),
            ((2 * IMG * BLOCKS, KEYS, WIDE), BF16),
            ((L, D), F32),
            ((L, D), F32),
        ]

        def forward(*refs):
            n = 2 + 2
            forward_kernel(plan, *refs[:n], refs[n : n + n_group - 1], *refs[n + n_group - 1 :])

        fwd = pl.pallas_call(
            forward,
            out_shape=out_specs + [shape(*s) for s in saved],
            in_specs=smem(2) + vmem(2 + n_group - 1 + 2) + [any_spec] * 6,
            out_specs=vmem(len(out_specs) - 1) + smem(1) + [any_spec] * len(saved),
            scratch_shapes=[pltpu.VMEM(*w) for w in weights] + [pltpu.VMEM(*s) for s in saved[:5]] + [
                pltpu.VMEM((L, D), F32),
                pltpu.VMEM((L, D), BF16),
                pltpu.VMEM((L, D), F32),
                pltpu.VMEM((L, D), BF16),
                pltpu.VMEM((L, D), F32),
                pltpu.VMEM((L, D), BF16),
                pltpu.VMEM((CTX, CTX), F32),
                pltpu.VMEM((D, CTX), BF16),
                pltpu.VMEM((L, D), BF16),
                pltpu.VMEM((L, FF), BF16),
                pltpu.VMEM((L, FF), BF16),
                pltpu.VMEM((L, D), BF16),
                pltpu.VMEM((plan.flat_rows - ROW_OUT, LANES), F32),
                pltpu.VMEM((L, LANES), F32),
                pltpu.SemaphoreType.DMA((6,)),
                pltpu.SemaphoreType.DMA((len(saved),)),
            ],
            compiler_params=params_of,
        )(
            target_length, own_s,
            vec, context, *ctx_got, segment_ids, cotangent[0],
            w_in_b, w_qkv_b, w_out_b, w_up_b, w_down_b, target_rows,
        )
        out, keep_e, send_e, mid, small_in, seg_s = fwd[: len(out_specs)]
        ctx_s, stream_s, qkv_s, probs_c_s, probs_t_s, d_mixed_s, d_middle_s = fwd[len(out_specs) :]

        got_e = lax.ppermute(send_e, both, core_pairs)
        spare = plan.shard_rows * LANES - share
        one2, two2 = [
            jnp.pad(m, (8 * LANES, spare)).reshape(8 + plan.shard_rows, LANES) for m in after((first_moment, second_moment), seg_s)
        ]

        xy_e = xy_blocks(keep_e, got_e, gh, dl)
        xy_got_e = xy_send(xy_e)
        qkv_s = after(qkv_s, *xy_e)

        dpk, own_mom, other_mom = pl.pallas_call(
            functools.partial(attention_back_kernel, plan),
            out_shape=[
                shape((L, 3 * D), BF16), shape((2, sub, LANES), F32), shape((2, sub + SMALL_PAD, LANES), F32),
            ],
            in_specs=smem(2) + [any_spec] * 6,
            out_specs=vmem(3),
            scratch_shapes=[pltpu.VMEM(*s) for s in saved[2:6]] + [
                pltpu.VMEM((L, 3 * D), F32),
                pltpu.VMEM((D, CTX), BF16),
                pltpu.VMEM((2, piece + 8, LANES), F32),
                pltpu.VMEM((2, 32, LANES), F32),
                pltpu.SemaphoreType.DMA((8,)),
            ],
            compiler_params=params_of,
            cost_estimate=pl.CostEstimate(flops=10**10, bytes_accessed=20 * 10**6, transcendentals=0),
        )(seg_s, own_s, qkv_s, probs_c_s, probs_t_s, d_mixed_s, one2, two2)

        xy_got_e = [after(x, dpk) for x in xy_got_e]
        z_e = z_blocks(xy_e[0], xy_got_e, dh, 1)
        z_got_e = z_send(z_e)
        swapped = lax.ppermute(other_mom, both, swap_pairs)
        dpk = after(dpk, *z_e)

        bwd_out = [
            shape((n_hi, 2, quarter, 2, late_rows, LANES), BF16),
            shape((n_hi, 2, quarter, 2, late_rows, LANES), BF16),
            shape((n_hi, stored, D_IN), BF16),
            shape((n_hi, stored, D_IN), BF16),
        ]
        bwd = pl.pallas_call(
            functools.partial(backward_kernel, plan),
            out_shape=bwd_out,
            in_specs=smem(1) + vmem(4) + [any_spec] * 5,
            out_specs=vmem(len(bwd_out)),
            scratch_shapes=[
                pltpu.VMEM((D_IN, D), BF16),
                pltpu.VMEM((D, 3 * D), BF16),
                pltpu.VMEM((CTX, D_IN), BF16),
                pltpu.VMEM((L, D), F32),
                pltpu.VMEM((L, D), F32),
                pltpu.VMEM((L, D), BF16),
                pltpu.VMEM((CTX, D), BF16),
                pltpu.VMEM((CTX, D_IN), BF16),
                pltpu.VMEM((SMALL_PAD, LANES), F32),
                pltpu.VMEM((ROW_OUT + plan.mid_rows, LANES), F32),
                pltpu.SemaphoreType.DMA((5,)),
            ],
            compiler_params=params_of,
            cost_estimate=pl.CostEstimate(flops=5 * 10**9, bytes_accessed=15 * 10**6, transcendentals=0),
        )(own_s, vec, small_in, mid, dpk, w_in_b, w_qkv_b, ctx_s, stream_s, d_middle_s)
        keep_l, send_l, ctx_same, ctx_cross = bwd

        upper = dh // quarter
        own_is_late = upper == 0

        def moments_of(early):
            return jnp.where(upper == early, own_mom, swapped[:, :sub])

        def all_after(values, *others):
            return [after(x, *others) for x in values]

        def joint(*groups):
            return lax.optimization_barrier(groups)

        z_got_e, swapped = joint(all_after(z_got_e, keep_l), after(swapped, keep_l))
        tails = swapped[:, sub:]
        got_l = lax.ppermute(after(send_l, *z_got_e), both, core_pairs)
        own_e = z_sum(z_e[0], z_got_e)
        mom = moments_of(1)
        new_e = adam(own_w[1], own_e, mom[0], mom[1]).astype(BF16)
        ctx_cross = lax.ppermute(after(ctx_cross, *z_got_e), both, core_pairs)
        got_l, ctx_cross, new_e = joint(got_l, ctx_cross, new_e)
        ctx_pairs = jnp.stack([ctx_same, ctx_cross], axis=1)

        xy_l = xy_blocks(keep_l, got_l, gh, dl)
        xy_got_l, z_new_e, own_e = joint(xy_send(xy_l), z_gather(after(new_e, *xy_l)), own_e)

        z_l = z_blocks(xy_l[0], xy_got_l, dh, 0)
        block_e = z_order([new_e] + list(z_new_e), lambda i: (dh - i) % half, 1)[None]
        z_got_l, near_e, ctx_far = joint(
            z_send(z_l), [lax.ppermute(block_e, both, xy_pairs(-a, 0)) for a in range(1, n_hi)],
            [lax.ppermute(after(ctx_pairs[a], *z_l), both, xy_pairs(a, 0)) for a in range(1, n_hi)],
        )
        own_l = z_sum(z_l[0], z_got_l)
        small_sum = own_l[sub:]
        small_w = jnp.pad(params[NP - SMALL :].reshape(SMALL_ROWS, LANES), ((0, SMALL_PAD - SMALL_ROWS), (0, 0)))
        mom = moments_of(0)
        new_l = jnp.concatenate([
            adam(own_w[0], own_l[:sub], mom[0], mom[1]), adam(small_w, small_sum, tails[0], tails[1])
        ]).astype(BF16)

        near_e = jnp.concatenate([block_e] + list(near_e))
        give = jnp.where(own_is_late, own_e, own_l[:sub])
        give = jnp.concatenate([give, small_sum]).astype(BF16)
        have = jnp.where(own_is_late, own_l[:sub], own_e).astype(BF16)
        z_new_l, y_near_e, taken = joint(
            z_gather(new_l), lax.ppermute(near_e, both, xy_pairs(0, 1)), lax.ppermute(give, both, swap_pairs)
        )

        block_l = z_order([new_l] + list(z_new_l), lambda i: (dh - i) % half, 0)
        near_e = jnp.concatenate([near_e, y_near_e])
        near_l = xy_gather(block_l)
        far_e = lax.ppermute(after(near_e, block_l), both, core_pairs)
        own = jnp.concatenate([have, taken[:sub]])
        quarters = jnp.stack(
            [own] + [lax.ppermute(after(own, block_l), both, xy_pairs(-a, 0)) for a in range(1, n_hi)]
        )
        other_quarters = lax.ppermute(quarters, both, core_pairs)

        n_parts = 2 * n_blocks
        base = plan.cut - 8

        half_done, edge = pl.pallas_call(
            functools.partial(early_kernel, plan),
            out_shape=[shape((ROWS_ALL, LANES), F32), shape((8, LANES), F32)],
            in_specs=smem(1) + [any_spec] * 2,
            out_specs=[any_spec, pl.BlockSpec(memory_space=pltpu.VMEM)],
            scratch_shapes=[
                pltpu.VMEM((2, n_hi, 2, quarter, 2, early_rows, LANES), BF16),
                pltpu.VMEM((plan.flat_rows - base, LANES), F32),
                pltpu.SemaphoreType.DMA((n_parts,)),
            ],
            compiler_params=params_of,
            cost_estimate=brief,
        )(after(own_s, block_l), near_e, far_e)

        new_first, new_second, context_grad = pl.pallas_call(
            functools.partial(moment_kernel, plan),
            out_shape=[shape((plan.shard_rows, LANES), F32)] * 2 + [shape(context.shape, BF16)],
            in_specs=smem(1) + vmem(6 + n_hi - 1),
            out_specs=vmem(3),
            scratch_shapes=[pltpu.VMEM((plan.shard_rows + 8, LANES), F32)],
            compiler_params=params_of,
            cost_estimate=brief,
        )(after(own_s, edge), quarters, other_quarters, taken, one2, two2, ctx_pairs, *ctx_far)
        new_first, new_second = [m.reshape(-1)[:share] for m in (new_first, new_second)]

        near_l, half_done, edge, new_first, new_second = joint(near_l, half_done, edge, new_first, new_second)
        near_l = [block_l] + list(near_l)
        all_l = near_l + core_gather(near_l)

        def late(own_ref, *refs):
            late_kernel(plan, own_ref, refs[:n_parts], *refs[n_parts:])

        new_params = pl.pallas_call(
            late,
            out_shape=shape((ROWS_ALL, LANES), F32),
            in_specs=smem(1) + [any_spec] * n_parts + vmem(1) + [any_spec],
            out_specs=any_spec,
            scratch_shapes=[
                pltpu.VMEM((2, n_hi, 2, quarter, 2, late_rows, LANES), BF16),
                pltpu.VMEM((plan.row0[plan.early0 - 1] + plan.shard_rows, LANES), F32),
                pltpu.VMEM((SMALL_ROWS, LANES), F32),
                pltpu.SemaphoreType.DMA((max(n_parts, 8),)),
            ],
            input_output_aliases={n_parts + 2: 0},
            compiler_params=params_of,
        )(own_s, *all_l, edge, half_done)

        return out[None], context_grad, new_params.reshape(-1), new_first, new_second

    return per_device


def solution(mesh):
    return jax.shard_map(
        build(mesh),
        mesh=mesh,
        in_specs=(
            P(("dp", "group"), None),
            P(("dp", "group"), None),
            P(("dp", "group"), None, None, None),
            P(("dp", "group"), None, None),
            P(),
            P(),
            P("dp"),
            P("dp"),
            P(("dp", "group"), None, None),
        ),
        out_specs=(P(("dp", "group"), None, None), P(("dp", "group"), None), P(), P("dp"), P("dp")),
        check_vma=False,
    )
```

```python
import functools

import jax
import jax.numpy as jnp
from jax import lax
from jax.experimental import pallas as pl
from jax.experimental.pallas import tpu as pltpu
from jax.sharding import PartitionSpec as P

D_IN = 768
D = 384
HEADS = 12
HD = 32
FF = 1536
GRID = 196
BLOCKS = 4
TMAX = 40
STEP = 10
IMG = 4
CTX = 384
TGT = IMG * BLOCKS * TMAX
L = CTX + TGT
NP = D_IN * D + 4 * D * D + 2 * D * FF + 5 * D
LANES = 128
GROUPS = D // LANES
PER = LANES // HD
WIN = 200
KEYS = WIN + TMAX
WIDE = 256
TILE = 256
MLP_TILE = 512
CHUNK = 512

ROW_IN = 0
ROW_QKV = D_IN * D // LANES
ROW_OUT = ROW_QKV + 3 * D * D // LANES
ROW_UP = ROW_OUT + D * D // LANES
ROW_DOWN = ROW_UP + D * FF // LANES
ROW_SMALL = ROW_DOWN + FF * D // LANES
ROWS_ALL = NP // LANES
SMALL = 5 * D
SMALL_ROWS = SMALL // LANES
SMALL_PAD = 16

norm_eps = 1e-06
mask_value = -1e30
LOG2E = 1.4426950408889634
SCALE = HD**-0.5
F32 = jnp.float32
BF16 = jnp.bfloat16
VMEM_CAP = 64000 * 1024


def dot(a, b):
    return jnp.dot(a, b, preferred_element_type=F32)


def dot_nt(a, b):
    return lax.dot_general(a, b, (((1,), (1,)), ((), ())), preferred_element_type=F32)


def dot_tn(a, b):
    return lax.dot_general(a, b, (((0,), (0,)), ((), ())), preferred_element_type=F32)


def ceil_to(n, m):
    return -(-n // m) * m


class Plan:
    def __init__(self, n_dp, n_group):
        self.n_dp, self.n_group = n_dp, n_group
        self.share = NP // n_dp
        self.row0 = [d * self.share // LANES for d in range(n_dp)]
        self.lane0 = [d * self.share % LANES for d in range(n_dp)]
        most = max(ceil_to(o + self.share, LANES) // LANES for o in self.lane0)
        self.sub = ceil_to(-(-most // (2 * n_group)), 16)
        self.piece = 2 * self.sub
        self.shard_rows = self.piece * n_group
        self.n_hi, self.half = n_group // 2, n_dp // 2
        self.quarter = self.half // 2
        self.early0 = n_dp // 2
        assert self.early0 * self.share >= ROW_OUT * LANES
        self.helper = 2 * (self.half - 1 - self.quarter) + 1
        self.tail = ROW_SMALL - self.row0[-1]
        self.flat_rows = ceil_to(max(r + self.shard_rows for r in self.row0), 16)
        self.mid_rows = ceil_to(self.row0[self.early0 - 1] + self.shard_rows - ROW_OUT, 8)
        self.cut = ceil_to(self.early0 * self.share, 8 * LANES) // LANES


def layer_norm_parts(x):
    mu = jnp.mean(x, axis=-1, keepdims=True)
    xc = x - mu
    rstd = lax.rsqrt(jnp.mean(xc * xc, axis=-1, keepdims=True) + norm_eps)
    return xc * rstd, rstd


def layer_norm_back(dy, gain, xhat, rstd):
    dx = dy * gain
    a = jnp.mean(dx, axis=-1, keepdims=True)
    b = jnp.mean(dx * xhat, axis=-1, keepdims=True)
    return rstd * (dx - a - xhat * b)


def reciprocal(x):
    r = pl.reciprocal(x, approx=True)
    return r * (2.0 - x * r)


def gelu_both(x):
    z = jnp.abs(x) * (0.5**0.5)
    t = reciprocal(1.0 + 0.3275911 * z)
    e = jnp.exp2(x * x * (-0.5 * LOG2E))
    poly = ((((1.061405429 * t - 1.453152027) * t + 1.421413741) * t - 0.284496736) * t + 0.254829592) * t
    tail = 0.5 * poly * e
    cdf = jnp.where(x >= 0, 1.0 - tail, tail)
    pdf = e * 0.3989422804014327
    return x * cdf, cdf + x * pdf


def head_masks(first, count, width):
    lane = lax.broadcasted_iota(jnp.int32, (1, width), 1)
    return [(lane // HD == first + h).astype(F32) for h in range(count)]


def stack_heads(x, masks):
    return jnp.concatenate([x * m for m in masks], axis=0)


def diagonal(x, rows):
    return jnp.concatenate(
        [x[h * HD : (h + 1) * HD, h * rows : (h + 1) * rows] for h in range(PER)], axis=0
    )


def stack_six(x, masks):
    gap = jnp.zeros((WIDE // 2 - 3 * TMAX, WIDE), F32)
    parts = [x * m for m in masks]
    return jnp.concatenate(parts[:3] + [gap] + parts[3:] + [gap], axis=0).astype(BF16)


def fold_six(x, masks):
    total = None
    for h in range(6):
        at = (h // 3) * (WIDE // 2) + (h % 3) * TMAX
        part = x[at : at + TMAX] * masks[h]
        total = part if total is None else total + part
    return total


def half_masks(half):
    lane = lax.broadcasted_iota(jnp.int32, (1, WIDE), 1)
    head = (lane + half * LANES) // HD
    return [(head == 6 * half + h).astype(F32) for h in range(6)]


def half_slice(half, part):
    return pl.ds(pl.multiple_of(part * D + half * LANES, LANES), WIDE)


def lane_slice(g, part):
    return pl.ds(pl.multiple_of(part * D + g * LANES, LANES), LANES)


def prep_kernel(
    plan,
    own_s,
    params_hbm, index_ref, pos_ref,
    vec, own_ref,
    w_in_hbm, w_qkv_hbm, w_out_hbm, w_up_hbm, w_down_hbm, stream_hbm,
    pbuf, w_in_b, w_qkv_b, w_out_b, w_up_b, w_down_b, stream, hot_ref, sems, out_sems,
):
    spans = [
        (ROW_SMALL, SMALL_ROWS), (ROW_IN, ROW_QKV - ROW_IN), (ROW_QKV, ROW_OUT - ROW_QKV),
        (ROW_OUT, ROW_UP - ROW_OUT), (ROW_UP, ROW_DOWN - ROW_UP), (ROW_DOWN, ROW_SMALL - ROW_DOWN),
    ]
    copies = [
        pltpu.make_async_copy(params_hbm.at[pl.ds(r, n)], pbuf.at[pl.ds(r, n)], sems.at[i])
        for i, (r, n) in enumerate(spans)
    ]
    for c in copies:
        c.start()
    outgoing = []

    def send_out(src, dst):
        copy = pltpu.make_async_copy(src, dst, out_sems.at[len(outgoing)])
        copy.start()
        outgoing.append(copy)

    def take(base, rows, tiles, dst, step):
        def body(i, _):
            for c in range(tiles):
                src = pl.ds(base + i * (step * tiles) + c, step, stride=tiles)
                dst[pl.ds(pl.multiple_of(i * step, step), step), c * LANES : (c + 1) * LANES] = pbuf[src, :].astype(BF16)
            return 0
        lax.fori_loop(0, rows // step, body, 0, unroll=True)

    eye = lax.broadcasted_iota(jnp.int32, (TMAX, TMAX), 0) == lax.broadcasted_iota(jnp.int32, (TMAX, TMAX), 1)
    grid_id = lax.broadcasted_iota(jnp.int32, (TMAX, GRID), 1)
    for j in range(IMG * BLOCKS):
        row = index_ref[0, j // BLOCKS, j % BLOCKS : j % BLOCKS + 1, :]
        col = jnp.sum(jnp.where(eye, row, 0), axis=1, keepdims=True)
        hot_ref[j * TMAX : (j + 1) * TMAX, :] = (col == grid_id).astype(F32)

    copies[0].wait()
    vec[...] = jnp.zeros_like(vec)
    for k in range(5):
        for c in range(D // LANES):
            vec[k : k + 1, c * LANES : (c + 1) * LANES] = pbuf[pl.ds(ROW_SMALL + k * 3 + c, 1), :]
    mask_tok = vec[4:5, :]
    pos = pos_ref[...]
    pos_hi = pos.astype(BF16)
    pos_lo = (pos - pos_hi.astype(F32)).astype(BF16)
    for i in range(TGT // 128):
        rows = slice(i * 128, (i + 1) * 128)
        hot = hot_ref[rows, :].astype(BF16)
        stream[rows, :] = mask_tok + (dot(hot, pos_hi) + dot(hot, pos_lo))
    send_out(stream, stream_hbm)

    for n, (base, rows, tiles, dst, out, step) in enumerate((
        (ROW_IN, D_IN, 3, w_in_b, w_in_hbm, 128), (ROW_QKV, D, 9, w_qkv_b, w_qkv_hbm, 128),
        (ROW_OUT, D, 3, w_out_b, w_out_hbm, 128), (ROW_UP, D, 12, w_up_b, w_up_hbm, 128),
        (ROW_DOWN, FF, 3, w_down_b, w_down_hbm, 128),
    )):
        copies[1 + n].wait()
        take(base, rows, tiles, dst, step)
        send_out(dst, out)
    for i in range(2):
        own_ref[i] = pbuf[pl.ds(own_s[8 + i], plan.sub), :]
    for copy in outgoing:
        copy.wait()


def place_pieces(own_s, dst, parts, rows):
    n = len(parts)
    for r, part in enumerate(parts):
        at = pl.multiple_of(lax.rem(own_s[6] + (n - r), n) * rows, 16)
        dst[pl.ds(at, rows), :] = part


def window(seg_s, img):
    return pl.multiple_of(jnp.minimum(seg_s[img] // 8 * 8, CTX - WIN), 8)


def forward_kernel(
    plan,
    len_s, own_s,
    vec, ctx_own, ctx_got, seg_row, cot_hbm,
    w_in_hbm, w_qkv_hbm, w_out_hbm, w_up_hbm, w_down_hbm, target_hbm,
    small_out, keep_ref, send_ref, seg_s,
    out_ref, mid_ref, ctx_hbm, stream_hbm, qkv_hbm, probs_c_hbm, probs_t_hbm, d_mixed_hbm, d_middle_hbm,
    w_in_b, w_qkv_b, w_out_b, w_up_b, w_down_b, ctx, stream, qkv, probs_c, probs_t,
    mixed, mixed_b, d_mixed, d_branch, d_middle, normed, bias, v_t, second, active, d_lift, e_down, gflat, live_col, cot, out_s,
    sems, out_sems,
):
    copies = [
        pltpu.make_async_copy(src, dst, sems.at[i])
        for i, (src, dst) in enumerate((
            (w_in_hbm, w_in_b), (w_qkv_hbm, w_qkv_b), (target_hbm, stream.at[pl.ds(CTX, TGT)]),
            (w_out_hbm, w_out_b), (w_up_hbm, w_up_b), (w_down_hbm, w_down_b), (cot_hbm, cot),
        ))
    ]
    for c in copies:
        c.start()
    outgoing = []

    def send_out(src, dst):
        copy = pltpu.make_async_copy(src, dst, out_sems.at[len(outgoing)])
        copy.start()
        outgoing.append(copy)

    gain1, bias1, gain2, bias2 = [vec[k : k + 1, :] for k in range(4)]
    seg = seg_row[...]
    for i in range(IMG + 1):
        seg_s[i] = jnp.sum((seg < i).astype(jnp.int32))
    row_id = lax.broadcasted_iota(jnp.int32, (CTX, CTX), 0)
    row_image = sum((row_id >= seg_s[i]).astype(jnp.int32) for i in range(1, IMG))
    bias[...] = jnp.where(row_image == seg, 0.0, mask_value)
    live_col[0:CTX, :] = jnp.ones((CTX, LANES), F32)
    slot_id = lax.broadcasted_iota(jnp.int32, (TMAX, LANES), 0)
    for j in range(IMG * BLOCKS):
        live_col[CTX + j * TMAX : CTX + (j + 1) * TMAX, :] = (slot_id < len_s[0, j // BLOCKS, j % BLOCKS]).astype(F32)

    stored = ctx_own.shape[0] // plan.n_group
    first = ctx_own[pl.ds(pl.multiple_of(own_s[6] * stored, 16), stored), :]
    place_pieces(own_s, ctx, [first] + [ref[...] for ref in ctx_got], stored)
    send_out(ctx, ctx_hbm)
    copies[0].wait()
    stream[0:CTX, :] = dot(ctx[...], w_in_b[...])
    copies[2].wait()
    send_out(stream, stream_hbm)
    copies[1].wait()

    def qkv_body(i, _):
        rows = pl.ds(pl.multiple_of(i * TILE, TILE), TILE)
        xhat, _r = layer_norm_parts(stream[rows, :])
        n = (xhat * gain1 + bias1).astype(BF16)
        normed[rows, :] = n
        qkv[rows, :] = dot(n, w_qkv_b[...]).astype(BF16).astype(F32)
        return 0

    lax.fori_loop(0, L // TILE, qkv_body, 0, unroll=4)

    send_out(qkv, qkv_hbm)
    masks = head_masks(0, PER, LANES)
    c2 = SCALE * LOG2E
    for g in range(GROUPS):
        v_t[g * LANES : (g + 1) * LANES, :] = qkv[0:CTX, 2 * D + g * LANES : 2 * D + (g + 1) * LANES].T.astype(BF16)

    def softmax_down(t):
        p = jnp.exp2(t - jnp.max(t, axis=0, keepdims=True))
        return (p * (1.0 / jnp.sum(p, axis=0, keepdims=True))).astype(BF16)

    def ctx_body(i, _):
        g, chunk = i // 3, i % 3
        rows = pl.ds(pl.multiple_of(chunk * LANES, LANES), LANES)
        lanes = pl.ds(pl.multiple_of(g * LANES, LANES), LANES)
        q = stack_heads(qkv[rows, lane_slice(g, 0)], masks).astype(BF16)
        st = dot_nt(qkv[0:CTX, lane_slice(g, 1)].astype(BF16), q)
        for h in range(PER):
            cols = slice(h * LANES, (h + 1) * LANES)
            probs_c[i, :, cols] = softmax_down(st[:, cols] * c2 + bias[:, rows])
        o = dot(v_t[lanes, :], probs_c[i])
        mixed[rows, lanes] = diagonal(o, LANES).T
        return 0

    lax.fori_loop(0, GROUPS * 3, ctx_body, 0, unroll=9)
    send_out(probs_c, probs_c_hbm)

    key_id = lax.broadcasted_iota(jnp.int32, (KEYS, 1), 0)
    mixed[CTX:, :] = jnp.zeros((TGT, D), F32)

    def tgt_body(i, _):
        half, img = i // IMG, i % IMG
        hmasks = half_masks(half)
        first = window(seg_s, img)
        kw = qkv[pl.ds(first, WIN), half_slice(half, 1)]
        vw = qkv[pl.ds(first, WIN), half_slice(half, 2)]
        lo, hi = seg_s[img] - first, seg_s[img + 1] - first
        in_win = (key_id >= lo) & (key_id < hi) & (key_id < WIN)
        units = []
        for blk in range(BLOCKS):
            j = img * BLOCKS + blk
            rows = pl.ds(pl.multiple_of(CTX + j * TMAX, 8), TMAX)
            k = jnp.concatenate([kw, qkv[rows, half_slice(half, 1)]], axis=0).astype(BF16)
            v = jnp.concatenate([vw, qkv[rows, half_slice(half, 2)]], axis=0).astype(BF16)
            q = stack_six(qkv[rows, half_slice(half, 0)], hmasks)
            ok = in_win | ((key_id >= WIN) & (key_id < WIN + len_s[0, img, blk]))
            units.append((rows, v, dot_nt(k, q), jnp.where(ok, 0.0, mask_value)))
        for blk, (rows, v, st, bias_col) in enumerate(units):
            for n in range(2):
                cols = slice(n * LANES, (n + 1) * LANES)
                probs_t[i * BLOCKS + blk, :, cols] = softmax_down(st[:, cols] * c2 + bias_col)
        for blk, (rows, v, st, bias_col) in enumerate(units):
            o = dot_tn(probs_t[i * BLOCKS + blk], v)
            mixed[rows, pl.ds(pl.multiple_of(half * LANES, LANES), WIDE)] += fold_six(o, hmasks)
        return 0

    lax.fori_loop(0, 2 * IMG, tgt_body, 0, unroll=4)
    send_out(probs_t, probs_t_hbm)

    for c in copies[3:]:
        c.wait()

    def mixed_of(rows):
        low = mixed[rows, :].astype(BF16)
        mixed_b[rows, :] = low
        return low

    def block_body(i, carry):
        dg2, db2 = carry
        rows = pl.ds(pl.multiple_of(i * MLP_TILE, MLP_TILE), MLP_TILE)
        live = live_col[rows, 0:1]
        middle = stream[rows, :] + dot(mixed_of(rows), w_out_b[...])
        xhat, rstd = layer_norm_parts(middle)
        sec = (xhat * gain2 + bias2).astype(BF16)
        second[rows, :] = sec
        top = live * cot[rows, :].astype(F32)
        e = top.astype(BF16)
        e_down[rows, :] = e
        out = middle
        d_second = jnp.zeros((MLP_TILE, D), F32)
        for j in range(FF // CHUNK):
            cols = slice(j * CHUNK, (j + 1) * CHUNK)
            lifted = dot(sec, w_up_b[:, cols])
            act, slope = gelu_both(lifted)
            act = act.astype(BF16)
            active[rows, cols] = act
            dl = (dot_nt(e, w_down_b[cols, :]) * slope).astype(BF16)
            d_lift[rows, cols] = dl
            out = out + dot(act, w_down_b[cols, :])
            d_second = d_second + dot_nt(dl, w_up_b[:, cols])
        out_s[rows, :] = (live * out).astype(BF16)
        dm = top + layer_norm_back(d_second, gain2, xhat, rstd)
        d_middle[rows, :] = dm
        db = dm.astype(BF16)
        d_branch[rows, :] = db
        d_mixed[rows, :] = dot_nt(db, w_out_b[...])
        dg2 = dg2 + jnp.sum(d_second * xhat, axis=0, keepdims=True)
        db2 = db2 + jnp.sum(d_second, axis=0, keepdims=True)
        return dg2, db2

    zero = jnp.zeros((1, D), F32)
    dg2, db2 = lax.fori_loop(0, L // MLP_TILE, block_body, (zero, zero))
    small_out[...] = jnp.concatenate([dg2, db2, jnp.zeros((6, D), F32)], axis=0)

    send_out(out_s, out_ref)
    send_out(d_mixed, d_mixed_hbm)
    send_out(d_middle, d_middle_hbm)

    end = ROW_SMALL - ROW_OUT
    gflat[end:, :] = jnp.zeros((gflat.shape[0] - end, LANES), F32)

    g = dot_tn(mixed_b[...], d_branch[...])
    for c in range(3):
        gflat[pl.ds(c, D, stride=3), :] = g[:, c * LANES : (c + 1) * LANES]

    def up_body(j, _):
        cols = pl.ds(pl.multiple_of(j * CHUNK, CHUNK), CHUNK)
        g = dot_tn(second[...], d_lift[:, cols])
        for c in range(CHUNK // LANES):
            gflat[pl.ds(ROW_UP - ROW_OUT + CHUNK // LANES * j + c, D, stride=12), :] = g[:, c * LANES : (c + 1) * LANES]
        return 0

    lax.fori_loop(0, FF // CHUNK, up_body, 0, unroll=3)

    send_out(gflat.at[pl.ds(0, plan.mid_rows)], mid_ref)

    def down_body(j, _):
        cols = pl.ds(pl.multiple_of(j * D, D), D)
        g = dot_tn(active[:, cols], e_down[...])
        for c in range(3):
            gflat[pl.ds(ROW_DOWN - ROW_OUT + j * (3 * D) + c, D, stride=3), :] = g[:, c * LANES : (c + 1) * LANES]
        return 0

    lax.fori_loop(0, 4, down_body, 0, unroll=4)

    store_pieces(plan, gflat, ROW_OUT, range(plan.early0, plan.n_dp), plan.quarter, own_s[1], keep_ref, send_ref)
    for copy in outgoing:
        copy.wait()


def store_pieces(plan, gflat, base, shards, hi0, core, keep_ref, send_ref, extra=None):
    for d in shards:
        for q in range(plan.n_group):
            start = plan.row0[d] - base + q * plan.piece
            blocks = [gflat[start + n * plan.sub : start + (n + 1) * plan.sub, :].astype(BF16) for n in range(2)]

            def put(ref):
                for n in range(2):
                    ref[q // 2, d % 2, d // 2 - hi0, n, 0 : plan.sub, :] = blocks[n]
                    if extra is not None:
                        ref[q // 2, d % 2, d // 2 - hi0, n, plan.sub :, :] = extra

            @pl.when(core == q % 2)
            def _():
                put(keep_ref)

            @pl.when(core != q % 2)
            def _():
                put(send_ref)


def attention_back_kernel(
    plan,
    seg_s, own_s, qkv_hbm, probs_c_hbm, probs_t_hbm, d_mixed_hbm, one_hbm, two_hbm,
    dpk, mine_ref, other_ref, qkv, probs_c, probs_t, d_mixed, d_qkv, k_t, mom, tail, sems,
):
    incoming = {}
    for n, (name, src, dst) in enumerate((
        ("qkv", qkv_hbm, qkv), ("d_mixed", d_mixed_hbm, d_mixed), ("probs_c", probs_c_hbm, probs_c),
        ("probs_t", probs_t_hbm, probs_t),
    )):
        incoming[name] = pltpu.make_async_copy(src, dst, sems.at[n])
        incoming[name].start()

    tail0 = plan.tail // 8 * 8
    moments = []
    for i, src in enumerate((one_hbm, two_hbm)):
        moments.append(pltpu.make_async_copy(src.at[pl.ds(own_s[4], plan.piece + 8)], mom.at[i], sems.at[4 + 2 * i]))
        moments.append(pltpu.make_async_copy(src.at[pl.ds(tail0, 32)], tail.at[i], sems.at[5 + 2 * i]))
    for copy in moments:
        copy.start()

    d_qkv[...] = jnp.zeros_like(d_qkv)
    masks = head_masks(0, PER, LANES)
    incoming["qkv"].wait()
    for g in range(GROUPS):
        k_t[g * LANES : (g + 1) * LANES, :] = qkv[0:CTX, D + g * LANES : D + (g + 1) * LANES].T.astype(BF16)
    incoming["d_mixed"].wait()
    incoming["probs_c"].wait()

    def back_down(p, dp):
        p = p.astype(F32)
        delta = jnp.sum(p * dp, axis=0, keepdims=True)
        return (p * (dp - delta)).astype(BF16)

    def ctx_body(i, _):
        g, chunk = i // 3, i % 3
        rows = pl.ds(pl.multiple_of(chunk * LANES, LANES), LANES)
        lanes = pl.ds(pl.multiple_of(g * LANES, LANES), LANES)
        do = stack_heads(d_mixed[rows, lanes], masks).astype(BF16)
        dpt = dot_nt(qkv[0:CTX, lane_slice(g, 2)].astype(BF16), do)
        ds = []
        for h in range(PER):
            cols = slice(h * LANES, (h + 1) * LANES)
            ds.append(back_down(probs_c[i, :, cols], dpt[:, cols]))
        ds = jnp.concatenate(ds, axis=1)
        q = stack_heads(qkv[rows, lane_slice(g, 0)], masks).astype(BF16)
        d_qkv[rows, lane_slice(g, 0)] = diagonal(dot(k_t[lanes, :], ds), LANES).T
        d_qkv[0:CTX, lane_slice(g, 1)] += dot(ds, q)
        d_qkv[0:CTX, lane_slice(g, 2)] += dot(probs_c[i], do)
        return 0

    lax.fori_loop(0, GROUPS * 3, ctx_body, 0, unroll=9)
    incoming["probs_t"].wait()

    def tgt_body(i, _):
        half, img = i // IMG, i % IMG
        hmasks = half_masks(half)
        first = window(seg_s, img)
        win = pl.ds(first, WIN)
        kw = qkv[win, half_slice(half, 1)]
        vw = qkv[win, half_slice(half, 2)]
        units = []
        for blk in range(BLOCKS):
            rows = pl.ds(pl.multiple_of(CTX + (img * BLOCKS + blk) * TMAX, 8), TMAX)
            v = jnp.concatenate([vw, qkv[rows, half_slice(half, 2)]], axis=0).astype(BF16)
            do = stack_six(d_mixed[rows, pl.ds(pl.multiple_of(half * LANES, LANES), WIDE)], hmasks)
            units.append((rows, do, dot_nt(v, do)))
        dkw = jnp.zeros((WIN, WIDE), F32)
        dvw = jnp.zeros((WIN, WIDE), F32)
        for blk, (rows, do, dpt) in enumerate(units):
            p = probs_t[i * BLOCKS + blk]
            ds = jnp.concatenate(
                [back_down(p[:, n * LANES : (n + 1) * LANES], dpt[:, n * LANES : (n + 1) * LANES]) for n in range(2)],
                axis=1,
            )
            k = jnp.concatenate([kw, qkv[rows, half_slice(half, 1)]], axis=0).astype(BF16)
            q = stack_six(qkv[rows, half_slice(half, 0)], hmasks)
            d_qkv[rows, half_slice(half, 0)] += fold_six(dot_tn(ds, k), hmasks)
            dk = dot(ds, q)
            dv = dot(p, do)
            d_qkv[rows, half_slice(half, 1)] += dk[WIN:]
            d_qkv[rows, half_slice(half, 2)] += dv[WIN:]
            dkw = dkw + dk[:WIN]
            dvw = dvw + dv[:WIN]
        d_qkv[win, half_slice(half, 1)] += dkw
        d_qkv[win, half_slice(half, 2)] += dvw
        return 0

    lax.fori_loop(0, 2 * IMG, tgt_body, 0, unroll=4)
    for copy in moments:
        copy.wait()
    lane = lax.broadcasted_iota(jnp.int32, (1, LANES), 1)
    for i in range(2):
        turned = pltpu.roll(mom[i], own_s[5], 1)
        aligned = jnp.where(lane >= own_s[5], turned[8:], turned[7:-1])
        mine_ref[i] = aligned[: plan.sub]
        other_ref[i, 0 : plan.sub, :] = aligned[plan.sub :]
        turned = pltpu.roll(tail[i], own_s[5], 1)
        aligned = jnp.where(lane >= own_s[5], turned[1:], turned[:-1])
        at = plan.tail - tail0 + 7
        other_ref[i, plan.sub : plan.sub + SMALL_PAD, :] = aligned[at : at + SMALL_PAD]

    def round_body(i, _):
        rows = pl.ds(pl.multiple_of(i * 128, 128), 128)
        dpk[rows, 0 : 2 * D] = (d_qkv[rows, 0 : 2 * D] * SCALE).astype(BF16)
        dpk[rows, 2 * D :] = d_qkv[rows, 2 * D :].astype(BF16)
        return 0

    lax.fori_loop(0, L // 128, round_body, 0, unroll=8)


def backward_kernel(
    plan,
    own_s,
    vec, small_in, mid_ref, dpk,
    w_in_hbm, w_qkv_hbm, ctx_hbm, stream_hbm, d_middle_hbm,
    keep_ref, send_ref, same_ref, cross_ref,
    w_in_b, w_qkv_b, ctx_ref, stream, d_middle, normed, d_hidden, ctx_grad, small_flat, gflat, sems,
):
    incoming = {}
    for n, (name, src, dst) in enumerate((
        ("w_qkv", w_qkv_hbm, w_qkv_b), ("stream", stream_hbm, stream), ("d_middle", d_middle_hbm, d_middle),
        ("w_in", w_in_hbm, w_in_b), ("ctx", ctx_hbm, ctx_ref),
    )):
        incoming[name] = pltpu.make_async_copy(src, dst, sems.at[n])
        incoming[name].start()
    gain1, bias1 = vec[0:1, :], vec[1:2, :]
    gflat[ROW_OUT : ROW_OUT + plan.mid_rows, :] = mid_ref[...]
    for name in ("w_qkv", "stream", "d_middle"):
        incoming[name].wait()

    def row_body(i, carry):
        dg1, db1, dmask = carry
        rows = pl.ds(pl.multiple_of(i * 128, 128), 128)
        xhat, rstd = layer_norm_parts(stream[rows, :])
        normed[rows, :] = (xhat * gain1 + bias1).astype(BF16)
        d_normed = dot_nt(dpk[rows, :], w_qkv_b[...])
        d_stream = d_middle[rows, :] + layer_norm_back(d_normed, gain1, xhat, rstd)
        dg1 = dg1 + jnp.sum(d_normed * xhat, axis=0, keepdims=True)
        db1 = db1 + jnp.sum(d_normed, axis=0, keepdims=True)
        is_tgt = (i >= CTX // 128).astype(F32)
        dmask = dmask + is_tgt * jnp.sum(d_stream, axis=0, keepdims=True)

        @pl.when(i < CTX // 128)
        def _():
            d_hidden[rows, :] = d_stream.astype(BF16)

        return dg1, db1, dmask

    zero = jnp.zeros((1, D), F32)
    dg1, db1, dmask = lax.fori_loop(0, L // 128, row_body, (zero, zero, zero), unroll=8)
    for k, row in enumerate((dg1, db1, small_in[0:1, :], small_in[1:2, :], dmask)):
        for c in range(3):
            small_flat[3 * k + c : 3 * k + c + 1, :] = row[:, c * LANES : (c + 1) * LANES]
    small_flat[SMALL_ROWS:, :] = jnp.zeros((SMALL_PAD - SMALL_ROWS, LANES), F32)

    incoming["w_in"].wait()
    incoming["ctx"].wait()
    ctx_grad[...] = dot_nt(d_hidden[...], w_in_b[...]).astype(BF16)
    stored = CTX // plan.n_group
    for a in range(plan.n_hi):
        hi = lax.rem(own_s[2] + a, plan.n_hi) * 2
        for ref, core in ((same_ref, own_s[1]), (cross_ref, 1 - own_s[1])):
            ref[a] = ctx_grad[pl.ds(pl.multiple_of((hi + core) * stored, 16), stored), :]
    for j in range(2):
        g = dot_tn(ctx_ref[:, j * D : (j + 1) * D], d_hidden[...])
        for c in range(3):
            gflat[pl.ds(ROW_IN + j * 3 * D + c, D, stride=3), :] = g[:, c * LANES : (c + 1) * LANES]
    for j in range(3):
        g = dot_tn(normed[...], dpk[:, j * D : (j + 1) * D])
        for c in range(3):
            gflat[pl.ds(ROW_QKV + 3 * j + c, D, stride=9), :] = g[:, c * LANES : (c + 1) * LANES]
    store_pieces(plan, gflat, 0, range(plan.early0), 0, own_s[1], keep_ref, send_ref, small_flat[...].astype(BF16))


def vmem(n):
    return [pl.BlockSpec(memory_space=pltpu.VMEM)] * n


def smem(n):
    return [pl.BlockSpec(memory_space=pltpu.SMEM)] * n


def shape(dims, dtype):
    return jax.ShapeDtypeStruct(dims, dtype)


def fetch_blocks(plan, own_s, refs, rels, dst, sems):
    for i, (ref, (c_rel, a_rel, b_rel)) in enumerate(zip(refs, rels)):
        core = lax.rem(own_s[1] + c_rel, 2)
        hi = lax.rem(own_s[2] + a_rel, plan.n_hi)
        lo = lax.rem(own_s[3] + b_rel, 2)
        for t in range(plan.quarter):
            pltpu.make_async_copy(ref.at[t], dst.at[core, hi, lo, t], sems.at[core, hi, lo, t]).start()


def wait_shard(plan, d, hi0, dst, sems):
    t = d // 2 - hi0
    for core in range(2):
        for hi in range(plan.n_hi):
            at = dst.at[core, hi, d % 2, t]
            pltpu.make_async_copy(at, at, sems.at[core, hi, d % 2, t]).wait()


def put_rows(plan, shards, hi0, src, out, base):
    for d in shards:
        lane0 = plan.lane0[d]
        rows = ceil_to(lane0 + plan.share, LANES) // LANES
        for q in range(plan.n_group):
            for n in range(2):
                start = q * plan.piece + n * plan.sub
                count = min(plan.sub, rows - start)
                if count <= 0:
                    continue
                block = src[q % 2, q // 2, d % 2, d // 2 - hi0, n, 0 : plan.sub, :].astype(F32)
                at = plan.row0[d] + start - base
                if start == 0 and lane0:
                    lane = lax.broadcasted_iota(jnp.int32, (1, LANES), 1)
                    out[at : at + 1, :] = jnp.where(lane < lane0, out[at : at + 1, :], block[0:1])
                    out[at + 1 : at + count, :] = block[1:count]
                else:
                    out[at : at + count, :] = block[:count]


def write_shards(plan, shards, hi0, blocks, fetched, buf, base, out_hbm, done, ends, sems):
    copies = []
    step = max(1, len(shards) // 4)
    for n, d in enumerate(shards):
        wait_shard(plan, d, hi0, blocks, fetched)
        put_rows(plan, [d], hi0, blocks, buf, base)
        if (n + 1) % step == 0 or n + 1 == len(shards):
            upto = ends(d)
            copies.append(pltpu.make_async_copy(
                buf.at[pl.ds(done - base, upto - done)], out_hbm.at[pl.ds(done, upto - done)], sems.at[len(copies)]
            ))
            copies[-1].start()
            done = upto
    return copies


def early_kernel(plan, own_s, near, far, out_hbm, edge_ref, blocks, buf, fetched, sems):
    rels = [(c, a, b) for c in range(2) for b in range(2) for a in range(plan.n_hi)]
    refs = [src.at[i] for src in (near, far) for i in range(2 * plan.n_hi)]
    fetch_blocks(plan, own_s, refs, rels, blocks, fetched)
    base = plan.cut - 8
    buf[0:8, :] = jnp.zeros((8, LANES), F32)
    copies = write_shards(
        plan, range(plan.early0, plan.n_dp), plan.quarter, blocks, fetched, buf, base, out_hbm, plan.cut,
        lambda d: ROW_SMALL if d + 1 == plan.n_dp else plan.row0[d + 1] // 8 * 8, sems,
    )
    edge_ref[...] = buf[0:8, :]
    for copy in copies:
        copy.wait()


def late_kernel(plan, own_s, refs, edge_ref, done_hbm, out_hbm, blocks, buf, tail, fetched, sems):
    rels = [(c, a, b) for c in range(2) for a in range(plan.n_hi) for b in range(2)]
    fetch_blocks(plan, own_s, refs, rels, blocks, fetched)

    def ends(d):
        if d + 1 < plan.early0:
            return plan.row0[d + 1] // 8 * 8
        at, lane0 = plan.row0[d + 1], plan.lane0[d + 1]
        if at < plan.cut:
            lane = lax.broadcasted_iota(jnp.int32, (1, LANES), 1)
            row = lax.broadcasted_iota(jnp.int32, (plan.cut - at, 1), 0)
            mine = buf[at : plan.cut, :]
            buf[at : plan.cut, :] = jnp.where((row == 0) & (lane < lane0), mine, edge_ref[at - plan.cut + 8 :, :])
        return plan.cut

    copies = write_shards(plan, range(plan.early0), 0, blocks, fetched, buf, 0, out_hbm, 0, ends, sems)
    small = blocks[0, 0, plan.helper % 2, plan.helper // 2, 0, plan.sub :, :].astype(F32)
    tail[...] = small[:SMALL_ROWS]
    copies.append(pltpu.make_async_copy(tail, out_hbm.at[pl.ds(ROW_SMALL, SMALL_ROWS)], sems.at[7]))
    copies[-1].start()
    for copy in copies:
        copy.wait()


def gradient_kernel(plan, own_s, same, cross, given, ctx_same, ctx_cross, *rest):
    ctx_far, (grad_ref, ctx_ref, grad) = rest[: plan.n_hi - 1], rest[plan.n_hi - 1 :]
    rows, stored = plan.shard_rows, ctx_ref.shape[0] // plan.n_group
    for a in range(plan.n_hi):
        back = lax.rem(own_s[2] + plan.n_hi - a, plan.n_hi) * 2
        ahead = lax.rem(own_s[2] + a, plan.n_hi) * 2
        for n, core in enumerate((own_s[1], 1 - own_s[1])):
            at = pl.multiple_of((back + core) * stored, 16)
            ctx_ref[pl.ds(at, stored), :] = ctx_far[a - 1][n] if a else (ctx_cross if n else ctx_same)[0]
            at = pl.multiple_of((ahead + core) * plan.piece, 16)
            grad[pl.ds(at, plan.piece), :] = (cross if n else same)[a].astype(F32)
    grad[rows:, :] = jnp.zeros((8, LANES), F32)

    @pl.when(own_s[7] == plan.n_dp - 1)
    def _():
        at = ROW_SMALL - plan.row0[-1]
        grad[at : at + SMALL_ROWS, :] = given[plan.sub :, :].astype(F32)[:SMALL_ROWS]

    lane = lax.broadcasted_iota(jnp.int32, (1, LANES), 1)
    back = LANES - own_s[5]
    for i in range(plan.n_group):
        at = slice(i * plan.piece, (i + 1) * plan.piece)
        turned = pltpu.roll(grad[i * plan.piece : (i + 1) * plan.piece + 8, :], back, 1)
        g = jnp.where(lane < back, turned[: plan.piece], turned[1 : plan.piece + 1])
        grad_ref[at, :] = g


def adam(weight, grad, one, two):
    first = 0.5 * one + 0.5 * grad
    second = 0.6 * two + 0.4 * grad * grad
    step = (first / (1.0 - 0.5**STEP)) / (jnp.sqrt(second / (1.0 - 0.6**STEP)) + 1e-08)
    return weight - 0.05 * (step + 0.05 * weight)


def after(value, *others):
    return lax.optimization_barrier((value, others))[0]


def build(mesh):
    n_dp, n_group = mesh.shape["dp"], mesh.shape["group"]
    plan = Plan(n_dp, n_group)
    both = ("dp", "group")
    n_hi, half, quarter = plan.n_hi, plan.half, plan.quarter
    piece, sub = plan.piece, plan.sub
    any_spec = pl.BlockSpec(memory_space=pl.ANY)
    brief = pl.CostEstimate(flops=0, bytes_accessed=0, transcendentals=0)
    params_of = pltpu.CompilerParams(vmem_limit_bytes=VMEM_CAP)

    def pairs(move):
        out = []
        for d in range(n_dp):
            for g in range(n_group):
                ghi, glo, dhi, dlo = move(g // 2, g % 2, d // 2, d % 2)
                out.append((d * n_group + g, (dhi * 2 + dlo) * n_group + ghi * 2 + glo))
        return out

    core_pairs = pairs(lambda gh, gl, dh, dl: (gh, 1 - gl, dh, dl))
    swap_pairs = pairs(lambda gh, gl, dh, dl: (gh, gl, (dh + quarter) % half, dl))

    def xy_pairs(a, b):
        return pairs(lambda gh, gl, dh, dl: ((gh + a) % n_hi, gl, dh, (dl + b) % 2))

    def z_pairs(r):
        return pairs(lambda gh, gl, dh, dl: (gh, gl, (dh + r) % half, dl))

    def group_pairs(r):
        return [(i, (i + r) % n_group) for i in range(n_group)]

    rels = [(a, b) for a in range(n_hi) for b in range(2)]
    def pick(array, index):
        return lax.dynamic_index_in_dim(array, index, 0, keepdims=False)

    def slot_of(h, early):
        return (h % quarter) * 2 + (h // quarter + early) % 2

    def xy_blocks(keep, got, gh, dl):
        def block(a, b):
            i, j = (gh + a) % n_hi, (dl + b) % 2
            mine, theirs = pick(pick(keep, i), j), pick(pick(got, i), j)
            return (mine.astype(F32) + theirs.astype(F32)).astype(BF16)
        return [block(a, b) for a, b in rels]

    def xy_send(blocks):
        return [lax.ppermute(x, both, xy_pairs(a, b)) for x, (a, b) in zip(blocks[1:], rels[1:])]

    def z_blocks(block, arrived, dh, early):
        total = block.astype(F32)
        for part in arrived:
            total = total + part.astype(F32)
        total = total.astype(BF16)
        total = total.reshape((2 * quarter,) + total.shape[2:])
        return [pick(total, slot_of((dh + r) % half, early)) for r in range(half)]

    def z_send(blocks):
        return [lax.ppermute(x, both, z_pairs(r)) for r, x in enumerate(blocks) if r]

    def z_sum(block, arrived):
        total = block.astype(F32)
        for part in arrived:
            total = total + part.astype(F32)
        return total

    def z_gather(mine):
        return [lax.ppermute(mine, both, z_pairs(r)) for r in range(1, half)]

    def z_order(got, sender, early):
        blocks = []
        for t in range(quarter):
            for n in range(2):
                want = (t + early * quarter + n * quarter) % half
                block = got[0]
                for i in range(1, half):
                    block = jnp.where(sender(i) == want, got[i], block)
                blocks.append(block)
        return jnp.stack(blocks).reshape((quarter, 2) + blocks[0].shape)

    def xy_gather(block):
        return [lax.ppermute(block, both, xy_pairs(-a, -b)) for a, b in rels[1:]]

    def core_gather(blocks):
        return [lax.ppermute(b, both, core_pairs) for b in blocks]

    def per_device(
        context, segment_ids, target_index, target_length, pos_table, params, first_moment, second_moment, cotangent
    ):
        stored = context.shape[0] // n_group
        dp, me = lax.axis_index("dp"), lax.axis_index("group")
        gh, gl, dh, dl = me // 2, me % 2, dp // 2, dp % 2
        share = plan.share

        ctx_got = [
            lax.ppermute(
                lax.dynamic_slice_in_dim(context, (me + r) % n_group * stored, stored), "group", group_pairs(r)
            )
            for r in range(1, n_group)
        ]

        lane0 = (dp * share) % LANES

        def own_row(early):
            t = dh % quarter + early * quarter
            n = (dh // quarter + early) % 2
            return ((t * 2 + dl) * share) // LANES + me * piece + n * sub

        own_s = jnp.stack(
            [0 * me, gl, gh, dl, me * piece, lane0, me, dp, own_row(0), own_row(1)]
        ).astype(jnp.int32)
        params2 = params.reshape(ROWS_ALL, LANES)

        weights = [((D_IN, D), BF16), ((D, 3 * D), BF16), ((D, D), BF16), ((D, FF), BF16), ((FF, D), BF16)]
        prep = pl.pallas_call(
            functools.partial(prep_kernel, plan),
            out_shape=[shape((8, D), F32), shape((2, sub, LANES), F32)]
            + [shape(*w) for w in weights] + [shape((TGT, D), F32)],
            in_specs=smem(1) + [any_spec] + vmem(2),
            out_specs=vmem(2) + [any_spec] * 6,
            scratch_shapes=[pltpu.VMEM((plan.flat_rows, LANES), F32)] + [pltpu.VMEM(*w) for w in weights] + [
                pltpu.VMEM((TGT, D), F32),
                pltpu.VMEM((TGT, GRID), F32),
                pltpu.SemaphoreType.DMA((6,)),
                pltpu.SemaphoreType.DMA((6,)),
            ],
            compiler_params=params_of,
        )(own_s, params2, target_index, pos_table)
        vec, own_w, w_in_b, w_qkv_b, w_out_b, w_up_b, w_down_b, target_rows = prep

        early_rows, late_rows = sub, sub + SMALL_PAD
        n_blocks = 2 * n_hi
        out_specs = [
            shape((8, D), F32),
            shape((n_hi, 2, quarter, 2, early_rows, LANES), BF16),
            shape((n_hi, 2, quarter, 2, early_rows, LANES), BF16),
            shape((8,), jnp.int32),
        ]
        saved = [
            ((CTX, D_IN), BF16),
            ((L, D), F32),
            ((L, 3 * D), F32),
            ((GROUPS * 3, CTX, PER * LANES), BF16),
            ((2 * IMG * BLOCKS, KEYS, WIDE), BF16),
            ((L, D), F32),
            ((L, D), F32),
        ]
        written = [
            ((L, D), BF16),
            ((plan.mid_rows, LANES), F32),
        ] + saved

        def forward(*refs):
            n = 2 + 2
            forward_kernel(plan, *refs[:n], refs[n : n + n_group - 1], *refs[n + n_group - 1 :])

        fwd = pl.pallas_call(
            forward,
            out_shape=out_specs + [shape(*s) for s in written],
            in_specs=smem(2) + vmem(2 + n_group - 1 + 1) + [any_spec] * 7,
            out_specs=vmem(3) + smem(1) + [any_spec] * len(written),
            scratch_shapes=[pltpu.VMEM(*w) for w in weights] + [pltpu.VMEM(*s) for s in saved[:5]] + [
                pltpu.VMEM((L, D), F32),
                pltpu.VMEM((L, D), BF16),
                pltpu.VMEM((L, D), F32),
                pltpu.VMEM((L, D), BF16),
                pltpu.VMEM((L, D), F32),
                pltpu.VMEM((L, D), BF16),
                pltpu.VMEM((CTX, CTX), F32),
                pltpu.VMEM((D, CTX), BF16),
                pltpu.VMEM((L, D), BF16),
                pltpu.VMEM((L, FF), BF16),
                pltpu.VMEM((L, FF), BF16),
                pltpu.VMEM((L, D), BF16),
                pltpu.VMEM((plan.flat_rows - ROW_OUT, LANES), F32),
                pltpu.VMEM((L, LANES), F32),
                pltpu.VMEM((L, D), BF16),
                pltpu.VMEM((L, D), BF16),
                pltpu.SemaphoreType.DMA((7,)),
                pltpu.SemaphoreType.DMA((len(written),)),
            ],
            compiler_params=params_of,
        )(
            target_length, own_s,
            vec, context, *ctx_got, segment_ids, cotangent[0],
            w_in_b, w_qkv_b, w_out_b, w_up_b, w_down_b, target_rows,
        )
        small_in, keep_e, send_e, seg_s, out, mid = fwd[: len(fwd) - len(saved)]
        ctx_s, stream_s, qkv_s, probs_c_s, probs_t_s, d_mixed_s, d_middle_s = fwd[len(fwd) - len(saved) :]

        got_e = lax.ppermute(send_e, both, core_pairs)
        spare = plan.shard_rows * LANES - share
        one2, two2 = [
            jnp.pad(m, (8 * LANES, spare)).reshape(8 + plan.shard_rows, LANES) for m in after((first_moment, second_moment), seg_s)
        ]

        xy_e = xy_blocks(keep_e, got_e, gh, dl)
        xy_got_e = xy_send(xy_e)
        qkv_s = after(qkv_s, *xy_e)

        dpk, own_mom, other_mom = pl.pallas_call(
            functools.partial(attention_back_kernel, plan),
            out_shape=[
                shape((L, 3 * D), BF16), shape((2, sub, LANES), F32), shape((2, sub + SMALL_PAD, LANES), F32),
            ],
            in_specs=smem(2) + [any_spec] * 6,
            out_specs=vmem(3),
            scratch_shapes=[pltpu.VMEM(*s) for s in saved[2:6]] + [
                pltpu.VMEM((L, 3 * D), F32),
                pltpu.VMEM((D, CTX), BF16),
                pltpu.VMEM((2, piece + 8, LANES), F32),
                pltpu.VMEM((2, 32, LANES), F32),
                pltpu.SemaphoreType.DMA((8,)),
            ],
            compiler_params=params_of,
            cost_estimate=pl.CostEstimate(flops=10**10, bytes_accessed=20 * 10**6, transcendentals=0),
        )(seg_s, own_s, qkv_s, probs_c_s, probs_t_s, d_mixed_s, one2, two2)

        xy_got_e = [after(x, dpk) for x in xy_got_e]
        z_e = z_blocks(xy_e[0], xy_got_e, dh, 1)
        z_got_e = z_send(z_e)
        swapped = lax.ppermute(other_mom, both, swap_pairs)
        dpk = after(dpk, *z_e)

        bwd_out = [
            shape((n_hi, 2, quarter, 2, late_rows, LANES), BF16),
            shape((n_hi, 2, quarter, 2, late_rows, LANES), BF16),
            shape((n_hi, stored, D_IN), BF16),
            shape((n_hi, stored, D_IN), BF16),
        ]
        bwd = pl.pallas_call(
            functools.partial(backward_kernel, plan),
            out_shape=bwd_out,
            in_specs=smem(1) + vmem(4) + [any_spec] * 5,
            out_specs=vmem(len(bwd_out)),
            scratch_shapes=[
                pltpu.VMEM((D_IN, D), BF16),
                pltpu.VMEM((D, 3 * D), BF16),
                pltpu.VMEM((CTX, D_IN), BF16),
                pltpu.VMEM((L, D), F32),
                pltpu.VMEM((L, D), F32),
                pltpu.VMEM((L, D), BF16),
                pltpu.VMEM((CTX, D), BF16),
                pltpu.VMEM((CTX, D_IN), BF16),
                pltpu.VMEM((SMALL_PAD, LANES), F32),
                pltpu.VMEM((ROW_OUT + plan.mid_rows, LANES), F32),
                pltpu.SemaphoreType.DMA((5,)),
            ],
            compiler_params=params_of,
            cost_estimate=pl.CostEstimate(flops=5 * 10**9, bytes_accessed=15 * 10**6, transcendentals=0),
        )(own_s, vec, small_in, mid, dpk, w_in_b, w_qkv_b, ctx_s, stream_s, d_middle_s)
        keep_l, send_l, ctx_same, ctx_cross = bwd

        upper = dh // quarter
        own_is_late = upper == 0

        def moments_of(early):
            return jnp.where(upper == early, own_mom, swapped[:, :sub])

        def all_after(values, *others):
            return [after(x, *others) for x in values]

        def joint(*groups):
            return lax.optimization_barrier(groups)

        z_got_e, swapped = joint(all_after(z_got_e, keep_l), after(swapped, keep_l))
        tails = swapped[:, sub:]
        got_l = lax.ppermute(after(send_l, *z_got_e), both, core_pairs)
        own_e = z_sum(z_e[0], z_got_e)
        mom = moments_of(1)
        new_e = adam(own_w[1], own_e, mom[0], mom[1]).astype(BF16)
        ctx_cross = lax.ppermute(after(ctx_cross, *z_got_e), both, core_pairs)
        got_l, ctx_cross, new_e = joint(got_l, ctx_cross, new_e)
        ctx_pairs = [jnp.stack([ctx_same[a], ctx_cross[a]]) for a in range(1, n_hi)]

        xy_l = xy_blocks(keep_l, got_l, gh, dl)
        xy_got_l, z_new_e, own_e = joint(xy_send(xy_l), z_gather(after(new_e, *xy_l)), own_e)

        z_l = z_blocks(xy_l[0], xy_got_l, dh, 0)
        block_e = z_order([new_e] + list(z_new_e), lambda i: (dh - i) % half, 1)[None]
        z_got_l, near_e, ctx_far = joint(
            z_send(z_l), [lax.ppermute(block_e, both, xy_pairs(-a, 0)) for a in range(1, n_hi)],
            [lax.ppermute(after(ctx_pairs[a - 1], *z_l), both, xy_pairs(a, 0)) for a in range(1, n_hi)],
        )
        own_l = z_sum(z_l[0], z_got_l)
        small_sum = own_l[sub:]
        small_w = jnp.pad(params[NP - SMALL :].reshape(SMALL_ROWS, LANES), ((0, SMALL_PAD - SMALL_ROWS), (0, 0)))
        mom = moments_of(0)
        new_l = jnp.concatenate([
            adam(own_w[0], own_l[:sub], mom[0], mom[1]), adam(small_w, small_sum, tails[0], tails[1])
        ]).astype(BF16)

        near_e = jnp.concatenate([block_e] + list(near_e))
        give = jnp.where(own_is_late, own_e, own_l[:sub])
        give = jnp.concatenate([give, small_sum]).astype(BF16)
        have = jnp.where(own_is_late, own_l[:sub], own_e).astype(BF16)
        z_new_l, y_near_e, taken = joint(
            z_gather(new_l), lax.ppermute(near_e, both, xy_pairs(0, 1)), lax.ppermute(give, both, swap_pairs)
        )

        block_l = z_order([new_l] + list(z_new_l), lambda i: (dh - i) % half, 0)
        near_e = jnp.concatenate([near_e, y_near_e])
        near_l = xy_gather(block_l)
        far_e = lax.ppermute(after(near_e, block_l), both, core_pairs)
        own = jnp.concatenate([have, taken[:sub]])
        quarters = jnp.stack(
            [own] + [lax.ppermute(after(own, block_l), both, xy_pairs(-a, 0)) for a in range(1, n_hi)]
        )
        other_quarters = lax.ppermute(quarters, both, core_pairs)

        n_parts = 2 * n_blocks
        base = plan.cut - 8

        half_done, edge = pl.pallas_call(
            functools.partial(early_kernel, plan),
            out_shape=[shape((ROWS_ALL, LANES), F32), shape((8, LANES), F32)],
            in_specs=smem(1) + [pl.BlockSpec(memory_space=pltpu.HBM)] * 2,
            out_specs=[any_spec, pl.BlockSpec(memory_space=pltpu.VMEM)],
            scratch_shapes=[
                pltpu.VMEM((2, n_hi, 2, quarter, 2, early_rows, LANES), BF16),
                pltpu.VMEM((plan.flat_rows - base, LANES), F32),
                pltpu.SemaphoreType.DMA((2, n_hi, 2, quarter)),
                pltpu.SemaphoreType.DMA((8,)),
            ],
            compiler_params=params_of,
            cost_estimate=brief,
        )(after(own_s, block_l), near_e, far_e)

        grad, context_grad = pl.pallas_call(
            functools.partial(gradient_kernel, plan),
            out_shape=[shape((plan.shard_rows, LANES), F32), shape(context.shape, BF16)],
            in_specs=smem(1) + vmem(5 + n_hi - 1),
            out_specs=vmem(2),
            scratch_shapes=[pltpu.VMEM((plan.shard_rows + 8, LANES), F32)],
            compiler_params=params_of,
            cost_estimate=brief,
        )(after(own_s, edge), quarters, other_quarters, taken, ctx_same, ctx_cross, *ctx_far)
        near_l, half_done, edge, grad = joint(near_l, half_done, edge, grad)
        near_l = [block_l] + list(near_l)
        all_l = near_l + core_gather(near_l)
        grad = grad.reshape(-1)[:share]
        new_first = 0.5 * first_moment + 0.5 * grad
        new_second = 0.6 * second_moment + 0.4 * grad * grad

        def late(own_ref, *refs):
            late_kernel(plan, own_ref, refs[:n_parts], *refs[n_parts:])

        new_params = pl.pallas_call(
            late,
            out_shape=shape((ROWS_ALL, LANES), F32),
            in_specs=smem(1) + [pl.BlockSpec(memory_space=pltpu.HBM)] * n_parts + vmem(1) + [any_spec],
            out_specs=any_spec,
            scratch_shapes=[
                pltpu.VMEM((2, n_hi, 2, quarter, 2, late_rows, LANES), BF16),
                pltpu.VMEM((plan.row0[plan.early0 - 1] + plan.shard_rows, LANES), F32),
                pltpu.VMEM((SMALL_ROWS, LANES), F32),
                pltpu.SemaphoreType.DMA((2, n_hi, 2, quarter)),
                pltpu.SemaphoreType.DMA((8,)),
            ],
            input_output_aliases={n_parts + 2: 0},
            compiler_params=params_of,
        )(after(own_s, new_first, new_second), *all_l, edge, half_done)

        return out[None], context_grad, new_params.reshape(-1), new_first, new_second

    return per_device


def solution(mesh):
    return jax.shard_map(
        build(mesh),
        mesh=mesh,
        in_specs=(
            P(("dp", "group"), None),
            P(("dp", "group"), None),
            P(("dp", "group"), None, None, None),
            P(("dp", "group"), None, None),
            P(),
            P(),
            P("dp"),
            P("dp"),
            P(("dp", "group"), None, None),
        ),
        out_specs=(P(("dp", "group"), None, None), P(("dp", "group"), None), P(), P("dp"), P("dp")),
        check_vma=False,
    )
```

```python
import functools

import jax
import jax.numpy as jnp
from jax import lax
from jax.experimental import pallas as pl
from jax.experimental.pallas import tpu as pltpu
from jax.sharding import PartitionSpec as P

D_IN = 768
D = 384
HEADS = 12
HD = 32
FF = 1536
GRID = 196
BLOCKS = 4
TMAX = 40
STEP = 10
IMG = 4
CTX = 384
TGT = IMG * BLOCKS * TMAX
L = CTX + TGT
NP = D_IN * D + 4 * D * D + 2 * D * FF + 5 * D
LANES = 128
GROUPS = D // LANES
PER = LANES // HD
WIN = 200
KEYS = WIN + TMAX
WIDE = 256
TILE = 256
MLP_TILE = 512
CHUNK = 512

ROW_IN = 0
ROW_QKV = D_IN * D // LANES
ROW_OUT = ROW_QKV + 3 * D * D // LANES
ROW_UP = ROW_OUT + D * D // LANES
ROW_DOWN = ROW_UP + D * FF // LANES
ROW_SMALL = ROW_DOWN + FF * D // LANES
ROWS_ALL = NP // LANES
SMALL = 5 * D
SMALL_ROWS = SMALL // LANES
SMALL_PAD = 16

norm_eps = 1e-06
mask_value = -1e30
LOG2E = 1.4426950408889634
SCALE = HD**-0.5
F32 = jnp.float32
BF16 = jnp.bfloat16
VMEM_CAP = 64000 * 1024


def dot(a, b):
    return jnp.dot(a, b, preferred_element_type=F32)


def dot_nt(a, b):
    return lax.dot_general(a, b, (((1,), (1,)), ((), ())), preferred_element_type=F32)


def dot_tn(a, b):
    return lax.dot_general(a, b, (((0,), (0,)), ((), ())), preferred_element_type=F32)


def ceil_to(n, m):
    return -(-n // m) * m


class Plan:
    def __init__(self, n_dp, n_group):
        self.n_dp, self.n_group = n_dp, n_group
        self.share = NP // n_dp
        self.row0 = [d * self.share // LANES for d in range(n_dp)]
        self.lane0 = [d * self.share % LANES for d in range(n_dp)]
        most = max(ceil_to(o + self.share, LANES) // LANES for o in self.lane0)
        self.sub = ceil_to(-(-most // (2 * n_group)), 16)
        self.piece = 2 * self.sub
        self.shard_rows = self.piece * n_group
        self.n_hi, self.half = n_group // 2, n_dp // 2
        self.quarter = self.half // 2
        self.early0 = n_dp // 2
        assert self.early0 * self.share >= ROW_OUT * LANES
        self.helper = 2 * (self.half - 1 - self.quarter) + 1
        self.tail = ROW_SMALL - self.row0[-1]
        self.flat_rows = ceil_to(max(r + self.shard_rows for r in self.row0), 16)
        self.mid_rows = ceil_to(self.row0[self.early0 - 1] + self.shard_rows - ROW_OUT, 8)
        self.cut = ceil_to(self.early0 * self.share, 8 * LANES) // LANES


def layer_norm_parts(x):
    mu = jnp.mean(x, axis=-1, keepdims=True)
    xc = x - mu
    rstd = lax.rsqrt(jnp.mean(xc * xc, axis=-1, keepdims=True) + norm_eps)
    return xc * rstd, rstd


def layer_norm_back(dy, gain, xhat, rstd):
    dx = dy * gain
    a = jnp.mean(dx, axis=-1, keepdims=True)
    b = jnp.mean(dx * xhat, axis=-1, keepdims=True)
    return rstd * (dx - a - xhat * b)


def reciprocal(x):
    r = pl.reciprocal(x, approx=True)
    return r * (2.0 - x * r)


def gelu_both(x):
    z = jnp.abs(x) * (0.5**0.5)
    t = reciprocal(1.0 + 0.3275911 * z)
    e = jnp.exp2(x * x * (-0.5 * LOG2E))
    poly = ((((1.061405429 * t - 1.453152027) * t + 1.421413741) * t - 0.284496736) * t + 0.254829592) * t
    tail = 0.5 * poly * e
    cdf = jnp.where(x >= 0, 1.0 - tail, tail)
    pdf = e * 0.3989422804014327
    return x * cdf, cdf + x * pdf


def head_masks(first, count, width):
    lane = lax.broadcasted_iota(jnp.int32, (1, width), 1)
    return [(lane // HD == first + h).astype(F32) for h in range(count)]


def stack_heads(x, masks):
    return jnp.concatenate([x * m for m in masks], axis=0)


def diagonal(x, rows):
    return jnp.concatenate(
        [x[h * HD : (h + 1) * HD, h * rows : (h + 1) * rows] for h in range(PER)], axis=0
    )


def stack_six(x, masks):
    gap = jnp.zeros((WIDE // 2 - 3 * TMAX, WIDE), F32)
    parts = [x * m for m in masks]
    return jnp.concatenate(parts[:3] + [gap] + parts[3:] + [gap], axis=0).astype(BF16)


def fold_six(x, masks):
    total = None
    for h in range(6):
        at = (h // 3) * (WIDE // 2) + (h % 3) * TMAX
        part = x[at : at + TMAX] * masks[h]
        total = part if total is None else total + part
    return total


def half_masks(half):
    lane = lax.broadcasted_iota(jnp.int32, (1, WIDE), 1)
    head = (lane + half * LANES) // HD
    return [(head == 6 * half + h).astype(F32) for h in range(6)]


def half_slice(half, part):
    return pl.ds(pl.multiple_of(part * D + half * LANES, LANES), WIDE)


def lane_slice(g, part):
    return pl.ds(pl.multiple_of(part * D + g * LANES, LANES), LANES)


def prep_kernel(
    plan,
    own_s,
    params_hbm, index_ref, pos_ref,
    vec, own_ref,
    w_in_hbm, w_qkv_hbm, w_out_hbm, w_up_hbm, w_down_hbm, stream_hbm,
    pbuf, w_in_b, w_qkv_b, w_out_b, w_up_b, w_down_b, stream, hot_ref, sems, out_sems,
):
    spans = [
        (ROW_SMALL, SMALL_ROWS), (ROW_IN, ROW_QKV - ROW_IN), (ROW_QKV, ROW_OUT - ROW_QKV),
        (ROW_OUT, ROW_UP - ROW_OUT), (ROW_UP, ROW_DOWN - ROW_UP), (ROW_DOWN, ROW_SMALL - ROW_DOWN),
    ]
    copies = [
        pltpu.make_async_copy(params_hbm.at[pl.ds(r, n)], pbuf.at[pl.ds(r, n)], sems.at[i])
        for i, (r, n) in enumerate(spans)
    ]
    for c in copies:
        c.start()
    outgoing = []

    def send_out(src, dst):
        copy = pltpu.make_async_copy(src, dst, out_sems.at[len(outgoing)])
        copy.start()
        outgoing.append(copy)

    def take(base, rows, tiles, dst, step):
        def body(i, _):
            for c in range(tiles):
                src = pl.ds(base + i * (step * tiles) + c, step, stride=tiles)
                dst[pl.ds(pl.multiple_of(i * step, step), step), c * LANES : (c + 1) * LANES] = pbuf[src, :].astype(BF16)
            return 0
        lax.fori_loop(0, rows // step, body, 0)

    eye = lax.broadcasted_iota(jnp.int32, (TMAX, TMAX), 0) == lax.broadcasted_iota(jnp.int32, (TMAX, TMAX), 1)
    grid_id = lax.broadcasted_iota(jnp.int32, (TMAX, GRID), 1)
    for j in range(IMG * BLOCKS):
        row = index_ref[0, j // BLOCKS, j % BLOCKS : j % BLOCKS + 1, :]
        col = jnp.sum(jnp.where(eye, row, 0), axis=1, keepdims=True)
        hot_ref[j * TMAX : (j + 1) * TMAX, :] = (col == grid_id).astype(F32)

    copies[0].wait()
    vec[...] = jnp.zeros_like(vec)
    for k in range(5):
        for c in range(D // LANES):
            vec[k : k + 1, c * LANES : (c + 1) * LANES] = pbuf[pl.ds(ROW_SMALL + k * 3 + c, 1), :]
    mask_tok = vec[4:5, :]
    pos = pos_ref[...]
    pos_hi = pos.astype(BF16)
    pos_lo = (pos - pos_hi.astype(F32)).astype(BF16)
    for i in range(TGT // 128):
        rows = slice(i * 128, (i + 1) * 128)
        hot = hot_ref[rows, :].astype(BF16)
        stream[rows, :] = mask_tok + (dot(hot, pos_hi) + dot(hot, pos_lo))
    send_out(stream, stream_hbm)

    for n, (base, rows, tiles, dst, out, step) in enumerate((
        (ROW_IN, D_IN, 3, w_in_b, w_in_hbm, 128), (ROW_QKV, D, 9, w_qkv_b, w_qkv_hbm, 128),
        (ROW_OUT, D, 3, w_out_b, w_out_hbm, 128), (ROW_UP, D, 12, w_up_b, w_up_hbm, 128),
        (ROW_DOWN, FF, 3, w_down_b, w_down_hbm, 128),
    )):
        copies[1 + n].wait()
        take(base, rows, tiles, dst, step)
        send_out(dst, out)
    for i in range(2):
        own_ref[i] = pbuf[pl.ds(own_s[8 + i], plan.sub), :]
    for copy in outgoing:
        copy.wait()


def place_pieces(own_s, dst, parts, rows):
    n = len(parts)
    for r, part in enumerate(parts):
        at = pl.multiple_of(lax.rem(own_s[6] + (n - r), n) * rows, 16)
        dst[pl.ds(at, rows), :] = part


def window(seg_s, img):
    return pl.multiple_of(jnp.minimum(seg_s[img] // 8 * 8, CTX - WIN), 8)


def forward_kernel(
    plan,
    len_s, own_s,
    vec, ctx_own, ctx_got, seg_row, cot_hbm,
    w_in_hbm, w_qkv_hbm, w_out_hbm, w_up_hbm, w_down_hbm, target_hbm,
    small_out, keep_ref, send_ref, seg_s,
    out_ref, mid_ref, ctx_hbm, stream_hbm, qkv_hbm, probs_c_hbm, probs_t_hbm, d_mixed_hbm, d_middle_hbm,
    w_in_b, w_qkv_b, w_out_b, w_up_b, w_down_b, ctx, stream, qkv, probs_c, probs_t,
    mixed, mixed_b, d_mixed, d_branch, d_middle, normed, bias, v_t, second, active, d_lift, e_down, gflat, live_col, cot, out_s,
    sems, out_sems,
):
    copies = [
        pltpu.make_async_copy(src, dst, sems.at[i])
        for i, (src, dst) in enumerate((
            (w_in_hbm, w_in_b), (w_qkv_hbm, w_qkv_b), (target_hbm, stream.at[pl.ds(CTX, TGT)]),
            (w_out_hbm, w_out_b), (w_up_hbm, w_up_b), (w_down_hbm, w_down_b), (cot_hbm, cot),
        ))
    ]
    for c in copies:
        c.start()
    outgoing = []

    def send_out(src, dst):
        copy = pltpu.make_async_copy(src, dst, out_sems.at[len(outgoing)])
        copy.start()
        outgoing.append(copy)

    gain1, bias1, gain2, bias2 = [vec[k : k + 1, :] for k in range(4)]
    seg = seg_row[...]
    for i in range(IMG + 1):
        seg_s[i] = jnp.sum((seg < i).astype(jnp.int32))
    row_id = lax.broadcasted_iota(jnp.int32, (CTX, CTX), 0)
    row_image = sum((row_id >= seg_s[i]).astype(jnp.int32) for i in range(1, IMG))
    bias[...] = jnp.where(row_image == seg, 0.0, mask_value)
    live_col[0:CTX, :] = jnp.ones((CTX, LANES), F32)
    slot_id = lax.broadcasted_iota(jnp.int32, (TMAX, LANES), 0)
    for j in range(IMG * BLOCKS):
        live_col[CTX + j * TMAX : CTX + (j + 1) * TMAX, :] = (slot_id < len_s[0, j // BLOCKS, j % BLOCKS]).astype(F32)

    stored = ctx_own.shape[0] // plan.n_group
    first = ctx_own[pl.ds(pl.multiple_of(own_s[6] * stored, 16), stored), :]
    place_pieces(own_s, ctx, [first] + [ref[...] for ref in ctx_got], stored)
    send_out(ctx, ctx_hbm)
    copies[0].wait()
    stream[0:CTX, :] = dot(ctx[...], w_in_b[...])
    copies[2].wait()
    send_out(stream, stream_hbm)
    copies[1].wait()

    def qkv_body(i, _):
        rows = pl.ds(pl.multiple_of(i * TILE, TILE), TILE)
        xhat, _r = layer_norm_parts(stream[rows, :])
        n = (xhat * gain1 + bias1).astype(BF16)
        normed[rows, :] = n
        qkv[rows, :] = dot(n, w_qkv_b[...]).astype(BF16).astype(F32)
        return 0

    lax.fori_loop(0, L // TILE, qkv_body, 0, unroll=4)

    send_out(qkv, qkv_hbm)
    masks = head_masks(0, PER, LANES)
    c2 = SCALE * LOG2E
    for g in range(GROUPS):
        v_t[g * LANES : (g + 1) * LANES, :] = qkv[0:CTX, 2 * D + g * LANES : 2 * D + (g + 1) * LANES].T.astype(BF16)

    def softmax_down(t):
        p = jnp.exp2(t - jnp.max(t, axis=0, keepdims=True))
        return (p * (1.0 / jnp.sum(p, axis=0, keepdims=True))).astype(BF16)

    def ctx_body(i, _):
        g, chunk = i // 3, i % 3
        rows = pl.ds(pl.multiple_of(chunk * LANES, LANES), LANES)
        lanes = pl.ds(pl.multiple_of(g * LANES, LANES), LANES)
        q = stack_heads(qkv[rows, lane_slice(g, 0)], masks).astype(BF16)
        st = dot_nt(qkv[0:CTX, lane_slice(g, 1)].astype(BF16), q)
        for h in range(PER):
            cols = slice(h * LANES, (h + 1) * LANES)
            probs_c[i, :, cols] = softmax_down(st[:, cols] * c2 + bias[:, rows])
        o = dot(v_t[lanes, :], probs_c[i])
        mixed[rows, lanes] = diagonal(o, LANES).T
        return 0

    lax.fori_loop(0, GROUPS * 3, ctx_body, 0, unroll=3)
    send_out(probs_c, probs_c_hbm)

    key_id = lax.broadcasted_iota(jnp.int32, (KEYS, 1), 0)
    mixed[CTX:, :] = jnp.zeros((TGT, D), F32)

    def tgt_body(i, _):
        half, img = i // IMG, i % IMG
        hmasks = half_masks(half)
        first = window(seg_s, img)
        kw = qkv[pl.ds(first, WIN), half_slice(half, 1)]
        vw = qkv[pl.ds(first, WIN), half_slice(half, 2)]
        lo, hi = seg_s[img] - first, seg_s[img + 1] - first
        in_win = (key_id >= lo) & (key_id < hi) & (key_id < WIN)
        units = []
        for blk in range(BLOCKS):
            j = img * BLOCKS + blk
            rows = pl.ds(pl.multiple_of(CTX + j * TMAX, 8), TMAX)
            k = jnp.concatenate([kw, qkv[rows, half_slice(half, 1)]], axis=0).astype(BF16)
            v = jnp.concatenate([vw, qkv[rows, half_slice(half, 2)]], axis=0).astype(BF16)
            q = stack_six(qkv[rows, half_slice(half, 0)], hmasks)
            ok = in_win | ((key_id >= WIN) & (key_id < WIN + len_s[0, img, blk]))
            units.append((rows, v, dot_nt(k, q), jnp.where(ok, 0.0, mask_value)))
        for blk, (rows, v, st, bias_col) in enumerate(units):
            for n in range(2):
                cols = slice(n * LANES, (n + 1) * LANES)
                probs_t[i * BLOCKS + blk, :, cols] = softmax_down(st[:, cols] * c2 + bias_col)
        for blk, (rows, v, st, bias_col) in enumerate(units):
            o = dot_tn(probs_t[i * BLOCKS + blk], v)
            mixed[rows, pl.ds(pl.multiple_of(half * LANES, LANES), WIDE)] += fold_six(o, hmasks)
        return 0

    lax.fori_loop(0, 2 * IMG, tgt_body, 0, unroll=2)
    send_out(probs_t, probs_t_hbm)

    for c in copies[3:]:
        c.wait()

    def mixed_of(rows):
        low = mixed[rows, :].astype(BF16)
        mixed_b[rows, :] = low
        return low

    def block_body(i, carry):
        dg2, db2 = carry
        rows = pl.ds(pl.multiple_of(i * MLP_TILE, MLP_TILE), MLP_TILE)
        live = live_col[rows, 0:1]
        middle = stream[rows, :] + dot(mixed_of(rows), w_out_b[...])
        xhat, rstd = layer_norm_parts(middle)
        sec = (xhat * gain2 + bias2).astype(BF16)
        second[rows, :] = sec
        top = live * cot[rows, :].astype(F32)
        e = top.astype(BF16)
        e_down[rows, :] = e
        out = middle
        d_second = jnp.zeros((MLP_TILE, D), F32)
        for j in range(FF // CHUNK):
            cols = slice(j * CHUNK, (j + 1) * CHUNK)
            lifted = dot(sec, w_up_b[:, cols])
            act, slope = gelu_both(lifted)
            act = act.astype(BF16)
            active[rows, cols] = act
            dl = (dot_nt(e, w_down_b[cols, :]) * slope).astype(BF16)
            d_lift[rows, cols] = dl
            out = out + dot(act, w_down_b[cols, :])
            d_second = d_second + dot_nt(dl, w_up_b[:, cols])
        out_s[rows, :] = (live * out).astype(BF16)
        dm = top + layer_norm_back(d_second, gain2, xhat, rstd)
        d_middle[rows, :] = dm
        db = dm.astype(BF16)
        d_branch[rows, :] = db
        d_mixed[rows, :] = dot_nt(db, w_out_b[...])
        dg2 = dg2 + jnp.sum(d_second * xhat, axis=0, keepdims=True)
        db2 = db2 + jnp.sum(d_second, axis=0, keepdims=True)
        return dg2, db2

    zero = jnp.zeros((1, D), F32)
    dg2, db2 = lax.fori_loop(0, L // MLP_TILE, block_body, (zero, zero))
    small_out[...] = jnp.concatenate([dg2, db2, jnp.zeros((6, D), F32)], axis=0)

    send_out(out_s, out_ref)
    send_out(d_mixed, d_mixed_hbm)
    send_out(d_middle, d_middle_hbm)

    end = ROW_SMALL - ROW_OUT
    gflat[end:, :] = jnp.zeros((gflat.shape[0] - end, LANES), F32)

    g = dot_tn(mixed_b[...], d_branch[...])
    for c in range(3):
        gflat[pl.ds(c, D, stride=3), :] = g[:, c * LANES : (c + 1) * LANES]

    def up_body(j, _):
        cols = pl.ds(pl.multiple_of(j * CHUNK, CHUNK), CHUNK)
        g = dot_tn(second[...], d_lift[:, cols])
        for c in range(CHUNK // LANES):
            gflat[pl.ds(ROW_UP - ROW_OUT + CHUNK // LANES * j + c, D, stride=12), :] = g[:, c * LANES : (c + 1) * LANES]
        return 0

    lax.fori_loop(0, FF // CHUNK, up_body, 0, unroll=3)

    send_out(gflat.at[pl.ds(0, plan.mid_rows)], mid_ref)

    def down_body(j, _):
        cols = pl.ds(pl.multiple_of(j * D, D), D)
        g = dot_tn(active[:, cols], e_down[...])
        for c in range(3):
            gflat[pl.ds(ROW_DOWN - ROW_OUT + j * (3 * D) + c, D, stride=3), :] = g[:, c * LANES : (c + 1) * LANES]
        return 0

    lax.fori_loop(0, 4, down_body, 0, unroll=4)

    store_pieces(plan, gflat, ROW_OUT, range(plan.early0, plan.n_dp), plan.quarter, own_s[1], keep_ref, send_ref)
    for copy in outgoing:
        copy.wait()


def store_pieces(plan, gflat, base, shards, hi0, core, keep_ref, send_ref, extra=None):
    for d in shards:
        for q in range(plan.n_group):
            start = plan.row0[d] - base + q * plan.piece
            blocks = [gflat[start + n * plan.sub : start + (n + 1) * plan.sub, :].astype(BF16) for n in range(2)]

            def put(ref):
                for n in range(2):
                    ref[q // 2, d % 2, d // 2 - hi0, n, 0 : plan.sub, :] = blocks[n]
                    if extra is not None:
                        ref[q // 2, d % 2, d // 2 - hi0, n, plan.sub :, :] = extra

            @pl.when(core == q % 2)
            def _():
                put(keep_ref)

            @pl.when(core != q % 2)
            def _():
                put(send_ref)


def attention_back_kernel(
    plan,
    seg_s, own_s, qkv_hbm, probs_c_hbm, probs_t_hbm, d_mixed_hbm, one_hbm, two_hbm,
    dpk, mine_ref, other_ref, qkv, probs_c, probs_t, d_mixed, d_qkv, k_t, mom, tail, sems,
):
    incoming = {}
    for n, (name, src, dst) in enumerate((
        ("qkv", qkv_hbm, qkv), ("d_mixed", d_mixed_hbm, d_mixed), ("probs_c", probs_c_hbm, probs_c),
        ("probs_t", probs_t_hbm, probs_t),
    )):
        incoming[name] = pltpu.make_async_copy(src, dst, sems.at[n])
        incoming[name].start()

    tail0 = plan.tail // 8 * 8
    moments = []
    for i, src in enumerate((one_hbm, two_hbm)):
        moments.append(pltpu.make_async_copy(src.at[pl.ds(own_s[4], plan.piece + 8)], mom.at[i], sems.at[4 + 2 * i]))
        moments.append(pltpu.make_async_copy(src.at[pl.ds(tail0, 32)], tail.at[i], sems.at[5 + 2 * i]))
    for copy in moments:
        copy.start()

    d_qkv[...] = jnp.zeros_like(d_qkv)
    masks = head_masks(0, PER, LANES)
    incoming["qkv"].wait()
    for g in range(GROUPS):
        k_t[g * LANES : (g + 1) * LANES, :] = qkv[0:CTX, D + g * LANES : D + (g + 1) * LANES].T.astype(BF16)
    incoming["d_mixed"].wait()
    incoming["probs_c"].wait()

    def back_down(p, dp):
        p = p.astype(F32)
        delta = jnp.sum(p * dp, axis=0, keepdims=True)
        return (p * (dp - delta)).astype(BF16)

    def ctx_body(i, _):
        g, chunk = i // 3, i % 3
        rows = pl.ds(pl.multiple_of(chunk * LANES, LANES), LANES)
        lanes = pl.ds(pl.multiple_of(g * LANES, LANES), LANES)
        do = stack_heads(d_mixed[rows, lanes], masks).astype(BF16)
        dpt = dot_nt(qkv[0:CTX, lane_slice(g, 2)].astype(BF16), do)
        ds = []
        for h in range(PER):
            cols = slice(h * LANES, (h + 1) * LANES)
            ds.append(back_down(probs_c[i, :, cols], dpt[:, cols]))
        ds = jnp.concatenate(ds, axis=1)
        q = stack_heads(qkv[rows, lane_slice(g, 0)], masks).astype(BF16)
        d_qkv[rows, lane_slice(g, 0)] = diagonal(dot(k_t[lanes, :], ds), LANES).T
        d_qkv[0:CTX, lane_slice(g, 1)] += dot(ds, q)
        d_qkv[0:CTX, lane_slice(g, 2)] += dot(probs_c[i], do)
        return 0

    lax.fori_loop(0, GROUPS * 3, ctx_body, 0, unroll=3)
    incoming["probs_t"].wait()

    def tgt_body(i, _):
        half, img = i // IMG, i % IMG
        hmasks = half_masks(half)
        first = window(seg_s, img)
        win = pl.ds(first, WIN)
        kw = qkv[win, half_slice(half, 1)]
        vw = qkv[win, half_slice(half, 2)]
        units = []
        for blk in range(BLOCKS):
            rows = pl.ds(pl.multiple_of(CTX + (img * BLOCKS + blk) * TMAX, 8), TMAX)
            v = jnp.concatenate([vw, qkv[rows, half_slice(half, 2)]], axis=0).astype(BF16)
            do = stack_six(d_mixed[rows, pl.ds(pl.multiple_of(half * LANES, LANES), WIDE)], hmasks)
            units.append((rows, do, dot_nt(v, do)))
        dkw = jnp.zeros((WIN, WIDE), F32)
        dvw = jnp.zeros((WIN, WIDE), F32)
        for blk, (rows, do, dpt) in enumerate(units):
            p = probs_t[i * BLOCKS + blk]
            ds = jnp.concatenate(
                [back_down(p[:, n * LANES : (n + 1) * LANES], dpt[:, n * LANES : (n + 1) * LANES]) for n in range(2)],
                axis=1,
            )
            k = jnp.concatenate([kw, qkv[rows, half_slice(half, 1)]], axis=0).astype(BF16)
            q = stack_six(qkv[rows, half_slice(half, 0)], hmasks)
            d_qkv[rows, half_slice(half, 0)] += fold_six(dot_tn(ds, k), hmasks)
            dk = dot(ds, q)
            dv = dot(p, do)
            d_qkv[rows, half_slice(half, 1)] += dk[WIN:]
            d_qkv[rows, half_slice(half, 2)] += dv[WIN:]
            dkw = dkw + dk[:WIN]
            dvw = dvw + dv[:WIN]
        d_qkv[win, half_slice(half, 1)] += dkw
        d_qkv[win, half_slice(half, 2)] += dvw
        return 0

    lax.fori_loop(0, 2 * IMG, tgt_body, 0, unroll=2)
    for copy in moments:
        copy.wait()
    lane = lax.broadcasted_iota(jnp.int32, (1, LANES), 1)
    for i in range(2):
        turned = pltpu.roll(mom[i], own_s[5], 1)
        aligned = jnp.where(lane >= own_s[5], turned[8:], turned[7:-1])
        mine_ref[i] = aligned[: plan.sub]
        other_ref[i, 0 : plan.sub, :] = aligned[plan.sub :]
        turned = pltpu.roll(tail[i], own_s[5], 1)
        aligned = jnp.where(lane >= own_s[5], turned[1:], turned[:-1])
        at = plan.tail - tail0 + 7
        other_ref[i, plan.sub : plan.sub + SMALL_PAD, :] = aligned[at : at + SMALL_PAD]

    def round_body(i, _):
        rows = pl.ds(pl.multiple_of(i * 128, 128), 128)
        dpk[rows, 0 : 2 * D] = (d_qkv[rows, 0 : 2 * D] * SCALE).astype(BF16)
        dpk[rows, 2 * D :] = d_qkv[rows, 2 * D :].astype(BF16)
        return 0

    lax.fori_loop(0, L // 128, round_body, 0, unroll=8)


def backward_kernel(
    plan,
    own_s,
    vec, small_in, mid_ref, dpk,
    w_in_hbm, w_qkv_hbm, ctx_hbm, stream_hbm, d_middle_hbm,
    keep_ref, send_ref, same_ref, cross_ref,
    w_in_b, w_qkv_b, ctx_ref, stream, d_middle, normed, d_hidden, ctx_grad, small_flat, gflat, sems,
):
    incoming = {}
    for n, (name, src, dst) in enumerate((
        ("w_qkv", w_qkv_hbm, w_qkv_b), ("stream", stream_hbm, stream), ("d_middle", d_middle_hbm, d_middle),
        ("w_in", w_in_hbm, w_in_b), ("ctx", ctx_hbm, ctx_ref),
    )):
        incoming[name] = pltpu.make_async_copy(src, dst, sems.at[n])
        incoming[name].start()
    gain1, bias1 = vec[0:1, :], vec[1:2, :]
    gflat[ROW_OUT : ROW_OUT + plan.mid_rows, :] = mid_ref[...]
    for name in ("w_qkv", "stream", "d_middle"):
        incoming[name].wait()

    def row_body(i, carry):
        dg1, db1, dmask = carry
        rows = pl.ds(pl.multiple_of(i * 128, 128), 128)
        xhat, rstd = layer_norm_parts(stream[rows, :])
        normed[rows, :] = (xhat * gain1 + bias1).astype(BF16)
        d_normed = dot_nt(dpk[rows, :], w_qkv_b[...])
        d_stream = d_middle[rows, :] + layer_norm_back(d_normed, gain1, xhat, rstd)
        dg1 = dg1 + jnp.sum(d_normed * xhat, axis=0, keepdims=True)
        db1 = db1 + jnp.sum(d_normed, axis=0, keepdims=True)
        is_tgt = (i >= CTX // 128).astype(F32)
        dmask = dmask + is_tgt * jnp.sum(d_stream, axis=0, keepdims=True)

        @pl.when(i < CTX // 128)
        def _():
            d_hidden[rows, :] = d_stream.astype(BF16)

        return dg1, db1, dmask

    zero = jnp.zeros((1, D), F32)
    dg1, db1, dmask = lax.fori_loop(0, L // 128, row_body, (zero, zero, zero), unroll=8)
    for k, row in enumerate((dg1, db1, small_in[0:1, :], small_in[1:2, :], dmask)):
        for c in range(3):
            small_flat[3 * k + c : 3 * k + c + 1, :] = row[:, c * LANES : (c + 1) * LANES]
    small_flat[SMALL_ROWS:, :] = jnp.zeros((SMALL_PAD - SMALL_ROWS, LANES), F32)

    incoming["w_in"].wait()
    incoming["ctx"].wait()
    ctx_grad[...] = dot_nt(d_hidden[...], w_in_b[...]).astype(BF16)
    stored = CTX // plan.n_group
    for a in range(plan.n_hi):
        hi = lax.rem(own_s[2] + a, plan.n_hi) * 2
        for ref, core in ((same_ref, own_s[1]), (cross_ref, 1 - own_s[1])):
            ref[a] = ctx_grad[pl.ds(pl.multiple_of((hi + core) * stored, 16), stored), :]
    for j in range(2):
        g = dot_tn(ctx_ref[:, j * D : (j + 1) * D], d_hidden[...])
        for c in range(3):
            gflat[pl.ds(ROW_IN + j * 3 * D + c, D, stride=3), :] = g[:, c * LANES : (c + 1) * LANES]
    def qkv_body(j, _):
        g = dot_tn(normed[...], dpk[:, pl.ds(pl.multiple_of(j * D, D), D)])
        for c in range(3):
            gflat[pl.ds(ROW_QKV + 3 * j + c, D, stride=9), :] = g[:, c * LANES : (c + 1) * LANES]
        return 0

    lax.fori_loop(0, 3, qkv_body, 0)
    store_pieces(plan, gflat, 0, range(plan.early0), 0, own_s[1], keep_ref, send_ref, small_flat[...].astype(BF16))


def vmem(n):
    return [pl.BlockSpec(memory_space=pltpu.VMEM)] * n


def smem(n):
    return [pl.BlockSpec(memory_space=pltpu.SMEM)] * n


def shape(dims, dtype):
    return jax.ShapeDtypeStruct(dims, dtype)


def fetch_blocks(plan, own_s, refs, rels, dst, sems):
    for i, (ref, (c_rel, a_rel, b_rel)) in enumerate(zip(refs, rels)):
        core = lax.rem(own_s[1] + c_rel, 2)
        hi = lax.rem(own_s[2] + a_rel, plan.n_hi)
        lo = lax.rem(own_s[3] + b_rel, 2)
        for t in range(plan.quarter):
            pltpu.make_async_copy(ref.at[t], dst.at[core, hi, lo, t], sems.at[core, hi, lo, t]).start()


def wait_shard(plan, d, hi0, dst, sems):
    t = d // 2 - hi0
    for core in range(2):
        for hi in range(plan.n_hi):
            at = dst.at[core, hi, d % 2, t]
            pltpu.make_async_copy(at, at, sems.at[core, hi, d % 2, t]).wait()


def put_rows(plan, shards, hi0, src, out, base):
    for d in shards:
        lane0 = plan.lane0[d]
        rows = ceil_to(lane0 + plan.share, LANES) // LANES
        for q in range(plan.n_group):
            for n in range(2):
                start = q * plan.piece + n * plan.sub
                count = min(plan.sub, rows - start)
                if count <= 0:
                    continue
                block = src[q % 2, q // 2, d % 2, d // 2 - hi0, n, 0 : plan.sub, :].astype(F32)
                at = plan.row0[d] + start - base
                if start == 0 and lane0:
                    lane = lax.broadcasted_iota(jnp.int32, (1, LANES), 1)
                    out[at : at + 1, :] = jnp.where(lane < lane0, out[at : at + 1, :], block[0:1])
                    out[at + 1 : at + count, :] = block[1:count]
                else:
                    out[at : at + count, :] = block[:count]


def write_shards(plan, shards, hi0, blocks, fetched, buf, base, out_hbm, done, ends, sems):
    copies = []
    step = max(1, len(shards) // 4)
    for n, d in enumerate(shards):
        wait_shard(plan, d, hi0, blocks, fetched)
        put_rows(plan, [d], hi0, blocks, buf, base)
        if (n + 1) % step == 0 or n + 1 == len(shards):
            upto = ends(d)
            copies.append(pltpu.make_async_copy(
                buf.at[pl.ds(done - base, upto - done)], out_hbm.at[pl.ds(done, upto - done)], sems.at[len(copies)]
            ))
            copies[-1].start()
            done = upto
    return copies


def early_kernel(plan, own_s, near, far, out_hbm, edge_ref, blocks, buf, fetched, sems):
    rels = [(c, a, b) for c in range(2) for b in range(2) for a in range(plan.n_hi)]
    refs = [src.at[i] for src in (near, far) for i in range(2 * plan.n_hi)]
    fetch_blocks(plan, own_s, refs, rels, blocks, fetched)
    base = plan.cut - 8
    buf[0:8, :] = jnp.zeros((8, LANES), F32)
    copies = write_shards(
        plan, range(plan.early0, plan.n_dp), plan.quarter, blocks, fetched, buf, base, out_hbm, plan.cut,
        lambda d: ROW_SMALL if d + 1 == plan.n_dp else plan.row0[d + 1] // 8 * 8, sems,
    )
    edge_ref[...] = buf[0:8, :]
    for copy in copies:
        copy.wait()


def late_kernel(plan, own_s, refs, edge_ref, done_hbm, out_hbm, blocks, buf, tail, fetched, sems):
    rels = [(c, a, b) for c in range(2) for a in range(plan.n_hi) for b in range(2)]
    fetch_blocks(plan, own_s, refs, rels, blocks, fetched)

    def ends(d):
        if d + 1 < plan.early0:
            return plan.row0[d + 1] // 8 * 8
        at, lane0 = plan.row0[d + 1], plan.lane0[d + 1]
        if at < plan.cut:
            lane = lax.broadcasted_iota(jnp.int32, (1, LANES), 1)
            row = lax.broadcasted_iota(jnp.int32, (plan.cut - at, 1), 0)
            mine = buf[at : plan.cut, :]
            buf[at : plan.cut, :] = jnp.where((row == 0) & (lane < lane0), mine, edge_ref[at - plan.cut + 8 :, :])
        return plan.cut

    copies = write_shards(plan, range(plan.early0), 0, blocks, fetched, buf, 0, out_hbm, 0, ends, sems)
    small = blocks[0, 0, plan.helper % 2, plan.helper // 2, 0, plan.sub :, :].astype(F32)
    tail[...] = small[:SMALL_ROWS]
    copies.append(pltpu.make_async_copy(tail, out_hbm.at[pl.ds(ROW_SMALL, SMALL_ROWS)], sems.at[7]))
    copies[-1].start()
    for copy in copies:
        copy.wait()


def gradient_kernel(plan, own_s, same, cross, given, ctx_same, ctx_cross, *rest):
    ctx_far, (grad_ref, ctx_ref, grad) = rest[: plan.n_hi - 1], rest[plan.n_hi - 1 :]
    rows, stored = plan.shard_rows, ctx_ref.shape[0] // plan.n_group
    for a in range(plan.n_hi):
        back = lax.rem(own_s[2] + plan.n_hi - a, plan.n_hi) * 2
        ahead = lax.rem(own_s[2] + a, plan.n_hi) * 2
        for n, core in enumerate((own_s[1], 1 - own_s[1])):
            at = pl.multiple_of((back + core) * stored, 16)
            ctx_ref[pl.ds(at, stored), :] = ctx_far[a - 1][n] if a else (ctx_cross if n else ctx_same)[0]
            at = pl.multiple_of((ahead + core) * plan.piece, 16)
            grad[pl.ds(at, plan.piece), :] = (cross if n else same)[a].astype(F32)
    grad[rows:, :] = jnp.zeros((8, LANES), F32)

    @pl.when(own_s[7] == plan.n_dp - 1)
    def _():
        at = ROW_SMALL - plan.row0[-1]
        grad[at : at + SMALL_ROWS, :] = given[plan.sub :, :].astype(F32)[:SMALL_ROWS]

    lane = lax.broadcasted_iota(jnp.int32, (1, LANES), 1)
    back = LANES - own_s[5]
    for i in range(plan.n_group):
        at = slice(i * plan.piece, (i + 1) * plan.piece)
        turned = pltpu.roll(grad[i * plan.piece : (i + 1) * plan.piece + 8, :], back, 1)
        g = jnp.where(lane < back, turned[: plan.piece], turned[1 : plan.piece + 1])
        grad_ref[at, :] = g


def adam(weight, grad, one, two):
    first = 0.5 * one + 0.5 * grad
    second = 0.6 * two + 0.4 * grad * grad
    step = (first / (1.0 - 0.5**STEP)) / (jnp.sqrt(second / (1.0 - 0.6**STEP)) + 1e-08)
    return weight - 0.05 * (step + 0.05 * weight)


def after(value, *others):
    return lax.optimization_barrier((value, others))[0]


def build(mesh):
    n_dp, n_group = mesh.shape["dp"], mesh.shape["group"]
    plan = Plan(n_dp, n_group)
    both = ("dp", "group")
    n_hi, half, quarter = plan.n_hi, plan.half, plan.quarter
    piece, sub = plan.piece, plan.sub
    any_spec = pl.BlockSpec(memory_space=pl.ANY)
    brief = pl.CostEstimate(flops=0, bytes_accessed=0, transcendentals=0)
    params_of = pltpu.CompilerParams(vmem_limit_bytes=VMEM_CAP)

    def pairs(move):
        out = []
        for d in range(n_dp):
            for g in range(n_group):
                ghi, glo, dhi, dlo = move(g // 2, g % 2, d // 2, d % 2)
                out.append((d * n_group + g, (dhi * 2 + dlo) * n_group + ghi * 2 + glo))
        return out

    core_pairs = pairs(lambda gh, gl, dh, dl: (gh, 1 - gl, dh, dl))
    swap_pairs = pairs(lambda gh, gl, dh, dl: (gh, gl, (dh + quarter) % half, dl))

    def xy_pairs(a, b):
        return pairs(lambda gh, gl, dh, dl: ((gh + a) % n_hi, gl, dh, (dl + b) % 2))

    def z_pairs(r):
        return pairs(lambda gh, gl, dh, dl: (gh, gl, (dh + r) % half, dl))

    def group_pairs(r):
        return [(i, (i + r) % n_group) for i in range(n_group)]

    rels = [(a, b) for a in range(n_hi) for b in range(2)]
    def pick(array, index):
        return lax.dynamic_index_in_dim(array, index, 0, keepdims=False)

    def slot_of(h, early):
        return (h % quarter) * 2 + (h // quarter + early) % 2

    def xy_blocks(keep, got, gh, dl):
        def block(a, b):
            i, j = (gh + a) % n_hi, (dl + b) % 2
            mine, theirs = pick(pick(keep, i), j), pick(pick(got, i), j)
            return (mine.astype(F32) + theirs.astype(F32)).astype(BF16)
        return [block(a, b) for a, b in rels]

    def xy_send(blocks):
        return [lax.ppermute(x, both, xy_pairs(a, b)) for x, (a, b) in zip(blocks[1:], rels[1:])]

    def z_blocks(block, arrived, dh, early):
        total = block.astype(F32)
        for part in arrived:
            total = total + part.astype(F32)
        total = total.astype(BF16)
        total = total.reshape((2 * quarter,) + total.shape[2:])
        return [pick(total, slot_of((dh + r) % half, early)) for r in range(half)]

    def z_send(blocks):
        return [lax.ppermute(x, both, z_pairs(r)) for r, x in enumerate(blocks) if r]

    def z_sum(block, arrived):
        total = block.astype(F32)
        for part in arrived:
            total = total + part.astype(F32)
        return total

    def z_gather(mine):
        return [lax.ppermute(mine, both, z_pairs(r)) for r in range(1, half)]

    def z_order(got, sender, early):
        blocks = []
        for t in range(quarter):
            for n in range(2):
                want = (t + early * quarter + n * quarter) % half
                block = got[0]
                for i in range(1, half):
                    block = jnp.where(sender(i) == want, got[i], block)
                blocks.append(block)
        return jnp.stack(blocks).reshape((quarter, 2) + blocks[0].shape)

    def xy_gather(block):
        return [lax.ppermute(block, both, xy_pairs(-a, -b)) for a, b in rels[1:]]

    def core_gather(blocks):
        return [lax.ppermute(b, both, core_pairs) for b in blocks]

    def per_device(
        context, segment_ids, target_index, target_length, pos_table, params, first_moment, second_moment, cotangent
    ):
        stored = context.shape[0] // n_group
        dp, me = lax.axis_index("dp"), lax.axis_index("group")
        gh, gl, dh, dl = me // 2, me % 2, dp // 2, dp % 2
        share = plan.share

        ctx_got = [
            lax.ppermute(
                lax.dynamic_slice_in_dim(context, (me + r) % n_group * stored, stored), "group", group_pairs(r)
            )
            for r in range(1, n_group)
        ]

        lane0 = (dp * share) % LANES

        def own_row(early):
            t = dh % quarter + early * quarter
            n = (dh // quarter + early) % 2
            return ((t * 2 + dl) * share) // LANES + me * piece + n * sub

        own_s = jnp.stack(
            [0 * me, gl, gh, dl, me * piece, lane0, me, dp, own_row(0), own_row(1)]
        ).astype(jnp.int32)
        params2 = params.reshape(ROWS_ALL, LANES)

        weights = [((D_IN, D), BF16), ((D, 3 * D), BF16), ((D, D), BF16), ((D, FF), BF16), ((FF, D), BF16)]
        prep = pl.pallas_call(
            functools.partial(prep_kernel, plan),
            out_shape=[shape((8, D), F32), shape((2, sub, LANES), F32)]
            + [shape(*w) for w in weights] + [shape((TGT, D), F32)],
            in_specs=smem(1) + [any_spec] + vmem(2),
            out_specs=vmem(2) + [any_spec] * 6,
            scratch_shapes=[pltpu.VMEM((plan.flat_rows, LANES), F32)] + [pltpu.VMEM(*w) for w in weights] + [
                pltpu.VMEM((TGT, D), F32),
                pltpu.VMEM((TGT, GRID), F32),
                pltpu.SemaphoreType.DMA((6,)),
                pltpu.SemaphoreType.DMA((6,)),
            ],
            compiler_params=params_of,
        )(own_s, params2, target_index, pos_table)
        vec, own_w, w_in_b, w_qkv_b, w_out_b, w_up_b, w_down_b, target_rows = prep

        early_rows, late_rows = sub, sub + SMALL_PAD
        n_blocks = 2 * n_hi
        out_specs = [
            shape((8, D), F32),
            shape((n_hi, 2, quarter, 2, early_rows, LANES), BF16),
            shape((n_hi, 2, quarter, 2, early_rows, LANES), BF16),
            shape((8,), jnp.int32),
        ]
        saved = [
            ((CTX, D_IN), BF16),
            ((L, D), F32),
            ((L, 3 * D), F32),
            ((GROUPS * 3, CTX, PER * LANES), BF16),
            ((2 * IMG * BLOCKS, KEYS, WIDE), BF16),
            ((L, D), F32),
            ((L, D), F32),
        ]
        written = [
            ((L, D), BF16),
            ((plan.mid_rows, LANES), F32),
        ] + saved

        def forward(*refs):
            n = 2 + 2
            forward_kernel(plan, *refs[:n], refs[n : n + n_group - 1], *refs[n + n_group - 1 :])

        fwd = pl.pallas_call(
            forward,
            out_shape=out_specs + [shape(*s) for s in written],
            in_specs=smem(2) + vmem(2 + n_group - 1 + 1) + [any_spec] * 7,
            out_specs=vmem(3) + smem(1) + [any_spec] * len(written),
            scratch_shapes=[pltpu.VMEM(*w) for w in weights] + [pltpu.VMEM(*s) for s in saved[:5]] + [
                pltpu.VMEM((L, D), F32),
                pltpu.VMEM((L, D), BF16),
                pltpu.VMEM((L, D), F32),
                pltpu.VMEM((L, D), BF16),
                pltpu.VMEM((L, D), F32),
                pltpu.VMEM((L, D), BF16),
                pltpu.VMEM((CTX, CTX), F32),
                pltpu.VMEM((D, CTX), BF16),
                pltpu.VMEM((L, D), BF16),
                pltpu.VMEM((L, FF), BF16),
                pltpu.VMEM((L, FF), BF16),
                pltpu.VMEM((L, D), BF16),
                pltpu.VMEM((plan.flat_rows - ROW_OUT, LANES), F32),
                pltpu.VMEM((L, LANES), F32),
                pltpu.VMEM((L, D), BF16),
                pltpu.VMEM((L, D), BF16),
                pltpu.SemaphoreType.DMA((7,)),
                pltpu.SemaphoreType.DMA((len(written),)),
            ],
            compiler_params=params_of,
        )(
            target_length, own_s,
            vec, context, *ctx_got, segment_ids, cotangent[0],
            w_in_b, w_qkv_b, w_out_b, w_up_b, w_down_b, target_rows,
        )
        small_in, keep_e, send_e, seg_s, out, mid = fwd[: len(fwd) - len(saved)]
        ctx_s, stream_s, qkv_s, probs_c_s, probs_t_s, d_mixed_s, d_middle_s = fwd[len(fwd) - len(saved) :]

        got_e = lax.ppermute(send_e, both, core_pairs)
        spare = plan.shard_rows * LANES - share
        one2, two2 = [
            jnp.pad(m, (8 * LANES, spare)).reshape(8 + plan.shard_rows, LANES) for m in after((first_moment, second_moment), seg_s)
        ]

        xy_e = xy_blocks(keep_e, got_e, gh, dl)
        xy_got_e = xy_send(xy_e)
        qkv_s = after(qkv_s, *xy_e)

        dpk, own_mom, other_mom = pl.pallas_call(
            functools.partial(attention_back_kernel, plan),
            out_shape=[
                shape((L, 3 * D), BF16), shape((2, sub, LANES), F32), shape((2, sub + SMALL_PAD, LANES), F32),
            ],
            in_specs=smem(2) + [any_spec] * 6,
            out_specs=vmem(3),
            scratch_shapes=[pltpu.VMEM(*s) for s in saved[2:6]] + [
                pltpu.VMEM((L, 3 * D), F32),
                pltpu.VMEM((D, CTX), BF16),
                pltpu.VMEM((2, piece + 8, LANES), F32),
                pltpu.VMEM((2, 32, LANES), F32),
                pltpu.SemaphoreType.DMA((8,)),
            ],
            compiler_params=params_of,
            cost_estimate=pl.CostEstimate(flops=10**10, bytes_accessed=20 * 10**6, transcendentals=0),
        )(seg_s, own_s, qkv_s, probs_c_s, probs_t_s, d_mixed_s, one2, two2)

        xy_got_e = [after(x, dpk) for x in xy_got_e]
        z_e = z_blocks(xy_e[0], xy_got_e, dh, 1)
        z_got_e = z_send(z_e)
        swapped = lax.ppermute(other_mom, both, swap_pairs)
        dpk = after(dpk, *z_e)

        bwd_out = [
            shape((n_hi, 2, quarter, 2, late_rows, LANES), BF16),
            shape((n_hi, 2, quarter, 2, late_rows, LANES), BF16),
            shape((n_hi, stored, D_IN), BF16),
            shape((n_hi, stored, D_IN), BF16),
        ]
        bwd = pl.pallas_call(
            functools.partial(backward_kernel, plan),
            out_shape=bwd_out,
            in_specs=smem(1) + vmem(4) + [any_spec] * 5,
            out_specs=vmem(len(bwd_out)),
            scratch_shapes=[
                pltpu.VMEM((D_IN, D), BF16),
                pltpu.VMEM((D, 3 * D), BF16),
                pltpu.VMEM((CTX, D_IN), BF16),
                pltpu.VMEM((L, D), F32),
                pltpu.VMEM((L, D), F32),
                pltpu.VMEM((L, D), BF16),
                pltpu.VMEM((CTX, D), BF16),
                pltpu.VMEM((CTX, D_IN), BF16),
                pltpu.VMEM((SMALL_PAD, LANES), F32),
                pltpu.VMEM((ROW_OUT + plan.mid_rows, LANES), F32),
                pltpu.SemaphoreType.DMA((5,)),
            ],
            compiler_params=params_of,
            cost_estimate=pl.CostEstimate(flops=5 * 10**9, bytes_accessed=15 * 10**6, transcendentals=0),
        )(own_s, vec, small_in, mid, dpk, w_in_b, w_qkv_b, ctx_s, stream_s, d_middle_s)
        keep_l, send_l, ctx_same, ctx_cross = bwd

        upper = dh // quarter
        own_is_late = upper == 0

        def moments_of(early):
            return jnp.where(upper == early, own_mom, swapped[:, :sub])

        def all_after(values, *others):
            return [after(x, *others) for x in values]

        def joint(*groups):
            return lax.optimization_barrier(groups)

        z_got_e, swapped = joint(all_after(z_got_e, keep_l), after(swapped, keep_l))
        tails = swapped[:, sub:]
        got_l = lax.ppermute(after(send_l, *z_got_e), both, core_pairs)
        own_e = z_sum(z_e[0], z_got_e)
        mom = moments_of(1)
        new_e = adam(own_w[1], own_e, mom[0], mom[1]).astype(BF16)
        ctx_cross = lax.ppermute(after(ctx_cross, *z_got_e), both, core_pairs)
        got_l, ctx_cross, new_e = joint(got_l, ctx_cross, new_e)
        ctx_pairs = [jnp.stack([ctx_same[a], ctx_cross[a]]) for a in range(1, n_hi)]

        xy_l = xy_blocks(keep_l, got_l, gh, dl)
        xy_got_l, z_new_e, own_e = joint(xy_send(xy_l), z_gather(after(new_e, *xy_l)), own_e)

        z_l = z_blocks(xy_l[0], xy_got_l, dh, 0)
        block_e = z_order([new_e] + list(z_new_e), lambda i: (dh - i) % half, 1)[None]
        z_got_l, near_e, ctx_far = joint(
            z_send(z_l), [lax.ppermute(block_e, both, xy_pairs(-a, 0)) for a in range(1, n_hi)],
            [lax.ppermute(after(ctx_pairs[a - 1], *z_l), both, xy_pairs(a, 0)) for a in range(1, n_hi)],
        )
        own_l = z_sum(z_l[0], z_got_l)
        small_sum = own_l[sub:]
        small_w = jnp.pad(params[NP - SMALL :].reshape(SMALL_ROWS, LANES), ((0, SMALL_PAD - SMALL_ROWS), (0, 0)))
        mom = moments_of(0)
        new_l = jnp.concatenate([
            adam(own_w[0], own_l[:sub], mom[0], mom[1]), adam(small_w, small_sum, tails[0], tails[1])
        ]).astype(BF16)

        near_e = jnp.concatenate([block_e] + list(near_e))
        give = jnp.where(own_is_late, own_e, own_l[:sub])
        give = jnp.concatenate([give, small_sum]).astype(BF16)
        have = jnp.where(own_is_late, own_l[:sub], own_e).astype(BF16)
        z_new_l, y_near_e, taken = joint(
            z_gather(new_l), lax.ppermute(near_e, both, xy_pairs(0, 1)), lax.ppermute(give, both, swap_pairs)
        )

        block_l = z_order([new_l] + list(z_new_l), lambda i: (dh - i) % half, 0)
        near_e = jnp.concatenate([near_e, y_near_e])
        near_l = xy_gather(block_l)
        far_e = lax.ppermute(after(near_e, block_l), both, core_pairs)
        own = jnp.concatenate([have, taken[:sub]])
        quarters = jnp.stack(
            [own] + [lax.ppermute(after(own, block_l), both, xy_pairs(-a, 0)) for a in range(1, n_hi)]
        )
        other_quarters = lax.ppermute(quarters, both, core_pairs)

        n_parts = 2 * n_blocks
        base = plan.cut - 8

        half_done, edge = pl.pallas_call(
            functools.partial(early_kernel, plan),
            out_shape=[shape((ROWS_ALL, LANES), F32), shape((8, LANES), F32)],
            in_specs=smem(1) + [pl.BlockSpec(memory_space=pltpu.HBM)] * 2,
            out_specs=[any_spec, pl.BlockSpec(memory_space=pltpu.VMEM)],
            scratch_shapes=[
                pltpu.VMEM((2, n_hi, 2, quarter, 2, early_rows, LANES), BF16),
                pltpu.VMEM((plan.flat_rows - base, LANES), F32),
                pltpu.SemaphoreType.DMA((2, n_hi, 2, quarter)),
                pltpu.SemaphoreType.DMA((8,)),
            ],
            compiler_params=params_of,
            cost_estimate=brief,
        )(after(own_s, block_l), near_e, far_e)

        grad, context_grad = pl.pallas_call(
            functools.partial(gradient_kernel, plan),
            out_shape=[shape((plan.shard_rows, LANES), F32), shape(context.shape, BF16)],
            in_specs=smem(1) + vmem(5 + n_hi - 1),
            out_specs=vmem(2),
            scratch_shapes=[pltpu.VMEM((plan.shard_rows + 8, LANES), F32)],
            compiler_params=params_of,
            cost_estimate=brief,
        )(after(own_s, edge), quarters, other_quarters, taken, ctx_same, ctx_cross, *ctx_far)
        near_l, half_done, edge, grad = joint(near_l, half_done, edge, grad)
        near_l = [block_l] + list(near_l)
        all_l = near_l + core_gather(near_l)
        grad = grad.reshape(-1)[:share]
        new_first = 0.5 * first_moment + 0.5 * grad
        new_second = 0.6 * second_moment + 0.4 * grad * grad

        def late(own_ref, *refs):
            late_kernel(plan, own_ref, refs[:n_parts], *refs[n_parts:])

        new_params = pl.pallas_call(
            late,
            out_shape=shape((ROWS_ALL, LANES), F32),
            in_specs=smem(1) + [pl.BlockSpec(memory_space=pltpu.HBM)] * n_parts + vmem(1) + [any_spec],
            out_specs=any_spec,
            scratch_shapes=[
                pltpu.VMEM((2, n_hi, 2, quarter, 2, late_rows, LANES), BF16),
                pltpu.VMEM((plan.row0[plan.early0 - 1] + plan.shard_rows, LANES), F32),
                pltpu.VMEM((SMALL_ROWS, LANES), F32),
                pltpu.SemaphoreType.DMA((2, n_hi, 2, quarter)),
                pltpu.SemaphoreType.DMA((8,)),
            ],
            input_output_aliases={n_parts + 2: 0},
            compiler_params=params_of,
        )(after(own_s, new_first, new_second), *all_l, edge, half_done)

        return out[None], context_grad, new_params.reshape(-1), new_first, new_second

    return per_device


def solution(mesh):
    return jax.shard_map(
        build(mesh),
        mesh=mesh,
        in_specs=(
            P(("dp", "group"), None),
            P(("dp", "group"), None),
            P(("dp", "group"), None, None, None),
            P(("dp", "group"), None, None),
            P(),
            P(),
            P("dp"),
            P("dp"),
            P(("dp", "group"), None, None),
        ),
        out_specs=(P(("dp", "group"), None, None), P(("dp", "group"), None), P(), P("dp"), P("dp")),
        check_vma=False,
    )
```

```python
import functools

import jax
import jax.numpy as jnp
from jax import lax
from jax.experimental import pallas as pl
from jax.experimental.pallas import tpu as pltpu
from jax.sharding import PartitionSpec as P

D_IN = 768
D = 384
HEADS = 12
HD = 32
FF = 1536
GRID = 196
BLOCKS = 4
TMAX = 40
STEP = 10
IMG = 4
CTX = 384
TGT = IMG * BLOCKS * TMAX
L = CTX + TGT
NP = D_IN * D + 4 * D * D + 2 * D * FF + 5 * D
LANES = 128
GROUPS = D // LANES
PER = LANES // HD
WIN = 200
KEYS = WIN + TMAX
WIDE = 256
TILE = 256
MLP_TILE = 512
CHUNK = 512

ROW_IN = 0
ROW_QKV = D_IN * D // LANES
ROW_OUT = ROW_QKV + 3 * D * D // LANES
ROW_UP = ROW_OUT + D * D // LANES
ROW_DOWN = ROW_UP + D * FF // LANES
ROW_SMALL = ROW_DOWN + FF * D // LANES
ROWS_ALL = NP // LANES
SMALL = 5 * D
SMALL_ROWS = SMALL // LANES
SMALL_PAD = 16

norm_eps = 1e-06
mask_value = -1e30
LOG2E = 1.4426950408889634
SCALE = HD**-0.5
F32 = jnp.float32
BF16 = jnp.bfloat16
VMEM_CAP = 64000 * 1024


def dot(a, b):
    return jnp.dot(a, b, preferred_element_type=F32)


def dot_nt(a, b):
    return lax.dot_general(a, b, (((1,), (1,)), ((), ())), preferred_element_type=F32)


def dot_tn(a, b):
    return lax.dot_general(a, b, (((0,), (0,)), ((), ())), preferred_element_type=F32)


def ceil_to(n, m):
    return -(-n // m) * m


class Plan:
    def __init__(self, n_dp, n_group):
        self.n_dp, self.n_group = n_dp, n_group
        self.share = NP // n_dp
        self.row0 = [d * self.share // LANES for d in range(n_dp)]
        self.lane0 = [d * self.share % LANES for d in range(n_dp)]
        most = max(ceil_to(o + self.share, LANES) // LANES for o in self.lane0)
        self.sub = ceil_to(-(-most // (2 * n_group)), 16)
        self.piece = 2 * self.sub
        self.shard_rows = self.piece * n_group
        self.n_hi, self.half = n_group // 2, n_dp // 2
        self.quarter = self.half // 2
        self.early0 = n_dp // 2
        assert self.early0 * self.share >= ROW_OUT * LANES
        self.helper = 2 * (self.half - 1 - self.quarter) + 1
        self.tail = ROW_SMALL - self.row0[-1]
        self.flat_rows = ceil_to(max(r + self.shard_rows for r in self.row0), 16)
        self.mid_rows = ceil_to(self.row0[self.early0 - 1] + self.shard_rows - ROW_OUT, 8)
        self.cut = ceil_to(self.early0 * self.share, 8 * LANES) // LANES


def layer_norm_parts(x):
    mu = jnp.mean(x, axis=-1, keepdims=True)
    xc = x - mu
    rstd = lax.rsqrt(jnp.mean(xc * xc, axis=-1, keepdims=True) + norm_eps)
    return xc * rstd, rstd


def layer_norm_back(dy, gain, xhat, rstd):
    dx = dy * gain
    a = jnp.mean(dx, axis=-1, keepdims=True)
    b = jnp.mean(dx * xhat, axis=-1, keepdims=True)
    return rstd * (dx - a - xhat * b)


def reciprocal(x):
    r = pl.reciprocal(x, approx=True)
    return r * (2.0 - x * r)


def gelu_both(x):
    z = jnp.abs(x) * (0.5**0.5)
    t = reciprocal(1.0 + 0.3275911 * z)
    e = jnp.exp2(x * x * (-0.5 * LOG2E))
    poly = ((((1.061405429 * t - 1.453152027) * t + 1.421413741) * t - 0.284496736) * t + 0.254829592) * t
    tail = 0.5 * poly * e
    cdf = jnp.where(x >= 0, 1.0 - tail, tail)
    pdf = e * 0.3989422804014327
    return x * cdf, cdf + x * pdf


def head_masks(first, count, width):
    lane = lax.broadcasted_iota(jnp.int32, (1, width), 1)
    return [(lane // HD == first + h).astype(F32) for h in range(count)]


def stack_heads(x, masks):
    return jnp.concatenate([x * m for m in masks], axis=0)


def diagonal(x, rows):
    return jnp.concatenate(
        [x[h * HD : (h + 1) * HD, h * rows : (h + 1) * rows] for h in range(PER)], axis=0
    )


def stack_six(x, masks):
    gap = jnp.zeros((WIDE // 2 - 3 * TMAX, WIDE), F32)
    parts = [x * m for m in masks]
    return jnp.concatenate(parts[:3] + [gap] + parts[3:] + [gap], axis=0).astype(BF16)


def fold_six(x, masks):
    total = None
    for h in range(6):
        at = (h // 3) * (WIDE // 2) + (h % 3) * TMAX
        part = x[at : at + TMAX] * masks[h]
        total = part if total is None else total + part
    return total


def half_masks(half):
    lane = lax.broadcasted_iota(jnp.int32, (1, WIDE), 1)
    head = (lane + half * LANES) // HD
    return [(head == 6 * half + h).astype(F32) for h in range(6)]


def half_slice(half, part):
    return pl.ds(pl.multiple_of(part * D + half * LANES, LANES), WIDE)


def lane_slice(g, part):
    return pl.ds(pl.multiple_of(part * D + g * LANES, LANES), LANES)


def prep_kernel(
    plan,
    own_s,
    params_hbm, index_ref, pos_ref,
    vec, own_ref,
    w_in_hbm, w_qkv_hbm, w_out_hbm, w_up_hbm, w_down_hbm, stream_hbm,
    pbuf, w_in_b, w_qkv_b, w_out_b, w_up_b, w_down_b, stream, hot_ref, sems, out_sems,
):
    spans = [
        (ROW_SMALL, SMALL_ROWS), (ROW_IN, ROW_QKV - ROW_IN), (ROW_QKV, ROW_OUT - ROW_QKV),
        (ROW_OUT, ROW_UP - ROW_OUT), (ROW_UP, ROW_DOWN - ROW_UP), (ROW_DOWN, ROW_SMALL - ROW_DOWN),
    ]
    copies = [
        pltpu.make_async_copy(params_hbm.at[pl.ds(r, n)], pbuf.at[pl.ds(r, n)], sems.at[i])
        for i, (r, n) in enumerate(spans)
    ]
    for c in copies:
        c.start()
    outgoing = []

    def send_out(src, dst):
        copy = pltpu.make_async_copy(src, dst, out_sems.at[len(outgoing)])
        copy.start()
        outgoing.append(copy)

    def take(base, rows, tiles, dst, step):
        def body(i, _):
            for c in range(tiles):
                src = pl.ds(base + i * (step * tiles) + c, step, stride=tiles)
                dst[pl.ds(pl.multiple_of(i * step, step), step), c * LANES : (c + 1) * LANES] = pbuf[src, :].astype(BF16)
            return 0
        lax.fori_loop(0, rows // step, body, 0)

    eye = lax.broadcasted_iota(jnp.int32, (TMAX, TMAX), 0) == lax.broadcasted_iota(jnp.int32, (TMAX, TMAX), 1)
    grid_id = lax.broadcasted_iota(jnp.int32, (TMAX, GRID), 1)
    for j in range(IMG * BLOCKS):
        row = index_ref[0, j // BLOCKS, j % BLOCKS : j % BLOCKS + 1, :]
        col = jnp.sum(jnp.where(eye, row, 0), axis=1, keepdims=True)
        hot_ref[j * TMAX : (j + 1) * TMAX, :] = (col == grid_id).astype(F32)

    copies[0].wait()
    vec[...] = jnp.zeros_like(vec)
    for k in range(5):
        for c in range(D // LANES):
            vec[k : k + 1, c * LANES : (c + 1) * LANES] = pbuf[pl.ds(ROW_SMALL + k * 3 + c, 1), :]
    mask_tok = vec[4:5, :]
    pos = pos_ref[...]
    pos_hi = pos.astype(BF16)
    pos_lo = (pos - pos_hi.astype(F32)).astype(BF16)
    for i in range(TGT // 128):
        rows = slice(i * 128, (i + 1) * 128)
        hot = hot_ref[rows, :].astype(BF16)
        stream[rows, :] = mask_tok + (dot(hot, pos_hi) + dot(hot, pos_lo))
    send_out(stream, stream_hbm)

    for n, (base, rows, tiles, dst, out, step) in enumerate((
        (ROW_IN, D_IN, 3, w_in_b, w_in_hbm, 128), (ROW_QKV, D, 9, w_qkv_b, w_qkv_hbm, 128),
        (ROW_OUT, D, 3, w_out_b, w_out_hbm, 128), (ROW_UP, D, 12, w_up_b, w_up_hbm, 128),
        (ROW_DOWN, FF, 3, w_down_b, w_down_hbm, 128),
    )):
        copies[1 + n].wait()
        take(base, rows, tiles, dst, step)
        send_out(dst, out)
    for i in range(2):
        own_ref[i] = pbuf[pl.ds(own_s[8 + i], plan.sub), :]
    for copy in outgoing:
        copy.wait()


def place_pieces(own_s, dst, parts, rows):
    n = len(parts)
    for r, part in enumerate(parts):
        at = pl.multiple_of(lax.rem(own_s[6] + (n - r), n) * rows, 16)
        dst[pl.ds(at, rows), :] = part


def window(seg_s, img):
    return pl.multiple_of(jnp.minimum(seg_s[img] // 8 * 8, CTX - WIN), 8)


def forward_kernel(
    plan,
    len_s, own_s,
    vec, ctx_own, ctx_got, seg_row, cot_hbm,
    w_in_hbm, w_qkv_hbm, w_out_hbm, w_up_hbm, w_down_hbm, target_hbm,
    small_out, keep_ref, send_ref, seg_s,
    out_ref, mid_ref, ctx_hbm, stream_hbm, qkv_hbm, probs_c_hbm, probs_t_hbm, d_mixed_hbm, d_middle_hbm,
    w_in_b, w_qkv_b, w_out_b, w_up_b, w_down_b, ctx, stream, qkv, probs_c, probs_t,
    mixed, mixed_b, d_mixed, d_branch, d_middle, normed, bias, v_t, second, active, d_lift, e_down, gflat, live_col, cot, out_s,
    sems, out_sems,
):
    copies = [
        pltpu.make_async_copy(src, dst, sems.at[i])
        for i, (src, dst) in enumerate((
            (w_in_hbm, w_in_b), (w_qkv_hbm, w_qkv_b), (target_hbm, stream.at[pl.ds(CTX, TGT)]),
            (w_out_hbm, w_out_b), (w_up_hbm, w_up_b), (w_down_hbm, w_down_b), (cot_hbm, cot),
        ))
    ]
    for c in copies:
        c.start()
    outgoing = []

    def send_out(src, dst):
        copy = pltpu.make_async_copy(src, dst, out_sems.at[len(outgoing)])
        copy.start()
        outgoing.append(copy)

    gain1, bias1, gain2, bias2 = [vec[k : k + 1, :] for k in range(4)]
    seg = seg_row[...]
    for i in range(IMG + 1):
        seg_s[i] = jnp.sum((seg < i).astype(jnp.int32))
    row_id = lax.broadcasted_iota(jnp.int32, (CTX, CTX), 0)
    row_image = sum((row_id >= seg_s[i]).astype(jnp.int32) for i in range(1, IMG))
    bias[...] = jnp.where(row_image == seg, 0.0, mask_value)
    live_col[0:CTX, :] = jnp.ones((CTX, LANES), F32)
    slot_id = lax.broadcasted_iota(jnp.int32, (TMAX, LANES), 0)
    for j in range(IMG * BLOCKS):
        live_col[CTX + j * TMAX : CTX + (j + 1) * TMAX, :] = (slot_id < len_s[0, j // BLOCKS, j % BLOCKS]).astype(F32)

    stored = ctx_own.shape[0] // plan.n_group
    first = ctx_own[pl.ds(pl.multiple_of(own_s[6] * stored, 16), stored), :]
    place_pieces(own_s, ctx, [first] + [ref[...] for ref in ctx_got], stored)
    send_out(ctx, ctx_hbm)
    copies[0].wait()
    stream[0:CTX, :] = dot(ctx[...], w_in_b[...])
    copies[2].wait()
    send_out(stream, stream_hbm)
    copies[1].wait()

    def qkv_body(i, _):
        rows = pl.ds(pl.multiple_of(i * TILE, TILE), TILE)
        xhat, _r = layer_norm_parts(stream[rows, :])
        n = (xhat * gain1 + bias1).astype(BF16)
        normed[rows, :] = n
        qkv[rows, :] = dot(n, w_qkv_b[...]).astype(BF16).astype(F32)
        return 0

    lax.fori_loop(0, L // TILE, qkv_body, 0, unroll=4)

    send_out(qkv, qkv_hbm)
    masks = head_masks(0, PER, LANES)
    c2 = SCALE * LOG2E
    for g in range(GROUPS):
        v_t[g * LANES : (g + 1) * LANES, :] = qkv[0:CTX, 2 * D + g * LANES : 2 * D + (g + 1) * LANES].T.astype(BF16)

    def softmax_down(t):
        p = jnp.exp2(t - jnp.max(t, axis=0, keepdims=True))
        return (p * (1.0 / jnp.sum(p, axis=0, keepdims=True))).astype(BF16)

    def ctx_body(i, _):
        g, chunk = i // 3, i % 3
        rows = pl.ds(pl.multiple_of(chunk * LANES, LANES), LANES)
        lanes = pl.ds(pl.multiple_of(g * LANES, LANES), LANES)
        q = stack_heads(qkv[rows, lane_slice(g, 0)], masks).astype(BF16)
        st = dot_nt(qkv[0:CTX, lane_slice(g, 1)].astype(BF16), q)
        for h in range(PER):
            cols = slice(h * LANES, (h + 1) * LANES)
            probs_c[i, :, cols] = softmax_down(st[:, cols] * c2 + bias[:, rows])
        o = dot(v_t[lanes, :], probs_c[i])
        mixed[rows, lanes] = diagonal(o, LANES).T
        return 0

    lax.fori_loop(0, GROUPS * 3, ctx_body, 0, unroll=9)
    send_out(probs_c, probs_c_hbm)

    key_id = lax.broadcasted_iota(jnp.int32, (KEYS, 1), 0)
    mixed[CTX:, :] = jnp.zeros((TGT, D), F32)

    def tgt_body(i, _):
        half, img = i // IMG, i % IMG
        hmasks = half_masks(half)
        first = window(seg_s, img)
        kw = qkv[pl.ds(first, WIN), half_slice(half, 1)]
        vw = qkv[pl.ds(first, WIN), half_slice(half, 2)]
        lo, hi = seg_s[img] - first, seg_s[img + 1] - first
        in_win = (key_id >= lo) & (key_id < hi) & (key_id < WIN)
        units = []
        for blk in range(BLOCKS):
            j = img * BLOCKS + blk
            rows = pl.ds(pl.multiple_of(CTX + j * TMAX, 8), TMAX)
            k = jnp.concatenate([kw, qkv[rows, half_slice(half, 1)]], axis=0).astype(BF16)
            v = jnp.concatenate([vw, qkv[rows, half_slice(half, 2)]], axis=0).astype(BF16)
            q = stack_six(qkv[rows, half_slice(half, 0)], hmasks)
            ok = in_win | ((key_id >= WIN) & (key_id < WIN + len_s[0, img, blk]))
            units.append((rows, v, dot_nt(k, q), jnp.where(ok, 0.0, mask_value)))
        for blk, (rows, v, st, bias_col) in enumerate(units):
            for n in range(2):
                cols = slice(n * LANES, (n + 1) * LANES)
                probs_t[i * BLOCKS + blk, :, cols] = softmax_down(st[:, cols] * c2 + bias_col)
        for blk, (rows, v, st, bias_col) in enumerate(units):
            o = dot_tn(probs_t[i * BLOCKS + blk], v)
            mixed[rows, pl.ds(pl.multiple_of(half * LANES, LANES), WIDE)] += fold_six(o, hmasks)
        return 0

    lax.fori_loop(0, 2 * IMG, tgt_body, 0, unroll=2)
    send_out(probs_t, probs_t_hbm)

    for c in copies[3:]:
        c.wait()

    def mixed_of(rows):
        low = mixed[rows, :].astype(BF16)
        mixed_b[rows, :] = low
        return low

    def block_body(i, carry):
        dg2, db2 = carry
        rows = pl.ds(pl.multiple_of(i * MLP_TILE, MLP_TILE), MLP_TILE)
        live = live_col[rows, 0:1]
        middle = stream[rows, :] + dot(mixed_of(rows), w_out_b[...])
        xhat, rstd = layer_norm_parts(middle)
        sec = (xhat * gain2 + bias2).astype(BF16)
        second[rows, :] = sec
        top = live * cot[rows, :].astype(F32)
        e = top.astype(BF16)
        e_down[rows, :] = e
        out = middle
        d_second = jnp.zeros((MLP_TILE, D), F32)
        for j in range(FF // CHUNK):
            cols = slice(j * CHUNK, (j + 1) * CHUNK)
            lifted = dot(sec, w_up_b[:, cols])
            act, slope = gelu_both(lifted)
            act = act.astype(BF16)
            active[rows, cols] = act
            dl = (dot_nt(e, w_down_b[cols, :]) * slope).astype(BF16)
            d_lift[rows, cols] = dl
            out = out + dot(act, w_down_b[cols, :])
            d_second = d_second + dot_nt(dl, w_up_b[:, cols])
        out_s[rows, :] = (live * out).astype(BF16)
        dm = top + layer_norm_back(d_second, gain2, xhat, rstd)
        d_middle[rows, :] = dm
        db = dm.astype(BF16)
        d_branch[rows, :] = db
        d_mixed[rows, :] = dot_nt(db, w_out_b[...])
        dg2 = dg2 + jnp.sum(d_second * xhat, axis=0, keepdims=True)
        db2 = db2 + jnp.sum(d_second, axis=0, keepdims=True)
        return dg2, db2

    zero = jnp.zeros((1, D), F32)
    dg2, db2 = lax.fori_loop(0, L // MLP_TILE, block_body, (zero, zero))
    small_out[...] = jnp.concatenate([dg2, db2, jnp.zeros((6, D), F32)], axis=0)

    send_out(out_s, out_ref)
    send_out(d_mixed, d_mixed_hbm)
    send_out(d_middle, d_middle_hbm)

    end = ROW_SMALL - ROW_OUT
    gflat[end:, :] = jnp.zeros((gflat.shape[0] - end, LANES), F32)

    g = dot_tn(mixed_b[...], d_branch[...])
    for c in range(3):
        gflat[pl.ds(c, D, stride=3), :] = g[:, c * LANES : (c + 1) * LANES]

    def up_body(j, _):
        cols = pl.ds(pl.multiple_of(j * CHUNK, CHUNK), CHUNK)
        g = dot_tn(second[...], d_lift[:, cols])
        for c in range(CHUNK // LANES):
            gflat[pl.ds(ROW_UP - ROW_OUT + CHUNK // LANES * j + c, D, stride=12), :] = g[:, c * LANES : (c + 1) * LANES]
        return 0

    lax.fori_loop(0, FF // CHUNK, up_body, 0, unroll=3)

    send_out(gflat.at[pl.ds(0, plan.mid_rows)], mid_ref)

    def down_body(j, _):
        cols = pl.ds(pl.multiple_of(j * D, D), D)
        g = dot_tn(active[:, cols], e_down[...])
        for c in range(3):
            gflat[pl.ds(ROW_DOWN - ROW_OUT + j * (3 * D) + c, D, stride=3), :] = g[:, c * LANES : (c + 1) * LANES]
        return 0

    lax.fori_loop(0, 4, down_body, 0, unroll=4)

    store_pieces(plan, gflat, ROW_OUT, range(plan.early0, plan.n_dp), plan.quarter, own_s[1], keep_ref, send_ref)
    for copy in outgoing:
        copy.wait()


def store_pieces(plan, gflat, base, shards, hi0, core, keep_ref, send_ref, extra=None):
    for d in shards:
        for q in range(plan.n_group):
            start = plan.row0[d] - base + q * plan.piece
            blocks = [gflat[start + n * plan.sub : start + (n + 1) * plan.sub, :].astype(BF16) for n in range(2)]

            def put(ref):
                for n in range(2):
                    ref[q // 2, d % 2, d // 2 - hi0, n, 0 : plan.sub, :] = blocks[n]
                    if extra is not None:
                        ref[q // 2, d % 2, d // 2 - hi0, n, plan.sub :, :] = extra

            @pl.when(core == q % 2)
            def _():
                put(keep_ref)

            @pl.when(core != q % 2)
            def _():
                put(send_ref)


def attention_back_kernel(
    plan,
    seg_s, own_s, qkv_hbm, probs_c_hbm, probs_t_hbm, d_mixed_hbm, one_hbm, two_hbm,
    dpk, mine_ref, other_ref, qkv, probs_c, probs_t, d_mixed, d_qkv, k_t, mom, tail, sems,
):
    incoming = {}
    for n, (name, src, dst) in enumerate((
        ("qkv", qkv_hbm, qkv), ("d_mixed", d_mixed_hbm, d_mixed), ("probs_c", probs_c_hbm, probs_c),
        ("probs_t", probs_t_hbm, probs_t),
    )):
        incoming[name] = pltpu.make_async_copy(src, dst, sems.at[n])
        incoming[name].start()

    tail0 = plan.tail // 8 * 8
    moments = []
    for i, src in enumerate((one_hbm, two_hbm)):
        moments.append(pltpu.make_async_copy(src.at[pl.ds(own_s[4], plan.piece + 8)], mom.at[i], sems.at[4 + 2 * i]))
        moments.append(pltpu.make_async_copy(src.at[pl.ds(tail0, 32)], tail.at[i], sems.at[5 + 2 * i]))
    for copy in moments:
        copy.start()

    d_qkv[...] = jnp.zeros_like(d_qkv)
    masks = head_masks(0, PER, LANES)
    incoming["qkv"].wait()
    for g in range(GROUPS):
        k_t[g * LANES : (g + 1) * LANES, :] = qkv[0:CTX, D + g * LANES : D + (g + 1) * LANES].T.astype(BF16)
    incoming["d_mixed"].wait()
    incoming["probs_c"].wait()

    def back_down(p, dp):
        p = p.astype(F32)
        delta = jnp.sum(p * dp, axis=0, keepdims=True)
        return (p * (dp - delta)).astype(BF16)

    def ctx_body(i, _):
        g, chunk = i // 3, i % 3
        rows = pl.ds(pl.multiple_of(chunk * LANES, LANES), LANES)
        lanes = pl.ds(pl.multiple_of(g * LANES, LANES), LANES)
        do = stack_heads(d_mixed[rows, lanes], masks).astype(BF16)
        dpt = dot_nt(qkv[0:CTX, lane_slice(g, 2)].astype(BF16), do)
        ds = []
        for h in range(PER):
            cols = slice(h * LANES, (h + 1) * LANES)
            ds.append(back_down(probs_c[i, :, cols], dpt[:, cols]))
        ds = jnp.concatenate(ds, axis=1)
        q = stack_heads(qkv[rows, lane_slice(g, 0)], masks).astype(BF16)
        d_qkv[rows, lane_slice(g, 0)] = diagonal(dot(k_t[lanes, :], ds), LANES).T
        d_qkv[0:CTX, lane_slice(g, 1)] += dot(ds, q)
        d_qkv[0:CTX, lane_slice(g, 2)] += dot(probs_c[i], do)
        return 0

    lax.fori_loop(0, GROUPS * 3, ctx_body, 0, unroll=3)
    incoming["probs_t"].wait()

    def tgt_body(i, _):
        half, img = i // IMG, i % IMG
        hmasks = half_masks(half)
        first = window(seg_s, img)
        win = pl.ds(first, WIN)
        kw = qkv[win, half_slice(half, 1)]
        vw = qkv[win, half_slice(half, 2)]
        units = []
        for blk in range(BLOCKS):
            rows = pl.ds(pl.multiple_of(CTX + (img * BLOCKS + blk) * TMAX, 8), TMAX)
            v = jnp.concatenate([vw, qkv[rows, half_slice(half, 2)]], axis=0).astype(BF16)
            do = stack_six(d_mixed[rows, pl.ds(pl.multiple_of(half * LANES, LANES), WIDE)], hmasks)
            units.append((rows, do, dot_nt(v, do)))
        dkw = jnp.zeros((WIN, WIDE), F32)
        dvw = jnp.zeros((WIN, WIDE), F32)
        for blk, (rows, do, dpt) in enumerate(units):
            p = probs_t[i * BLOCKS + blk]
            ds = jnp.concatenate(
                [back_down(p[:, n * LANES : (n + 1) * LANES], dpt[:, n * LANES : (n + 1) * LANES]) for n in range(2)],
                axis=1,
            )
            k = jnp.concatenate([kw, qkv[rows, half_slice(half, 1)]], axis=0).astype(BF16)
            q = stack_six(qkv[rows, half_slice(half, 0)], hmasks)
            d_qkv[rows, half_slice(half, 0)] += fold_six(dot_tn(ds, k), hmasks)
            dk = dot(ds, q)
            dv = dot(p, do)
            d_qkv[rows, half_slice(half, 1)] += dk[WIN:]
            d_qkv[rows, half_slice(half, 2)] += dv[WIN:]
            dkw = dkw + dk[:WIN]
            dvw = dvw + dv[:WIN]
        d_qkv[win, half_slice(half, 1)] += dkw
        d_qkv[win, half_slice(half, 2)] += dvw
        return 0

    lax.fori_loop(0, 2 * IMG, tgt_body, 0, unroll=2)
    for copy in moments:
        copy.wait()
    lane = lax.broadcasted_iota(jnp.int32, (1, LANES), 1)
    for i in range(2):
        turned = pltpu.roll(mom[i], own_s[5], 1)
        aligned = jnp.where(lane >= own_s[5], turned[8:], turned[7:-1])
        mine_ref[i] = aligned[: plan.sub]
        other_ref[i, 0 : plan.sub, :] = aligned[plan.sub :]
        turned = pltpu.roll(tail[i], own_s[5], 1)
        aligned = jnp.where(lane >= own_s[5], turned[1:], turned[:-1])
        at = plan.tail - tail0 + 7
        other_ref[i, plan.sub : plan.sub + SMALL_PAD, :] = aligned[at : at + SMALL_PAD]

    def round_body(i, _):
        rows = pl.ds(pl.multiple_of(i * 128, 128), 128)
        dpk[rows, 0 : 2 * D] = (d_qkv[rows, 0 : 2 * D] * SCALE).astype(BF16)
        dpk[rows, 2 * D :] = d_qkv[rows, 2 * D :].astype(BF16)
        return 0

    lax.fori_loop(0, L // 128, round_body, 0, unroll=8)


def backward_kernel(
    plan,
    own_s,
    vec, small_in, dpk,
    mid_hbm, w_in_hbm, w_qkv_hbm, ctx_hbm, stream_hbm, d_middle_hbm,
    keep_ref, send_ref, same_ref, cross_ref,
    w_in_b, w_qkv_b, ctx_ref, stream, d_middle, normed, d_hidden, ctx_grad, small_flat, gflat, sems,
):
    incoming = {}
    for n, (name, src, dst) in enumerate((
        ("w_qkv", w_qkv_hbm, w_qkv_b), ("stream", stream_hbm, stream), ("d_middle", d_middle_hbm, d_middle),
        ("w_in", w_in_hbm, w_in_b), ("ctx", ctx_hbm, ctx_ref),
        ("mid", mid_hbm, gflat.at[pl.ds(ROW_OUT, plan.mid_rows)]),
    )):
        incoming[name] = pltpu.make_async_copy(src, dst, sems.at[n])
        incoming[name].start()
    gain1, bias1 = vec[0:1, :], vec[1:2, :]
    for name in ("w_qkv", "stream", "d_middle"):
        incoming[name].wait()

    def row_body(i, carry):
        dg1, db1, dmask = carry
        rows = pl.ds(pl.multiple_of(i * 128, 128), 128)
        xhat, rstd = layer_norm_parts(stream[rows, :])
        normed[rows, :] = (xhat * gain1 + bias1).astype(BF16)
        d_normed = dot_nt(dpk[rows, :], w_qkv_b[...])
        d_stream = d_middle[rows, :] + layer_norm_back(d_normed, gain1, xhat, rstd)
        dg1 = dg1 + jnp.sum(d_normed * xhat, axis=0, keepdims=True)
        db1 = db1 + jnp.sum(d_normed, axis=0, keepdims=True)
        is_tgt = (i >= CTX // 128).astype(F32)
        dmask = dmask + is_tgt * jnp.sum(d_stream, axis=0, keepdims=True)

        @pl.when(i < CTX // 128)
        def _():
            d_hidden[rows, :] = d_stream.astype(BF16)

        return dg1, db1, dmask

    zero = jnp.zeros((1, D), F32)
    dg1, db1, dmask = lax.fori_loop(0, L // 128, row_body, (zero, zero, zero), unroll=8)
    for k, row in enumerate((dg1, db1, small_in[0:1, :], small_in[1:2, :], dmask)):
        for c in range(3):
            small_flat[3 * k + c : 3 * k + c + 1, :] = row[:, c * LANES : (c + 1) * LANES]
    small_flat[SMALL_ROWS:, :] = jnp.zeros((SMALL_PAD - SMALL_ROWS, LANES), F32)

    incoming["w_in"].wait()
    incoming["ctx"].wait()
    ctx_grad[...] = dot_nt(d_hidden[...], w_in_b[...]).astype(BF16)
    stored = CTX // plan.n_group
    for a in range(plan.n_hi):
        hi = lax.rem(own_s[2] + a, plan.n_hi) * 2
        for ref, core in ((same_ref, own_s[1]), (cross_ref, 1 - own_s[1])):
            ref[a] = ctx_grad[pl.ds(pl.multiple_of((hi + core) * stored, 16), stored), :]
    for j in range(2):
        g = dot_tn(ctx_ref[:, j * D : (j + 1) * D], d_hidden[...])
        for c in range(3):
            gflat[pl.ds(ROW_IN + j * 3 * D + c, D, stride=3), :] = g[:, c * LANES : (c + 1) * LANES]
    def qkv_body(j, _):
        g = dot_tn(normed[...], dpk[:, pl.ds(pl.multiple_of(j * D, D), D)])
        for c in range(3):
            gflat[pl.ds(ROW_QKV + 3 * j + c, D, stride=9), :] = g[:, c * LANES : (c + 1) * LANES]
        return 0

    lax.fori_loop(0, 3, qkv_body, 0)
    incoming["mid"].wait()
    store_pieces(plan, gflat, 0, range(plan.early0), 0, own_s[1], keep_ref, send_ref, small_flat[...].astype(BF16))


def vmem(n):
    return [pl.BlockSpec(memory_space=pltpu.VMEM)] * n


def smem(n):
    return [pl.BlockSpec(memory_space=pltpu.SMEM)] * n


def shape(dims, dtype):
    return jax.ShapeDtypeStruct(dims, dtype)


def fetch_blocks(plan, own_s, refs, rels, dst, sems):
    for i, (ref, (c_rel, a_rel, b_rel)) in enumerate(zip(refs, rels)):
        core = lax.rem(own_s[1] + c_rel, 2)
        hi = lax.rem(own_s[2] + a_rel, plan.n_hi)
        lo = lax.rem(own_s[3] + b_rel, 2)
        for t in range(plan.quarter):
            pltpu.make_async_copy(ref.at[t], dst.at[core, hi, lo, t], sems.at[core, hi, lo, t]).start()


def wait_shard(plan, d, hi0, dst, sems):
    t = d // 2 - hi0
    for core in range(2):
        for hi in range(plan.n_hi):
            at = dst.at[core, hi, d % 2, t]
            pltpu.make_async_copy(at, at, sems.at[core, hi, d % 2, t]).wait()


def put_rows(plan, shards, hi0, src, out, base):
    for d in shards:
        lane0 = plan.lane0[d]
        rows = ceil_to(lane0 + plan.share, LANES) // LANES
        for q in range(plan.n_group):
            for n in range(2):
                start = q * plan.piece + n * plan.sub
                count = min(plan.sub, rows - start)
                if count <= 0:
                    continue
                block = src[q % 2, q // 2, d % 2, d // 2 - hi0, n, 0 : plan.sub, :].astype(F32)
                at = plan.row0[d] + start - base
                if start == 0 and lane0:
                    lane = lax.broadcasted_iota(jnp.int32, (1, LANES), 1)
                    out[at : at + 1, :] = jnp.where(lane < lane0, out[at : at + 1, :], block[0:1])
                    out[at + 1 : at + count, :] = block[1:count]
                else:
                    out[at : at + count, :] = block[:count]


def write_shards(plan, shards, hi0, blocks, fetched, buf, base, out_hbm, done, ends, sems):
    copies = []
    step = max(1, len(shards) // 4)
    for n, d in enumerate(shards):
        wait_shard(plan, d, hi0, blocks, fetched)
        put_rows(plan, [d], hi0, blocks, buf, base)
        if (n + 1) % step == 0 or n + 1 == len(shards):
            upto = ends(d)
            copies.append(pltpu.make_async_copy(
                buf.at[pl.ds(done - base, upto - done)], out_hbm.at[pl.ds(done, upto - done)], sems.at[len(copies)]
            ))
            copies[-1].start()
            done = upto
    return copies


def early_kernel(plan, own_s, near, far, out_hbm, edge_ref, blocks, buf, fetched, sems):
    rels = [(c, a, b) for c in range(2) for b in range(2) for a in range(plan.n_hi)]
    refs = [src.at[i] for src in (near, far) for i in range(2 * plan.n_hi)]
    fetch_blocks(plan, own_s, refs, rels, blocks, fetched)
    base = plan.cut - 8
    buf[0:8, :] = jnp.zeros((8, LANES), F32)
    copies = write_shards(
        plan, range(plan.early0, plan.n_dp), plan.quarter, blocks, fetched, buf, base, out_hbm, plan.cut,
        lambda d: ROW_SMALL if d + 1 == plan.n_dp else plan.row0[d + 1] // 8 * 8, sems,
    )
    edge_ref[...] = buf[0:8, :]
    for copy in copies:
        copy.wait()


def late_kernel(plan, own_s, refs, edge_ref, done_hbm, out_hbm, blocks, buf, tail, fetched, sems):
    rels = [(c, a, b) for c in range(2) for a in range(plan.n_hi) for b in range(2)]
    fetch_blocks(plan, own_s, refs, rels, blocks, fetched)

    def ends(d):
        if d + 1 < plan.early0:
            return plan.row0[d + 1] // 8 * 8
        at, lane0 = plan.row0[d + 1], plan.lane0[d + 1]
        if at < plan.cut:
            lane = lax.broadcasted_iota(jnp.int32, (1, LANES), 1)
            row = lax.broadcasted_iota(jnp.int32, (plan.cut - at, 1), 0)
            mine = buf[at : plan.cut, :]
            buf[at : plan.cut, :] = jnp.where((row == 0) & (lane < lane0), mine, edge_ref[at - plan.cut + 8 :, :])
        return plan.cut

    copies = write_shards(plan, range(plan.early0), 0, blocks, fetched, buf, 0, out_hbm, 0, ends, sems)
    small = blocks[0, 0, plan.helper % 2, plan.helper // 2, 0, plan.sub :, :].astype(F32)
    tail[...] = small[:SMALL_ROWS]
    copies.append(pltpu.make_async_copy(tail, out_hbm.at[pl.ds(ROW_SMALL, SMALL_ROWS)], sems.at[7]))
    copies[-1].start()
    for copy in copies:
        copy.wait()


def gradient_kernel(plan, own_s, same, cross, given, ctx_same, ctx_cross, *rest):
    ctx_far, (grad_ref, ctx_ref, grad) = rest[: plan.n_hi - 1], rest[plan.n_hi - 1 :]
    rows, stored = plan.shard_rows, ctx_ref.shape[0] // plan.n_group
    for a in range(plan.n_hi):
        back = lax.rem(own_s[2] + plan.n_hi - a, plan.n_hi) * 2
        ahead = lax.rem(own_s[2] + a, plan.n_hi) * 2
        for n, core in enumerate((own_s[1], 1 - own_s[1])):
            at = pl.multiple_of((back + core) * stored, 16)
            ctx_ref[pl.ds(at, stored), :] = ctx_far[a - 1][n] if a else (ctx_cross if n else ctx_same)[0]
            at = pl.multiple_of((ahead + core) * plan.piece, 16)
            grad[pl.ds(at, plan.piece), :] = (cross if n else same)[a].astype(F32)
    grad[rows:, :] = jnp.zeros((8, LANES), F32)

    @pl.when(own_s[7] == plan.n_dp - 1)
    def _():
        at = ROW_SMALL - plan.row0[-1]
        grad[at : at + SMALL_ROWS, :] = given[plan.sub :, :].astype(F32)[:SMALL_ROWS]

    lane = lax.broadcasted_iota(jnp.int32, (1, LANES), 1)
    back = LANES - own_s[5]
    for i in range(plan.n_group):
        at = slice(i * plan.piece, (i + 1) * plan.piece)
        turned = pltpu.roll(grad[i * plan.piece : (i + 1) * plan.piece + 8, :], back, 1)
        g = jnp.where(lane < back, turned[: plan.piece], turned[1 : plan.piece + 1])
        grad_ref[at, :] = g


def adam(weight, grad, one, two):
    first = 0.5 * one + 0.5 * grad
    second = 0.6 * two + 0.4 * grad * grad
    step = (first / (1.0 - 0.5**STEP)) / (jnp.sqrt(second / (1.0 - 0.6**STEP)) + 1e-08)
    return weight - 0.05 * (step + 0.05 * weight)


def after(value, *others):
    return lax.optimization_barrier((value, others))[0]


def build(mesh):
    n_dp, n_group = mesh.shape["dp"], mesh.shape["group"]
    plan = Plan(n_dp, n_group)
    both = ("dp", "group")
    n_hi, half, quarter = plan.n_hi, plan.half, plan.quarter
    piece, sub = plan.piece, plan.sub
    any_spec = pl.BlockSpec(memory_space=pl.ANY)
    brief = pl.CostEstimate(flops=0, bytes_accessed=0, transcendentals=0)
    params_of = pltpu.CompilerParams(vmem_limit_bytes=VMEM_CAP)

    def pairs(move):
        out = []
        for d in range(n_dp):
            for g in range(n_group):
                ghi, glo, dhi, dlo = move(g // 2, g % 2, d // 2, d % 2)
                out.append((d * n_group + g, (dhi * 2 + dlo) * n_group + ghi * 2 + glo))
        return out

    core_pairs = pairs(lambda gh, gl, dh, dl: (gh, 1 - gl, dh, dl))
    swap_pairs = pairs(lambda gh, gl, dh, dl: (gh, gl, (dh + quarter) % half, dl))

    def xy_pairs(a, b):
        return pairs(lambda gh, gl, dh, dl: ((gh + a) % n_hi, gl, dh, (dl + b) % 2))

    def z_pairs(r):
        return pairs(lambda gh, gl, dh, dl: (gh, gl, (dh + r) % half, dl))

    def group_pairs(r):
        return [(i, (i + r) % n_group) for i in range(n_group)]

    rels = [(a, b) for a in range(n_hi) for b in range(2)]
    def pick(array, index):
        return lax.dynamic_index_in_dim(array, index, 0, keepdims=False)

    def slot_of(h, early):
        return (h % quarter) * 2 + (h // quarter + early) % 2

    def xy_blocks(keep, got, gh, dl):
        def block(a, b):
            i, j = (gh + a) % n_hi, (dl + b) % 2
            mine, theirs = pick(pick(keep, i), j), pick(pick(got, i), j)
            return (mine.astype(F32) + theirs.astype(F32)).astype(BF16)
        return [block(a, b) for a, b in rels]

    def xy_send(blocks):
        return [lax.ppermute(x, both, xy_pairs(a, b)) for x, (a, b) in zip(blocks[1:], rels[1:])]

    def z_blocks(block, arrived, dh, early):
        total = block.astype(F32)
        for part in arrived:
            total = total + part.astype(F32)
        total = total.astype(BF16)
        total = total.reshape((2 * quarter,) + total.shape[2:])
        return [pick(total, slot_of((dh + r) % half, early)) for r in range(half)]

    def z_send(blocks):
        return [lax.ppermute(x, both, z_pairs(r)) for r, x in enumerate(blocks) if r]

    def z_sum(block, arrived):
        total = block.astype(F32)
        for part in arrived:
            total = total + part.astype(F32)
        return total

    def z_gather(mine):
        return [lax.ppermute(mine, both, z_pairs(r)) for r in range(1, half)]

    def z_order(got, sender, early):
        blocks = []
        for t in range(quarter):
            for n in range(2):
                want = (t + early * quarter + n * quarter) % half
                block = got[0]
                for i in range(1, half):
                    block = jnp.where(sender(i) == want, got[i], block)
                blocks.append(block)
        return jnp.stack(blocks).reshape((quarter, 2) + blocks[0].shape)

    def xy_gather(block):
        return [lax.ppermute(block, both, xy_pairs(-a, -b)) for a, b in rels[1:]]

    def core_gather(blocks):
        return [lax.ppermute(b, both, core_pairs) for b in blocks]

    def per_device(
        context, segment_ids, target_index, target_length, pos_table, params, first_moment, second_moment, cotangent
    ):
        stored = context.shape[0] // n_group
        dp, me = lax.axis_index("dp"), lax.axis_index("group")
        gh, gl, dh, dl = me // 2, me % 2, dp // 2, dp % 2
        share = plan.share

        ctx_got = [
            lax.ppermute(
                lax.dynamic_slice_in_dim(context, (me + r) % n_group * stored, stored), "group", group_pairs(r)
            )
            for r in range(1, n_group)
        ]

        lane0 = (dp * share) % LANES

        def own_row(early):
            t = dh % quarter + early * quarter
            n = (dh // quarter + early) % 2
            return ((t * 2 + dl) * share) // LANES + me * piece + n * sub

        own_s = jnp.stack(
            [0 * me, gl, gh, dl, me * piece, lane0, me, dp, own_row(0), own_row(1)]
        ).astype(jnp.int32)
        params2 = params.reshape(ROWS_ALL, LANES)

        weights = [((D_IN, D), BF16), ((D, 3 * D), BF16), ((D, D), BF16), ((D, FF), BF16), ((FF, D), BF16)]
        prep = pl.pallas_call(
            functools.partial(prep_kernel, plan),
            out_shape=[shape((8, D), F32), shape((2, sub, LANES), F32)]
            + [shape(*w) for w in weights] + [shape((TGT, D), F32)],
            in_specs=smem(1) + [any_spec] + vmem(2),
            out_specs=vmem(2) + [any_spec] * 6,
            scratch_shapes=[pltpu.VMEM((plan.flat_rows, LANES), F32)] + [pltpu.VMEM(*w) for w in weights] + [
                pltpu.VMEM((TGT, D), F32),
                pltpu.VMEM((TGT, GRID), F32),
                pltpu.SemaphoreType.DMA((6,)),
                pltpu.SemaphoreType.DMA((6,)),
            ],
            compiler_params=params_of,
        )(own_s, params2, target_index, pos_table)
        vec, own_w, w_in_b, w_qkv_b, w_out_b, w_up_b, w_down_b, target_rows = prep

        early_rows, late_rows = sub, sub + SMALL_PAD
        n_blocks = 2 * n_hi
        out_specs = [
            shape((8, D), F32),
            shape((n_hi, 2, quarter, 2, early_rows, LANES), BF16),
            shape((n_hi, 2, quarter, 2, early_rows, LANES), BF16),
            shape((8,), jnp.int32),
        ]
        saved = [
            ((CTX, D_IN), BF16),
            ((L, D), F32),
            ((L, 3 * D), F32),
            ((GROUPS * 3, CTX, PER * LANES), BF16),
            ((2 * IMG * BLOCKS, KEYS, WIDE), BF16),
            ((L, D), F32),
            ((L, D), F32),
        ]
        written = [
            ((L, D), BF16),
            ((plan.mid_rows, LANES), F32),
        ] + saved

        def forward(*refs):
            n = 2 + 2
            forward_kernel(plan, *refs[:n], refs[n : n + n_group - 1], *refs[n + n_group - 1 :])

        fwd = pl.pallas_call(
            forward,
            out_shape=out_specs + [shape(*s) for s in written],
            in_specs=smem(2) + vmem(2 + n_group - 1 + 1) + [any_spec] * 7,
            out_specs=vmem(3) + smem(1) + [any_spec] * len(written),
            scratch_shapes=[pltpu.VMEM(*w) for w in weights] + [pltpu.VMEM(*s) for s in saved[:5]] + [
                pltpu.VMEM((L, D), F32),
                pltpu.VMEM((L, D), BF16),
                pltpu.VMEM((L, D), F32),
                pltpu.VMEM((L, D), BF16),
                pltpu.VMEM((L, D), F32),
                pltpu.VMEM((L, D), BF16),
                pltpu.VMEM((CTX, CTX), F32),
                pltpu.VMEM((D, CTX), BF16),
                pltpu.VMEM((L, D), BF16),
                pltpu.VMEM((L, FF), BF16),
                pltpu.VMEM((L, FF), BF16),
                pltpu.VMEM((L, D), BF16),
                pltpu.VMEM((plan.flat_rows - ROW_OUT, LANES), F32),
                pltpu.VMEM((L, LANES), F32),
                pltpu.VMEM((L, D), BF16),
                pltpu.VMEM((L, D), BF16),
                pltpu.SemaphoreType.DMA((7,)),
                pltpu.SemaphoreType.DMA((len(written),)),
            ],
            compiler_params=params_of,
        )(
            target_length, own_s,
            vec, context, *ctx_got, segment_ids, cotangent[0],
            w_in_b, w_qkv_b, w_out_b, w_up_b, w_down_b, target_rows,
        )
        small_in, keep_e, send_e, seg_s, out, mid = fwd[: len(fwd) - len(saved)]
        ctx_s, stream_s, qkv_s, probs_c_s, probs_t_s, d_mixed_s, d_middle_s = fwd[len(fwd) - len(saved) :]

        got_e = lax.ppermute(send_e, both, core_pairs)
        spare = plan.shard_rows * LANES - share
        one2, two2 = [
            jnp.pad(m, (8 * LANES, spare)).reshape(8 + plan.shard_rows, LANES) for m in after((first_moment, second_moment), seg_s)
        ]

        xy_e = xy_blocks(keep_e, got_e, gh, dl)
        xy_got_e = xy_send(xy_e)
        qkv_s = after(qkv_s, *xy_e)

        dpk, own_mom, other_mom = pl.pallas_call(
            functools.partial(attention_back_kernel, plan),
            out_shape=[
                shape((L, 3 * D), BF16), shape((2, sub, LANES), F32), shape((2, sub + SMALL_PAD, LANES), F32),
            ],
            in_specs=smem(2) + [any_spec] * 6,
            out_specs=vmem(3),
            scratch_shapes=[pltpu.VMEM(*s) for s in saved[2:6]] + [
                pltpu.VMEM((L, 3 * D), F32),
                pltpu.VMEM((D, CTX), BF16),
                pltpu.VMEM((2, piece + 8, LANES), F32),
                pltpu.VMEM((2, 32, LANES), F32),
                pltpu.SemaphoreType.DMA((8,)),
            ],
            compiler_params=params_of,
            cost_estimate=pl.CostEstimate(flops=10**10, bytes_accessed=20 * 10**6, transcendentals=0),
        )(seg_s, own_s, qkv_s, probs_c_s, probs_t_s, d_mixed_s, one2, two2)

        xy_got_e = [after(x, dpk) for x in xy_got_e]
        z_e = z_blocks(xy_e[0], xy_got_e, dh, 1)
        z_got_e = z_send(z_e)
        swapped = lax.ppermute(other_mom, both, swap_pairs)
        dpk = after(dpk, *z_e)

        bwd_out = [
            shape((n_hi, 2, quarter, 2, late_rows, LANES), BF16),
            shape((n_hi, 2, quarter, 2, late_rows, LANES), BF16),
            shape((n_hi, stored, D_IN), BF16),
            shape((n_hi, stored, D_IN), BF16),
        ]
        bwd = pl.pallas_call(
            functools.partial(backward_kernel, plan),
            out_shape=bwd_out,
            in_specs=smem(1) + vmem(3) + [any_spec] * 6,
            out_specs=vmem(len(bwd_out)),
            scratch_shapes=[
                pltpu.VMEM((D_IN, D), BF16),
                pltpu.VMEM((D, 3 * D), BF16),
                pltpu.VMEM((CTX, D_IN), BF16),
                pltpu.VMEM((L, D), F32),
                pltpu.VMEM((L, D), F32),
                pltpu.VMEM((L, D), BF16),
                pltpu.VMEM((CTX, D), BF16),
                pltpu.VMEM((CTX, D_IN), BF16),
                pltpu.VMEM((SMALL_PAD, LANES), F32),
                pltpu.VMEM((ROW_OUT + plan.mid_rows, LANES), F32),
                pltpu.SemaphoreType.DMA((6,)),
            ],
            compiler_params=params_of,
            cost_estimate=pl.CostEstimate(flops=5 * 10**9, bytes_accessed=15 * 10**6, transcendentals=0),
        )(own_s, vec, small_in, dpk, mid, w_in_b, w_qkv_b, ctx_s, stream_s, d_middle_s)
        keep_l, send_l, ctx_same, ctx_cross = bwd

        upper = dh // quarter
        own_is_late = upper == 0

        def moments_of(early):
            return jnp.where(upper == early, own_mom, swapped[:, :sub])

        def all_after(values, *others):
            return [after(x, *others) for x in values]

        def joint(*groups):
            return lax.optimization_barrier(groups)

        z_got_e, swapped = joint(all_after(z_got_e, keep_l), after(swapped, keep_l))
        tails = swapped[:, sub:]
        got_l = lax.ppermute(after(send_l, *z_got_e), both, core_pairs)
        own_e = z_sum(z_e[0], z_got_e)
        mom = moments_of(1)
        new_e = adam(own_w[1], own_e, mom[0], mom[1]).astype(BF16)
        ctx_cross = lax.ppermute(after(ctx_cross, *z_got_e), both, core_pairs)
        got_l, ctx_cross, new_e = joint(got_l, ctx_cross, new_e)
        ctx_pairs = [jnp.stack([ctx_same[a], ctx_cross[a]]) for a in range(1, n_hi)]

        xy_l = xy_blocks(keep_l, got_l, gh, dl)
        xy_got_l, z_new_e, own_e = joint(xy_send(xy_l), z_gather(after(new_e, *xy_l)), own_e)

        z_l = z_blocks(xy_l[0], xy_got_l, dh, 0)
        block_e = z_order([new_e] + list(z_new_e), lambda i: (dh - i) % half, 1)[None]
        z_got_l, near_e, ctx_far = joint(
            z_send(z_l), [lax.ppermute(block_e, both, xy_pairs(-a, 0)) for a in range(1, n_hi)],
            [lax.ppermute(after(ctx_pairs[a - 1], *z_l), both, xy_pairs(a, 0)) for a in range(1, n_hi)],
        )
        own_l = z_sum(z_l[0], z_got_l)
        small_sum = own_l[sub:]
        small_w = jnp.pad(params[NP - SMALL :].reshape(SMALL_ROWS, LANES), ((0, SMALL_PAD - SMALL_ROWS), (0, 0)))
        mom = moments_of(0)
        new_l = jnp.concatenate([
            adam(own_w[0], own_l[:sub], mom[0], mom[1]), adam(small_w, small_sum, tails[0], tails[1])
        ]).astype(BF16)

        near_e = jnp.concatenate([block_e] + list(near_e))
        give = jnp.where(own_is_late, own_e, own_l[:sub])
        give = jnp.concatenate([give, small_sum]).astype(BF16)
        have = jnp.where(own_is_late, own_l[:sub], own_e).astype(BF16)
        z_new_l, y_near_e, taken = joint(
            z_gather(new_l), lax.ppermute(near_e, both, xy_pairs(0, 1)), lax.ppermute(give, both, swap_pairs)
        )

        block_l = z_order([new_l] + list(z_new_l), lambda i: (dh - i) % half, 0)
        near_e = jnp.concatenate([near_e, y_near_e])
        near_l = xy_gather(block_l)
        far_e = lax.ppermute(after(near_e, block_l), both, core_pairs)
        own = jnp.concatenate([have, taken[:sub]])
        quarters = jnp.stack(
            [own] + [lax.ppermute(after(own, block_l), both, xy_pairs(-a, 0)) for a in range(1, n_hi)]
        )
        other_quarters = lax.ppermute(quarters, both, core_pairs)

        n_parts = 2 * n_blocks
        base = plan.cut - 8

        half_done, edge = pl.pallas_call(
            functools.partial(early_kernel, plan),
            out_shape=[shape((ROWS_ALL, LANES), F32), shape((8, LANES), F32)],
            in_specs=smem(1) + [pl.BlockSpec(memory_space=pltpu.HBM)] * 2,
            out_specs=[any_spec, pl.BlockSpec(memory_space=pltpu.VMEM)],
            scratch_shapes=[
                pltpu.VMEM((2, n_hi, 2, quarter, 2, early_rows, LANES), BF16),
                pltpu.VMEM((plan.flat_rows - base, LANES), F32),
                pltpu.SemaphoreType.DMA((2, n_hi, 2, quarter)),
                pltpu.SemaphoreType.DMA((8,)),
            ],
            compiler_params=params_of,
            cost_estimate=brief,
        )(after(own_s, block_l), near_e, far_e)

        grad, context_grad = pl.pallas_call(
            functools.partial(gradient_kernel, plan),
            out_shape=[shape((plan.shard_rows, LANES), F32), shape(context.shape, BF16)],
            in_specs=smem(1) + vmem(5 + n_hi - 1),
            out_specs=vmem(2),
            scratch_shapes=[pltpu.VMEM((plan.shard_rows + 8, LANES), F32)],
            compiler_params=params_of,
            cost_estimate=brief,
        )(after(own_s, edge), quarters, other_quarters, taken, ctx_same, ctx_cross, *ctx_far)
        near_l, half_done, edge, grad = joint(near_l, half_done, edge, grad)
        near_l = [block_l] + list(near_l)
        all_l = near_l + core_gather(near_l)
        grad = grad.reshape(-1)[:share]
        new_first = 0.5 * first_moment + 0.5 * grad
        new_second = 0.6 * second_moment + 0.4 * grad * grad

        def late(own_ref, *refs):
            late_kernel(plan, own_ref, refs[:n_parts], *refs[n_parts:])

        new_params = pl.pallas_call(
            late,
            out_shape=shape((ROWS_ALL, LANES), F32),
            in_specs=smem(1) + [pl.BlockSpec(memory_space=pltpu.HBM)] * n_parts + vmem(1) + [any_spec],
            out_specs=any_spec,
            scratch_shapes=[
                pltpu.VMEM((2, n_hi, 2, quarter, 2, late_rows, LANES), BF16),
                pltpu.VMEM((plan.row0[plan.early0 - 1] + plan.shard_rows, LANES), F32),
                pltpu.VMEM((SMALL_ROWS, LANES), F32),
                pltpu.SemaphoreType.DMA((2, n_hi, 2, quarter)),
                pltpu.SemaphoreType.DMA((8,)),
            ],
            input_output_aliases={n_parts + 2: 0},
            compiler_params=params_of,
        )(after(own_s, new_first, new_second), *all_l, edge, half_done)

        return out[None], context_grad, new_params.reshape(-1), new_first, new_second

    return per_device


def solution(mesh):
    return jax.shard_map(
        build(mesh),
        mesh=mesh,
        in_specs=(
            P(("dp", "group"), None),
            P(("dp", "group"), None),
            P(("dp", "group"), None, None, None),
            P(("dp", "group"), None, None),
            P(),
            P(),
            P("dp"),
            P("dp"),
            P(("dp", "group"), None, None),
        ),
        out_specs=(P(("dp", "group"), None, None), P(("dp", "group"), None), P(), P("dp"), P("dp")),
        check_vma=False,
    )
```

```python
import functools

import jax
import jax.numpy as jnp
from jax import lax
from jax.experimental import pallas as pl
from jax.experimental.pallas import tpu as pltpu
from jax.sharding import PartitionSpec as P

D_IN = 768
D = 384
HEADS = 12
HD = 32
FF = 1536
GRID = 196
BLOCKS = 4
TMAX = 40
STEP = 10
IMG = 4
CTX = 384
TGT = IMG * BLOCKS * TMAX
L = CTX + TGT
NP = D_IN * D + 4 * D * D + 2 * D * FF + 5 * D
LANES = 128
GROUPS = D // LANES
PER = LANES // HD
WIN = 200
KEYS = WIN + TMAX
WIDE = 256
TILE = 256
MLP_TILE = 512
CHUNK = 768

ROW_IN = 0
ROW_QKV = D_IN * D // LANES
ROW_OUT = ROW_QKV + 3 * D * D // LANES
ROW_UP = ROW_OUT + D * D // LANES
ROW_DOWN = ROW_UP + D * FF // LANES
ROW_SMALL = ROW_DOWN + FF * D // LANES
ROWS_ALL = NP // LANES
SMALL = 5 * D
SMALL_ROWS = SMALL // LANES
SMALL_PAD = 16

norm_eps = 1e-06
mask_value = -1e30
LOG2E = 1.4426950408889634
SCALE = HD**-0.5
F32 = jnp.float32
BF16 = jnp.bfloat16
VMEM_CAP = 64000 * 1024


def dot(a, b):
    return jnp.dot(a, b, preferred_element_type=F32)


def dot_nt(a, b):
    return lax.dot_general(a, b, (((1,), (1,)), ((), ())), preferred_element_type=F32)


def dot_tn(a, b):
    return lax.dot_general(a, b, (((0,), (0,)), ((), ())), preferred_element_type=F32)


def ceil_to(n, m):
    return -(-n // m) * m


class Plan:
    def __init__(self, n_dp, n_group):
        self.n_dp, self.n_group = n_dp, n_group
        self.share = NP // n_dp
        self.row0 = [d * self.share // LANES for d in range(n_dp)]
        self.lane0 = [d * self.share % LANES for d in range(n_dp)]
        most = max(ceil_to(o + self.share, LANES) // LANES for o in self.lane0)
        self.sub = ceil_to(-(-most // (2 * n_group)), 16)
        self.piece = 2 * self.sub
        self.shard_rows = self.piece * n_group
        self.n_hi, self.half = n_group // 2, n_dp // 2
        self.quarter = self.half // 2
        self.early0 = n_dp // 2
        assert self.early0 * self.share >= ROW_OUT * LANES
        self.helper = 2 * (self.half - 1 - self.quarter) + 1
        self.tail = ROW_SMALL - self.row0[-1]
        self.flat_rows = ceil_to(max(r + self.shard_rows for r in self.row0), 16)
        self.mid_rows = ceil_to(self.row0[self.early0 - 1] + self.shard_rows - ROW_OUT, 8)
        self.cut = ceil_to(self.early0 * self.share, 8 * LANES) // LANES


def layer_norm_parts(x):
    mu = jnp.mean(x, axis=-1, keepdims=True)
    xc = x - mu
    rstd = lax.rsqrt(jnp.mean(xc * xc, axis=-1, keepdims=True) + norm_eps)
    return xc * rstd, rstd


def layer_norm_back(dy, gain, xhat, rstd):
    dx = dy * gain
    a = jnp.mean(dx, axis=-1, keepdims=True)
    b = jnp.mean(dx * xhat, axis=-1, keepdims=True)
    return rstd * (dx - a - xhat * b)


def reciprocal(x):
    r = pl.reciprocal(x, approx=True)
    return r * (2.0 - x * r)


def gelu_both(x):
    z = jnp.abs(x) * (0.5**0.5)
    t = reciprocal(1.0 + 0.3275911 * z)
    e = jnp.exp2(x * x * (-0.5 * LOG2E))
    poly = ((((1.061405429 * t - 1.453152027) * t + 1.421413741) * t - 0.284496736) * t + 0.254829592) * t
    tail = 0.5 * poly * e
    cdf = jnp.where(x >= 0, 1.0 - tail, tail)
    pdf = e * 0.3989422804014327
    return x * cdf, cdf + x * pdf


def head_masks(first, count, width):
    lane = lax.broadcasted_iota(jnp.int32, (1, width), 1)
    return [(lane // HD == first + h).astype(F32) for h in range(count)]


def stack_heads(x, masks):
    return jnp.concatenate([x * m for m in masks], axis=0)


def diagonal(x, rows):
    return jnp.concatenate(
        [x[h * HD : (h + 1) * HD, h * rows : (h + 1) * rows] for h in range(PER)], axis=0
    )


def stack_six(x, masks):
    gap = jnp.zeros((WIDE // 2 - 3 * TMAX, WIDE), F32)
    parts = [x * m for m in masks]
    return jnp.concatenate(parts[:3] + [gap] + parts[3:] + [gap], axis=0).astype(BF16)


def fold_six(x, masks):
    total = None
    for h in range(6):
        at = (h // 3) * (WIDE // 2) + (h % 3) * TMAX
        part = x[at : at + TMAX] * masks[h]
        total = part if total is None else total + part
    return total


def half_masks(half):
    lane = lax.broadcasted_iota(jnp.int32, (1, WIDE), 1)
    head = (lane + half * LANES) // HD
    return [(head == 6 * half + h).astype(F32) for h in range(6)]


def half_slice(half, part):
    return pl.ds(pl.multiple_of(part * D + half * LANES, LANES), WIDE)


def lane_slice(g, part):
    return pl.ds(pl.multiple_of(part * D + g * LANES, LANES), LANES)


def prep_kernel(
    plan,
    own_s,
    params_hbm, index_ref, pos_ref,
    vec, own_ref,
    w_in_hbm, w_qkv_hbm, w_out_hbm, w_up_hbm, w_down_hbm, stream_hbm,
    pbuf, w_in_b, w_qkv_b, w_out_b, w_up_b, w_down_b, stream, hot_ref, sems, out_sems,
):
    spans = [
        (ROW_SMALL, SMALL_ROWS), (ROW_IN, ROW_QKV - ROW_IN), (ROW_QKV, ROW_OUT - ROW_QKV),
        (ROW_OUT, ROW_UP - ROW_OUT), (ROW_UP, ROW_DOWN - ROW_UP), (ROW_DOWN, ROW_SMALL - ROW_DOWN),
    ]
    copies = [
        pltpu.make_async_copy(params_hbm.at[pl.ds(r, n)], pbuf.at[pl.ds(r, n)], sems.at[i])
        for i, (r, n) in enumerate(spans)
    ]
    for c in copies:
        c.start()
    outgoing = []

    def send_out(src, dst):
        copy = pltpu.make_async_copy(src, dst, out_sems.at[len(outgoing)])
        copy.start()
        outgoing.append(copy)

    def take(base, rows, tiles, dst, step):
        def body(i, _):
            for c in range(tiles):
                src = pl.ds(base + i * (step * tiles) + c, step, stride=tiles)
                dst[pl.ds(pl.multiple_of(i * step, step), step), c * LANES : (c + 1) * LANES] = pbuf[src, :].astype(BF16)
            return 0
        lax.fori_loop(0, rows // step, body, 0)

    eye = lax.broadcasted_iota(jnp.int32, (TMAX, TMAX), 0) == lax.broadcasted_iota(jnp.int32, (TMAX, TMAX), 1)
    grid_id = lax.broadcasted_iota(jnp.int32, (TMAX, GRID), 1)
    for j in range(IMG * BLOCKS):
        row = index_ref[0, j // BLOCKS, j % BLOCKS : j % BLOCKS + 1, :]
        col = jnp.sum(jnp.where(eye, row, 0), axis=1, keepdims=True)
        hot_ref[j * TMAX : (j + 1) * TMAX, :] = (col == grid_id).astype(F32)

    copies[0].wait()
    vec[...] = jnp.zeros_like(vec)
    for k in range(5):
        for c in range(D // LANES):
            vec[k : k + 1, c * LANES : (c + 1) * LANES] = pbuf[pl.ds(ROW_SMALL + k * 3 + c, 1), :]
    mask_tok = vec[4:5, :]
    pos = pos_ref[...]
    pos_hi = pos.astype(BF16)
    pos_lo = (pos - pos_hi.astype(F32)).astype(BF16)
    for i in range(TGT // 128):
        rows = slice(i * 128, (i + 1) * 128)
        hot = hot_ref[rows, :].astype(BF16)
        stream[rows, :] = mask_tok + (dot(hot, pos_hi) + dot(hot, pos_lo))
    send_out(stream, stream_hbm)

    for n, (base, rows, tiles, dst, out, step) in enumerate((
        (ROW_IN, D_IN, 3, w_in_b, w_in_hbm, 128), (ROW_QKV, D, 9, w_qkv_b, w_qkv_hbm, 128),
        (ROW_OUT, D, 3, w_out_b, w_out_hbm, 128), (ROW_UP, D, 12, w_up_b, w_up_hbm, 128),
        (ROW_DOWN, FF, 3, w_down_b, w_down_hbm, 128),
    )):
        copies[1 + n].wait()
        take(base, rows, tiles, dst, step)
        send_out(dst, out)
    for i in range(2):
        own_ref[i] = pbuf[pl.ds(own_s[8 + i], plan.sub), :]
    for copy in outgoing:
        copy.wait()


def place_pieces(own_s, dst, parts, rows):
    n = len(parts)
    for r, part in enumerate(parts):
        at = pl.multiple_of(lax.rem(own_s[6] + (n - r), n) * rows, 16)
        dst[pl.ds(at, rows), :] = part


def window(seg_s, img):
    return pl.multiple_of(jnp.minimum(seg_s[img] // 8 * 8, CTX - WIN), 8)


def forward_kernel(
    plan,
    len_s, own_s,
    vec, ctx_own, ctx_got, seg_row, cot_hbm,
    w_in_hbm, w_qkv_hbm, w_out_hbm, w_up_hbm, w_down_hbm, target_hbm,
    small_out, keep_ref, send_ref, seg_s,
    out_ref, mid_ref, ctx_hbm, stream_hbm, qkv_hbm, probs_c_hbm, probs_t_hbm, d_mixed_hbm, d_middle_hbm,
    w_in_b, w_qkv_b, w_out_b, w_up_b, w_down_b, ctx, stream, qkv, probs_c, probs_t,
    mixed, mixed_b, d_mixed, d_branch, d_middle, normed, bias, v_t, second, active, d_lift, e_down, gflat, live_col, cot, out_s,
    sems, out_sems,
):
    copies = [
        pltpu.make_async_copy(src, dst, sems.at[i])
        for i, (src, dst) in enumerate((
            (w_in_hbm, w_in_b), (w_qkv_hbm, w_qkv_b), (target_hbm, stream.at[pl.ds(CTX, TGT)]),
            (w_out_hbm, w_out_b), (w_up_hbm, w_up_b), (w_down_hbm, w_down_b), (cot_hbm, cot),
        ))
    ]
    for c in copies:
        c.start()
    outgoing = []

    def send_out(src, dst):
        copy = pltpu.make_async_copy(src, dst, out_sems.at[len(outgoing)])
        copy.start()
        outgoing.append(copy)

    gain1, bias1, gain2, bias2 = [vec[k : k + 1, :] for k in range(4)]
    seg = seg_row[...]
    for i in range(IMG + 1):
        seg_s[i] = jnp.sum((seg < i).astype(jnp.int32))
    row_id = lax.broadcasted_iota(jnp.int32, (CTX, CTX), 0)
    row_image = sum((row_id >= seg_s[i]).astype(jnp.int32) for i in range(1, IMG))
    bias[...] = jnp.where(row_image == seg, 0.0, mask_value)
    live_col[0:CTX, :] = jnp.ones((CTX, LANES), F32)
    slot_id = lax.broadcasted_iota(jnp.int32, (TMAX, LANES), 0)
    for j in range(IMG * BLOCKS):
        live_col[CTX + j * TMAX : CTX + (j + 1) * TMAX, :] = (slot_id < len_s[0, j // BLOCKS, j % BLOCKS]).astype(F32)

    stored = ctx_own.shape[0] // plan.n_group
    first = ctx_own[pl.ds(pl.multiple_of(own_s[6] * stored, 16), stored), :]
    place_pieces(own_s, ctx, [first] + [ref[...] for ref in ctx_got], stored)
    send_out(ctx, ctx_hbm)
    copies[0].wait()
    stream[0:CTX, :] = dot(ctx[...], w_in_b[...])
    copies[2].wait()
    send_out(stream, stream_hbm)
    copies[1].wait()

    def qkv_body(i, _):
        rows = pl.ds(pl.multiple_of(i * TILE, TILE), TILE)
        xhat, _r = layer_norm_parts(stream[rows, :])
        n = (xhat * gain1 + bias1).astype(BF16)
        normed[rows, :] = n
        qkv[rows, :] = dot(n, w_qkv_b[...]).astype(BF16).astype(F32)
        return 0

    lax.fori_loop(0, L // TILE, qkv_body, 0, unroll=4)

    send_out(qkv, qkv_hbm)
    masks = head_masks(0, PER, LANES)
    c2 = SCALE * LOG2E
    for g in range(GROUPS):
        v_t[g * LANES : (g + 1) * LANES, :] = qkv[0:CTX, 2 * D + g * LANES : 2 * D + (g + 1) * LANES].T.astype(BF16)

    def softmax_down(t):
        p = jnp.exp2(t - jnp.max(t, axis=0, keepdims=True))
        return (p * (1.0 / jnp.sum(p, axis=0, keepdims=True))).astype(BF16)

    def ctx_body(i, _):
        g, chunk = i // 3, i % 3
        rows = pl.ds(pl.multiple_of(chunk * LANES, LANES), LANES)
        lanes = pl.ds(pl.multiple_of(g * LANES, LANES), LANES)
        q = stack_heads(qkv[rows, lane_slice(g, 0)], masks).astype(BF16)
        st = dot_nt(qkv[0:CTX, lane_slice(g, 1)].astype(BF16), q)
        for h in range(PER):
            cols = slice(h * LANES, (h + 1) * LANES)
            probs_c[i, :, cols] = softmax_down(st[:, cols] * c2 + bias[:, rows])
        o = dot(v_t[lanes, :], probs_c[i])
        mixed[rows, lanes] = diagonal(o, LANES).T
        return 0

    lax.fori_loop(0, GROUPS * 3, ctx_body, 0, unroll=9)
    send_out(probs_c, probs_c_hbm)

    key_id = lax.broadcasted_iota(jnp.int32, (KEYS, 1), 0)
    mixed[CTX:, :] = jnp.zeros((TGT, D), F32)

    def tgt_body(i, _):
        half, img = i // IMG, i % IMG
        hmasks = half_masks(half)
        first = window(seg_s, img)
        kw = qkv[pl.ds(first, WIN), half_slice(half, 1)]
        vw = qkv[pl.ds(first, WIN), half_slice(half, 2)]
        lo, hi = seg_s[img] - first, seg_s[img + 1] - first
        in_win = (key_id >= lo) & (key_id < hi) & (key_id < WIN)
        units = []
        for blk in range(BLOCKS):
            j = img * BLOCKS + blk
            rows = pl.ds(pl.multiple_of(CTX + j * TMAX, 8), TMAX)
            k = jnp.concatenate([kw, qkv[rows, half_slice(half, 1)]], axis=0).astype(BF16)
            v = jnp.concatenate([vw, qkv[rows, half_slice(half, 2)]], axis=0).astype(BF16)
            q = stack_six(qkv[rows, half_slice(half, 0)], hmasks)
            ok = in_win | ((key_id >= WIN) & (key_id < WIN + len_s[0, img, blk]))
            units.append((rows, v, dot_nt(k, q), jnp.where(ok, 0.0, mask_value)))
        for blk, (rows, v, st, bias_col) in enumerate(units):
            for n in range(2):
                cols = slice(n * LANES, (n + 1) * LANES)
                probs_t[i * BLOCKS + blk, :, cols] = softmax_down(st[:, cols] * c2 + bias_col)
        for blk, (rows, v, st, bias_col) in enumerate(units):
            o = dot_tn(probs_t[i * BLOCKS + blk], v)
            mixed[rows, pl.ds(pl.multiple_of(half * LANES, LANES), WIDE)] += fold_six(o, hmasks)
        return 0

    lax.fori_loop(0, 2 * IMG, tgt_body, 0, unroll=2)
    send_out(probs_t, probs_t_hbm)

    for c in copies[3:]:
        c.wait()

    def mixed_of(rows):
        low = mixed[rows, :].astype(BF16)
        mixed_b[rows, :] = low
        return low

    def block_body(i, carry):
        dg2, db2 = carry
        rows = pl.ds(pl.multiple_of(i * MLP_TILE, MLP_TILE), MLP_TILE)
        live = live_col[rows, 0:1]
        middle = stream[rows, :] + dot(mixed_of(rows), w_out_b[...])
        xhat, rstd = layer_norm_parts(middle)
        sec = (xhat * gain2 + bias2).astype(BF16)
        second[rows, :] = sec
        top = live * cot[rows, :].astype(F32)
        e = top.astype(BF16)
        e_down[rows, :] = e
        out = middle
        d_second = jnp.zeros((MLP_TILE, D), F32)
        for j in range(FF // CHUNK):
            cols = slice(j * CHUNK, (j + 1) * CHUNK)
            lifted = dot(sec, w_up_b[:, cols])
            act, slope = gelu_both(lifted)
            act = act.astype(BF16)
            active[rows, cols] = act
            dl = (dot_nt(e, w_down_b[cols, :]) * slope).astype(BF16)
            d_lift[rows, cols] = dl
            out = out + dot(act, w_down_b[cols, :])
            d_second = d_second + dot_nt(dl, w_up_b[:, cols])
        out_s[rows, :] = (live * out).astype(BF16)
        dm = top + layer_norm_back(d_second, gain2, xhat, rstd)
        d_middle[rows, :] = dm
        db = dm.astype(BF16)
        d_branch[rows, :] = db
        d_mixed[rows, :] = dot_nt(db, w_out_b[...])
        dg2 = dg2 + jnp.sum(d_second * xhat, axis=0, keepdims=True)
        db2 = db2 + jnp.sum(d_second, axis=0, keepdims=True)
        return dg2, db2

    zero = jnp.zeros((1, D), F32)
    dg2, db2 = lax.fori_loop(0, L // MLP_TILE, block_body, (zero, zero))
    small_out[...] = jnp.concatenate([dg2, db2, jnp.zeros((6, D), F32)], axis=0)

    send_out(out_s, out_ref)
    send_out(d_mixed, d_mixed_hbm)
    send_out(d_middle, d_middle_hbm)

    end = ROW_SMALL - ROW_OUT
    gflat[end:, :] = jnp.zeros((gflat.shape[0] - end, LANES), F32)

    g = dot_tn(mixed_b[...], d_branch[...])
    for c in range(3):
        gflat[pl.ds(c, D, stride=3), :] = g[:, c * LANES : (c + 1) * LANES]

    def up_body(j, _):
        cols = pl.ds(pl.multiple_of(j * CHUNK, CHUNK), CHUNK)
        g = dot_tn(second[...], d_lift[:, cols])
        for c in range(CHUNK // LANES):
            gflat[pl.ds(ROW_UP - ROW_OUT + CHUNK // LANES * j + c, D, stride=12), :] = g[:, c * LANES : (c + 1) * LANES]
        return 0

    lax.fori_loop(0, FF // CHUNK, up_body, 0, unroll=True)

    send_out(gflat.at[pl.ds(0, plan.mid_rows)], mid_ref)

    def down_body(j, _):
        cols = pl.ds(pl.multiple_of(j * D, D), D)
        g = dot_tn(active[:, cols], e_down[...])
        for c in range(3):
            gflat[pl.ds(ROW_DOWN - ROW_OUT + j * (3 * D) + c, D, stride=3), :] = g[:, c * LANES : (c + 1) * LANES]
        return 0

    lax.fori_loop(0, 4, down_body, 0, unroll=4)

    store_pieces(plan, gflat, ROW_OUT, range(plan.early0, plan.n_dp), plan.quarter, own_s[1], keep_ref, send_ref)
    for copy in outgoing:
        copy.wait()


def store_pieces(plan, gflat, base, shards, hi0, core, keep_ref, send_ref, extra=None):
    for d in shards:
        for q in range(plan.n_group):
            start = plan.row0[d] - base + q * plan.piece
            blocks = [gflat[start + n * plan.sub : start + (n + 1) * plan.sub, :].astype(BF16) for n in range(2)]

            def put(ref):
                for n in range(2):
                    ref[q // 2, d % 2, d // 2 - hi0, n, 0 : plan.sub, :] = blocks[n]
                    if extra is not None:
                        ref[q // 2, d % 2, d // 2 - hi0, n, plan.sub :, :] = extra

            @pl.when(core == q % 2)
            def _():
                put(keep_ref)

            @pl.when(core != q % 2)
            def _():
                put(send_ref)


def attention_back_kernel(
    plan,
    seg_s, own_s, qkv_hbm, probs_c_hbm, probs_t_hbm, d_mixed_hbm, one_hbm, two_hbm,
    dpk, mine_ref, other_ref, qkv, probs_c, probs_t, d_mixed, d_qkv, k_t, mom, tail, sems,
):
    incoming = {}
    for n, (name, src, dst) in enumerate((
        ("qkv", qkv_hbm, qkv), ("d_mixed", d_mixed_hbm, d_mixed), ("probs_c", probs_c_hbm, probs_c),
        ("probs_t", probs_t_hbm, probs_t),
    )):
        incoming[name] = pltpu.make_async_copy(src, dst, sems.at[n])
        incoming[name].start()

    tail0 = plan.tail // 8 * 8
    moments = []
    for i, src in enumerate((one_hbm, two_hbm)):
        moments.append(pltpu.make_async_copy(src.at[pl.ds(own_s[4], plan.piece + 8)], mom.at[i], sems.at[4 + 2 * i]))
        moments.append(pltpu.make_async_copy(src.at[pl.ds(tail0, 32)], tail.at[i], sems.at[5 + 2 * i]))
    for copy in moments:
        copy.start()

    d_qkv[...] = jnp.zeros_like(d_qkv)
    masks = head_masks(0, PER, LANES)
    incoming["qkv"].wait()
    for g in range(GROUPS):
        k_t[g * LANES : (g + 1) * LANES, :] = qkv[0:CTX, D + g * LANES : D + (g + 1) * LANES].T.astype(BF16)
    incoming["d_mixed"].wait()
    incoming["probs_c"].wait()

    def back_down(p, dp):
        p = p.astype(F32)
        delta = jnp.sum(p * dp, axis=0, keepdims=True)
        return (p * (dp - delta)).astype(BF16)

    def ctx_body(i, _):
        g, chunk = i // 3, i % 3
        rows = pl.ds(pl.multiple_of(chunk * LANES, LANES), LANES)
        lanes = pl.ds(pl.multiple_of(g * LANES, LANES), LANES)
        do = stack_heads(d_mixed[rows, lanes], masks).astype(BF16)
        dpt = dot_nt(qkv[0:CTX, lane_slice(g, 2)].astype(BF16), do)
        ds = []
        for h in range(PER):
            cols = slice(h * LANES, (h + 1) * LANES)
            ds.append(back_down(probs_c[i, :, cols], dpt[:, cols]))
        ds = jnp.concatenate(ds, axis=1)
        q = stack_heads(qkv[rows, lane_slice(g, 0)], masks).astype(BF16)
        d_qkv[rows, lane_slice(g, 0)] = diagonal(dot(k_t[lanes, :], ds), LANES).T
        d_qkv[0:CTX, lane_slice(g, 1)] += dot(ds, q)
        d_qkv[0:CTX, lane_slice(g, 2)] += dot(probs_c[i], do)
        return 0

    lax.fori_loop(0, GROUPS * 3, ctx_body, 0, unroll=3)
    incoming["probs_t"].wait()

    def tgt_body(i, _):
        half, img = i // IMG, i % IMG
        hmasks = half_masks(half)
        first = window(seg_s, img)
        win = pl.ds(first, WIN)
        kw = qkv[win, half_slice(half, 1)]
        vw = qkv[win, half_slice(half, 2)]
        units = []
        for blk in range(BLOCKS):
            rows = pl.ds(pl.multiple_of(CTX + (img * BLOCKS + blk) * TMAX, 8), TMAX)
            v = jnp.concatenate([vw, qkv[rows, half_slice(half, 2)]], axis=0).astype(BF16)
            do = stack_six(d_mixed[rows, pl.ds(pl.multiple_of(half * LANES, LANES), WIDE)], hmasks)
            units.append((rows, do, dot_nt(v, do)))
        dkw = jnp.zeros((WIN, WIDE), F32)
        dvw = jnp.zeros((WIN, WIDE), F32)
        for blk, (rows, do, dpt) in enumerate(units):
            p = probs_t[i * BLOCKS + blk]
            ds = jnp.concatenate(
                [back_down(p[:, n * LANES : (n + 1) * LANES], dpt[:, n * LANES : (n + 1) * LANES]) for n in range(2)],
                axis=1,
            )
            k = jnp.concatenate([kw, qkv[rows, half_slice(half, 1)]], axis=0).astype(BF16)
            q = stack_six(qkv[rows, half_slice(half, 0)], hmasks)
            d_qkv[rows, half_slice(half, 0)] += fold_six(dot_tn(ds, k), hmasks)
            dk = dot(ds, q)
            dv = dot(p, do)
            d_qkv[rows, half_slice(half, 1)] += dk[WIN:]
            d_qkv[rows, half_slice(half, 2)] += dv[WIN:]
            dkw = dkw + dk[:WIN]
            dvw = dvw + dv[:WIN]
        d_qkv[win, half_slice(half, 1)] += dkw
        d_qkv[win, half_slice(half, 2)] += dvw
        return 0

    lax.fori_loop(0, 2 * IMG, tgt_body, 0, unroll=2)
    for copy in moments:
        copy.wait()
    lane = lax.broadcasted_iota(jnp.int32, (1, LANES), 1)
    for i in range(2):
        turned = pltpu.roll(mom[i], own_s[5], 1)
        aligned = jnp.where(lane >= own_s[5], turned[8:], turned[7:-1])
        mine_ref[i] = aligned[: plan.sub]
        other_ref[i, 0 : plan.sub, :] = aligned[plan.sub :]
        turned = pltpu.roll(tail[i], own_s[5], 1)
        aligned = jnp.where(lane >= own_s[5], turned[1:], turned[:-1])
        at = plan.tail - tail0 + 7
        other_ref[i, plan.sub : plan.sub + SMALL_PAD, :] = aligned[at : at + SMALL_PAD]

    def round_body(i, _):
        rows = pl.ds(pl.multiple_of(i * 128, 128), 128)
        dpk[rows, 0 : 2 * D] = (d_qkv[rows, 0 : 2 * D] * SCALE).astype(BF16)
        dpk[rows, 2 * D :] = d_qkv[rows, 2 * D :].astype(BF16)
        return 0

    lax.fori_loop(0, L // 128, round_body, 0, unroll=8)


def backward_kernel(
    plan,
    own_s,
    vec, small_in, dpk,
    mid_hbm, w_in_hbm, w_qkv_hbm, ctx_hbm, stream_hbm, d_middle_hbm,
    keep_ref, send_ref, same_ref, cross_ref,
    w_in_b, w_qkv_b, ctx_ref, stream, d_middle, normed, d_hidden, ctx_grad, small_flat, gflat, sems,
):
    incoming = {}
    for n, (name, src, dst) in enumerate((
        ("w_qkv", w_qkv_hbm, w_qkv_b), ("stream", stream_hbm, stream), ("d_middle", d_middle_hbm, d_middle),
        ("w_in", w_in_hbm, w_in_b), ("ctx", ctx_hbm, ctx_ref),
        ("mid", mid_hbm, gflat.at[pl.ds(ROW_OUT, plan.mid_rows)]),
    )):
        incoming[name] = pltpu.make_async_copy(src, dst, sems.at[n])
        incoming[name].start()
    gain1, bias1 = vec[0:1, :], vec[1:2, :]
    for name in ("w_qkv", "stream", "d_middle"):
        incoming[name].wait()

    def row_body(i, carry):
        dg1, db1, dmask = carry
        rows = pl.ds(pl.multiple_of(i * 128, 128), 128)
        xhat, rstd = layer_norm_parts(stream[rows, :])
        normed[rows, :] = (xhat * gain1 + bias1).astype(BF16)
        d_normed = dot_nt(dpk[rows, :], w_qkv_b[...])
        d_stream = d_middle[rows, :] + layer_norm_back(d_normed, gain1, xhat, rstd)
        dg1 = dg1 + jnp.sum(d_normed * xhat, axis=0, keepdims=True)
        db1 = db1 + jnp.sum(d_normed, axis=0, keepdims=True)
        is_tgt = (i >= CTX // 128).astype(F32)
        dmask = dmask + is_tgt * jnp.sum(d_stream, axis=0, keepdims=True)

        @pl.when(i < CTX // 128)
        def _():
            d_hidden[rows, :] = d_stream.astype(BF16)

        return dg1, db1, dmask

    zero = jnp.zeros((1, D), F32)
    dg1, db1, dmask = lax.fori_loop(0, L // 128, row_body, (zero, zero, zero), unroll=8)
    for k, row in enumerate((dg1, db1, small_in[0:1, :], small_in[1:2, :], dmask)):
        for c in range(3):
            small_flat[3 * k + c : 3 * k + c + 1, :] = row[:, c * LANES : (c + 1) * LANES]
    small_flat[SMALL_ROWS:, :] = jnp.zeros((SMALL_PAD - SMALL_ROWS, LANES), F32)

    incoming["w_in"].wait()
    incoming["ctx"].wait()
    ctx_grad[...] = dot_nt(d_hidden[...], w_in_b[...]).astype(BF16)
    stored = CTX // plan.n_group
    for a in range(plan.n_hi):
        hi = lax.rem(own_s[2] + a, plan.n_hi) * 2
        for ref, core in ((same_ref, own_s[1]), (cross_ref, 1 - own_s[1])):
            ref[a] = ctx_grad[pl.ds(pl.multiple_of((hi + core) * stored, 16), stored), :]
    for j in range(2):
        g = dot_tn(ctx_ref[:, j * D : (j + 1) * D], d_hidden[...])
        for c in range(3):
            gflat[pl.ds(ROW_IN + j * 3 * D + c, D, stride=3), :] = g[:, c * LANES : (c + 1) * LANES]
    def qkv_body(j, _):
        g = dot_tn(normed[...], dpk[:, pl.ds(pl.multiple_of(j * D, D), D)])
        for c in range(3):
            gflat[pl.ds(ROW_QKV + 3 * j + c, D, stride=9), :] = g[:, c * LANES : (c + 1) * LANES]
        return 0

    lax.fori_loop(0, 3, qkv_body, 0)
    incoming["mid"].wait()
    store_pieces(plan, gflat, 0, range(plan.early0), 0, own_s[1], keep_ref, send_ref, small_flat[...].astype(BF16))


def vmem(n):
    return [pl.BlockSpec(memory_space=pltpu.VMEM)] * n


def smem(n):
    return [pl.BlockSpec(memory_space=pltpu.SMEM)] * n


def shape(dims, dtype):
    return jax.ShapeDtypeStruct(dims, dtype)


def fetch_blocks(plan, own_s, refs, rels, dst, sems):
    for i, (ref, (c_rel, a_rel, b_rel)) in enumerate(zip(refs, rels)):
        core = lax.rem(own_s[1] + c_rel, 2)
        hi = lax.rem(own_s[2] + a_rel, plan.n_hi)
        lo = lax.rem(own_s[3] + b_rel, 2)
        for t in range(plan.quarter):
            pltpu.make_async_copy(ref.at[t], dst.at[core, hi, lo, t], sems.at[core, hi, lo, t]).start()


def wait_shard(plan, d, hi0, dst, sems):
    t = d // 2 - hi0
    for core in range(2):
        for hi in range(plan.n_hi):
            at = dst.at[core, hi, d % 2, t]
            pltpu.make_async_copy(at, at, sems.at[core, hi, d % 2, t]).wait()


def put_rows(plan, shards, hi0, src, out, base):
    for d in shards:
        lane0 = plan.lane0[d]
        rows = ceil_to(lane0 + plan.share, LANES) // LANES
        for q in range(plan.n_group):
            for n in range(2):
                start = q * plan.piece + n * plan.sub
                count = min(plan.sub, rows - start)
                if count <= 0:
                    continue
                block = src[q % 2, q // 2, d % 2, d // 2 - hi0, n, 0 : plan.sub, :].astype(F32)
                at = plan.row0[d] + start - base
                if start == 0 and lane0:
                    lane = lax.broadcasted_iota(jnp.int32, (1, LANES), 1)
                    out[at : at + 1, :] = jnp.where(lane < lane0, out[at : at + 1, :], block[0:1])
                    out[at + 1 : at + count, :] = block[1:count]
                else:
                    out[at : at + count, :] = block[:count]


def write_shards(plan, shards, hi0, blocks, fetched, buf, base, out_hbm, done, ends, sems):
    copies = []
    step = max(1, len(shards) // 4)
    for n, d in enumerate(shards):
        wait_shard(plan, d, hi0, blocks, fetched)
        put_rows(plan, [d], hi0, blocks, buf, base)
        if (n + 1) % step == 0 or n + 1 == len(shards):
            upto = ends(d)
            copies.append(pltpu.make_async_copy(
                buf.at[pl.ds(done - base, upto - done)], out_hbm.at[pl.ds(done, upto - done)], sems.at[len(copies)]
            ))
            copies[-1].start()
            done = upto
    return copies


def early_kernel(plan, own_s, near, far, out_hbm, edge_ref, blocks, buf, fetched, sems):
    rels = [(c, a, b) for c in range(2) for b in range(2) for a in range(plan.n_hi)]
    refs = [src.at[i] for src in (near, far) for i in range(2 * plan.n_hi)]
    fetch_blocks(plan, own_s, refs, rels, blocks, fetched)
    base = plan.cut - 8
    buf[0:8, :] = jnp.zeros((8, LANES), F32)
    copies = write_shards(
        plan, range(plan.early0, plan.n_dp), plan.quarter, blocks, fetched, buf, base, out_hbm, plan.cut,
        lambda d: ROW_SMALL if d + 1 == plan.n_dp else plan.row0[d + 1] // 8 * 8, sems,
    )
    edge_ref[...] = buf[0:8, :]
    for copy in copies:
        copy.wait()


def late_kernel(plan, own_s, refs, edge_ref, done_hbm, out_hbm, blocks, buf, tail, fetched, sems):
    rels = [(c, a, b) for c in range(2) for a in range(plan.n_hi) for b in range(2)]
    fetch_blocks(plan, own_s, refs, rels, blocks, fetched)

    def ends(d):
        if d + 1 < plan.early0:
            return plan.row0[d + 1] // 8 * 8
        at, lane0 = plan.row0[d + 1], plan.lane0[d + 1]
        if at < plan.cut:
            lane = lax.broadcasted_iota(jnp.int32, (1, LANES), 1)
            row = lax.broadcasted_iota(jnp.int32, (plan.cut - at, 1), 0)
            mine = buf[at : plan.cut, :]
            buf[at : plan.cut, :] = jnp.where((row == 0) & (lane < lane0), mine, edge_ref[at - plan.cut + 8 :, :])
        return plan.cut

    copies = write_shards(plan, range(plan.early0), 0, blocks, fetched, buf, 0, out_hbm, 0, ends, sems)
    small = blocks[0, 0, plan.helper % 2, plan.helper // 2, 0, plan.sub :, :].astype(F32)
    tail[...] = small[:SMALL_ROWS]
    copies.append(pltpu.make_async_copy(tail, out_hbm.at[pl.ds(ROW_SMALL, SMALL_ROWS)], sems.at[7]))
    copies[-1].start()
    for copy in copies:
        copy.wait()


def gradient_kernel(plan, own_s, same, cross, given, ctx_same, ctx_cross, *rest):
    ctx_far, (grad_ref, ctx_ref, grad) = rest[: plan.n_hi - 1], rest[plan.n_hi - 1 :]
    rows, stored = plan.shard_rows, ctx_ref.shape[0] // plan.n_group
    for a in range(plan.n_hi):
        back = lax.rem(own_s[2] + plan.n_hi - a, plan.n_hi) * 2
        ahead = lax.rem(own_s[2] + a, plan.n_hi) * 2
        for n, core in enumerate((own_s[1], 1 - own_s[1])):
            at = pl.multiple_of((back + core) * stored, 16)
            ctx_ref[pl.ds(at, stored), :] = ctx_far[a - 1][n] if a else (ctx_cross if n else ctx_same)[0]
            at = pl.multiple_of((ahead + core) * plan.piece, 16)
            grad[pl.ds(at, plan.piece), :] = (cross if n else same)[a].astype(F32)
    grad[rows:, :] = jnp.zeros((8, LANES), F32)

    @pl.when(own_s[7] == plan.n_dp - 1)
    def _():
        at = ROW_SMALL - plan.row0[-1]
        grad[at : at + SMALL_ROWS, :] = given[plan.sub :, :].astype(F32)[:SMALL_ROWS]

    lane = lax.broadcasted_iota(jnp.int32, (1, LANES), 1)
    back = LANES - own_s[5]
    for i in range(plan.n_group):
        at = slice(i * plan.piece, (i + 1) * plan.piece)
        turned = pltpu.roll(grad[i * plan.piece : (i + 1) * plan.piece + 8, :], back, 1)
        g = jnp.where(lane < back, turned[: plan.piece], turned[1 : plan.piece + 1])
        grad_ref[at, :] = g


def adam(weight, grad, one, two):
    first = 0.5 * one + 0.5 * grad
    second = 0.6 * two + 0.4 * grad * grad
    step = (first / (1.0 - 0.5**STEP)) / (jnp.sqrt(second / (1.0 - 0.6**STEP)) + 1e-08)
    return weight - 0.05 * (step + 0.05 * weight)


def after(value, *others):
    return lax.optimization_barrier((value, others))[0]


def build(mesh):
    n_dp, n_group = mesh.shape["dp"], mesh.shape["group"]
    plan = Plan(n_dp, n_group)
    both = ("dp", "group")
    n_hi, half, quarter = plan.n_hi, plan.half, plan.quarter
    piece, sub = plan.piece, plan.sub
    any_spec = pl.BlockSpec(memory_space=pl.ANY)
    brief = pl.CostEstimate(flops=0, bytes_accessed=0, transcendentals=0)
    params_of = pltpu.CompilerParams(vmem_limit_bytes=VMEM_CAP)

    def pairs(move):
        out = []
        for d in range(n_dp):
            for g in range(n_group):
                ghi, glo, dhi, dlo = move(g // 2, g % 2, d // 2, d % 2)
                out.append((d * n_group + g, (dhi * 2 + dlo) * n_group + ghi * 2 + glo))
        return out

    core_pairs = pairs(lambda gh, gl, dh, dl: (gh, 1 - gl, dh, dl))
    swap_pairs = pairs(lambda gh, gl, dh, dl: (gh, gl, (dh + quarter) % half, dl))

    def xy_pairs(a, b):
        return pairs(lambda gh, gl, dh, dl: ((gh + a) % n_hi, gl, dh, (dl + b) % 2))

    def z_pairs(r):
        return pairs(lambda gh, gl, dh, dl: (gh, gl, (dh + r) % half, dl))

    def group_pairs(r):
        return [(i, (i + r) % n_group) for i in range(n_group)]

    rels = [(a, b) for a in range(n_hi) for b in range(2)]
    def pick(array, index):
        return lax.dynamic_index_in_dim(array, index, 0, keepdims=False)

    def slot_of(h, early):
        return (h % quarter) * 2 + (h // quarter + early) % 2

    def xy_blocks(keep, got, gh, dl):
        def block(a, b):
            i, j = (gh + a) % n_hi, (dl + b) % 2
            mine, theirs = pick(pick(keep, i), j), pick(pick(got, i), j)
            return (mine.astype(F32) + theirs.astype(F32)).astype(BF16)
        return [block(a, b) for a, b in rels]

    def xy_send(blocks):
        return [lax.ppermute(x, both, xy_pairs(a, b)) for x, (a, b) in zip(blocks[1:], rels[1:])]

    def z_blocks(block, arrived, dh, early):
        total = block.astype(F32)
        for part in arrived:
            total = total + part.astype(F32)
        total = total.astype(BF16)
        total = total.reshape((2 * quarter,) + total.shape[2:])
        return [pick(total, slot_of((dh + r) % half, early)) for r in range(half)]

    def z_send(blocks):
        return [lax.ppermute(x, both, z_pairs(r)) for r, x in enumerate(blocks) if r]

    def z_sum(block, arrived):
        total = block.astype(F32)
        for part in arrived:
            total = total + part.astype(F32)
        return total

    def z_gather(mine):
        return [lax.ppermute(mine, both, z_pairs(r)) for r in range(1, half)]

    def z_order(got, sender, early):
        blocks = []
        for t in range(quarter):
            for n in range(2):
                want = (t + early * quarter + n * quarter) % half
                block = got[0]
                for i in range(1, half):
                    block = jnp.where(sender(i) == want, got[i], block)
                blocks.append(block)
        return jnp.stack(blocks).reshape((quarter, 2) + blocks[0].shape)

    def xy_gather(block):
        return [lax.ppermute(block, both, xy_pairs(-a, -b)) for a, b in rels[1:]]

    def core_gather(blocks):
        return [lax.ppermute(b, both, core_pairs) for b in blocks]

    def per_device(
        context, segment_ids, target_index, target_length, pos_table, params, first_moment, second_moment, cotangent
    ):
        stored = context.shape[0] // n_group
        dp, me = lax.axis_index("dp"), lax.axis_index("group")
        gh, gl, dh, dl = me // 2, me % 2, dp // 2, dp % 2
        share = plan.share

        ctx_got = [
            lax.ppermute(
                lax.dynamic_slice_in_dim(context, (me + r) % n_group * stored, stored), "group", group_pairs(r)
            )
            for r in range(1, n_group)
        ]

        lane0 = (dp * share) % LANES

        def own_row(early):
            t = dh % quarter + early * quarter
            n = (dh // quarter + early) % 2
            return ((t * 2 + dl) * share) // LANES + me * piece + n * sub

        own_s = jnp.stack(
            [0 * me, gl, gh, dl, me * piece, lane0, me, dp, own_row(0), own_row(1)]
        ).astype(jnp.int32)
        params2 = params.reshape(ROWS_ALL, LANES)

        weights = [((D_IN, D), BF16), ((D, 3 * D), BF16), ((D, D), BF16), ((D, FF), BF16), ((FF, D), BF16)]
        prep = pl.pallas_call(
            functools.partial(prep_kernel, plan),
            out_shape=[shape((8, D), F32), shape((2, sub, LANES), F32)]
            + [shape(*w) for w in weights] + [shape((TGT, D), F32)],
            in_specs=smem(1) + [any_spec] + vmem(2),
            out_specs=vmem(2) + [any_spec] * 6,
            scratch_shapes=[pltpu.VMEM((plan.flat_rows, LANES), F32)] + [pltpu.VMEM(*w) for w in weights] + [
                pltpu.VMEM((TGT, D), F32),
                pltpu.VMEM((TGT, GRID), F32),
                pltpu.SemaphoreType.DMA((6,)),
                pltpu.SemaphoreType.DMA((6,)),
            ],
            compiler_params=params_of,
        )(own_s, params2, target_index, pos_table)
        vec, own_w, w_in_b, w_qkv_b, w_out_b, w_up_b, w_down_b, target_rows = prep

        early_rows, late_rows = sub, sub + SMALL_PAD
        n_blocks = 2 * n_hi
        out_specs = [
            shape((8, D), F32),
            shape((n_hi, 2, quarter, 2, early_rows, LANES), BF16),
            shape((n_hi, 2, quarter, 2, early_rows, LANES), BF16),
            shape((8,), jnp.int32),
        ]
        saved = [
            ((CTX, D_IN), BF16),
            ((L, D), F32),
            ((L, 3 * D), F32),
            ((GROUPS * 3, CTX, PER * LANES), BF16),
            ((2 * IMG * BLOCKS, KEYS, WIDE), BF16),
            ((L, D), F32),
            ((L, D), F32),
        ]
        written = [
            ((L, D), BF16),
            ((plan.mid_rows, LANES), F32),
        ] + saved

        def forward(*refs):
            n = 2 + 2
            forward_kernel(plan, *refs[:n], refs[n : n + n_group - 1], *refs[n + n_group - 1 :])

        fwd = pl.pallas_call(
            forward,
            out_shape=out_specs + [shape(*s) for s in written],
            in_specs=smem(2) + vmem(2 + n_group - 1 + 1) + [any_spec] * 7,
            out_specs=vmem(3) + smem(1) + [any_spec] * len(written),
            scratch_shapes=[pltpu.VMEM(*w) for w in weights] + [pltpu.VMEM(*s) for s in saved[:5]] + [
                pltpu.VMEM((L, D), F32),
                pltpu.VMEM((L, D), BF16),
                pltpu.VMEM((L, D), F32),
                pltpu.VMEM((L, D), BF16),
                pltpu.VMEM((L, D), F32),
                pltpu.VMEM((L, D), BF16),
                pltpu.VMEM((CTX, CTX), F32),
                pltpu.VMEM((D, CTX), BF16),
                pltpu.VMEM((L, D), BF16),
                pltpu.VMEM((L, FF), BF16),
                pltpu.VMEM((L, FF), BF16),
                pltpu.VMEM((L, D), BF16),
                pltpu.VMEM((plan.flat_rows - ROW_OUT, LANES), F32),
                pltpu.VMEM((L, LANES), F32),
                pltpu.VMEM((L, D), BF16),
                pltpu.VMEM((L, D), BF16),
                pltpu.SemaphoreType.DMA((7,)),
                pltpu.SemaphoreType.DMA((len(written),)),
            ],
            compiler_params=params_of,
        )(
            target_length, own_s,
            vec, context, *ctx_got, segment_ids, cotangent[0],
            w_in_b, w_qkv_b, w_out_b, w_up_b, w_down_b, target_rows,
        )
        small_in, keep_e, send_e, seg_s, out, mid = fwd[: len(fwd) - len(saved)]
        ctx_s, stream_s, qkv_s, probs_c_s, probs_t_s, d_mixed_s, d_middle_s = fwd[len(fwd) - len(saved) :]

        got_e = lax.ppermute(send_e, both, core_pairs)
        spare = plan.shard_rows * LANES - share
        one2, two2 = [
            jnp.pad(m, (8 * LANES, spare)).reshape(8 + plan.shard_rows, LANES) for m in after((first_moment, second_moment), seg_s)
        ]

        xy_e = xy_blocks(keep_e, got_e, gh, dl)
        xy_got_e = xy_send(xy_e)
        qkv_s = after(qkv_s, *xy_e)

        dpk, own_mom, other_mom = pl.pallas_call(
            functools.partial(attention_back_kernel, plan),
            out_shape=[
                shape((L, 3 * D), BF16), shape((2, sub, LANES), F32), shape((2, sub + SMALL_PAD, LANES), F32),
            ],
            in_specs=smem(2) + [any_spec] * 6,
            out_specs=vmem(3),
            scratch_shapes=[pltpu.VMEM(*s) for s in saved[2:6]] + [
                pltpu.VMEM((L, 3 * D), F32),
                pltpu.VMEM((D, CTX), BF16),
                pltpu.VMEM((2, piece + 8, LANES), F32),
                pltpu.VMEM((2, 32, LANES), F32),
                pltpu.SemaphoreType.DMA((8,)),
            ],
            compiler_params=params_of,
            cost_estimate=pl.CostEstimate(flops=10**10, bytes_accessed=20 * 10**6, transcendentals=0),
        )(seg_s, own_s, qkv_s, probs_c_s, probs_t_s, d_mixed_s, one2, two2)

        xy_got_e = [after(x, dpk) for x in xy_got_e]
        z_e = z_blocks(xy_e[0], xy_got_e, dh, 1)
        z_got_e = z_send(z_e)
        swapped = lax.ppermute(other_mom, both, swap_pairs)
        dpk = after(dpk, *z_e)

        bwd_out = [
            shape((n_hi, 2, quarter, 2, late_rows, LANES), BF16),
            shape((n_hi, 2, quarter, 2, late_rows, LANES), BF16),
            shape((n_hi, stored, D_IN), BF16),
            shape((n_hi, stored, D_IN), BF16),
        ]
        bwd = pl.pallas_call(
            functools.partial(backward_kernel, plan),
            out_shape=bwd_out,
            in_specs=smem(1) + vmem(3) + [any_spec] * 6,
            out_specs=vmem(len(bwd_out)),
            scratch_shapes=[
                pltpu.VMEM((D_IN, D), BF16),
                pltpu.VMEM((D, 3 * D), BF16),
                pltpu.VMEM((CTX, D_IN), BF16),
                pltpu.VMEM((L, D), F32),
                pltpu.VMEM((L, D), F32),
                pltpu.VMEM((L, D), BF16),
                pltpu.VMEM((CTX, D), BF16),
                pltpu.VMEM((CTX, D_IN), BF16),
                pltpu.VMEM((SMALL_PAD, LANES), F32),
                pltpu.VMEM((ROW_OUT + plan.mid_rows, LANES), F32),
                pltpu.SemaphoreType.DMA((6,)),
            ],
            compiler_params=params_of,
            cost_estimate=pl.CostEstimate(flops=5 * 10**9, bytes_accessed=15 * 10**6, transcendentals=0),
        )(own_s, vec, small_in, dpk, mid, w_in_b, w_qkv_b, ctx_s, stream_s, d_middle_s)
        keep_l, send_l, ctx_same, ctx_cross = bwd

        upper = dh // quarter
        own_is_late = upper == 0

        def moments_of(early):
            return jnp.where(upper == early, own_mom, swapped[:, :sub])

        def all_after(values, *others):
            return [after(x, *others) for x in values]

        def joint(*groups):
            return lax.optimization_barrier(groups)

        z_got_e, swapped = joint(all_after(z_got_e, keep_l), after(swapped, keep_l))
        tails = swapped[:, sub:]
        got_l = lax.ppermute(after(send_l, *z_got_e), both, core_pairs)
        own_e = z_sum(z_e[0], z_got_e)
        mom = moments_of(1)
        new_e = adam(own_w[1], own_e, mom[0], mom[1]).astype(BF16)
        ctx_cross = lax.ppermute(after(ctx_cross, *z_got_e), both, core_pairs)
        got_l, ctx_cross, new_e = joint(got_l, ctx_cross, new_e)
        ctx_pairs = [jnp.stack([ctx_same[a], ctx_cross[a]]) for a in range(1, n_hi)]

        xy_l = xy_blocks(keep_l, got_l, gh, dl)
        xy_got_l, z_new_e, own_e = joint(xy_send(xy_l), z_gather(after(new_e, *xy_l)), own_e)

        z_l = z_blocks(xy_l[0], xy_got_l, dh, 0)
        block_e = z_order([new_e] + list(z_new_e), lambda i: (dh - i) % half, 1)[None]
        z_got_l, near_e, ctx_far = joint(
            z_send(z_l), [lax.ppermute(block_e, both, xy_pairs(-a, 0)) for a in range(1, n_hi)],
            [lax.ppermute(after(ctx_pairs[a - 1], *z_l), both, xy_pairs(a, 0)) for a in range(1, n_hi)],
        )
        own_l = z_sum(z_l[0], z_got_l)
        small_sum = own_l[sub:]
        small_w = jnp.pad(params[NP - SMALL :].reshape(SMALL_ROWS, LANES), ((0, SMALL_PAD - SMALL_ROWS), (0, 0)))
        mom = moments_of(0)
        new_l = jnp.concatenate([
            adam(own_w[0], own_l[:sub], mom[0], mom[1]), adam(small_w, small_sum, tails[0], tails[1])
        ]).astype(BF16)

        near_e = jnp.concatenate([block_e] + list(near_e))
        give = jnp.where(own_is_late, own_e, own_l[:sub])
        give = jnp.concatenate([give, small_sum]).astype(BF16)
        have = jnp.where(own_is_late, own_l[:sub], own_e).astype(BF16)
        z_new_l, y_near_e, taken = joint(
            z_gather(new_l), lax.ppermute(near_e, both, xy_pairs(0, 1)), lax.ppermute(give, both, swap_pairs)
        )

        block_l = z_order([new_l] + list(z_new_l), lambda i: (dh - i) % half, 0)
        near_e = jnp.concatenate([near_e, y_near_e])
        near_l = xy_gather(block_l)
        far_e = lax.ppermute(after(near_e, block_l), both, core_pairs)
        own = jnp.concatenate([have, taken[:sub]])
        quarters = jnp.stack(
            [own] + [lax.ppermute(after(own, block_l), both, xy_pairs(-a, 0)) for a in range(1, n_hi)]
        )
        other_quarters = lax.ppermute(quarters, both, core_pairs)

        n_parts = 2 * n_blocks
        base = plan.cut - 8

        half_done, edge = pl.pallas_call(
            functools.partial(early_kernel, plan),
            out_shape=[shape((ROWS_ALL, LANES), F32), shape((8, LANES), F32)],
            in_specs=smem(1) + [pl.BlockSpec(memory_space=pltpu.HBM)] * 2,
            out_specs=[any_spec, pl.BlockSpec(memory_space=pltpu.VMEM)],
            scratch_shapes=[
                pltpu.VMEM((2, n_hi, 2, quarter, 2, early_rows, LANES), BF16),
                pltpu.VMEM((plan.flat_rows - base, LANES), F32),
                pltpu.SemaphoreType.DMA((2, n_hi, 2, quarter)),
                pltpu.SemaphoreType.DMA((8,)),
            ],
            compiler_params=params_of,
            cost_estimate=brief,
        )(after(own_s, block_l), near_e, far_e)

        grad, context_grad = pl.pallas_call(
            functools.partial(gradient_kernel, plan),
            out_shape=[shape((plan.shard_rows, LANES), F32), shape(context.shape, BF16)],
            in_specs=smem(1) + vmem(5 + n_hi - 1),
            out_specs=vmem(2),
            scratch_shapes=[pltpu.VMEM((plan.shard_rows + 8, LANES), F32)],
            compiler_params=params_of,
            cost_estimate=brief,
        )(after(own_s, edge), quarters, other_quarters, taken, ctx_same, ctx_cross, *ctx_far)
        near_l, half_done, edge, grad = joint(near_l, half_done, edge, grad)
        near_l = [block_l] + list(near_l)
        all_l = near_l + core_gather(near_l)
        grad = grad.reshape(-1)[:share]
        new_first = 0.5 * first_moment + 0.5 * grad
        new_second = 0.6 * second_moment + 0.4 * grad * grad

        def late(own_ref, *refs):
            late_kernel(plan, own_ref, refs[:n_parts], *refs[n_parts:])

        new_params = pl.pallas_call(
            late,
            out_shape=shape((ROWS_ALL, LANES), F32),
            in_specs=smem(1) + [pl.BlockSpec(memory_space=pltpu.HBM)] * n_parts + vmem(1) + [any_spec],
            out_specs=any_spec,
            scratch_shapes=[
                pltpu.VMEM((2, n_hi, 2, quarter, 2, late_rows, LANES), BF16),
                pltpu.VMEM((plan.row0[plan.early0 - 1] + plan.shard_rows, LANES), F32),
                pltpu.VMEM((SMALL_ROWS, LANES), F32),
                pltpu.SemaphoreType.DMA((2, n_hi, 2, quarter)),
                pltpu.SemaphoreType.DMA((8,)),
            ],
            input_output_aliases={n_parts + 2: 0},
            compiler_params=params_of,
        )(after(own_s, new_first, new_second), *all_l, edge, half_done)

        return out[None], context_grad, new_params.reshape(-1), new_first, new_second

    return per_device


def solution(mesh):
    return jax.shard_map(
        build(mesh),
        mesh=mesh,
        in_specs=(
            P(("dp", "group"), None),
            P(("dp", "group"), None),
            P(("dp", "group"), None, None, None),
            P(("dp", "group"), None, None),
            P(),
            P(),
            P("dp"),
            P("dp"),
            P(("dp", "group"), None, None),
        ),
        out_specs=(P(("dp", "group"), None, None), P(("dp", "group"), None), P(), P("dp"), P("dp")),
        check_vma=False,
    )
```

```python
import functools

import jax
import jax.numpy as jnp
from jax import lax
from jax.experimental import pallas as pl
from jax.experimental.pallas import tpu as pltpu
from jax.sharding import PartitionSpec as P

D_IN = 768
D = 384
HEADS = 12
HD = 32
FF = 1536
GRID = 196
BLOCKS = 4
TMAX = 40
STEP = 10
IMG = 4
CTX = 384
TGT = IMG * BLOCKS * TMAX
L = CTX + TGT
NP = D_IN * D + 4 * D * D + 2 * D * FF + 5 * D
LANES = 128
GROUPS = D // LANES
PER = LANES // HD
WIN = 200
KEYS = WIN + TMAX
WIDE = 256
TILE = 256
MLP_TILE = 512
CHUNK = 768

ROW_IN = 0
ROW_QKV = D_IN * D // LANES
ROW_OUT = ROW_QKV + 3 * D * D // LANES
ROW_UP = ROW_OUT + D * D // LANES
ROW_DOWN = ROW_UP + D * FF // LANES
ROW_SMALL = ROW_DOWN + FF * D // LANES
ROWS_ALL = NP // LANES
SMALL = 5 * D
SMALL_ROWS = SMALL // LANES
SMALL_PAD = 16

norm_eps = 1e-06
mask_value = -1e30
LOG2E = 1.4426950408889634
SCALE = HD**-0.5
F32 = jnp.float32
BF16 = jnp.bfloat16
VMEM_CAP = 64000 * 1024


def dot(a, b):
    return jnp.dot(a, b, preferred_element_type=F32)


def dot_nt(a, b):
    return lax.dot_general(a, b, (((1,), (1,)), ((), ())), preferred_element_type=F32)


def dot_tn(a, b):
    return lax.dot_general(a, b, (((0,), (0,)), ((), ())), preferred_element_type=F32)


def ceil_to(n, m):
    return -(-n // m) * m


class Plan:
    def __init__(self, n_dp, n_group):
        self.n_dp, self.n_group = n_dp, n_group
        self.share = NP // n_dp
        self.row0 = [d * self.share // LANES for d in range(n_dp)]
        self.lane0 = [d * self.share % LANES for d in range(n_dp)]
        most = max(ceil_to(o + self.share, LANES) // LANES for o in self.lane0)
        self.sub = ceil_to(-(-most // (2 * n_group)), 16)
        self.piece = 2 * self.sub
        self.shard_rows = self.piece * n_group
        self.n_hi, self.half = n_group // 2, n_dp // 2
        self.quarter = self.half // 2
        self.early0 = n_dp // 2
        assert self.early0 * self.share >= ROW_OUT * LANES
        self.helper = 2 * (self.half - 1 - self.quarter) + 1
        self.tail = ROW_SMALL - self.row0[-1]
        self.flat_rows = ceil_to(max(r + self.shard_rows for r in self.row0), 16)
        self.mid_rows = ceil_to(self.row0[self.early0 - 1] + self.shard_rows - ROW_OUT, 8)
        self.cut = ceil_to(self.early0 * self.share, 8 * LANES) // LANES


def layer_norm_parts(x):
    mu = jnp.mean(x, axis=-1, keepdims=True)
    xc = x - mu
    rstd = lax.rsqrt(jnp.mean(xc * xc, axis=-1, keepdims=True) + norm_eps)
    return xc * rstd, rstd


def layer_norm_back(dy, gain, xhat, rstd):
    dx = dy * gain
    a = jnp.mean(dx, axis=-1, keepdims=True)
    b = jnp.mean(dx * xhat, axis=-1, keepdims=True)
    return rstd * (dx - a - xhat * b)


def reciprocal(x):
    r = pl.reciprocal(x, approx=True)
    return r * (2.0 - x * r)


def gelu_both(x):
    z = jnp.abs(x) * (0.5**0.5)
    t = reciprocal(1.0 + 0.3275911 * z)
    e = jnp.exp2(x * x * (-0.5 * LOG2E))
    poly = ((((1.061405429 * t - 1.453152027) * t + 1.421413741) * t - 0.284496736) * t + 0.254829592) * t
    tail = 0.5 * poly * e
    cdf = jnp.where(x >= 0, 1.0 - tail, tail)
    pdf = e * 0.3989422804014327
    return x * cdf, cdf + x * pdf


def head_masks(first, count, width):
    lane = lax.broadcasted_iota(jnp.int32, (1, width), 1)
    return [(lane // HD == first + h).astype(F32) for h in range(count)]


def stack_heads(x, masks):
    return jnp.concatenate([x * m for m in masks], axis=0)


def diagonal(x, rows):
    return jnp.concatenate(
        [x[h * HD : (h + 1) * HD, h * rows : (h + 1) * rows] for h in range(PER)], axis=0
    )


def stack_six(x, masks):
    gap = jnp.zeros((WIDE // 2 - 3 * TMAX, WIDE), F32)
    parts = [x * m for m in masks]
    return jnp.concatenate(parts[:3] + [gap] + parts[3:] + [gap], axis=0).astype(BF16)


def fold_six(x, masks):
    total = None
    for h in range(6):
        at = (h // 3) * (WIDE // 2) + (h % 3) * TMAX
        part = x[at : at + TMAX] * masks[h]
        total = part if total is None else total + part
    return total


def half_masks(half):
    lane = lax.broadcasted_iota(jnp.int32, (1, WIDE), 1)
    head = (lane + half * LANES) // HD
    return [(head == 6 * half + h).astype(F32) for h in range(6)]


def half_slice(half, part):
    return pl.ds(pl.multiple_of(part * D + half * LANES, LANES), WIDE)


def lane_slice(g, part):
    return pl.ds(pl.multiple_of(part * D + g * LANES, LANES), LANES)


def prep_kernel(
    plan,
    own_s,
    params_hbm, index_ref, pos_ref,
    vec, own_ref,
    w_in_hbm, w_qkv_hbm, w_out_hbm, w_up_hbm, w_down_hbm, stream_hbm,
    pbuf, w_in_b, w_qkv_b, w_out_b, w_up_b, w_down_b, stream, hot_ref, sems, out_sems,
):
    spans = [
        (ROW_SMALL, SMALL_ROWS), (ROW_IN, ROW_QKV - ROW_IN), (ROW_QKV, ROW_OUT - ROW_QKV),
        (ROW_OUT, ROW_UP - ROW_OUT), (ROW_UP, ROW_DOWN - ROW_UP), (ROW_DOWN, ROW_SMALL - ROW_DOWN),
    ]
    copies = [
        pltpu.make_async_copy(params_hbm.at[pl.ds(r, n)], pbuf.at[pl.ds(r, n)], sems.at[i])
        for i, (r, n) in enumerate(spans)
    ]
    for c in copies:
        c.start()
    outgoing = []

    def send_out(src, dst):
        copy = pltpu.make_async_copy(src, dst, out_sems.at[len(outgoing)])
        copy.start()
        outgoing.append(copy)

    def take(base, rows, tiles, dst, step):
        def body(i, _):
            for c in range(tiles):
                src = pl.ds(base + i * (step * tiles) + c, step, stride=tiles)
                dst[pl.ds(pl.multiple_of(i * step, step), step), c * LANES : (c + 1) * LANES] = pbuf[src, :].astype(BF16)
            return 0
        lax.fori_loop(0, rows // step, body, 0)

    eye = lax.broadcasted_iota(jnp.int32, (TMAX, TMAX), 0) == lax.broadcasted_iota(jnp.int32, (TMAX, TMAX), 1)
    grid_id = lax.broadcasted_iota(jnp.int32, (TMAX, GRID), 1)
    for j in range(IMG * BLOCKS):
        row = index_ref[0, j // BLOCKS, j % BLOCKS : j % BLOCKS + 1, :]
        col = jnp.sum(jnp.where(eye, row, 0), axis=1, keepdims=True)
        hot_ref[j * TMAX : (j + 1) * TMAX, :] = (col == grid_id).astype(F32)

    copies[0].wait()
    vec[...] = jnp.zeros_like(vec)
    for k in range(5):
        for c in range(D // LANES):
            vec[k : k + 1, c * LANES : (c + 1) * LANES] = pbuf[pl.ds(ROW_SMALL + k * 3 + c, 1), :]
    mask_tok = vec[4:5, :]
    pos = pos_ref[...]
    pos_hi = pos.astype(BF16)
    pos_lo = (pos - pos_hi.astype(F32)).astype(BF16)
    for i in range(TGT // 128):
        rows = slice(i * 128, (i + 1) * 128)
        hot = hot_ref[rows, :].astype(BF16)
        stream[rows, :] = mask_tok + (dot(hot, pos_hi) + dot(hot, pos_lo))
    send_out(stream, stream_hbm)

    for n, (base, rows, tiles, dst, out, step) in enumerate((
        (ROW_IN, D_IN, 3, w_in_b, w_in_hbm, 128), (ROW_QKV, D, 9, w_qkv_b, w_qkv_hbm, 128),
        (ROW_OUT, D, 3, w_out_b, w_out_hbm, 128), (ROW_UP, D, 12, w_up_b, w_up_hbm, 128),
        (ROW_DOWN, FF, 3, w_down_b, w_down_hbm, 128),
    )):
        copies[1 + n].wait()
        take(base, rows, tiles, dst, step)
        send_out(dst, out)
    for i in range(2):
        own_ref[i] = pbuf[pl.ds(own_s[8 + i], plan.sub), :]
    for copy in outgoing:
        copy.wait()


def place_pieces(own_s, dst, parts, rows):
    n = len(parts)
    for r, part in enumerate(parts):
        at = pl.multiple_of(lax.rem(own_s[6] + (n - r), n) * rows, 16)
        dst[pl.ds(at, rows), :] = part


def window(seg_s, img):
    return pl.multiple_of(jnp.minimum(seg_s[img] // 8 * 8, CTX - WIN), 8)


def forward_kernel(
    plan,
    len_s, own_s,
    vec, ctx_own, ctx_got, seg_row, cot_hbm,
    w_in_hbm, w_qkv_hbm, w_out_hbm, w_up_hbm, w_down_hbm, target_hbm,
    small_out, keep_ref, send_ref, seg_s,
    out_ref, mid_ref, ctx_hbm, stream_hbm, qkv_hbm, probs_c_hbm, probs_t_hbm, d_mixed_hbm, d_middle_hbm,
    w_in_b, w_qkv_b, w_out_b, w_up_b, w_down_b, ctx, stream, qkv, probs_c, probs_t,
    mixed, mixed_b, d_mixed, d_branch, d_middle, normed, bias, v_t, second, active, d_lift, e_down, gflat, live_col, cot, out_s,
    sems, out_sems,
):
    copies = [
        pltpu.make_async_copy(src, dst, sems.at[i])
        for i, (src, dst) in enumerate((
            (w_in_hbm, w_in_b), (w_qkv_hbm, w_qkv_b), (target_hbm, stream.at[pl.ds(CTX, TGT)]),
            (w_out_hbm, w_out_b), (w_up_hbm, w_up_b), (w_down_hbm, w_down_b), (cot_hbm, cot),
        ))
    ]
    for c in copies:
        c.start()
    outgoing = []

    def send_out(src, dst):
        copy = pltpu.make_async_copy(src, dst, out_sems.at[len(outgoing)])
        copy.start()
        outgoing.append(copy)

    gain1, bias1, gain2, bias2 = [vec[k : k + 1, :] for k in range(4)]
    seg = seg_row[...]
    for i in range(IMG + 1):
        seg_s[i] = jnp.sum((seg < i).astype(jnp.int32))
    row_id = lax.broadcasted_iota(jnp.int32, (CTX, CTX), 0)
    row_image = sum((row_id >= seg_s[i]).astype(jnp.int32) for i in range(1, IMG))
    bias[...] = jnp.where(row_image == seg, 0.0, mask_value)
    live_col[0:CTX, :] = jnp.ones((CTX, LANES), F32)
    slot_id = lax.broadcasted_iota(jnp.int32, (TMAX, LANES), 0)
    for j in range(IMG * BLOCKS):
        live_col[CTX + j * TMAX : CTX + (j + 1) * TMAX, :] = (slot_id < len_s[0, j // BLOCKS, j % BLOCKS]).astype(F32)

    stored = ctx_own.shape[0] // plan.n_group
    first = ctx_own[pl.ds(pl.multiple_of(own_s[6] * stored, 16), stored), :]
    place_pieces(own_s, ctx, [first] + [ref[...] for ref in ctx_got], stored)
    send_out(ctx, ctx_hbm)
    copies[0].wait()
    stream[0:CTX, :] = dot(ctx[...], w_in_b[...])
    copies[2].wait()
    send_out(stream, stream_hbm)
    copies[1].wait()

    def qkv_body(i, _):
        rows = pl.ds(pl.multiple_of(i * TILE, TILE), TILE)
        xhat, _r = layer_norm_parts(stream[rows, :])
        n = (xhat * gain1 + bias1).astype(BF16)
        normed[rows, :] = n
        qkv[rows, :] = dot(n, w_qkv_b[...]).astype(BF16).astype(F32)
        return 0

    lax.fori_loop(0, L // TILE, qkv_body, 0, unroll=4)

    send_out(qkv, qkv_hbm)
    masks = head_masks(0, PER, LANES)
    c2 = SCALE * LOG2E
    for g in range(GROUPS):
        v_t[g * LANES : (g + 1) * LANES, :] = qkv[0:CTX, 2 * D + g * LANES : 2 * D + (g + 1) * LANES].T.astype(BF16)

    def softmax_down(t):
        p = jnp.exp2(t - jnp.max(t, axis=0, keepdims=True))
        return (p * (1.0 / jnp.sum(p, axis=0, keepdims=True))).astype(BF16)

    def ctx_body(i, _):
        g, chunk = i // 3, i % 3
        rows = pl.ds(pl.multiple_of(chunk * LANES, LANES), LANES)
        lanes = pl.ds(pl.multiple_of(g * LANES, LANES), LANES)
        q = stack_heads(qkv[rows, lane_slice(g, 0)], masks).astype(BF16)
        st = dot_nt(qkv[0:CTX, lane_slice(g, 1)].astype(BF16), q)
        for h in range(PER):
            cols = slice(h * LANES, (h + 1) * LANES)
            probs_c[i, :, cols] = softmax_down(st[:, cols] * c2 + bias[:, rows])
        o = dot(v_t[lanes, :], probs_c[i])
        mixed[rows, lanes] = diagonal(o, LANES).T
        return 0

    lax.fori_loop(0, GROUPS * 3, ctx_body, 0, unroll=9)
    send_out(probs_c, probs_c_hbm)

    key_id = lax.broadcasted_iota(jnp.int32, (KEYS, 1), 0)
    mixed[CTX:, :] = jnp.zeros((TGT, D), F32)

    def tgt_body(i, _):
        half, img = i // IMG, i % IMG
        hmasks = half_masks(half)
        first = window(seg_s, img)
        kw = qkv[pl.ds(first, WIN), half_slice(half, 1)]
        vw = qkv[pl.ds(first, WIN), half_slice(half, 2)]
        lo, hi = seg_s[img] - first, seg_s[img + 1] - first
        in_win = (key_id >= lo) & (key_id < hi) & (key_id < WIN)
        units = []
        for blk in range(BLOCKS):
            j = img * BLOCKS + blk
            rows = pl.ds(pl.multiple_of(CTX + j * TMAX, 8), TMAX)
            k = jnp.concatenate([kw, qkv[rows, half_slice(half, 1)]], axis=0).astype(BF16)
            v = jnp.concatenate([vw, qkv[rows, half_slice(half, 2)]], axis=0).astype(BF16)
            q = stack_six(qkv[rows, half_slice(half, 0)], hmasks)
            ok = in_win | ((key_id >= WIN) & (key_id < WIN + len_s[0, img, blk]))
            units.append((rows, v, dot_nt(k, q), jnp.where(ok, 0.0, mask_value)))
        for blk, (rows, v, st, bias_col) in enumerate(units):
            for n in range(2):
                cols = slice(n * LANES, (n + 1) * LANES)
                probs_t[i * BLOCKS + blk, :, cols] = softmax_down(st[:, cols] * c2 + bias_col)
        for blk, (rows, v, st, bias_col) in enumerate(units):
            o = dot_tn(probs_t[i * BLOCKS + blk], v)
            mixed[rows, pl.ds(pl.multiple_of(half * LANES, LANES), WIDE)] += fold_six(o, hmasks)
        return 0

    lax.fori_loop(0, 2 * IMG, tgt_body, 0, unroll=4)
    send_out(probs_t, probs_t_hbm)

    for c in copies[3:]:
        c.wait()

    def mixed_of(rows):
        low = mixed[rows, :].astype(BF16)
        mixed_b[rows, :] = low
        return low

    def block_body(i, carry):
        dg2, db2 = carry
        rows = pl.ds(pl.multiple_of(i * MLP_TILE, MLP_TILE), MLP_TILE)
        live = live_col[rows, 0:1]
        middle = stream[rows, :] + dot(mixed_of(rows), w_out_b[...])
        xhat, rstd = layer_norm_parts(middle)
        sec = (xhat * gain2 + bias2).astype(BF16)
        second[rows, :] = sec
        top = live * cot[rows, :].astype(F32)
        e = top.astype(BF16)
        e_down[rows, :] = e
        out = middle
        d_second = jnp.zeros((MLP_TILE, D), F32)
        for j in range(FF // CHUNK):
            cols = slice(j * CHUNK, (j + 1) * CHUNK)
            lifted = dot(sec, w_up_b[:, cols])
            act, slope = gelu_both(lifted)
            act = act.astype(BF16)
            active[rows, cols] = act
            dl = (dot_nt(e, w_down_b[cols, :]) * slope).astype(BF16)
            d_lift[rows, cols] = dl
            out = out + dot(act, w_down_b[cols, :])
            d_second = d_second + dot_nt(dl, w_up_b[:, cols])
        out_s[rows, :] = (live * out).astype(BF16)
        dm = top + layer_norm_back(d_second, gain2, xhat, rstd)
        d_middle[rows, :] = dm
        db = dm.astype(BF16)
        d_branch[rows, :] = db
        d_mixed[rows, :] = dot_nt(db, w_out_b[...])
        dg2 = dg2 + jnp.sum(d_second * xhat, axis=0, keepdims=True)
        db2 = db2 + jnp.sum(d_second, axis=0, keepdims=True)
        return dg2, db2

    zero = jnp.zeros((1, D), F32)
    dg2, db2 = lax.fori_loop(0, L // MLP_TILE, block_body, (zero, zero))
    small_out[...] = jnp.concatenate([dg2, db2, jnp.zeros((6, D), F32)], axis=0)

    send_out(out_s, out_ref)
    send_out(d_mixed, d_mixed_hbm)
    send_out(d_middle, d_middle_hbm)

    end = ROW_SMALL - ROW_OUT
    gflat[end:, :] = jnp.zeros((gflat.shape[0] - end, LANES), F32)

    g = dot_tn(mixed_b[...], d_branch[...])
    for c in range(3):
        gflat[pl.ds(c, D, stride=3), :] = g[:, c * LANES : (c + 1) * LANES]

    def up_body(j, _):
        cols = pl.ds(pl.multiple_of(j * CHUNK, CHUNK), CHUNK)
        g = dot_tn(second[...], d_lift[:, cols])
        for c in range(CHUNK // LANES):
            gflat[pl.ds(ROW_UP - ROW_OUT + CHUNK // LANES * j + c, D, stride=12), :] = g[:, c * LANES : (c + 1) * LANES]
        return 0

    lax.fori_loop(0, FF // CHUNK, up_body, 0, unroll=True)

    send_out(gflat.at[pl.ds(0, plan.mid_rows)], mid_ref)

    def down_body(j, _):
        cols = pl.ds(pl.multiple_of(j * D, D), D)
        g = dot_tn(active[:, cols], e_down[...])
        for c in range(3):
            gflat[pl.ds(ROW_DOWN - ROW_OUT + j * (3 * D) + c, D, stride=3), :] = g[:, c * LANES : (c + 1) * LANES]
        return 0

    lax.fori_loop(0, 4, down_body, 0, unroll=4)

    store_pieces(plan, gflat, ROW_OUT, range(plan.early0, plan.n_dp), plan.quarter, own_s[1], keep_ref, send_ref)
    for copy in outgoing:
        copy.wait()


def store_pieces(plan, gflat, base, shards, hi0, core, keep_ref, send_ref, extra=None):
    for d in shards:
        for q in range(plan.n_group):
            start = plan.row0[d] - base + q * plan.piece
            blocks = [gflat[start + n * plan.sub : start + (n + 1) * plan.sub, :].astype(BF16) for n in range(2)]

            def put(ref):
                for n in range(2):
                    ref[q // 2, d % 2, d // 2 - hi0, n, 0 : plan.sub, :] = blocks[n]
                    if extra is not None:
                        ref[q // 2, d % 2, d // 2 - hi0, n, plan.sub :, :] = extra

            @pl.when(core == q % 2)
            def _():
                put(keep_ref)

            @pl.when(core != q % 2)
            def _():
                put(send_ref)


def attention_back_kernel(
    plan,
    seg_s, own_s, qkv_hbm, probs_c_hbm, probs_t_hbm, d_mixed_hbm, one_hbm, two_hbm,
    dpk, mine_ref, other_ref, qkv, probs_c, probs_t, d_mixed, d_qkv, k_t, mom, tail, sems,
):
    incoming = {}
    for n, (name, src, dst) in enumerate((
        ("qkv", qkv_hbm, qkv), ("d_mixed", d_mixed_hbm, d_mixed), ("probs_c", probs_c_hbm, probs_c),
        ("probs_t", probs_t_hbm, probs_t),
    )):
        incoming[name] = pltpu.make_async_copy(src, dst, sems.at[n])
        incoming[name].start()

    tail0 = plan.tail // 8 * 8
    moments = []
    for i, src in enumerate((one_hbm, two_hbm)):
        moments.append(pltpu.make_async_copy(src.at[pl.ds(own_s[4], plan.piece + 8)], mom.at[i], sems.at[4 + 2 * i]))
        moments.append(pltpu.make_async_copy(src.at[pl.ds(tail0, 32)], tail.at[i], sems.at[5 + 2 * i]))
    for copy in moments:
        copy.start()

    d_qkv[...] = jnp.zeros_like(d_qkv)
    masks = head_masks(0, PER, LANES)
    incoming["qkv"].wait()
    for g in range(GROUPS):
        k_t[g * LANES : (g + 1) * LANES, :] = qkv[0:CTX, D + g * LANES : D + (g + 1) * LANES].T.astype(BF16)
    incoming["d_mixed"].wait()
    incoming["probs_c"].wait()

    def back_down(p, dp):
        p = p.astype(F32)
        delta = jnp.sum(p * dp, axis=0, keepdims=True)
        return (p * (dp - delta)).astype(BF16)

    def ctx_body(i, _):
        g, chunk = i // 3, i % 3
        rows = pl.ds(pl.multiple_of(chunk * LANES, LANES), LANES)
        lanes = pl.ds(pl.multiple_of(g * LANES, LANES), LANES)
        do = stack_heads(d_mixed[rows, lanes], masks).astype(BF16)
        dpt = dot_nt(qkv[0:CTX, lane_slice(g, 2)].astype(BF16), do)
        ds = []
        for h in range(PER):
            cols = slice(h * LANES, (h + 1) * LANES)
            ds.append(back_down(probs_c[i, :, cols], dpt[:, cols]))
        ds = jnp.concatenate(ds, axis=1)
        q = stack_heads(qkv[rows, lane_slice(g, 0)], masks).astype(BF16)
        d_qkv[rows, lane_slice(g, 0)] = diagonal(dot(k_t[lanes, :], ds), LANES).T
        d_qkv[0:CTX, lane_slice(g, 1)] += dot(ds, q)
        d_qkv[0:CTX, lane_slice(g, 2)] += dot(probs_c[i], do)
        return 0

    lax.fori_loop(0, GROUPS * 3, ctx_body, 0, unroll=3)
    incoming["probs_t"].wait()

    def tgt_body(i, _):
        half, img = i // IMG, i % IMG
        hmasks = half_masks(half)
        first = window(seg_s, img)
        win = pl.ds(first, WIN)
        kw = qkv[win, half_slice(half, 1)]
        vw = qkv[win, half_slice(half, 2)]
        units = []
        for blk in range(BLOCKS):
            rows = pl.ds(pl.multiple_of(CTX + (img * BLOCKS + blk) * TMAX, 8), TMAX)
            v = jnp.concatenate([vw, qkv[rows, half_slice(half, 2)]], axis=0).astype(BF16)
            do = stack_six(d_mixed[rows, pl.ds(pl.multiple_of(half * LANES, LANES), WIDE)], hmasks)
            units.append((rows, do, dot_nt(v, do)))
        dkw = jnp.zeros((WIN, WIDE), F32)
        dvw = jnp.zeros((WIN, WIDE), F32)
        for blk, (rows, do, dpt) in enumerate(units):
            p = probs_t[i * BLOCKS + blk]
            ds = jnp.concatenate(
                [back_down(p[:, n * LANES : (n + 1) * LANES], dpt[:, n * LANES : (n + 1) * LANES]) for n in range(2)],
                axis=1,
            )
            k = jnp.concatenate([kw, qkv[rows, half_slice(half, 1)]], axis=0).astype(BF16)
            q = stack_six(qkv[rows, half_slice(half, 0)], hmasks)
            d_qkv[rows, half_slice(half, 0)] += fold_six(dot_tn(ds, k), hmasks)
            dk = dot(ds, q)
            dv = dot(p, do)
            d_qkv[rows, half_slice(half, 1)] += dk[WIN:]
            d_qkv[rows, half_slice(half, 2)] += dv[WIN:]
            dkw = dkw + dk[:WIN]
            dvw = dvw + dv[:WIN]
        d_qkv[win, half_slice(half, 1)] += dkw
        d_qkv[win, half_slice(half, 2)] += dvw
        return 0

    lax.fori_loop(0, 2 * IMG, tgt_body, 0, unroll=2)
    for copy in moments:
        copy.wait()
    lane = lax.broadcasted_iota(jnp.int32, (1, LANES), 1)
    for i in range(2):
        turned = pltpu.roll(mom[i], own_s[5], 1)
        aligned = jnp.where(lane >= own_s[5], turned[8:], turned[7:-1])
        mine_ref[i] = aligned[: plan.sub]
        other_ref[i, 0 : plan.sub, :] = aligned[plan.sub :]
        turned = pltpu.roll(tail[i], own_s[5], 1)
        aligned = jnp.where(lane >= own_s[5], turned[1:], turned[:-1])
        at = plan.tail - tail0 + 7
        other_ref[i, plan.sub : plan.sub + SMALL_PAD, :] = aligned[at : at + SMALL_PAD]

    def round_body(i, _):
        rows = pl.ds(pl.multiple_of(i * 128, 128), 128)
        dpk[rows, 0 : 2 * D] = (d_qkv[rows, 0 : 2 * D] * SCALE).astype(BF16)
        dpk[rows, 2 * D :] = d_qkv[rows, 2 * D :].astype(BF16)
        return 0

    lax.fori_loop(0, L // 128, round_body, 0, unroll=8)


def backward_kernel(
    plan,
    own_s,
    vec, small_in, dpk,
    mid_hbm, w_in_hbm, w_qkv_hbm, ctx_hbm, stream_hbm, d_middle_hbm,
    keep_ref, send_ref, same_ref, cross_ref,
    w_in_b, w_qkv_b, ctx_ref, stream, d_middle, normed, d_hidden, ctx_grad, small_flat, gflat, sems,
):
    incoming = {}
    for n, (name, src, dst) in enumerate((
        ("w_qkv", w_qkv_hbm, w_qkv_b), ("stream", stream_hbm, stream), ("d_middle", d_middle_hbm, d_middle),
        ("w_in", w_in_hbm, w_in_b), ("ctx", ctx_hbm, ctx_ref),
        ("mid", mid_hbm, gflat.at[pl.ds(ROW_OUT, plan.mid_rows)]),
    )):
        incoming[name] = pltpu.make_async_copy(src, dst, sems.at[n])
        incoming[name].start()
    gain1, bias1 = vec[0:1, :], vec[1:2, :]
    for name in ("w_qkv", "stream", "d_middle"):
        incoming[name].wait()

    def row_body(i, carry):
        dg1, db1, dmask = carry
        rows = pl.ds(pl.multiple_of(i * 128, 128), 128)
        xhat, rstd = layer_norm_parts(stream[rows, :])
        normed[rows, :] = (xhat * gain1 + bias1).astype(BF16)
        d_normed = dot_nt(dpk[rows, :], w_qkv_b[...])
        d_stream = d_middle[rows, :] + layer_norm_back(d_normed, gain1, xhat, rstd)
        dg1 = dg1 + jnp.sum(d_normed * xhat, axis=0, keepdims=True)
        db1 = db1 + jnp.sum(d_normed, axis=0, keepdims=True)
        is_tgt = (i >= CTX // 128).astype(F32)
        dmask = dmask + is_tgt * jnp.sum(d_stream, axis=0, keepdims=True)

        @pl.when(i < CTX // 128)
        def _():
            d_hidden[rows, :] = d_stream.astype(BF16)

        return dg1, db1, dmask

    zero = jnp.zeros((1, D), F32)
    dg1, db1, dmask = lax.fori_loop(0, L // 128, row_body, (zero, zero, zero), unroll=8)
    for k, row in enumerate((dg1, db1, small_in[0:1, :], small_in[1:2, :], dmask)):
        for c in range(3):
            small_flat[3 * k + c : 3 * k + c + 1, :] = row[:, c * LANES : (c + 1) * LANES]
    small_flat[SMALL_ROWS:, :] = jnp.zeros((SMALL_PAD - SMALL_ROWS, LANES), F32)

    incoming["w_in"].wait()
    incoming["ctx"].wait()
    ctx_grad[...] = dot_nt(d_hidden[...], w_in_b[...]).astype(BF16)
    stored = CTX // plan.n_group
    for a in range(plan.n_hi):
        hi = lax.rem(own_s[2] + a, plan.n_hi) * 2
        for ref, core in ((same_ref, own_s[1]), (cross_ref, 1 - own_s[1])):
            ref[a] = ctx_grad[pl.ds(pl.multiple_of((hi + core) * stored, 16), stored), :]
    for j in range(2):
        g = dot_tn(ctx_ref[:, j * D : (j + 1) * D], d_hidden[...])
        for c in range(3):
            gflat[pl.ds(ROW_IN + j * 3 * D + c, D, stride=3), :] = g[:, c * LANES : (c + 1) * LANES]
    def qkv_body(j, _):
        g = dot_tn(normed[...], dpk[:, pl.ds(pl.multiple_of(j * D, D), D)])
        for c in range(3):
            gflat[pl.ds(ROW_QKV + 3 * j + c, D, stride=9), :] = g[:, c * LANES : (c + 1) * LANES]
        return 0

    lax.fori_loop(0, 3, qkv_body, 0)
    incoming["mid"].wait()
    store_pieces(plan, gflat, 0, range(plan.early0), 0, own_s[1], keep_ref, send_ref, small_flat[...].astype(BF16))


def vmem(n):
    return [pl.BlockSpec(memory_space=pltpu.VMEM)] * n


def smem(n):
    return [pl.BlockSpec(memory_space=pltpu.SMEM)] * n


def shape(dims, dtype):
    return jax.ShapeDtypeStruct(dims, dtype)


def fetch_blocks(plan, own_s, refs, rels, dst, sems):
    for i, (ref, (c_rel, a_rel, b_rel)) in enumerate(zip(refs, rels)):
        core = lax.rem(own_s[1] + c_rel, 2)
        hi = lax.rem(own_s[2] + a_rel, plan.n_hi)
        lo = lax.rem(own_s[3] + b_rel, 2)
        for t in range(plan.quarter):
            pltpu.make_async_copy(ref.at[t], dst.at[core, hi, lo, t], sems.at[core, hi, lo, t]).start()


def wait_shard(plan, d, hi0, dst, sems):
    t = d // 2 - hi0
    for core in range(2):
        for hi in range(plan.n_hi):
            at = dst.at[core, hi, d % 2, t]
            pltpu.make_async_copy(at, at, sems.at[core, hi, d % 2, t]).wait()


def put_rows(plan, shards, hi0, src, out, base):
    for d in shards:
        lane0 = plan.lane0[d]
        rows = ceil_to(lane0 + plan.share, LANES) // LANES
        for q in range(plan.n_group):
            for n in range(2):
                start = q * plan.piece + n * plan.sub
                count = min(plan.sub, rows - start)
                if count <= 0:
                    continue
                block = src[q % 2, q // 2, d % 2, d // 2 - hi0, n, 0 : plan.sub, :].astype(F32)
                at = plan.row0[d] + start - base
                if start == 0 and lane0:
                    lane = lax.broadcasted_iota(jnp.int32, (1, LANES), 1)
                    out[at : at + 1, :] = jnp.where(lane < lane0, out[at : at + 1, :], block[0:1])
                    out[at + 1 : at + count, :] = block[1:count]
                else:
                    out[at : at + count, :] = block[:count]


def write_shards(plan, shards, hi0, blocks, fetched, buf, base, out_hbm, done, ends, sems):
    copies = []
    step = max(1, len(shards) // 4)
    for n, d in enumerate(shards):
        wait_shard(plan, d, hi0, blocks, fetched)
        put_rows(plan, [d], hi0, blocks, buf, base)
        if (n + 1) % step == 0 or n + 1 == len(shards):
            upto = ends(d)
            copies.append(pltpu.make_async_copy(
                buf.at[pl.ds(done - base, upto - done)], out_hbm.at[pl.ds(done, upto - done)], sems.at[len(copies)]
            ))
            copies[-1].start()
            done = upto
    return copies


def early_kernel(plan, own_s, near, far, out_hbm, edge_ref, blocks, buf, fetched, sems):
    rels = [(c, a, b) for c in range(2) for b in range(2) for a in range(plan.n_hi)]
    refs = [src.at[i] for src in (near, far) for i in range(2 * plan.n_hi)]
    fetch_blocks(plan, own_s, refs, rels, blocks, fetched)
    base = plan.cut - 8
    buf[0:8, :] = jnp.zeros((8, LANES), F32)
    copies = write_shards(
        plan, range(plan.early0, plan.n_dp), plan.quarter, blocks, fetched, buf, base, out_hbm, plan.cut,
        lambda d: ROW_SMALL if d + 1 == plan.n_dp else plan.row0[d + 1] // 8 * 8, sems,
    )
    edge_ref[...] = buf[0:8, :]
    for copy in copies:
        copy.wait()


def late_kernel(plan, own_s, refs, edge_ref, done_hbm, out_hbm, blocks, buf, tail, fetched, sems):
    rels = [(c, a, b) for c in range(2) for a in range(plan.n_hi) for b in range(2)]
    fetch_blocks(plan, own_s, refs, rels, blocks, fetched)

    def ends(d):
        if d + 1 < plan.early0:
            return plan.row0[d + 1] // 8 * 8
        at, lane0 = plan.row0[d + 1], plan.lane0[d + 1]
        if at < plan.cut:
            lane = lax.broadcasted_iota(jnp.int32, (1, LANES), 1)
            row = lax.broadcasted_iota(jnp.int32, (plan.cut - at, 1), 0)
            mine = buf[at : plan.cut, :]
            buf[at : plan.cut, :] = jnp.where((row == 0) & (lane < lane0), mine, edge_ref[at - plan.cut + 8 :, :])
        return plan.cut

    copies = write_shards(plan, range(plan.early0), 0, blocks, fetched, buf, 0, out_hbm, 0, ends, sems)
    small = blocks[0, 0, plan.helper % 2, plan.helper // 2, 0, plan.sub :, :].astype(F32)
    tail[...] = small[:SMALL_ROWS]
    copies.append(pltpu.make_async_copy(tail, out_hbm.at[pl.ds(ROW_SMALL, SMALL_ROWS)], sems.at[7]))
    copies[-1].start()
    for copy in copies:
        copy.wait()


def gradient_kernel(plan, own_s, same, cross, given, ctx_same, ctx_cross, *rest):
    ctx_far, (grad_ref, ctx_ref, grad) = rest[: plan.n_hi - 1], rest[plan.n_hi - 1 :]
    rows, stored = plan.shard_rows, ctx_ref.shape[0] // plan.n_group
    for a in range(plan.n_hi):
        back = lax.rem(own_s[2] + plan.n_hi - a, plan.n_hi) * 2
        ahead = lax.rem(own_s[2] + a, plan.n_hi) * 2
        for n, core in enumerate((own_s[1], 1 - own_s[1])):
            at = pl.multiple_of((back + core) * stored, 16)
            ctx_ref[pl.ds(at, stored), :] = ctx_far[a - 1][n] if a else (ctx_cross if n else ctx_same)[0]
            at = pl.multiple_of((ahead + core) * plan.piece, 16)
            grad[pl.ds(at, plan.piece), :] = (cross if n else same)[a].astype(F32)
    grad[rows:, :] = jnp.zeros((8, LANES), F32)

    @pl.when(own_s[7] == plan.n_dp - 1)
    def _():
        at = ROW_SMALL - plan.row0[-1]
        grad[at : at + SMALL_ROWS, :] = given[plan.sub :, :].astype(F32)[:SMALL_ROWS]

    lane = lax.broadcasted_iota(jnp.int32, (1, LANES), 1)
    back = LANES - own_s[5]
    for i in range(plan.n_group):
        at = slice(i * plan.piece, (i + 1) * plan.piece)
        turned = pltpu.roll(grad[i * plan.piece : (i + 1) * plan.piece + 8, :], back, 1)
        g = jnp.where(lane < back, turned[: plan.piece], turned[1 : plan.piece + 1])
        grad_ref[at, :] = g


def adam(weight, grad, one, two):
    first = 0.5 * one + 0.5 * grad
    second = 0.6 * two + 0.4 * grad * grad
    step = (first / (1.0 - 0.5**STEP)) / (jnp.sqrt(second / (1.0 - 0.6**STEP)) + 1e-08)
    return weight - 0.05 * (step + 0.05 * weight)


def after(value, *others):
    return lax.optimization_barrier((value, others))[0]


def build(mesh):
    n_dp, n_group = mesh.shape["dp"], mesh.shape["group"]
    plan = Plan(n_dp, n_group)
    both = ("dp", "group")
    n_hi, half, quarter = plan.n_hi, plan.half, plan.quarter
    piece, sub = plan.piece, plan.sub
    any_spec = pl.BlockSpec(memory_space=pl.ANY)
    brief = pl.CostEstimate(flops=0, bytes_accessed=0, transcendentals=0)
    params_of = pltpu.CompilerParams(vmem_limit_bytes=VMEM_CAP)

    def pairs(move):
        out = []
        for d in range(n_dp):
            for g in range(n_group):
                ghi, glo, dhi, dlo = move(g // 2, g % 2, d // 2, d % 2)
                out.append((d * n_group + g, (dhi * 2 + dlo) * n_group + ghi * 2 + glo))
        return out

    core_pairs = pairs(lambda gh, gl, dh, dl: (gh, 1 - gl, dh, dl))
    swap_pairs = pairs(lambda gh, gl, dh, dl: (gh, gl, (dh + quarter) % half, dl))

    def xy_pairs(a, b):
        return pairs(lambda gh, gl, dh, dl: ((gh + a) % n_hi, gl, dh, (dl + b) % 2))

    def z_pairs(r):
        return pairs(lambda gh, gl, dh, dl: (gh, gl, (dh + r) % half, dl))

    def group_pairs(r):
        return [(i, (i + r) % n_group) for i in range(n_group)]

    rels = [(a, b) for a in range(n_hi) for b in range(2)]
    def pick(array, index):
        return lax.dynamic_index_in_dim(array, index, 0, keepdims=False)

    def slot_of(h, early):
        return (h % quarter) * 2 + (h // quarter + early) % 2

    def xy_blocks(keep, got, gh, dl):
        def block(a, b):
            i, j = (gh + a) % n_hi, (dl + b) % 2
            mine, theirs = pick(pick(keep, i), j), pick(pick(got, i), j)
            return (mine.astype(F32) + theirs.astype(F32)).astype(BF16)
        return [block(a, b) for a, b in rels]

    def xy_send(blocks):
        return [lax.ppermute(x, both, xy_pairs(a, b)) for x, (a, b) in zip(blocks[1:], rels[1:])]

    def z_blocks(block, arrived, dh, early):
        total = block.astype(F32)
        for part in arrived:
            total = total + part.astype(F32)
        total = total.astype(BF16)
        total = total.reshape((2 * quarter,) + total.shape[2:])
        return [pick(total, slot_of((dh + r) % half, early)) for r in range(half)]

    def z_send(blocks):
        return [lax.ppermute(x, both, z_pairs(r)) for r, x in enumerate(blocks) if r]

    def z_sum(block, arrived):
        total = block.astype(F32)
        for part in arrived:
            total = total + part.astype(F32)
        return total

    def z_gather(mine):
        return [lax.ppermute(mine, both, z_pairs(r)) for r in range(1, half)]

    def z_order(got, sender, early):
        blocks = []
        for t in range(quarter):
            for n in range(2):
                want = (t + early * quarter + n * quarter) % half
                block = got[0]
                for i in range(1, half):
                    block = jnp.where(sender(i) == want, got[i], block)
                blocks.append(block)
        return jnp.stack(blocks).reshape((quarter, 2) + blocks[0].shape)

    def xy_gather(block):
        return [lax.ppermute(block, both, xy_pairs(-a, -b)) for a, b in rels[1:]]

    def core_gather(blocks):
        return [lax.ppermute(b, both, core_pairs) for b in blocks]

    def per_device(
        context, segment_ids, target_index, target_length, pos_table, params, first_moment, second_moment, cotangent
    ):
        stored = context.shape[0] // n_group
        dp, me = lax.axis_index("dp"), lax.axis_index("group")
        gh, gl, dh, dl = me // 2, me % 2, dp // 2, dp % 2
        share = plan.share

        ctx_got = [
            lax.ppermute(
                lax.dynamic_slice_in_dim(context, (me + r) % n_group * stored, stored), "group", group_pairs(r)
            )
            for r in range(1, n_group)
        ]

        lane0 = (dp * share) % LANES

        def own_row(early):
            t = dh % quarter + early * quarter
            n = (dh // quarter + early) % 2
            return ((t * 2 + dl) * share) // LANES + me * piece + n * sub

        own_s = jnp.stack(
            [0 * me, gl, gh, dl, me * piece, lane0, me, dp, own_row(0), own_row(1)]
        ).astype(jnp.int32)
        params2 = params.reshape(ROWS_ALL, LANES)

        weights = [((D_IN, D), BF16), ((D, 3 * D), BF16), ((D, D), BF16), ((D, FF), BF16), ((FF, D), BF16)]
        prep = pl.pallas_call(
            functools.partial(prep_kernel, plan),
            out_shape=[shape((8, D), F32), shape((2, sub, LANES), F32)]
            + [shape(*w) for w in weights] + [shape((TGT, D), F32)],
            in_specs=smem(1) + [any_spec] + vmem(2),
            out_specs=vmem(2) + [any_spec] * 6,
            scratch_shapes=[pltpu.VMEM((plan.flat_rows, LANES), F32)] + [pltpu.VMEM(*w) for w in weights] + [
                pltpu.VMEM((TGT, D), F32),
                pltpu.VMEM((TGT, GRID), F32),
                pltpu.SemaphoreType.DMA((6,)),
                pltpu.SemaphoreType.DMA((6,)),
            ],
            compiler_params=params_of,
        )(own_s, params2, target_index, pos_table)
        vec, own_w, w_in_b, w_qkv_b, w_out_b, w_up_b, w_down_b, target_rows = prep

        early_rows, late_rows = sub, sub + SMALL_PAD
        n_blocks = 2 * n_hi
        out_specs = [
            shape((8, D), F32),
            shape((n_hi, 2, quarter, 2, early_rows, LANES), BF16),
            shape((n_hi, 2, quarter, 2, early_rows, LANES), BF16),
            shape((8,), jnp.int32),
        ]
        saved = [
            ((CTX, D_IN), BF16),
            ((L, D), F32),
            ((L, 3 * D), F32),
            ((GROUPS * 3, CTX, PER * LANES), BF16),
            ((2 * IMG * BLOCKS, KEYS, WIDE), BF16),
            ((L, D), F32),
            ((L, D), F32),
        ]
        written = [
            ((L, D), BF16),
            ((plan.mid_rows, LANES), F32),
        ] + saved

        def forward(*refs):
            n = 2 + 2
            forward_kernel(plan, *refs[:n], refs[n : n + n_group - 1], *refs[n + n_group - 1 :])

        fwd = pl.pallas_call(
            forward,
            out_shape=out_specs + [shape(*s) for s in written],
            in_specs=smem(2) + vmem(2 + n_group - 1 + 1) + [any_spec] * 7,
            out_specs=vmem(3) + smem(1) + [any_spec] * len(written),
            scratch_shapes=[pltpu.VMEM(*w) for w in weights] + [pltpu.VMEM(*s) for s in saved[:5]] + [
                pltpu.VMEM((L, D), F32),
                pltpu.VMEM((L, D), BF16),
                pltpu.VMEM((L, D), F32),
                pltpu.VMEM((L, D), BF16),
                pltpu.VMEM((L, D), F32),
                pltpu.VMEM((L, D), BF16),
                pltpu.VMEM((CTX, CTX), F32),
                pltpu.VMEM((D, CTX), BF16),
                pltpu.VMEM((L, D), BF16),
                pltpu.VMEM((L, FF), BF16),
                pltpu.VMEM((L, FF), BF16),
                pltpu.VMEM((L, D), BF16),
                pltpu.VMEM((plan.flat_rows - ROW_OUT, LANES), F32),
                pltpu.VMEM((L, LANES), F32),
                pltpu.VMEM((L, D), BF16),
                pltpu.VMEM((L, D), BF16),
                pltpu.SemaphoreType.DMA((7,)),
                pltpu.SemaphoreType.DMA((len(written),)),
            ],
            compiler_params=params_of,
        )(
            target_length, own_s,
            vec, context, *ctx_got, segment_ids, cotangent[0],
            w_in_b, w_qkv_b, w_out_b, w_up_b, w_down_b, target_rows,
        )
        small_in, keep_e, send_e, seg_s, out, mid = fwd[: len(fwd) - len(saved)]
        ctx_s, stream_s, qkv_s, probs_c_s, probs_t_s, d_mixed_s, d_middle_s = fwd[len(fwd) - len(saved) :]

        got_e = lax.ppermute(send_e, both, core_pairs)
        spare = plan.shard_rows * LANES - share
        one2, two2 = [
            jnp.pad(m, (8 * LANES, spare)).reshape(8 + plan.shard_rows, LANES) for m in after((first_moment, second_moment), seg_s)
        ]

        xy_e = xy_blocks(keep_e, got_e, gh, dl)
        xy_got_e = xy_send(xy_e)
        qkv_s = after(qkv_s, *xy_e)

        dpk, own_mom, other_mom = pl.pallas_call(
            functools.partial(attention_back_kernel, plan),
            out_shape=[
                shape((L, 3 * D), BF16), shape((2, sub, LANES), F32), shape((2, sub + SMALL_PAD, LANES), F32),
            ],
            in_specs=smem(2) + [any_spec] * 6,
            out_specs=vmem(3),
            scratch_shapes=[pltpu.VMEM(*s) for s in saved[2:6]] + [
                pltpu.VMEM((L, 3 * D), F32),
                pltpu.VMEM((D, CTX), BF16),
                pltpu.VMEM((2, piece + 8, LANES), F32),
                pltpu.VMEM((2, 32, LANES), F32),
                pltpu.SemaphoreType.DMA((8,)),
            ],
            compiler_params=params_of,
            cost_estimate=pl.CostEstimate(flops=10**10, bytes_accessed=20 * 10**6, transcendentals=0),
        )(seg_s, own_s, qkv_s, probs_c_s, probs_t_s, d_mixed_s, one2, two2)

        xy_got_e = [after(x, dpk) for x in xy_got_e]
        z_e = z_blocks(xy_e[0], xy_got_e, dh, 1)
        z_got_e = z_send(z_e)
        swapped = lax.ppermute(other_mom, both, swap_pairs)
        dpk = after(dpk, *z_e)

        bwd_out = [
            shape((n_hi, 2, quarter, 2, late_rows, LANES), BF16),
            shape((n_hi, 2, quarter, 2, late_rows, LANES), BF16),
            shape((n_hi, stored, D_IN), BF16),
            shape((n_hi, stored, D_IN), BF16),
        ]
        bwd = pl.pallas_call(
            functools.partial(backward_kernel, plan),
            out_shape=bwd_out,
            in_specs=smem(1) + vmem(3) + [any_spec] * 6,
            out_specs=vmem(len(bwd_out)),
            scratch_shapes=[
                pltpu.VMEM((D_IN, D), BF16),
                pltpu.VMEM((D, 3 * D), BF16),
                pltpu.VMEM((CTX, D_IN), BF16),
                pltpu.VMEM((L, D), F32),
                pltpu.VMEM((L, D), F32),
                pltpu.VMEM((L, D), BF16),
                pltpu.VMEM((CTX, D), BF16),
                pltpu.VMEM((CTX, D_IN), BF16),
                pltpu.VMEM((SMALL_PAD, LANES), F32),
                pltpu.VMEM((ROW_OUT + plan.mid_rows, LANES), F32),
                pltpu.SemaphoreType.DMA((6,)),
            ],
            compiler_params=params_of,
            cost_estimate=pl.CostEstimate(flops=5 * 10**9, bytes_accessed=15 * 10**6, transcendentals=0),
        )(own_s, vec, small_in, dpk, mid, w_in_b, w_qkv_b, ctx_s, stream_s, d_middle_s)
        keep_l, send_l, ctx_same, ctx_cross = bwd

        upper = dh // quarter
        own_is_late = upper == 0

        def moments_of(early):
            return jnp.where(upper == early, own_mom, swapped[:, :sub])

        def all_after(values, *others):
            return [after(x, *others) for x in values]

        def joint(*groups):
            return lax.optimization_barrier(groups)

        z_got_e, swapped = joint(all_after(z_got_e, keep_l), after(swapped, keep_l))
        tails = swapped[:, sub:]
        got_l = lax.ppermute(after(send_l, *z_got_e), both, core_pairs)
        own_e = z_sum(z_e[0], z_got_e)
        mom = moments_of(1)
        new_e = adam(own_w[1], own_e, mom[0], mom[1]).astype(BF16)
        ctx_cross = lax.ppermute(after(ctx_cross, *z_got_e), both, core_pairs)
        got_l, ctx_cross, new_e = joint(got_l, ctx_cross, new_e)
        ctx_pairs = [jnp.stack([ctx_same[a], ctx_cross[a]]) for a in range(1, n_hi)]

        xy_l = xy_blocks(keep_l, got_l, gh, dl)
        xy_got_l, z_new_e, own_e = joint(xy_send(xy_l), z_gather(after(new_e, *xy_l)), own_e)

        z_l = z_blocks(xy_l[0], xy_got_l, dh, 0)
        block_e = z_order([new_e] + list(z_new_e), lambda i: (dh - i) % half, 1)[None]
        z_got_l, near_e, ctx_far = joint(
            z_send(z_l), [lax.ppermute(block_e, both, xy_pairs(-a, 0)) for a in range(1, n_hi)],
            [lax.ppermute(after(ctx_pairs[a - 1], *z_l), both, xy_pairs(a, 0)) for a in range(1, n_hi)],
        )
        own_l = z_sum(z_l[0], z_got_l)
        small_sum = own_l[sub:]
        small_w = jnp.pad(params[NP - SMALL :].reshape(SMALL_ROWS, LANES), ((0, SMALL_PAD - SMALL_ROWS), (0, 0)))
        mom = moments_of(0)
        new_l = jnp.concatenate([
            adam(own_w[0], own_l[:sub], mom[0], mom[1]), adam(small_w, small_sum, tails[0], tails[1])
        ]).astype(BF16)

        near_e = jnp.concatenate([block_e] + list(near_e))
        give = jnp.where(own_is_late, own_e, own_l[:sub])
        give = jnp.concatenate([give, small_sum]).astype(BF16)
        have = jnp.where(own_is_late, own_l[:sub], own_e).astype(BF16)
        z_new_l, y_near_e, taken = joint(
            z_gather(new_l), lax.ppermute(near_e, both, xy_pairs(0, 1)), lax.ppermute(give, both, swap_pairs)
        )

        block_l = z_order([new_l] + list(z_new_l), lambda i: (dh - i) % half, 0)
        near_e = jnp.concatenate([near_e, y_near_e])
        near_l = xy_gather(block_l)
        far_e = lax.ppermute(after(near_e, block_l), both, core_pairs)
        own = jnp.concatenate([have, taken[:sub]])
        quarters = jnp.stack(
            [own] + [lax.ppermute(after(own, block_l), both, xy_pairs(-a, 0)) for a in range(1, n_hi)]
        )
        other_quarters = lax.ppermute(quarters, both, core_pairs)

        n_parts = 2 * n_blocks
        base = plan.cut - 8

        half_done, edge = pl.pallas_call(
            functools.partial(early_kernel, plan),
            out_shape=[shape((ROWS_ALL, LANES), F32), shape((8, LANES), F32)],
            in_specs=smem(1) + [pl.BlockSpec(memory_space=pltpu.HBM)] * 2,
            out_specs=[any_spec, pl.BlockSpec(memory_space=pltpu.VMEM)],
            scratch_shapes=[
                pltpu.VMEM((2, n_hi, 2, quarter, 2, early_rows, LANES), BF16),
                pltpu.VMEM((plan.flat_rows - base, LANES), F32),
                pltpu.SemaphoreType.DMA((2, n_hi, 2, quarter)),
                pltpu.SemaphoreType.DMA((8,)),
            ],
            compiler_params=params_of,
            cost_estimate=brief,
        )(after(own_s, block_l), near_e, far_e)

        grad, context_grad = pl.pallas_call(
            functools.partial(gradient_kernel, plan),
            out_shape=[shape((plan.shard_rows, LANES), F32), shape(context.shape, BF16)],
            in_specs=smem(1) + vmem(5 + n_hi - 1),
            out_specs=vmem(2),
            scratch_shapes=[pltpu.VMEM((plan.shard_rows + 8, LANES), F32)],
            compiler_params=params_of,
            cost_estimate=brief,
        )(after(own_s, edge), quarters, other_quarters, taken, ctx_same, ctx_cross, *ctx_far)
        near_l, half_done, edge, grad = joint(near_l, half_done, edge, grad)
        near_l = [block_l] + list(near_l)
        all_l = near_l + core_gather(near_l)
        grad = grad.reshape(-1)[:share]
        new_first = 0.5 * first_moment + 0.5 * grad
        new_second = 0.6 * second_moment + 0.4 * grad * grad

        def late(own_ref, *refs):
            late_kernel(plan, own_ref, refs[:n_parts], *refs[n_parts:])

        new_params = pl.pallas_call(
            late,
            out_shape=shape((ROWS_ALL, LANES), F32),
            in_specs=smem(1) + [pl.BlockSpec(memory_space=pltpu.HBM)] * n_parts + vmem(1) + [any_spec],
            out_specs=any_spec,
            scratch_shapes=[
                pltpu.VMEM((2, n_hi, 2, quarter, 2, late_rows, LANES), BF16),
                pltpu.VMEM((plan.row0[plan.early0 - 1] + plan.shard_rows, LANES), F32),
                pltpu.VMEM((SMALL_ROWS, LANES), F32),
                pltpu.SemaphoreType.DMA((2, n_hi, 2, quarter)),
                pltpu.SemaphoreType.DMA((8,)),
            ],
            input_output_aliases={n_parts + 2: 0},
            compiler_params=params_of,
        )(after(own_s, new_first, new_second), *all_l, edge, half_done)

        return out[None], context_grad, new_params.reshape(-1), new_first, new_second

    return per_device


def solution(mesh):
    return jax.shard_map(
        build(mesh),
        mesh=mesh,
        in_specs=(
            P(("dp", "group"), None),
            P(("dp", "group"), None),
            P(("dp", "group"), None, None, None),
            P(("dp", "group"), None, None),
            P(),
            P(),
            P("dp"),
            P("dp"),
            P(("dp", "group"), None, None),
        ),
        out_specs=(P(("dp", "group"), None, None), P(("dp", "group"), None), P(), P("dp"), P("dp")),
        check_vma=False,
    )
```
